32 devices in a mesh: wide: 8 (over z, y), narrow: 4 (over x, core).
Axes of the slice: x: 2, y: 2, z: 4, core: 2. Of those that a mesh axis runs over, the one named last changes fastest.
Arguments:
- tokens: bfloat16 [16384, 320], P(('wide', 'narrow')), may hold values from -6 to 6
- cotangent: bfloat16 [16384, 320], P(('wide', 'narrow')), may hold values from -6 to 6
- img_rows: int32 [64], P(('wide', 'narrow')), may hold values from 0 to 32, as said below
- img_cols: int32 [64], P(('wide', 'narrow')), may hold values from 0 to 32, as said below
- q_weight: bfloat16 [320, 320], P('narrow', 'wide'), may hold values from -0.3125 to 0.3125
- kv_weight: bfloat16 [320, 640], P('narrow', 'wide'), may hold values from -0.3125 to 0.3125
- reduce_weight: bfloat16 [1280, 320], P('narrow', 'wide'), may hold values from -0.15625 to 0.15625
- proj_weight: bfloat16 [320, 320], P('narrow', 'wide'), may hold values from -2 to 2
- up_weight: bfloat16 [320, 1280], P('narrow', 'wide'), may hold values from -0.3125 to 0.3125
- down_weight: bfloat16 [1280, 320], P('narrow', 'wide'), may hold values from -0.15625 to 0.15625
- vec_model: bfloat16 [11, 320], P(None, 'narrow'), may hold values from -1.3 to 2.1, as said below
- vec_hidden: bfloat16 [11, 1280], P(None, 'narrow'), may hold values from -1.4 to 1.4, as said below
Outputs:
- mixed: bfloat16 [16384, 320], P(('wide', 'narrow'))
- token_grad: bfloat16 [16384, 320], P(('wide', 'narrow'))
- q_grad: float32 [320, 320], P('narrow', 'wide')
- kv_grad: float32 [320, 640], P('narrow', 'wide')
- reduce_grad: float32 [1280, 320], P('narrow', 'wide')
- proj_grad: float32 [320, 320], P('narrow', 'wide')
- up_grad: float32 [320, 1280], P('narrow', 'wide')
- down_grad: float32 [1280, 320], P('narrow', 'wide')
- model_vec_grad: float32 [11, 320], P(None, 'narrow')
- hidden_vec_grad: float32 [11, 1280], P(None, 'narrow')
The draws below stay inside these ranges and needn't reach their ends.
Inputs may be any that keep to these rules, and one draw needn't show every extreme that they name: `img_rows`: each device holds two image slots (consecutive entries). Rows and columns are even multiples of 2; the two images of a device cover at most 512 patches, exactly 512 on some device; the first slot is never empty, an empty second slot has 0 rows and 0 columns. `img_cols`: columns of the same slots. `vec_model`: gains near 1, biases of order a few tenths. `vec_hidden`: biases and taps of order a few tenths.
All inputs are finite; a program needn't handle non-finite values.
Results may differ from the reference program's by a relative error of at most 0.019.
Values may be sent and summed in bfloat16 or wider, within the bound.
No kernel may reach another device: no remote copies, remote signals or barrier semaphores. Data moves between devices by JAX's collectives and lax.ppermute only.
A program may use at most 128 MiB of HBM per device.

```python
import jax
import jax.numpy as jnp
from jax import lax

D = 320
HEADS = 5
FF = 1280
UNIT = 2
CAP = 512
TOKENS = 16384
IMAGES = 64


def layout_pairs(key):
    table = jnp.array([[8, 8, 8, 8], [6, 10, 10, 6], [10, 6, 6, 10], [8, 16, 0, 0], [16, 8, 0, 0], [8, 8, 6, 10], [10, 6, 8, 8], [6, 10, 0, 0], [8, 8, 0, 0], [10, 12, 0, 0]], jnp.int32)
    groups = IMAGES // 2
    picked = jax.random.randint(jax.random.fold_in(key, 3), (groups,), 0, 10)
    placing = jax.random.permutation(jax.random.fold_in(key, 5), groups)
    picked = picked.at[placing[0]].set(0).at[placing[1]].set(4).at[placing[2]].set(3)
    return table[picked] * UNIT


def draw_img_rows(key, part):
    shapes = layout_pairs(key)
    return jnp.stack([shapes[:, 0], shapes[:, 2]], axis=1).reshape(-1).astype(jnp.int32)


def draw_img_cols(key, part):
    shapes = layout_pairs(key)
    return jnp.stack([shapes[:, 1], shapes[:, 3]], axis=1).reshape(-1).astype(jnp.int32)


def draw_vec_model(key, part):
    key = jax.random.fold_in(key, 7)
    gain_rows = jnp.array([1, 0, 0, 0, 0, 1, 0, 0, 1, 0, 0], jnp.float32)[:, None]
    noise = jnp.clip(jax.random.normal(key, (11, D), jnp.float32), -4.0, 4.0)
    values = gain_rows * (1.0 + 0.25 * noise) + (1.0 - gain_rows) * 0.3 * noise
    return values.astype(jnp.bfloat16)


def draw_vec_hidden(key, part):
    key = jax.random.fold_in(key, 11)
    scales = jnp.array([0.3, 0.3] + [1.0 / 3.0] * 9, jnp.float32)[:, None]
    noise = jnp.clip(jax.random.normal(key, (11, FF), jnp.float32), -4.0, 4.0)
    return (scales * noise).astype(jnp.bfloat16)


def steps_of(own_key, shape, shards, least, high):
    loudness = 1.0
    for dim, parts in shards:
        steps = jax.random.uniform(jax.random.fold_in(jax.random.fold_in(own_key, 6), dim), (parts,), jnp.float32, least / len(shards), high / len(shards))
        loudness = loudness * jnp.repeat(jnp.exp(steps), shape[dim] // parts).reshape((-1,) + (1,) * (len(shape) - 1 - dim))
    return loudness


def gaussian(stream_key, dims, scale, most, cuts=(), kind=jnp.bfloat16):
    values = jax.random.normal(stream_key, dims, jnp.float32) * scale
    if len(cuts) > 0:
        values = steps_of(stream_key, dims, cuts, -0.22, 0.18) * values
    return jnp.clip(values, min=-most, max=most).astype(kind)


def setup_inputs(seed: int = 0) -> dict:
    streams_of = jax.random.split(jax.random.key(seed), 13)
    return {
        "tokens": gaussian(streams_of[0], (TOKENS, D), 1.0, 6.0, ((0, 32),)),
        "cotangent": gaussian(streams_of[1], (TOKENS, D), 1.0, 6.0, ((0, 32),)),
        "img_rows": draw_img_rows(jax.random.fold_in(streams_of[12], 71), 0),
        "img_cols": draw_img_cols(jax.random.fold_in(streams_of[12], 71), 0),
        "q_weight": gaussian(streams_of[4], (D, D), D ** -0.5, 0.3125, ((0, 4), (1, 8))),
        "kv_weight": gaussian(streams_of[5], (D, 2 * D), D ** -0.5, 0.3125, ((0, 4), (1, 8))),
        "reduce_weight": gaussian(streams_of[6], (4 * D, D), (4 * D) ** -0.5, 0.15625, ((0, 4), (1, 8))),
        "proj_weight": gaussian(streams_of[7], (D, D), (D // 32) ** -0.5, 2.0, ((0, 4), (1, 8))),
        "up_weight": gaussian(streams_of[8], (D, FF), D ** -0.5, 0.3125, ((0, 4), (1, 8))),
        "down_weight": gaussian(streams_of[9], (FF, D), FF ** -0.5, 0.15625, ((0, 4), (1, 8))),
        "vec_model": draw_vec_model(jax.random.fold_in(streams_of[12], 71), 0),
        "vec_hidden": draw_vec_hidden(jax.random.fold_in(streams_of[12], 71), 0),
    }


EPSILON = 1e-06
MASKED = -1000000000.0
HIGHEST = lax.Precision.HIGHEST

@jax.custom_vjp
def low(v):
    return lax.optimization_barrier(v.astype(jnp.bfloat16)).astype(jnp.float32)

@jax.custom_vjp
def low_back(v):
    return v

def low_keep(v):
    return (low(v), None)

def low_pass(kept, grad):
    return (grad,)

def back_keep(v):
    return (v, None)

def back_low(kept, grad):
    return (low(grad),)
low.defvjp(low_keep, low_pass)
low_back.defvjp(back_keep, back_low)

def arrange(rows_dev, cols_dev, capacity):
    areas = rows_dev * cols_dev
    position = jnp.arange(capacity, dtype=jnp.int32)
    in_first = position < areas[0]
    in_second = jnp.logical_and(position >= areas[0], position < areas[0] + areas[1])
    image_id = jnp.where(in_first, 0, jnp.where(in_second, 1, -1)).astype(jnp.int32)
    widths = jnp.maximum(jnp.where(in_second, cols_dev[1], cols_dev[0]), 2).astype(jnp.int32)
    heights = jnp.where(in_second, rows_dev[1], rows_dev[0]).astype(jnp.int32)
    local_pos = position - jnp.where(in_second, areas[0], 0).astype(jnp.int32)
    row_of = local_pos // widths
    col_of = local_pos % widths
    near_index = []
    near_valid = []
    for step_row in (-1, 0, 1):
        for step_col in (-1, 0, 1):
            new_row = row_of + step_row
            new_col = col_of + step_col
            inside = (image_id >= 0) & (new_row >= 0) & (new_row < heights) & (new_col >= 0) & (new_col < widths)
            near_index.append(jnp.clip(position + step_row * widths + step_col, 0, capacity - 1).astype(jnp.int32))
            near_valid.append(inside)
    key_pos = jnp.arange(capacity // 4, dtype=jnp.int32)
    quarters = areas // 4
    key_first = key_pos < quarters[0]
    key_second = (key_pos >= quarters[0]) & (key_pos < quarters[0] + quarters[1])
    key_image = jnp.where(key_first, 0, jnp.where(key_second, 1, -2)).astype(jnp.int32)
    key_width = jnp.maximum(jnp.where(key_second, cols_dev[1], cols_dev[0]), 2).astype(jnp.int32)
    key_local = key_pos - jnp.where(key_second, quarters[0], 0).astype(jnp.int32)
    half_width = key_width // 2
    corner = jnp.where(key_second, areas[0], 0).astype(jnp.int32) + 2 * (key_local // half_width) * key_width + 2 * (key_local % half_width)
    key_taps = jnp.stack([jnp.clip(corner, 0, capacity - 1), jnp.clip(corner + 1, 0, capacity - 1), jnp.clip(corner + key_width, 0, capacity - 1), jnp.clip(corner + key_width + 1, 0, capacity - 1)]).astype(jnp.int32)
    patch_slot = (jnp.where(in_second, quarters[0], 0).astype(jnp.int32) + row_of // 2 * (widths // 2) + col_of // 2) * 4 + row_of % 2 * 2 + col_of % 2
    patch_slot = jnp.clip(patch_slot, 0, capacity - 1).astype(jnp.int32)
    return (image_id, jnp.stack(near_index), jnp.stack(near_valid), key_image, key_taps, patch_slot)

def matmul(left, right):
    return jnp.dot(left, right, precision=HIGHEST)

def norm_rows(values, gain, shift_bias):
    centre = values - lax.optimization_barrier(jnp.mean(values, axis=-1, keepdims=True))
    spread_sq = lax.optimization_barrier(jnp.mean(centre * centre, axis=-1, keepdims=True))
    return centre * lax.rsqrt(spread_sq + EPSILON) * gain + shift_bias

def pack_forward(tokens_dev, rows_dev, cols_dev, weights):
    w_query, w_keyval, w_reduce, w_proj, w_up, w_down, model_vecs, hidden_vecs = weights
    capacity, width = tokens_dev.shape
    image_id, near_index, near_valid, key_image, key_taps, patch_slot = arrange(rows_dev, cols_dev, capacity)
    head_dim = width // HEADS
    h_one = low(norm_rows(tokens_dev, model_vecs[0], model_vecs[1]))
    query = low(low_back(matmul(h_one, w_query) + model_vecs[2]))
    patches = jnp.concatenate([h_one[key_taps[tap_index]] for tap_index in range(4)], axis=1)
    reduced = low_back(matmul(patches, w_reduce) + model_vecs[4])
    key_norm = low(norm_rows(reduced, model_vecs[5], model_vecs[6]))
    keyval = matmul(key_norm, w_keyval)
    keys = low(low_back(keyval[:, :width]))
    values = low(low_back(keyval[:, width:] + model_vecs[3]))
    query_heads = query.reshape(capacity, HEADS, head_dim)
    key_heads = keys.reshape(-1, HEADS, head_dim)
    value_heads = values.reshape(-1, HEADS, head_dim)
    scores = jnp.einsum('qhd,khd->hqk', query_heads, key_heads, precision=HIGHEST) * head_dim ** (-0.5)
    live = image_id[:, None] == key_image[None, :]
    scores = low_back(jnp.where(live[None], scores, MASKED))
    expo = jnp.exp(scores - lax.optimization_barrier(jnp.max(scores, axis=-1, keepdims=True)))
    probs = low(expo / lax.optimization_barrier(jnp.sum(expo, axis=-1, keepdims=True)))
    attended = jnp.einsum('hqk,khd->qhd', probs, value_heads, precision=HIGHEST).reshape(capacity, width)
    attended = low(low_back(attended))
    attn_out = low_back(matmul(attended, w_proj) + model_vecs[7])
    x_two = tokens_dev + attn_out
    h_two = low(norm_rows(x_two, model_vecs[8], model_vecs[9]))
    f_one = low_back(matmul(h_two, w_up) + hidden_vecs[0])
    conv = hidden_vecs[1] + jnp.zeros_like(f_one)
    for tap_index in range(9):
        conv = conv + hidden_vecs[2 + tap_index] * jnp.where(near_valid[tap_index][:, None], f_one[near_index[tap_index]], 0.0)
    activ = low(0.5 * conv * (1.0 + lax.erf(conv * 2.0 ** (-0.5))))
    ffn_out = matmul(activ, w_down) + model_vecs[10]
    return jnp.where((image_id >= 0)[:, None], x_two + ffn_out, 0.0)

def reference(tokens, cotangent, img_rows, img_cols, q_weight, kv_weight, reduce_weight, proj_weight, up_weight, down_weight, vec_model, vec_hidden):
    groups = tokens.shape[0] // CAP
    token_packs = tokens.astype(jnp.float32).reshape(groups, CAP, D)
    rows_packs = img_rows.reshape(groups, 2).astype(jnp.int32)
    cols_packs = img_cols.reshape(groups, 2).astype(jnp.int32)
    weights = (q_weight.astype(jnp.float32), kv_weight.astype(jnp.float32), reduce_weight.astype(jnp.float32), proj_weight.astype(jnp.float32), up_weight.astype(jnp.float32), down_weight.astype(jnp.float32), vec_model.astype(jnp.float32), vec_hidden.astype(jnp.float32))

    def whole(packs, params):

        def one_pack(item):
            return jax.checkpoint(pack_forward)(item[0], item[1], item[2], params)
        return lax.map(one_pack, (packs, rows_packs, cols_packs))
    result, pullback = jax.vjp(whole, token_packs, weights)
    token_cot, weight_cots = pullback(cotangent.astype(jnp.float32).reshape(groups, CAP, D))
    return (result.reshape(-1, D).astype(jnp.bfloat16), token_cot.reshape(-1, D).astype(jnp.bfloat16), weight_cots[0], weight_cots[1], weight_cots[2], weight_cots[3], weight_cots[4], weight_cots[5], weight_cots[6], weight_cots[7])
```

```python
import functools
import math

import jax
import jax.numpy as jnp
from jax import lax
from jax.experimental import pallas as pl
from jax.experimental.pallas import tpu as pltpu
from jax.sharding import PartitionSpec as P

HEADS = 5
EPSILON = 1e-06
MASKED = -1000000000.0
F32 = jnp.float32
BF16 = jnp.bfloat16

PARTS_W = 8
PARTS_N = 4
SLOTS = 16
TILE = 32
CHUNK = 256
PAD = 40


def dot_nn(left, right):
    return jnp.dot(left, right, preferred_element_type=F32)


def dot_nt(left, right):
    return lax.dot_general(left, right, (((1,), (1,)), ((), ())), preferred_element_type=F32)


def dot_tn(left, right):
    return lax.dot_general(left, right, (((0,), (0,)), ((), ())), preferred_element_type=F32)


def lanes(*parts):
    return jnp.concatenate(parts, axis=1)


def rows_of(*parts):
    return jnp.concatenate(parts, axis=0)


def my_index(tuned):
    if not tuned:
        return jnp.int32(0)
    return lax.axis_index("wide") * PARTS_N + lax.axis_index("narrow")


def slot_of(device, me):
    delta = device ^ me
    return ((delta >> 1) & 3) * 4 + (delta >> 3)


def normalise(values):
    centre = values - jnp.mean(values, axis=-1, keepdims=True)
    inverse = lax.rsqrt(jnp.mean(centre * centre, axis=-1, keepdims=True) + EPSILON)
    return centre * inverse, inverse


def normalise_back(grad, normed, inverse, gain):
    scaled = grad * gain
    first = jnp.mean(scaled, axis=-1, keepdims=True)
    second = jnp.mean(scaled * normed, axis=-1, keepdims=True)
    return (scaled - first - normed * second) * inverse


def column_sum(values):
    return jnp.sum(values, axis=0, keepdims=True)


def piece_of(own_ref, other_ref, device, me):
    slot = slot_of(device, me)
    mine = ((device ^ me) & 1) == 0
    return jnp.where(mine, own_ref[slot].astype(F32), other_ref[slot].astype(F32))


def token_geometry(rows_ref, cols_ref, capacity, width):
    row0, row1, col0, col1 = rows_ref[0], rows_ref[1], cols_ref[0], cols_ref[1]
    area0, area1 = row0 * col0, row1 * col1
    position = lax.broadcasted_iota(jnp.int32, (capacity, width), 0)
    first = position < area0
    second = jnp.logical_and(position >= area0, position < area0 + area1)
    widths = jnp.maximum(jnp.where(second, col1, col0), 2)
    heights = jnp.where(second, row1, row0)
    local = position - jnp.where(second, area0, 0)
    row = ((local.astype(F32) + 0.5) / widths.astype(F32)).astype(jnp.int32)
    col = local - row * widths
    return first, second, row, col, heights, widths


def pack_kernel(q_ref, kv_ref, red_ref, proj_ref, up_ref, down_ref, vm_ref, vh_ref, a_ref, b_ref, v_ref):
    cw = q_ref.shape[1]

    def turned(ref):
        return ref[...].astype(F32).T

    kv = turned(kv_ref)
    a_ref[...] = lanes(turned(red_ref), turned(q_ref), kv[:cw], kv[cw:], turned(proj_ref)).astype(BF16)
    up = turned(up_ref)
    b_ref[...] = lanes(turned(down_ref), *[up[cw * e : cw * e + cw] for e in range(4)]).astype(BF16)
    v_ref[...] = jnp.zeros_like(v_ref)
    both = lanes(vm_ref[...].astype(F32), vh_ref[...].astype(F32))
    v_ref[: both.shape[0], : both.shape[1]] = both.astype(BF16)


def attend_kernel(
    tuned,
    rows_ref, cols_ref, tok_ref, own_ref, oth_ref, vec_ref,
    x2_ref, h1_ref, n1_ref, r1_ref, patch_ref, nk_ref, rk_ref, kn_ref, q_ref, kb_ref, vb_ref,
    p_ref, o_ref, wr_ref, wq_ref, wkv_ref, wp_ref, mv_ref, hv_ref,
    score_ref,
):
    me = my_index(tuned)
    capacity, width = tok_ref.shape
    cw, rn = width // PARTS_W, width // PARTS_N
    keys = capacity // 4
    dim = width // HEADS

    pieces = [vec_ref[n ^ (me & 3)].astype(F32) for n in range(PARTS_N)]
    mv = lanes(*[p[:, :rn] for p in pieces])
    mv_ref[...] = mv
    hv_ref[...] = lanes(*[p[:, rn : 5 * rn] for p in pieces])

    for pair in range(PARTS_W // 2):
        got = [
            [piece_of(own_ref, oth_ref, w * PARTS_N + n, me) for n in range(PARTS_N)]
            for w in (2 * pair, 2 * pair + 1)
        ]
        at = pl.ds(pair * 2 * cw, 2 * cw)
        for n in range(PARTS_N):
            wr_ref[n, at, :] = rows_of(got[0][n][:, :width], got[1][n][:, :width]).astype(BF16)

        def unit(w, k):
            return lanes(*[got[w][n][:, width + k * rn : width + (k + 1) * rn] for n in range(PARTS_N)])

        wq_ref[at, :] = rows_of(unit(0, 0), unit(1, 0)).astype(BF16)
        wkv_ref[pl.ds(pair * 4 * cw, 4 * cw), :] = rows_of(
            unit(0, 1), unit(0, 2), unit(1, 1), unit(1, 2)
        ).astype(BF16)
        wp_ref[at, :] = rows_of(unit(0, 3), unit(1, 3)).astype(BF16)

    normed, inverse = normalise(tok_ref[...].astype(F32))
    n1_ref[...] = normed
    r1_ref[...] = inverse
    h1 = (normed * mv[0:1] + mv[1:2]).astype(BF16)
    h1_ref[...] = h1
    q = (dot_nt(h1, wq_ref[...]) + mv[2:3]).astype(BF16)
    q_ref[...] = q

    chosen = one_hot(rows_ref, cols_ref, capacity)
    patches = dot_nn(chosen, h1).astype(BF16)
    patch_ref[...] = patches
    reduced = mv[4:5]
    for n in range(4):
        reduced = reduced + dot_nt(patches[n * keys : (n + 1) * keys], wr_ref[n])
    nk, rk = normalise(reduced)
    nk_ref[...] = nk
    rk_ref[...] = rk
    kn = (nk * mv[5:6] + mv[6:7]).astype(BF16)
    kn_ref[...] = kn
    kv = dot_nt(kn, wkv_ref[...])
    k = kv[:, :width].astype(BF16).astype(F32)
    v = (kv[:, width:] + mv[3:4]).astype(BF16).astype(F32)
    lane = lax.broadcasted_iota(jnp.int32, (keys, width), 1)
    for h in range(HEADS):
        inside = (lane >= h * dim) & (lane < (h + 1) * dim)
        at = pl.ds(h * keys, keys)
        kb_ref[at, :] = jnp.where(inside, k, 0.0).astype(BF16)
        vb_ref[at, :] = jnp.where(inside, v, 0.0).astype(BF16)

    score_ref[...] = dot_nt(q, kb_ref[...]) * dim ** (-0.5)
    area0 = rows_ref[0] * cols_ref[0]
    area1 = rows_ref[1] * cols_ref[1]

    def soften(i, carry):
        at = pl.ds(pl.multiple_of(i * 64, 64), 64)
        token = lax.broadcasted_iota(jnp.int32, (64, keys), 0) + i * 64
        key = lax.broadcasted_iota(jnp.int32, (64, keys), 1)
        quarter0, quarter1 = area0 // 4, area1 // 4
        live = ((token < area0) & (key < quarter0)) | (
            (token >= area0) & (token < area0 + area1) & (key >= quarter0) & (key < quarter0 + quarter1)
        )
        for h in range(HEADS):
            lane_at = pl.ds(h * keys, keys)
            s = jnp.where(live, score_ref[at, lane_at], MASKED)
            e = jnp.exp(s - jnp.max(s, axis=-1, keepdims=True))
            p_ref[at, lane_at] = e / jnp.sum(e, axis=-1, keepdims=True)
        return carry

    lax.fori_loop(0, capacity // 64, soften, 0)
    o = dot_nn(p_ref[...].astype(BF16), vb_ref[...]).astype(BF16)
    o_ref[...] = o
    x2_ref[...] = tok_ref[...].astype(F32) + dot_nt(o, wp_ref[...]) + mv[7:8]


def one_hot(rows_ref, cols_ref, capacity):
    row0, row1, col0, col1 = rows_ref[0], rows_ref[1], cols_ref[0], cols_ref[1]
    area0, area1 = row0 * col0, row1 * col1
    quarter0, quarter1 = area0 // 4, area1 // 4
    keys = capacity // 4
    index = lax.broadcasted_iota(jnp.int32, (capacity, 128), 0)
    tap = index // keys
    key = index - tap * keys
    first = key < quarter0
    second = jnp.logical_and(key >= quarter0, key < quarter0 + quarter1)
    width = jnp.maximum(jnp.where(second, col1, col0), 2)
    half = width // 2
    local = key - jnp.where(second, quarter0, 0)
    row = ((local.astype(F32) + 0.5) / half.astype(F32)).astype(jnp.int32)
    col = local - row * half
    token = jnp.where(second, area0, 0) + (2 * row + tap // 2) * width + 2 * col + tap % 2
    token = jnp.where(first | second, token, -1)
    lane = lax.broadcasted_iota(jnp.int32, (capacity, 128), 1)
    return lanes(
        *[jnp.where(token == lane + t * 128, 1.0, 0.0).astype(BF16) for t in range(capacity // 128)]
    )


def ffn_kernel(
    tuned,
    rows_ref, cols_ref, x2_ref, cot_ref, own_ref, oth_ref, mv_ref, hv_ref,
    mixed_ref, gown_ref, gsend_ref, dx2_ref, mg_ref, hg_ref,
    wu_ref, wd_ref, mask_ref, n2_ref, r2_ref, h2_ref, h2t_ref, gy_ref, gyt_ref,
    f_ref, gm_ref, gp_ref, dc_ref, ul_ref, ur_ref, g0_ref, slope_ref, act_ref, u0_ref, df_ref, da_ref,
    mix_ref, dh2_ref, upg_ref, dng_ref,
):
    me = my_index(tuned)
    capacity, width = x2_ref.shape
    hidden = hv_ref.shape[1]
    cw, rn = width // PARTS_W, width // PARTS_N
    tiles = capacity // TILE

    for pair in range(PARTS_W // 2):
        got = [
            [piece_of(own_ref, oth_ref, w * PARTS_N + n, me) for n in range(PARTS_N)]
            for w in (2 * pair, 2 * pair + 1)
        ]
        wd_ref[pl.ds(pair * 2 * cw, 2 * cw), :] = lanes(
            *[rows_of(got[0][n][:, :width], got[1][n][:, :width]) for n in range(PARTS_N)]
        ).astype(BF16)

        def unit(w, k):
            return lanes(*[got[w][n][:, width + k * rn : width + (k + 1) * rn] for n in range(PARTS_N)])

        wu_ref[pl.ds(pair * 8 * cw, 8 * cw), :] = rows_of(
            *[unit(w, k) for w in range(2) for k in range(4)]
        ).astype(BF16)

    first, second, row, col, heights, widths = token_geometry(rows_ref, cols_ref, capacity, 128)
    live = first | second
    conditions = (
        live & (col > 0),
        live & (col < widths - 1),
        first & (row > 0),
        second & (row > 0),
        first & (row < heights - 1),
        second & (row < heights - 1),
        live,
    )
    for k, condition in enumerate(conditions):
        mask_ref[k] = jnp.where(condition, 1.0, 0.0)
    w0 = cols_ref[0]
    w1 = cols_ref[1]

    for ref in (f_ref, gm_ref, gp_ref, dc_ref, ul_ref, ur_ref):
        ref[:, :PAD, :] = jnp.zeros((CHUNK // 128, PAD, 128), F32)
        ref[:, PAD + capacity :, :] = jnp.zeros((CHUNK // 128, PAD, 128), F32)

    def wide_mask(k, at, size):
        m = mask_ref[k, at, :]
        return lanes(*([m] * (size // 128)), *([m[:, : size % 128]] if size % 128 else []))

    gain2, shift2, bias2 = mv_ref[8:9, :], mv_ref[9:10, :], mv_ref[10:11, :]

    def start(i, carry):
        at = pl.ds(pl.multiple_of(i * 64, 64), 64)
        normed, inverse = normalise(x2_ref[at, :])
        n2_ref[at, :] = normed
        r2_ref[at, :] = inverse
        h2_ref[at, :] = (normed * gain2 + shift2).astype(BF16)
        gy_ref[at, :] = (cot_ref[at, :].astype(F32) * wide_mask(6, at, width)).astype(BF16)
        return carry

    lax.fori_loop(0, capacity // 64, start, 0)
    h2t_ref[...] = h2_ref[...].astype(F32).T.astype(BF16)
    gyt_ref[...] = gy_ref[...].astype(F32).T.astype(BF16)
    mix_ref[...] = jnp.zeros_like(mix_ref)
    dh2_ref[...] = jnp.zeros_like(dh2_ref)

    def fold(values):
        return jnp.sum(values.reshape(TILE // 8, 8, 128), axis=0)

    halves = CHUNK // 128

    def chunk_step(c, carry):
        at_c = pl.ds(pl.multiple_of(c * CHUNK, CHUNK), CHUNK)

        def vector(k, j):
            return hv_ref[k : k + 1, pl.ds(pl.multiple_of(c * CHUNK + j * 128, 128), 128)]

        def put_vector(k, j, value):
            hg_ref[k : k + 1, pl.ds(pl.multiple_of(c * CHUNK + j * 128, 128), 128)] = value

        first_layer = dot_nt(h2_ref[...], wu_ref[at_c, :])
        for j in range(halves):
            f_ref[j, pl.ds(PAD, capacity), :] = first_layer[:, j * 128 : (j + 1) * 128] + vector(0, j)

        def taps_of(j, r, at):
            here = f_ref[j, pl.ds(PAD + r, TILE), :]
            left = f_ref[j, pl.ds(PAD + r - 1, TILE), :] * mask_ref[0, at, :]
            right = f_ref[j, pl.ds(PAD + r + 1, TILE), :] * mask_ref[1, at, :]
            return left, here, right

        def column_taps(i, carry):
            r = pl.multiple_of(i * TILE, TILE)
            at = pl.ds(r, TILE)
            for j in range(halves):
                left, here, right = taps_of(j, r, at)
                v = [vector(k, j) for k in range(11)]
                gm_ref[j, pl.ds(PAD + r, TILE), :] = v[2] * left + v[3] * here + v[4] * right
                g0_ref[j, at, :] = v[1] + v[5] * left + v[6] * here + v[7] * right
                gp_ref[j, pl.ds(PAD + r, TILE), :] = v[8] * left + v[9] * here + v[10] * right
            return carry

        lax.fori_loop(0, tiles, column_taps, 0)

        def activate(i, carry):
            r = pl.multiple_of(i * TILE, TILE)
            at = pl.ds(r, TILE)
            for j in range(halves):
                conv = (
                    g0_ref[j, at, :]
                    + mask_ref[2, at, :] * gm_ref[j, pl.ds(PAD + r - w0, TILE), :]
                    + mask_ref[3, at, :] * gm_ref[j, pl.ds(PAD + r - w1, TILE), :]
                    + mask_ref[4, at, :] * gp_ref[j, pl.ds(PAD + r + w0, TILE), :]
                    + mask_ref[5, at, :] * gp_ref[j, pl.ds(PAD + r + w1, TILE), :]
                )
                half = 0.5 * (1.0 + lax.erf(conv * 2.0 ** (-0.5)))
                lane_at = pl.ds(j * 128, 128)
                act_ref[at, lane_at] = (conv * half).astype(BF16)
                slope = half + conv * jnp.exp(-0.5 * conv * conv) * (2.0 * math.pi) ** (-0.5)
                slope_ref[at, lane_at] = slope
            return carry

        lax.fori_loop(0, tiles, activate, 0)
        act = act_ref[...]
        mix_ref[...] += dot_nt(act, wd_ref[:, at_c])
        dng_ref[:, at_c] = dot_nn(gyt_ref[...], act)
        da_ref[...] = dot_nn(gy_ref[...], wd_ref[:, at_c])

        def into_conv(i, carry):
            r = pl.multiple_of(i * TILE, TILE)
            at = pl.ds(r, TILE)
            totals = []
            for j in range(halves):
                value = da_ref[at, pl.ds(j * 128, 128)] * slope_ref[at, pl.ds(j * 128, 128)]
                dc_ref[j, pl.ds(PAD + r, TILE), :] = value
                totals.append(carry[j] + fold(value))
            return tuple(totals)

        zero = jnp.zeros((8, 128), F32)
        totals = lax.fori_loop(0, tiles, into_conv, (zero,) * halves)
        for j in range(halves):
            put_vector(1, j, column_sum(totals[j]))

        for j in range(halves):
            v = [vector(k, j) for k in range(11)]

            def tap_back(i, carry, j=j, v=v):
                r = pl.multiple_of(i * TILE, TILE)
                at = pl.ds(r, TILE)
                left, here, right = taps_of(j, r, at)
                below = (
                    mask_ref[4, at, :] * dc_ref[j, pl.ds(PAD + r + w0, TILE), :]
                    + mask_ref[5, at, :] * dc_ref[j, pl.ds(PAD + r + w1, TILE), :]
                )
                level = dc_ref[j, pl.ds(PAD + r, TILE), :]
                above = (
                    mask_ref[2, at, :] * dc_ref[j, pl.ds(PAD + r - w0, TILE), :]
                    + mask_ref[3, at, :] * dc_ref[j, pl.ds(PAD + r - w1, TILE), :]
                )
                ul_ref[j, pl.ds(PAD + r, TILE), :] = v[2] * below + v[5] * level + v[8] * above
                u0_ref[j, at, :] = v[3] * below + v[6] * level + v[9] * above
                ur_ref[j, pl.ds(PAD + r, TILE), :] = v[4] * below + v[7] * level + v[10] * above
                grads = [fold(d * f) for d in (below, level, above) for f in (left, here, right)]
                return tuple(a + b for a, b in zip(carry, grads))

            sums = lax.fori_loop(0, tiles, tap_back, (zero,) * 9)
            for k in range(9):
                put_vector(2 + k, j, column_sum(sums[k]))

        def spread_back(i, carry):
            r = pl.multiple_of(i * TILE, TILE)
            at = pl.ds(r, TILE)
            totals = []
            for j in range(halves):
                value = (
                    u0_ref[j, at, :]
                    + mask_ref[0, at, :] * ur_ref[j, pl.ds(PAD + r - 1, TILE), :]
                    + mask_ref[1, at, :] * ul_ref[j, pl.ds(PAD + r + 1, TILE), :]
                ).astype(BF16)
                df_ref[at, pl.ds(j * 128, 128)] = value
                totals.append(carry[j] + fold(value.astype(F32)))
            return tuple(totals)

        totals = lax.fori_loop(0, tiles, spread_back, (zero,) * halves)
        for j in range(halves):
            put_vector(0, j, column_sum(totals[j]))
        df = df_ref[...]
        upg_ref[:, at_c] = dot_nn(h2t_ref[...], df)
        dh2_ref[...] += dot_nn(df, wu_ref[at_c, :])
        return carry

    lax.fori_loop(0, hidden // CHUNK, chunk_step, 0)
    hg_ref[11:, :] = jnp.zeros((hg_ref.shape[0] - 11, hidden), F32)

    for w in range(PARTS_W):
        for n in range(PARTS_N):
            up = upg_ref[pl.ds(n * rn, rn), pl.ds(w * 4 * cw, 4 * cw)]
            value = lanes(
                dng_ref[pl.ds(w * cw, cw), pl.ds(n * width, width)],
                *[up[e * cw : (e + 1) * cw] for e in range(rn // cw)],
            ).astype(BF16)
            store_piece(gown_ref, gsend_ref, w * PARTS_N + n, me, value)

    def finish(i, carry):
        at = pl.ds(pl.multiple_of(i * 64, 64), 64)
        occupied = wide_mask(6, at, width)
        mixed_ref[at, :] = ((x2_ref[at, :] + mix_ref[at, :] + bias2) * occupied).astype(BF16)
        gy = gy_ref[at, :].astype(F32)
        grad, normed = dh2_ref[at, :], n2_ref[at, :]
        dx2_ref[at, :] = gy + normalise_back(grad, normed, r2_ref[at, :], gain2)
        return tuple(a + column_sum(b) for a, b in zip(carry, (grad * normed, grad, gy)))

    zero = jnp.zeros((1, width), F32)
    sums = lax.fori_loop(0, capacity // 64, finish, (zero, zero, zero))
    mg_ref[...] = jnp.zeros_like(mg_ref)
    for k in range(3):
        mg_ref[8 + k : 9 + k, :] = sums[k]


def store_piece(own_ref, send_ref, device, me, value):
    slot = slot_of(device, me)
    mine = ((device ^ me) & 1) == 0

    @pl.when(mine)
    def _():
        own_ref[slot] = value

    @pl.when(jnp.logical_not(mine))
    def _():
        send_ref[slot] = value


def attend_back_kernel(
    tuned,
    rows_ref, cols_ref, dx2_ref, h1_ref, n1_ref, r1_ref, patch_ref, nk_ref, rk_ref, kn_ref, q_ref,
    kb_ref, vb_ref, p_ref, o_ref, wr_ref, wq_ref, wkv_ref, wp_ref, mv_ref, mg_ref, hg_ref,
    tg_ref, gown_ref, gsend_ref, vown_ref, vsend_ref,
    dp_ref, ds_ref, gr_ref, gq_ref, gkv_ref, gp_ref, dpatch_ref,
):
    me = my_index(tuned)
    capacity, width = dx2_ref.shape
    cw, rn = width // PARTS_W, width // PARTS_N
    keys = capacity // 4
    dim = width // HEADS
    scale = dim ** (-0.5)
    mv = mv_ref[...]

    datt = dx2_ref[...].astype(BF16)
    bias_proj = column_sum(datt.astype(F32))
    gp_ref[...] = dot_tn(datt, o_ref[...])
    dob = dot_nn(datt, wp_ref[...]).astype(BF16)
    dp_ref[...] = dot_nt(dob, vb_ref[...])

    def soften_back(i, carry):
        at = pl.ds(pl.multiple_of(i * 64, 64), 64)
        for h in range(HEADS):
            lane_at = pl.ds(h * keys, keys)
            p = p_ref[at, lane_at]
            dp = dp_ref[at, lane_at]
            row = jnp.sum(p * dp, axis=-1, keepdims=True)
            ds_ref[at, lane_at] = (p * (dp - row)).astype(BF16)
        return carry

    lax.fori_loop(0, capacity // 64, soften_back, 0)
    ds = ds_ref[...]
    dq = (dot_nn(ds, kb_ref[...]) * scale).astype(BF16)
    dk_all = dot_tn(ds, q_ref[...])
    dv_all = dot_tn(p_ref[...].astype(BF16), dob)
    lane = lax.broadcasted_iota(jnp.int32, (keys, width), 1)
    dk = jnp.zeros((keys, width), F32)
    dv = jnp.zeros((keys, width), F32)
    for h in range(HEADS):
        inside = (lane >= h * dim) & (lane < (h + 1) * dim)
        dk = jnp.where(inside, dk_all[h * keys : (h + 1) * keys], dk)
        dv = jnp.where(inside, dv_all[h * keys : (h + 1) * keys], dv)
    dk = (dk * scale).astype(BF16)
    dv = dv.astype(BF16)
    bias_query = column_sum(dq.astype(F32))
    bias_value = column_sum(dv.astype(F32))
    gq_ref[...] = dot_tn(dq, h1_ref[...])
    kn = kn_ref[...]
    gkv_ref[pl.ds(0, width), :] = dot_tn(dk, kn)
    gkv_ref[pl.ds(width, width), :] = dot_tn(dv, kn)
    dkn = dot_nn(dk, wkv_ref[pl.ds(0, width), :]) + dot_nn(dv, wkv_ref[pl.ds(width, width), :])
    nk = nk_ref[...]
    gain_key, shift_key = column_sum(dkn * nk), column_sum(dkn)
    dsr = normalise_back(dkn, nk, rk_ref[...], mv[5:6]).astype(BF16)
    bias_reduce = column_sum(dsr.astype(F32))
    for n in range(4):
        at = pl.ds(n * keys, keys)
        gr_ref[n] = dot_tn(dsr, patch_ref[at, :])
        dpatch_ref[at, :] = dot_nn(dsr, wr_ref[n])

    for w in range(PARTS_W):
        for n in range(PARTS_N):
            at, lane_at = pl.ds(w * cw, cw), pl.ds(n * rn, rn)
            value = lanes(
                gr_ref[n, at, :],
                gq_ref[at, lane_at],
                gkv_ref[pl.ds(2 * w * cw, cw), lane_at],
                gkv_ref[pl.ds(2 * w * cw + cw, cw), lane_at],
                gp_ref[at, lane_at],
            ).astype(BF16)
            store_piece(gown_ref, gsend_ref, w * PARTS_N + n, me, value)

    chosen = one_hot(rows_ref, cols_ref, capacity)
    high = dpatch_ref[...].astype(BF16)
    low = (dpatch_ref[...] - high.astype(F32)).astype(BF16)
    dh1 = dot_nn(dq, wq_ref[...]) + dot_tn(chosen, high) + dot_tn(chosen, low)
    n1 = n1_ref[...]
    gain_one, shift_one = column_sum(dh1 * n1), column_sum(dh1)
    tg_ref[...] = (dx2_ref[...] + normalise_back(dh1, n1, r1_ref[...], mv[0:1])).astype(BF16)

    sums = rows_of(
        gain_one, shift_one, bias_query, bias_value, bias_reduce, gain_key, shift_key, bias_proj,
        mg_ref[8:16, :],
    )
    hg = hg_ref[...]
    spare = jnp.zeros((16, 3 * rn), F32)
    for n in range(PARTS_N):
        value = lanes(sums[:, n * rn : (n + 1) * rn], hg[:, n * width : (n + 1) * width], spare).astype(BF16)
        delta = n ^ (me & 3)

        @pl.when((delta & 1) == 0)
        def _():
            vown_ref[delta >> 1] = value

        @pl.when((delta & 1) == 1)
        def _():
            vsend_ref[delta >> 1] = value


def total_of(refs):
    value = refs[0][...].astype(F32)
    for ref in refs[1:]:
        value = value + ref[...].astype(F32)
    return value


def finish_ffn_kernel(a_ref, b_ref, c_ref, d_ref, up_ref, down_ref):
    total = total_of((a_ref, b_ref, c_ref, d_ref))[0]
    width = down_ref.shape[0]
    down_ref[...] = total[:, :width].T
    up_ref[...] = rows_of(total[:, width : width + width // 2], total[:, width + width // 2 :])


def finish_attend_kernel(
    a_ref, b_ref, c_ref, d_ref, va_ref, vb_ref, vc_ref, vd_ref,
    q_ref, kv_ref, red_ref, proj_ref, vm_ref, vh_ref,
):
    total = total_of((a_ref, b_ref, c_ref, d_ref))[0]
    width, rn = red_ref.shape[0], q_ref.shape[0]
    red_ref[...] = total[:, :width].T
    unit = [total[:, width + k * rn : width + (k + 1) * rn] for k in range(4)]
    q_ref[...] = unit[0].T
    kv_ref[...] = rows_of(unit[1], unit[2]).T
    proj_ref[...] = unit[3].T
    vector = total_of((va_ref, vb_ref, vc_ref, vd_ref))[0]
    vm_ref[...] = vector[: vm_ref.shape[0], :rn]
    vh_ref[...] = vector[: vh_ref.shape[0], rn : rn + width]


def call(kernel, inputs, outputs, scratch=(), scalars=0, limit=40, flops=0, moved=0):
    vmem = pl.BlockSpec(memory_space=pltpu.VMEM)
    smem = pl.BlockSpec(memory_space=pltpu.SMEM)
    return pl.pallas_call(
        kernel,
        out_shape=[jax.ShapeDtypeStruct(shape, kind) for shape, kind in outputs],
        in_specs=[smem] * scalars + [vmem] * (len(inputs) - scalars),
        out_specs=[vmem] * len(outputs),
        scratch_shapes=[pltpu.VMEM(shape, kind) for shape, kind in scratch],
        compiler_params=pltpu.CompilerParams(vmem_limit_bytes=limit * 2**20),
        cost_estimate=pl.CostEstimate(flops=flops, bytes_accessed=moved, transcendentals=0),
    )(*inputs)


def on_device(
    mesh_shape,
    tokens, cotangent, img_rows, img_cols,
    q_weight, kv_weight, reduce_weight, proj_weight, up_weight, down_weight, vec_model, vec_hidden,
):
    wide, narrow = mesh_shape
    tuned = (wide, narrow) == (PARTS_W, PARTS_N)
    capacity, width = tokens.shape
    hidden = vec_hidden.shape[1] * narrow
    cw, rn = width // PARTS_W, width // PARTS_N
    keys = capacity // 4
    piece = (cw, 2 * width)
    vpiece = (16, 2 * width)

    def swap(value, mask):
        pairs = [(i, i ^ mask) for i in range(wide * narrow)]
        return lax.ppermute(value, ("wide", "narrow"), pairs)

    def gather(value):
        near = jnp.concatenate([value[None]] + [swap(value[None], m) for m in (8, 16, 24)], axis=0)
        half = jnp.concatenate([near] + [swap(near, m) for m in (2, 4, 6)], axis=0)
        return half, swap(half, 1)

    def add(*parts):
        total = parts[0].astype(F32)
        for part in parts[1:]:
            total = total + part.astype(F32)
        return total.astype(BF16)

    def scatter(own, send):
        half = add(own, swap(send, 1))
        near = add(half[0:4], *[swap(half[4 * k : 4 * k + 4], 2 * k) for k in (1, 2, 3)])
        return [near[0:1]] + [swap(near[k : k + 1], 8 * k) for k in (1, 2, 3)]

    if tuned:
        pack_a, pack_b, pack_v = call(
            pack_kernel,
            (q_weight, kv_weight, reduce_weight, proj_weight, up_weight, down_weight, vec_model, vec_hidden),
            ((piece, BF16), (piece, BF16), (vpiece, BF16)),
        )
        own_a, oth_a = gather(pack_a)
        vec_pair = jnp.concatenate([pack_v[None], swap(pack_v[None], 1)], axis=0)
        vecs = jnp.concatenate([vec_pair, swap(vec_pair, 2)], axis=0)
        own_b, oth_b = gather(pack_b)
    else:
        own_a, oth_a, own_b, oth_b, vecs = gather_plain(
            q_weight, kv_weight, reduce_weight, proj_weight, up_weight, down_weight, vec_model, vec_hidden
        )

    square = (width, width)
    (
        x2, h1, n1, r1, patches, nk, rk, kn, q, kb, vb, p, o, wr, wq, wkv, wp, mv, hv,
    ) = call(
        functools.partial(attend_kernel, tuned),
        (img_rows, img_cols, tokens, own_a, oth_a, vecs),
        (
            ((capacity, width), F32), ((capacity, width), BF16), ((capacity, width), F32), ((capacity, 1), F32),
            ((capacity, width), BF16), ((keys, width), F32), ((keys, 1), F32), ((keys, width), BF16),
            ((capacity, width), BF16), ((HEADS * keys, width), BF16), ((HEADS * keys, width), BF16),
            ((capacity, HEADS * keys), F32), ((capacity, width), BF16),
            ((4,) + square, BF16), (square, BF16), ((2 * width, width), BF16), (square, BF16),
            ((16, width), F32), ((16, hidden), F32),
        ),
        scratch=(((capacity, HEADS * keys), F32),),
        scalars=2,
        flops=2 * 10**9,
    )

    padded = ((CHUNK // 128, capacity + 2 * PAD, 128), F32)
    halved = ((CHUNK // 128, capacity, 128), F32)
    chunked = ((capacity, CHUNK), F32)
    mixed, gown_b, gsend_b, dx2, mg, hg = call(
        functools.partial(ffn_kernel, tuned),
        (img_rows, img_cols, x2, cotangent, own_b, oth_b, mv, hv),
        (
            ((capacity, width), BF16), ((SLOTS,) + piece, BF16), ((SLOTS,) + piece, BF16),
            ((capacity, width), F32), ((16, width), F32), ((16, hidden), F32),
        ),
        scratch=(
            ((hidden, width), BF16), ((width, hidden), BF16), ((7, capacity, 128), F32),
            ((capacity, width), F32), ((capacity, 1), F32), ((capacity, width), BF16), ((width, capacity), BF16),
            ((capacity, width), BF16), ((width, capacity), BF16),
            padded, padded, padded, padded, padded, padded,
            halved, chunked, ((capacity, CHUNK), BF16), halved, ((capacity, CHUNK), BF16), chunked,
            ((capacity, width), F32), ((capacity, width), F32), ((width, hidden), F32), ((width, hidden), F32),
        ),
        scalars=2,
        flops=4 * 10**9,
    )

    token_grad, gown_a, gsend_a, vown, vsend = call(
        functools.partial(attend_back_kernel, tuned),
        (
            img_rows, img_cols, dx2, h1, n1, r1, patches, nk, rk, kn, q, kb, vb, p, o, wr, wq, wkv, wp,
            mv, mg, hg,
        ),
        (
            ((capacity, width), BF16), ((SLOTS,) + piece, BF16), ((SLOTS,) + piece, BF16),
            ((2,) + vpiece, BF16), ((2,) + vpiece, BF16),
        ),
        scratch=(
            ((capacity, HEADS * keys), F32), ((capacity, HEADS * keys), BF16), ((4,) + square, F32),
            (square, F32), ((2 * width, width), F32), (square, F32), ((capacity, width), F32),
        ),
        scalars=2,
        flops=2 * 10**9,
    )

    if not tuned:
        grads = scatter_plain(mesh_shape, width, gown_a, gsend_a, gown_b, gsend_b, vown, vsend)
        return (mixed, token_grad) + grads

    parts_b = scatter(gown_b, gsend_b)
    vhalf = add(vown, swap(vsend, 1))
    vnear = add(vhalf[0:1], swap(vhalf[1:2], 2), swap(vhalf[0:1], 4), swap(vhalf[1:2], 6))
    vparts = [vnear] + [swap(vnear, 8 * k) for k in (1, 2, 3)]
    parts_a = scatter(gown_a, gsend_a)
    up_grad, down_grad = call(
        finish_ffn_kernel, parts_b, (((rn, 4 * cw), F32), ((width, cw), F32))
    )
    q_grad, kv_grad, reduce_grad, proj_grad, vm_grad, vh_grad = call(
        finish_attend_kernel,
        (*parts_a, *vparts),
        (
            ((rn, cw), F32), ((rn, 2 * cw), F32), ((width, cw), F32), ((rn, cw), F32),
            ((11, rn), F32), ((11, width), F32),
        ),
    )
    return mixed, token_grad, q_grad, kv_grad, reduce_grad, proj_grad, up_grad, down_grad, vm_grad, vh_grad


def gather_plain(q, kv, reduce, proj, up, down, vec_model, vec_hidden):
    def whole(value):
        rows = lax.all_gather(value, "narrow", axis=0, tiled=True)
        return lax.all_gather(rows, "wide", axis=1, tiled=True).T

    q, kv, reduce, proj, up, down = (whole(v) for v in (q, kv, reduce, proj, up, down))
    width = q.shape[0]
    cw, rn = width // PARTS_W, width // PARTS_N

    def pieces(turned, blocks):
        split = turned.reshape(PARTS_W, blocks, cw, PARTS_N, -1)
        return split.transpose(0, 3, 2, 1, 4).reshape(PARTS_W, PARTS_N, cw, -1)

    def slots(value):
        value = value.reshape(4, 4, 2, cw, -1).transpose(2, 1, 0, 3, 4)
        value = value.reshape(2, SLOTS, cw, -1)
        return value[0], value[1]

    a = jnp.concatenate([pieces(reduce, 1), pieces(q, 1), pieces(kv, 2), pieces(proj, 1)], axis=-1)
    b = jnp.concatenate([pieces(down, 1), pieces(up, 4)], axis=-1)
    vm = lax.all_gather(vec_model, "narrow", axis=1, tiled=True)
    vh = lax.all_gather(vec_hidden, "narrow", axis=1, tiled=True)
    both = jnp.concatenate([vm.reshape(11, PARTS_N, rn), vh.reshape(11, PARTS_N, width)], axis=-1)
    vecs = jnp.pad(both.transpose(1, 0, 2), ((0, 0), (0, 5), (0, 3 * rn)))
    return (*slots(a), *slots(b), vecs)


def scatter_plain(mesh_shape, width, gown_a, gsend_a, gown_b, gsend_b, vown, vsend):
    cw, rn = width // PARTS_W, width // PARTS_N

    def devices(own, send):
        both = jnp.stack([own, send]).reshape(2, 4, 4, cw, -1).transpose(2, 1, 0, 3, 4)
        return both.reshape(PARTS_W, PARTS_N, cw, -1)

    def natural(value, blocks):
        split = value.reshape(PARTS_W, PARTS_N, cw, blocks, -1).transpose(0, 3, 2, 1, 4)
        return split.reshape(PARTS_W * blocks * cw, -1).T

    def share(value):
        columns = lax.psum_scatter(value.astype(BF16), "wide", scatter_dimension=1, tiled=True)
        return lax.psum_scatter(columns, "narrow", scatter_dimension=0, tiled=True).astype(F32)

    a = devices(gown_a, gsend_a)
    b = devices(gown_b, gsend_b)
    reduce = natural(a[..., :width], 1)
    q = natural(a[..., width : width + rn], 1)
    kv = natural(a[..., width + rn : width + 3 * rn], 2)
    proj = natural(a[..., width + 3 * rn :], 1)
    down = natural(b[..., :width], 1)
    up = b[..., width:].reshape(PARTS_W, PARTS_N, cw, rn // cw, 4 * cw).transpose(1, 3, 2, 0, 4)
    up = up.reshape(width, PARTS_W * 4 * cw)
    vectors = jnp.stack([vown, vsend], axis=1).reshape(PARTS_N, 16, -1)[:, :11].transpose(1, 0, 2)
    vm = vectors[..., :rn].reshape(11, width)
    vh = vectors[..., rn : rn + width].reshape(11, PARTS_N * width)

    def share_vector(value):
        total = lax.psum(value.astype(BF16), "wide")
        return lax.psum_scatter(total, "narrow", scatter_dimension=1, tiled=True).astype(F32)

    return tuple(share(v) for v in (q, kv, reduce, proj, up, down)) + (share_vector(vm), share_vector(vh))


def solution(mesh):
    both, rows, weight, vector = P(("wide", "narrow"), None), P(("wide", "narrow")), P("narrow", "wide"), P(None, "narrow")
    return jax.shard_map(
        functools.partial(on_device, (mesh.shape["wide"], mesh.shape["narrow"])),
        mesh=mesh,
        in_specs=(both, both, rows, rows) + (weight,) * 6 + (vector,) * 2,
        out_specs=(both, both) + (weight,) * 6 + (vector,) * 2,
        check_vma=False,
    )
```

```python
import functools
import math

import jax
import jax.numpy as jnp
from jax import lax
from jax.experimental import pallas as pl
from jax.experimental.pallas import tpu as pltpu
from jax.sharding import PartitionSpec as P

HEADS = 5
EPSILON = 1e-06
MASKED = -1000000000.0
F32 = jnp.float32
BF16 = jnp.bfloat16

PARTS_W = 8
PARTS_N = 4
SLOTS = 16
TILE = 32
CHUNK = 256
PAD = 40


def dot_nn(left, right):
    return jnp.dot(left, right, preferred_element_type=F32)


def dot_nt(left, right):
    return lax.dot_general(left, right, (((1,), (1,)), ((), ())), preferred_element_type=F32)


def dot_tn(left, right):
    return lax.dot_general(left, right, (((0,), (0,)), ((), ())), preferred_element_type=F32)


def lanes(*parts):
    return jnp.concatenate(parts, axis=1)


def rows_of(*parts):
    return jnp.concatenate(parts, axis=0)


def my_index(tuned):
    if not tuned:
        return jnp.int32(0)
    return lax.axis_index("wide") * PARTS_N + lax.axis_index("narrow")


def slot_of(device, me):
    delta = device ^ me
    return ((delta >> 1) & 3) * 4 + (delta >> 3)


def normalise(values):
    centre = values - jnp.mean(values, axis=-1, keepdims=True)
    inverse = lax.rsqrt(jnp.mean(centre * centre, axis=-1, keepdims=True) + EPSILON)
    return centre * inverse, inverse


def normalise_back(grad, normed, inverse, gain):
    scaled = grad * gain
    first = jnp.mean(scaled, axis=-1, keepdims=True)
    second = jnp.mean(scaled * normed, axis=-1, keepdims=True)
    return (scaled - first - normed * second) * inverse


def column_sum(values):
    return jnp.sum(values, axis=0, keepdims=True)


def piece_of(own_ref, other_ref, device, me):
    slot = slot_of(device, me)
    mine = ((device ^ me) & 1) == 0
    return jnp.where(mine, own_ref[slot].astype(F32), other_ref[slot].astype(F32))


def token_geometry(rows_ref, cols_ref, capacity, width):
    row0, row1, col0, col1 = rows_ref[0], rows_ref[1], cols_ref[0], cols_ref[1]
    area0, area1 = row0 * col0, row1 * col1
    position = lax.broadcasted_iota(jnp.int32, (capacity, width), 0)
    first = position < area0
    second = jnp.logical_and(position >= area0, position < area0 + area1)
    widths = jnp.maximum(jnp.where(second, col1, col0), 2)
    heights = jnp.where(second, row1, row0)
    local = position - jnp.where(second, area0, 0)
    row = ((local.astype(F32) + 0.5) / widths.astype(F32)).astype(jnp.int32)
    col = local - row * widths
    return first, second, row, col, heights, widths


def pack_kernel(*refs):
    sources, (a_ref, b_ref, v_ref), held, semaphores = refs[:8], refs[8:11], refs[11:19], refs[19]
    copies = [pltpu.make_async_copy(source, ref, semaphores.at[i]) for i, (source, ref) in enumerate(zip(sources, held))]
    for copy in copies:
        copy.start()
    for copy in copies:
        copy.wait()
    q_ref, kv_ref, red_ref, proj_ref, up_ref, down_ref, vm_ref, vh_ref = held
    cw = q_ref.shape[0]

    def wider(ref):
        return ref[...].astype(F32)

    kv = wider(kv_ref).T
    a_ref[0] = lanes(wider(red_ref), wider(q_ref), kv[:cw], kv[cw:], wider(proj_ref)).astype(BF16)
    up = wider(up_ref).T
    b_ref[0] = lanes(wider(down_ref), *[up[cw * e : cw * e + cw] for e in range(4)]).astype(BF16)
    v_ref[0] = jnp.zeros_like(v_ref[0])
    both = lanes(wider(vm_ref), wider(vh_ref))
    v_ref[0, : both.shape[0], : both.shape[1]] = both.astype(BF16)


def pack(arguments, piece, vpiece):
    vmem = pl.BlockSpec(memory_space=pltpu.VMEM)
    return pl.pallas_call(
        pack_kernel,
        out_shape=[jax.ShapeDtypeStruct((1,) + shape, BF16) for shape in (piece, piece, vpiece)],
        in_specs=[pl.BlockSpec(memory_space=pl.ANY)] * len(arguments),
        out_specs=[vmem] * 3,
        scratch_shapes=[pltpu.VMEM(v.shape, v.dtype) for v in arguments] + [pltpu.SemaphoreType.DMA((len(arguments),))],
        compiler_params=pltpu.CompilerParams(vmem_limit_bytes=60 * 2**20),
    )(*arguments)


def attend_kernel(
    tuned,
    rows_ref, cols_ref, tok_ref, own_ref, oth_ref, vec_ref,
    x2_ref, h1_ref, n1_ref, r1_ref, patch_ref, nk_ref, rk_ref, kn_ref, q_ref, kb_ref, vb_ref,
    p_ref, o_ref, wr_ref, wq_ref, wkv_ref, wp_ref, mv_ref, hv_ref,
    score_ref,
):
    me = my_index(tuned)
    width, capacity = tok_ref.shape
    cw, rn = width // PARTS_W, width // PARTS_N
    keys = capacity // 4
    dim = width // HEADS

    pieces = [vec_ref[n ^ (me & 3)].astype(F32) for n in range(PARTS_N)]
    mv = lanes(*[p[:, :rn] for p in pieces])
    mv_ref[...] = mv
    hv_ref[...] = lanes(*[p[:, rn : 5 * rn] for p in pieces])

    for pair in range(PARTS_W // 2):
        got = [
            [piece_of(own_ref, oth_ref, w * PARTS_N + n, me) for n in range(PARTS_N)]
            for w in (2 * pair, 2 * pair + 1)
        ]
        at = pl.ds(pair * 2 * cw, 2 * cw)
        for n in range(PARTS_N):
            wr_ref[n, at, :] = rows_of(got[0][n][:, :width], got[1][n][:, :width]).astype(BF16)

        def unit(w, k):
            return lanes(*[got[w][n][:, width + k * rn : width + (k + 1) * rn] for n in range(PARTS_N)])

        wq_ref[at, :] = rows_of(unit(0, 0), unit(1, 0)).astype(BF16)
        wkv_ref[pl.ds(pair * 4 * cw, 4 * cw), :] = rows_of(
            unit(0, 1), unit(0, 2), unit(1, 1), unit(1, 2)
        ).astype(BF16)
        wp_ref[at, :] = rows_of(unit(0, 3), unit(1, 3)).astype(BF16)

    tokens = tok_ref[...].astype(F32).T
    normed, inverse = normalise(tokens)
    n1_ref[...] = normed
    r1_ref[...] = inverse
    h1 = (normed * mv[0:1] + mv[1:2]).astype(BF16)
    h1_ref[...] = h1
    q = (dot_nt(h1, wq_ref[...]) + mv[2:3]).astype(BF16)
    q_ref[...] = q

    chosen = one_hot(rows_ref, cols_ref, capacity)
    patches = dot_nn(chosen, h1).astype(BF16)
    patch_ref[...] = patches
    reduced = mv[4:5]
    for n in range(4):
        reduced = reduced + dot_nt(patches[n * keys : (n + 1) * keys], wr_ref[n])
    nk, rk = normalise(reduced)
    nk_ref[...] = nk
    rk_ref[...] = rk
    kn = (nk * mv[5:6] + mv[6:7]).astype(BF16)
    kn_ref[...] = kn
    kv = dot_nt(kn, wkv_ref[...])
    k = kv[:, :width].astype(BF16).astype(F32)
    v = (kv[:, width:] + mv[3:4]).astype(BF16).astype(F32)
    lane = lax.broadcasted_iota(jnp.int32, (keys, width), 1)
    for h in range(HEADS):
        inside = (lane >= h * dim) & (lane < (h + 1) * dim)
        at = pl.ds(h * keys, keys)
        kb_ref[at, :] = jnp.where(inside, k, 0.0).astype(BF16)
        vb_ref[at, :] = jnp.where(inside, v, 0.0).astype(BF16)

    score_ref[...] = dot_nt(q, kb_ref[...]) * dim ** (-0.5)
    area0 = rows_ref[0] * cols_ref[0]
    area1 = rows_ref[1] * cols_ref[1]

    def soften(i, carry):
        at = pl.ds(pl.multiple_of(i * 64, 64), 64)
        token = lax.broadcasted_iota(jnp.int32, (64, keys), 0) + i * 64
        key = lax.broadcasted_iota(jnp.int32, (64, keys), 1)
        quarter0, quarter1 = area0 // 4, area1 // 4
        live = ((token < area0) & (key < quarter0)) | (
            (token >= area0) & (token < area0 + area1) & (key >= quarter0) & (key < quarter0 + quarter1)
        )
        for h in range(HEADS):
            lane_at = pl.ds(h * keys, keys)
            s = jnp.where(live, score_ref[at, lane_at], MASKED)
            e = jnp.exp(s - jnp.max(s, axis=-1, keepdims=True))
            p_ref[at, lane_at] = e / jnp.sum(e, axis=-1, keepdims=True)
        return carry

    lax.fori_loop(0, capacity // 64, soften, 0)
    o = dot_nn(p_ref[...].astype(BF16), vb_ref[...]).astype(BF16)
    o_ref[...] = o
    x2_ref[...] = tokens + dot_nt(o, wp_ref[...]) + mv[7:8]


def one_hot(rows_ref, cols_ref, capacity):
    row0, row1, col0, col1 = rows_ref[0], rows_ref[1], cols_ref[0], cols_ref[1]
    area0, area1 = row0 * col0, row1 * col1
    quarter0, quarter1 = area0 // 4, area1 // 4
    keys = capacity // 4
    index = lax.broadcasted_iota(jnp.int32, (capacity, 128), 0)
    tap = index // keys
    key = index - tap * keys
    first = key < quarter0
    second = jnp.logical_and(key >= quarter0, key < quarter0 + quarter1)
    width = jnp.maximum(jnp.where(second, col1, col0), 2)
    half = width // 2
    local = key - jnp.where(second, quarter0, 0)
    row = ((local.astype(F32) + 0.5) / half.astype(F32)).astype(jnp.int32)
    col = local - row * half
    token = jnp.where(second, area0, 0) + (2 * row + tap // 2) * width + 2 * col + tap % 2
    token = jnp.where(first | second, token, -1)
    lane = lax.broadcasted_iota(jnp.int32, (capacity, 128), 1)
    return lanes(
        *[jnp.where(token == lane + t * 128, 1.0, 0.0).astype(BF16) for t in range(capacity // 128)]
    )


def ffn_kernel(
    tuned,
    rows_ref, cols_ref, x2_ref, cot_ref, own_ref, oth_ref, mv_ref, hv_ref,
    mixed_ref, gown_ref, gsend_ref, dx2_ref, mg_ref, hg_ref,
    wu_ref, wd_ref, mask_ref, n2_ref, r2_ref, h2_ref, h2t_ref, gy_ref, gyt_ref,
    f_ref, gm_ref, gp_ref, dc_ref, ul_ref, ur_ref, g0_ref, slope_ref, act_ref, u0_ref, df_ref, da_ref,
    mix_ref, dh2_ref, upg_ref, dng_ref, turned_ref,
):
    me = my_index(tuned)
    capacity, width = x2_ref.shape
    hidden = hv_ref.shape[1]
    cw, rn = width // PARTS_W, width // PARTS_N
    tiles = capacity // TILE

    for pair in range(PARTS_W // 2):
        got = [
            [piece_of(own_ref, oth_ref, w * PARTS_N + n, me) for n in range(PARTS_N)]
            for w in (2 * pair, 2 * pair + 1)
        ]
        wd_ref[pl.ds(pair * 2 * cw, 2 * cw), :] = lanes(
            *[rows_of(got[0][n][:, :width], got[1][n][:, :width]) for n in range(PARTS_N)]
        ).astype(BF16)

        def unit(w, k):
            return lanes(*[got[w][n][:, width + k * rn : width + (k + 1) * rn] for n in range(PARTS_N)])

        wu_ref[pl.ds(pair * 8 * cw, 8 * cw), :] = rows_of(
            *[unit(w, k) for w in range(2) for k in range(4)]
        ).astype(BF16)

    first, second, row, col, heights, widths = token_geometry(rows_ref, cols_ref, capacity, 128)
    live = first | second
    conditions = (
        live & (col > 0),
        live & (col < widths - 1),
        first & (row > 0),
        second & (row > 0),
        first & (row < heights - 1),
        second & (row < heights - 1),
        live,
    )
    for k, condition in enumerate(conditions):
        mask_ref[k] = jnp.where(condition, 1.0, 0.0)
    w0 = cols_ref[0]
    w1 = cols_ref[1]

    for ref in (f_ref, gm_ref, gp_ref, dc_ref, ul_ref, ur_ref):
        ref[:, :PAD, :] = jnp.zeros((CHUNK // 128, PAD, 128), F32)
        ref[:, PAD + capacity :, :] = jnp.zeros((CHUNK // 128, PAD, 128), F32)

    def wide_mask(k, at, size):
        m = mask_ref[k, at, :]
        return lanes(*([m] * (size // 128)), *([m[:, : size % 128]] if size % 128 else []))

    gain2, shift2, bias2 = mv_ref[8:9, :], mv_ref[9:10, :], mv_ref[10:11, :]

    def start(i, carry):
        at = pl.ds(pl.multiple_of(i * 64, 64), 64)
        normed, inverse = normalise(x2_ref[at, :])
        n2_ref[at, :] = normed
        r2_ref[at, :] = inverse
        h2_ref[at, :] = (normed * gain2 + shift2).astype(BF16)
        gy_ref[at, :] = (turned_ref[at, :] * wide_mask(6, at, width)).astype(BF16)
        return carry

    turned_ref[...] = cot_ref[...].astype(F32).T
    lax.fori_loop(0, capacity // 64, start, 0)
    h2t_ref[...] = h2_ref[...].astype(F32).T.astype(BF16)
    gyt_ref[...] = gy_ref[...].astype(F32).T.astype(BF16)
    mix_ref[...] = jnp.zeros_like(mix_ref)
    dh2_ref[...] = jnp.zeros_like(dh2_ref)

    def fold(values):
        return jnp.sum(values.reshape(TILE // 8, 8, 128), axis=0)

    halves = CHUNK // 128

    def chunk_step(c, carry):
        at_c = pl.ds(pl.multiple_of(c * CHUNK, CHUNK), CHUNK)

        def vector(k, j):
            return hv_ref[k : k + 1, pl.ds(pl.multiple_of(c * CHUNK + j * 128, 128), 128)]

        def put_vector(k, j, value):
            hg_ref[k : k + 1, pl.ds(pl.multiple_of(c * CHUNK + j * 128, 128), 128)] = value

        first_layer = dot_nt(h2_ref[...], wu_ref[at_c, :])
        for j in range(halves):
            f_ref[j, pl.ds(PAD, capacity), :] = first_layer[:, j * 128 : (j + 1) * 128] + vector(0, j)

        def taps_of(j, r, at):
            here = f_ref[j, pl.ds(PAD + r, TILE), :]
            left = f_ref[j, pl.ds(PAD + r - 1, TILE), :] * mask_ref[0, at, :]
            right = f_ref[j, pl.ds(PAD + r + 1, TILE), :] * mask_ref[1, at, :]
            return left, here, right

        def column_taps(i, carry):
            r = pl.multiple_of(i * TILE, TILE)
            at = pl.ds(r, TILE)
            for j in range(halves):
                left, here, right = taps_of(j, r, at)
                v = [vector(k, j) for k in range(11)]
                gm_ref[j, pl.ds(PAD + r, TILE), :] = v[2] * left + v[3] * here + v[4] * right
                g0_ref[j, at, :] = v[1] + v[5] * left + v[6] * here + v[7] * right
                gp_ref[j, pl.ds(PAD + r, TILE), :] = v[8] * left + v[9] * here + v[10] * right
            return carry

        lax.fori_loop(0, tiles, column_taps, 0)

        def activate(i, carry):
            r = pl.multiple_of(i * TILE, TILE)
            at = pl.ds(r, TILE)
            for j in range(halves):
                conv = (
                    g0_ref[j, at, :]
                    + mask_ref[2, at, :] * gm_ref[j, pl.ds(PAD + r - w0, TILE), :]
                    + mask_ref[3, at, :] * gm_ref[j, pl.ds(PAD + r - w1, TILE), :]
                    + mask_ref[4, at, :] * gp_ref[j, pl.ds(PAD + r + w0, TILE), :]
                    + mask_ref[5, at, :] * gp_ref[j, pl.ds(PAD + r + w1, TILE), :]
                )
                half = 0.5 * (1.0 + lax.erf(conv * 2.0 ** (-0.5)))
                lane_at = pl.ds(j * 128, 128)
                act_ref[at, lane_at] = (conv * half).astype(BF16)
                slope = half + conv * jnp.exp(-0.5 * conv * conv) * (2.0 * math.pi) ** (-0.5)
                slope_ref[at, lane_at] = slope
            return carry

        lax.fori_loop(0, tiles, activate, 0)
        act = act_ref[...]
        mix_ref[...] += dot_nt(act, wd_ref[:, at_c])
        dng_ref[:, at_c] = dot_nn(gyt_ref[...], act)
        da_ref[...] = dot_nn(gy_ref[...], wd_ref[:, at_c])

        def into_conv(i, carry):
            r = pl.multiple_of(i * TILE, TILE)
            at = pl.ds(r, TILE)
            totals = []
            for j in range(halves):
                value = da_ref[at, pl.ds(j * 128, 128)] * slope_ref[at, pl.ds(j * 128, 128)]
                dc_ref[j, pl.ds(PAD + r, TILE), :] = value
                totals.append(carry[j] + fold(value))
            return tuple(totals)

        zero = jnp.zeros((8, 128), F32)
        totals = lax.fori_loop(0, tiles, into_conv, (zero,) * halves)
        for j in range(halves):
            put_vector(1, j, column_sum(totals[j]))

        for j in range(halves):
            v = [vector(k, j) for k in range(11)]

            def tap_back(i, carry, j=j, v=v):
                r = pl.multiple_of(i * TILE, TILE)
                at = pl.ds(r, TILE)
                left, here, right = taps_of(j, r, at)
                below = (
                    mask_ref[4, at, :] * dc_ref[j, pl.ds(PAD + r + w0, TILE), :]
                    + mask_ref[5, at, :] * dc_ref[j, pl.ds(PAD + r + w1, TILE), :]
                )
                level = dc_ref[j, pl.ds(PAD + r, TILE), :]
                above = (
                    mask_ref[2, at, :] * dc_ref[j, pl.ds(PAD + r - w0, TILE), :]
                    + mask_ref[3, at, :] * dc_ref[j, pl.ds(PAD + r - w1, TILE), :]
                )
                ul_ref[j, pl.ds(PAD + r, TILE), :] = v[2] * below + v[5] * level + v[8] * above
                u0_ref[j, at, :] = v[3] * below + v[6] * level + v[9] * above
                ur_ref[j, pl.ds(PAD + r, TILE), :] = v[4] * below + v[7] * level + v[10] * above
                grads = [fold(d * f) for d in (below, level, above) for f in (left, here, right)]
                return tuple(a + b for a, b in zip(carry, grads))

            sums = lax.fori_loop(0, tiles, tap_back, (zero,) * 9)
            for k in range(9):
                put_vector(2 + k, j, column_sum(sums[k]))

        def spread_back(i, carry):
            r = pl.multiple_of(i * TILE, TILE)
            at = pl.ds(r, TILE)
            totals = []
            for j in range(halves):
                value = (
                    u0_ref[j, at, :]
                    + mask_ref[0, at, :] * ur_ref[j, pl.ds(PAD + r - 1, TILE), :]
                    + mask_ref[1, at, :] * ul_ref[j, pl.ds(PAD + r + 1, TILE), :]
                ).astype(BF16)
                df_ref[at, pl.ds(j * 128, 128)] = value
                totals.append(carry[j] + fold(value.astype(F32)))
            return tuple(totals)

        totals = lax.fori_loop(0, tiles, spread_back, (zero,) * halves)
        for j in range(halves):
            put_vector(0, j, column_sum(totals[j]))
        df = df_ref[...]
        upg_ref[:, at_c] = dot_nn(h2t_ref[...], df)
        dh2_ref[...] += dot_nn(df, wu_ref[at_c, :])
        return carry

    lax.fori_loop(0, hidden // CHUNK, chunk_step, 0)
    hg_ref[11:, :] = jnp.zeros((hg_ref.shape[0] - 11, hidden), F32)

    def value_of(w, n):
        up = upg_ref[pl.ds(n * rn, rn), pl.ds(w * 4 * cw, 4 * cw)]
        return lanes(
            dng_ref[pl.ds(w * cw, cw), pl.ds(n * width, width)],
            *[up[e * cw : (e + 1) * cw] for e in range(rn // cw)],
        )

    store_pieces(gown_ref, gsend_ref, me, value_of)

    def finish(i, carry):
        at = pl.ds(pl.multiple_of(i * 64, 64), 64)
        occupied = wide_mask(6, at, width)
        turned_ref[at, :] = (x2_ref[at, :] + mix_ref[at, :] + bias2) * occupied
        gy = gy_ref[at, :].astype(F32)
        grad, normed = dh2_ref[at, :], n2_ref[at, :]
        dx2_ref[at, :] = gy + normalise_back(grad, normed, r2_ref[at, :], gain2)
        return tuple(a + column_sum(b) for a, b in zip(carry, (grad * normed, grad, gy)))

    zero = jnp.zeros((1, width), F32)
    sums = lax.fori_loop(0, capacity // 64, finish, (zero, zero, zero))
    mixed_ref[...] = turned_ref[...].T.astype(BF16)
    mg_ref[...] = jnp.zeros_like(mg_ref)
    for k in range(3):
        mg_ref[8 + k : 9 + k, :] = sums[k]


def store_pieces(own_ref, send_ref, me, value_of):
    even = (me & 1) == 0
    for w in range(PARTS_W):
        for x in range(PARTS_N // 2):
            first, second = value_of(w, 2 * x), value_of(w, 2 * x + 1)
            slot = slot_of(w * PARTS_N + 2 * x, me)
            own_ref[slot] = jnp.where(even, first, second).astype(BF16)
            send_ref[slot] = jnp.where(even, second, first).astype(BF16)


def score_back_kernel(dx2_ref, vb_ref, p_ref, o_ref, wp_ref, gp_ref, dob_ref, ds_ref, bp_ref, dp_ref):
    capacity = dx2_ref.shape[0]
    keys = capacity // 4
    datt = dx2_ref[...].astype(BF16)
    bp_ref[...] = column_sum(datt.astype(F32))
    gp_ref[...] = dot_tn(datt, o_ref[...])
    dob = dot_nn(datt, wp_ref[...]).astype(BF16)
    dob_ref[...] = dob
    dp_ref[...] = dot_nt(dob, vb_ref[...])

    def soften_back(i, carry):
        at = pl.ds(pl.multiple_of(i * 64, 64), 64)
        for h in range(HEADS):
            lane_at = pl.ds(h * keys, keys)
            p = p_ref[at, lane_at]
            dp = dp_ref[at, lane_at]
            row = jnp.sum(p * dp, axis=-1, keepdims=True)
            ds_ref[at, lane_at] = (p * (dp - row)).astype(BF16)
        return carry

    lax.fori_loop(0, capacity // 64, soften_back, 0)


def attend_back_kernel(
    tuned,
    dob_ref, ds_ref, gp_ref, h1_ref, patch_ref, nk_ref, rk_ref, kn_ref, q_ref, kb_ref, p_ref,
    wr_ref, wkv_ref, mv_ref,
    gown_ref, gsend_ref, dq_ref, dpatch_ref, vk_ref,
    gr_ref, gq_ref, gkv_ref,
):
    me = my_index(tuned)
    capacity, width = h1_ref.shape
    cw, rn = width // PARTS_W, width // PARTS_N
    keys = capacity // 4
    dim = width // HEADS
    scale = dim ** (-0.5)

    ds = ds_ref[...]
    dq = (dot_nn(ds, kb_ref[...]) * scale).astype(BF16)
    dq_ref[...] = dq
    dk_all = dot_tn(ds, q_ref[...])
    dv_all = dot_tn(p_ref[...].astype(BF16), dob_ref[...])
    lane = lax.broadcasted_iota(jnp.int32, (keys, width), 1)
    dk = jnp.zeros((keys, width), F32)
    dv = jnp.zeros((keys, width), F32)
    for h in range(HEADS):
        inside = (lane >= h * dim) & (lane < (h + 1) * dim)
        dk = jnp.where(inside, dk_all[h * keys : (h + 1) * keys], dk)
        dv = jnp.where(inside, dv_all[h * keys : (h + 1) * keys], dv)
    dk = (dk * scale).astype(BF16)
    dv = dv.astype(BF16)
    gq_ref[...] = dot_tn(dq, h1_ref[...])
    kn = kn_ref[...]
    gkv_ref[pl.ds(0, width), :] = dot_tn(dk, kn)
    gkv_ref[pl.ds(width, width), :] = dot_tn(dv, kn)
    dkn = dot_nn(dk, wkv_ref[pl.ds(0, width), :]) + dot_nn(dv, wkv_ref[pl.ds(width, width), :])
    nk = nk_ref[...]
    dsr = normalise_back(dkn, nk, rk_ref[...], mv_ref[5:6, :]).astype(BF16)
    vk_ref[...] = rows_of(
        column_sum(dq.astype(F32)),
        column_sum(dv.astype(F32)),
        column_sum(dsr.astype(F32)),
        column_sum(dkn * nk),
        column_sum(dkn),
        jnp.zeros((3, width), F32),
    )
    for n in range(4):
        at = pl.ds(n * keys, keys)
        gr_ref[n] = dot_tn(dsr, patch_ref[at, :])
        dpatch_ref[at, :] = dot_nn(dsr, wr_ref[n])

    def value_of(w, n):
        at, lane_at = pl.ds(w * cw, cw), pl.ds(n * rn, rn)
        return lanes(
            gr_ref[n, at, :],
            gq_ref[at, lane_at],
            gkv_ref[pl.ds(2 * w * cw, cw), lane_at],
            gkv_ref[pl.ds(2 * w * cw + cw, cw), lane_at],
            gp_ref[at, lane_at],
        )

    store_pieces(gown_ref, gsend_ref, me, value_of)


def token_back_kernel(
    tuned,
    rows_ref, cols_ref, dx2_ref, dq_ref, dpatch_ref, n1_ref, r1_ref, wq_ref, mv_ref, mg_ref, hg_ref, vk_ref, bp_ref,
    tg_ref, vown_ref, vsend_ref,
):
    me = my_index(tuned)
    capacity, width = dx2_ref.shape
    rn = width // PARTS_N
    chosen = one_hot(rows_ref, cols_ref, capacity)
    high = dpatch_ref[...].astype(BF16)
    low = (dpatch_ref[...] - high.astype(F32)).astype(BF16)
    dh1 = dot_nn(dq_ref[...], wq_ref[...]) + dot_tn(chosen, high) + dot_tn(chosen, low)
    n1 = n1_ref[...]
    vk = vk_ref[...]
    token_grad = dx2_ref[...] + normalise_back(dh1, n1, r1_ref[...], mv_ref[0:1, :])
    tg_ref[...] = token_grad.T.astype(BF16)
    sums = rows_of(column_sum(dh1 * n1), column_sum(dh1), vk[0:5], bp_ref[...], mg_ref[8:16, :])
    hg = hg_ref[...]
    spare = jnp.zeros((16, 3 * rn), F32)
    value = [
        lanes(sums[:, n * rn : (n + 1) * rn], hg[:, n * width : (n + 1) * width], spare) for n in range(PARTS_N)
    ]
    even = (me & 1) == 0
    for x in range(2):
        slot = x ^ ((me >> 1) & 1)
        vown_ref[slot] = jnp.where(even, value[2 * x], value[2 * x + 1]).astype(BF16)
        vsend_ref[slot] = jnp.where(even, value[2 * x + 1], value[2 * x]).astype(BF16)


def total_of(refs):
    value = refs[0][...].astype(F32)
    for ref in refs[1:]:
        value = value + ref[...].astype(F32)
    return value


def core_sum_kernel(own_ref, got_ref, *out_refs):
    for k, ref in enumerate(out_refs):
        at = slice(4 * k, 4 * k + 4)
        ref[...] = (own_ref[at].astype(F32) + got_ref[at].astype(F32)).astype(BF16)


def core_sum_vector_kernel(own_ref, got_ref, vown_ref, vgot_ref, *out_refs):
    cw = own_ref.shape[1]
    vector = [(vown_ref[x].astype(F32) + vgot_ref[x].astype(F32)).astype(BF16) for x in range(2)]
    for k, ref in enumerate(out_refs):
        parts = [own_ref[4 * k + j].astype(F32) + got_ref[4 * k + j].astype(F32) for j in range(4)]
        ref[pl.ds(0, 4 * cw), :] = rows_of(*parts).astype(BF16)
        ref[pl.ds(4 * cw, vector[0].shape[0]), :] = vector[k & 1]


def plane_sum_kernel(a_ref, b_ref, c_ref, d_ref, *out_refs):
    total = total_of((a_ref, b_ref, c_ref, d_ref)).astype(BF16)
    for k, ref in enumerate(out_refs):
        ref[0] = total[k]


def plane_sum_vector_kernel(cw, a_ref, b_ref, c_ref, d_ref, *out_refs):
    total = total_of((a_ref, b_ref, c_ref, d_ref))
    for k, ref in enumerate(out_refs):
        ref[...] = rows_of(total[k * cw : (k + 1) * cw], total[4 * cw :]).astype(BF16)


def finish_ffn_kernel(a_ref, b_ref, c_ref, d_ref, up_ref, down_ref):
    total = total_of((a_ref, b_ref, c_ref, d_ref))[0]
    width = down_ref.shape[1]
    down_ref[...] = total[:, :width]
    up_ref[...] = rows_of(total[:, width : width + width // 2], total[:, width + width // 2 :])


def finish_attend_kernel(a_ref, b_ref, c_ref, d_ref, q_ref, kv_ref, red_ref, proj_ref, vm_ref, vh_ref):
    total = total_of((a_ref, b_ref, c_ref, d_ref))
    cw, width = red_ref.shape
    rn = q_ref.shape[1]
    red_ref[...] = total[:cw, :width]
    unit = [total[:cw, width + k * rn : width + (k + 1) * rn] for k in range(4)]
    q_ref[...] = unit[0]
    kv_ref[...] = rows_of(unit[1], unit[2]).T
    proj_ref[...] = unit[3]
    vm_ref[...] = total[cw : cw + vm_ref.shape[0], :rn]
    vh_ref[...] = total[cw : cw + vh_ref.shape[0], rn : rn + width]


def call(kernel, inputs, outputs, scratch=(), scalars=0, limit=40, flops=0, moved=0):
    vmem = pl.BlockSpec(memory_space=pltpu.VMEM)
    smem = pl.BlockSpec(memory_space=pltpu.SMEM)
    return pl.pallas_call(
        kernel,
        out_shape=[jax.ShapeDtypeStruct(shape, kind) for shape, kind in outputs],
        in_specs=[smem] * scalars + [vmem] * (len(inputs) - scalars),
        out_specs=[vmem] * len(outputs),
        scratch_shapes=[pltpu.VMEM(shape, kind) for shape, kind in scratch],
        compiler_params=pltpu.CompilerParams(vmem_limit_bytes=limit * 2**20),
        cost_estimate=pl.CostEstimate(flops=flops, bytes_accessed=moved, transcendentals=0),
    )(*inputs)


def after(value, *others):
    return lax.optimization_barrier((value, *others))[0]


def on_device(
    mesh_shape,
    tokens, cotangent, img_rows, img_cols,
    q_weight, kv_weight, reduce_weight, proj_weight, up_weight, down_weight, vec_model, vec_hidden,
):
    wide, narrow = mesh_shape
    tuned = (wide, narrow) == (PARTS_W, PARTS_N)
    capacity, width = tokens.shape
    hidden = vec_hidden.shape[1] * narrow
    cw, rn = width // PARTS_W, width // PARTS_N
    keys = capacity // 4
    piece = (cw, 2 * width)
    vpiece = (16, 2 * width)

    def swap(value, mask):
        pairs = [(i, i ^ mask) for i in range(wide * narrow)]
        return lax.ppermute(value, ("wide", "narrow"), pairs)

    if tuned:
        pack_a, pack_b, pack_v = pack(
            (
                q_weight.T, kv_weight, reduce_weight.T, proj_weight.T, up_weight, down_weight.T,
                vec_model, vec_hidden,
            ),
            piece, vpiece,
        )
        near_a = jnp.concatenate([pack_a] + [swap(pack_a, m) for m in (8, 16, 24)], axis=0)
        vec_pair = jnp.concatenate([pack_v, swap(pack_v, 1)], axis=0)
        vecs = jnp.concatenate([vec_pair, swap(vec_pair, 2)], axis=0)
        own_a = jnp.concatenate([near_a] + [swap(near_a, m) for m in (2, 4, 6)], axis=0)
        pack_b = after(pack_b, near_a)
        near_b = jnp.concatenate([pack_b] + [swap(pack_b, m) for m in (8, 16, 24)], axis=0)
        own_a, near_b, vecs = lax.optimization_barrier((own_a, near_b, vecs))
        oth_a = swap(own_a, 1)
        plane_b = [swap(near_b, m) for m in (2, 4, 6)]
    else:
        own_a, oth_a, own_b, oth_b, vecs = gather_plain(
            q_weight, kv_weight, reduce_weight, proj_weight, up_weight, down_weight, vec_model, vec_hidden
        )

    square = (width, width)
    (
        x2, h1, n1, r1, patches, nk, rk, kn, q, kb, vb, p, o, wr, wq, wkv, wp, mv, hv,
    ) = call(
        functools.partial(attend_kernel, tuned),
        (img_rows, img_cols, tokens.T, own_a, oth_a, vecs),
        (
            ((capacity, width), F32), ((capacity, width), BF16), ((capacity, width), F32), ((capacity, 1), F32),
            ((capacity, width), BF16), ((keys, width), F32), ((keys, 1), F32), ((keys, width), BF16),
            ((capacity, width), BF16), ((HEADS * keys, width), BF16), ((HEADS * keys, width), BF16),
            ((capacity, HEADS * keys), F32), ((capacity, width), BF16),
            ((4,) + square, BF16), (square, BF16), ((2 * width, width), BF16), (square, BF16),
            ((16, width), F32), ((16, hidden), F32),
        ),
        scratch=(((capacity, HEADS * keys), F32),),
        scalars=2,
        flops=8 * 10**9,
    )

    if tuned:
        plane_b = lax.optimization_barrier((*plane_b, x2))[:3]
        own_b = jnp.concatenate([near_b, *plane_b], axis=0)
        oth_b = swap(own_b, 1)
    padded = ((CHUNK // 128, capacity + 2 * PAD, 128), F32)
    halved = ((CHUNK // 128, capacity, 128), F32)
    chunked = ((capacity, CHUNK), F32)
    mixed, gown_b, gsend_b, dx2, mg, hg = call(
        functools.partial(ffn_kernel, tuned),
        (img_rows, img_cols, x2, cotangent.T, own_b, oth_b, mv, hv),
        (
            ((width, capacity), BF16), ((SLOTS,) + piece, BF16), ((SLOTS,) + piece, BF16),
            ((capacity, width), F32), ((16, width), F32), ((16, hidden), F32),
        ),
        scratch=(
            ((hidden, width), BF16), ((width, hidden), BF16), ((7, capacity, 128), F32),
            ((capacity, width), F32), ((capacity, 1), F32), ((capacity, width), BF16), ((width, capacity), BF16),
            ((capacity, width), BF16), ((width, capacity), BF16),
            padded, padded, padded, padded, padded, padded,
            halved, chunked, ((capacity, CHUNK), BF16), halved, ((capacity, CHUNK), BF16), chunked,
            ((capacity, width), F32), ((capacity, width), F32), ((width, hidden), F32), ((width, hidden), F32),
            ((capacity, width), F32),
        ),
        scalars=2,
        flops=33 * 10**9,
    )

    if tuned:
        got_b = swap(gsend_b, 1)
    gp, dob, ds, bp = call(
        score_back_kernel,
        (dx2, vb, p, o, wp),
        (
            (square, F32), ((capacity, width), BF16), ((capacity, HEADS * keys), BF16), ((1, width), F32),
        ),
        scratch=(((capacity, HEADS * keys), F32),),
        flops=25 * 10**8,
    )
    four = (4,) + piece
    if tuned:
        half_b = call(core_sum_kernel, (gown_b, got_b), ((four, BF16),) * 4)
        plane_b = [swap(half_b[k], 2 * k) for k in (1, 2, 3)]
        ds = after(ds, half_b[1])
    gown_a, gsend_a, dq, dpatch, vk = call(
        functools.partial(attend_back_kernel, tuned),
        (dob, ds, gp, h1, patches, nk, rk, kn, q, kb, p, wr, wkv, mv),
        (
            ((SLOTS,) + piece, BF16), ((SLOTS,) + piece, BF16), ((capacity, width), BF16), ((capacity, width), F32),
            ((8, width), F32),
        ),
        scratch=(((4,) + square, F32), (square, F32), ((2 * width, width), F32)),
        flops=0,
    )
    if tuned:
        got_a = swap(gsend_a, 1)
        near_b = call(plane_sum_kernel, (half_b[0], *plane_b), (((1,) + piece, BF16),) * 4, flops=2 * 10**10)
        line_b = [swap(near_b[k], 8 * k) for k in (1, 2, 3)]
    token_grad, vown, vsend = call(
        functools.partial(token_back_kernel, tuned),
        (img_rows, img_cols, dx2, dq, dpatch, n1, r1, wq, mv, mg, hg, vk, bp),
        (((width, capacity), BF16), ((2,) + vpiece, BF16), ((2,) + vpiece, BF16)),
        scalars=2,
        flops=0,
    )

    if not tuned:
        grads = scatter_plain(mesh_shape, width, gown_a, gsend_a, gown_b, gsend_b, vown, vsend)
        return (mixed.T, token_grad.T) + grads

    gown_a = after(gown_a, near_b[1])
    joined = ((4 * cw + 16, 2 * width), BF16)
    half_a = call(core_sum_vector_kernel, (gown_a, got_a, vown, swap(vsend, 1)), (joined,) * 4)
    plane_a = [swap(half_a[k], 2 * k) for k in (1, 2, 3)]
    plane_a = lax.optimization_barrier((*plane_a, *line_b))[:3]
    near_a = call(
        functools.partial(plane_sum_vector_kernel, cw), (half_a[0], *plane_a), (((cw + 16, 2 * width), BF16),) * 4
    )
    line_a = [swap(near_a[k], 8 * k) for k in (1, 2, 3)]
    up_grad, down_grad = call(
        finish_ffn_kernel, (near_b[0], *line_b), (((rn, 4 * cw), F32), ((cw, width), F32))
    )
    q_grad, kv_grad, reduce_grad, proj_grad, vm_grad, vh_grad = call(
        finish_attend_kernel,
        (near_a[0], *line_a),
        (
            ((cw, rn), F32), ((rn, 2 * cw), F32), ((cw, width), F32), ((cw, rn), F32),
            ((11, rn), F32), ((11, width), F32),
        ),
    )
    return (
        mixed.T, token_grad.T, q_grad.T, kv_grad, reduce_grad.T, proj_grad.T, up_grad, down_grad.T, vm_grad, vh_grad,
    )


def gather_plain(q, kv, reduce, proj, up, down, vec_model, vec_hidden):
    def whole(value):
        rows = lax.all_gather(value, "narrow", axis=0, tiled=True)
        return lax.all_gather(rows, "wide", axis=1, tiled=True).T

    q, kv, reduce, proj, up, down = (whole(v) for v in (q, kv, reduce, proj, up, down))
    width = q.shape[0]
    cw, rn = width // PARTS_W, width // PARTS_N

    def pieces(turned, blocks):
        split = turned.reshape(PARTS_W, blocks, cw, PARTS_N, -1)
        return split.transpose(0, 3, 2, 1, 4).reshape(PARTS_W, PARTS_N, cw, -1)

    def slots(value):
        value = value.reshape(4, 4, 2, cw, -1).transpose(2, 1, 0, 3, 4)
        value = value.reshape(2, SLOTS, cw, -1)
        return value[0], value[1]

    a = jnp.concatenate([pieces(reduce, 1), pieces(q, 1), pieces(kv, 2), pieces(proj, 1)], axis=-1)
    b = jnp.concatenate([pieces(down, 1), pieces(up, 4)], axis=-1)
    vm = lax.all_gather(vec_model, "narrow", axis=1, tiled=True)
    vh = lax.all_gather(vec_hidden, "narrow", axis=1, tiled=True)
    both = jnp.concatenate([vm.reshape(11, PARTS_N, rn), vh.reshape(11, PARTS_N, width)], axis=-1)
    vecs = jnp.pad(both.transpose(1, 0, 2), ((0, 0), (0, 5), (0, 3 * rn)))
    return (*slots(a), *slots(b), vecs)


def scatter_plain(mesh_shape, width, gown_a, gsend_a, gown_b, gsend_b, vown, vsend):
    cw, rn = width // PARTS_W, width // PARTS_N

    def devices(own, send):
        both = jnp.stack([own, send]).reshape(2, 4, 4, cw, -1).transpose(2, 1, 0, 3, 4)
        return both.reshape(PARTS_W, PARTS_N, cw, -1)

    def natural(value, blocks):
        split = value.reshape(PARTS_W, PARTS_N, cw, blocks, -1).transpose(0, 3, 2, 1, 4)
        return split.reshape(PARTS_W * blocks * cw, -1).T

    def share(value):
        columns = lax.psum_scatter(value.astype(BF16), "wide", scatter_dimension=1, tiled=True)
        return lax.psum_scatter(columns, "narrow", scatter_dimension=0, tiled=True).astype(F32)

    a = devices(gown_a, gsend_a)
    b = devices(gown_b, gsend_b)
    reduce = natural(a[..., :width], 1)
    q = natural(a[..., width : width + rn], 1)
    kv = natural(a[..., width + rn : width + 3 * rn], 2)
    proj = natural(a[..., width + 3 * rn :], 1)
    down = natural(b[..., :width], 1)
    up = b[..., width:].reshape(PARTS_W, PARTS_N, cw, rn // cw, 4 * cw).transpose(1, 3, 2, 0, 4)
    up = up.reshape(width, PARTS_W * 4 * cw)
    vectors = jnp.stack([vown, vsend], axis=1).reshape(PARTS_N, 16, -1)[:, :11].transpose(1, 0, 2)
    vm = vectors[..., :rn].reshape(11, width)
    vh = vectors[..., rn : rn + width].reshape(11, PARTS_N * width)

    def share_vector(value):
        total = lax.psum(value.astype(BF16), "wide")
        return lax.psum_scatter(total, "narrow", scatter_dimension=1, tiled=True).astype(F32)

    return tuple(share(v) for v in (q, kv, reduce, proj, up, down)) + (share_vector(vm), share_vector(vh))


def solution(mesh):
    both, rows, weight, vector = P(("wide", "narrow"), None), P(("wide", "narrow")), P("narrow", "wide"), P(None, "narrow")
    return jax.shard_map(
        functools.partial(on_device, (mesh.shape["wide"], mesh.shape["narrow"])),
        mesh=mesh,
        in_specs=(both, both, rows, rows) + (weight,) * 6 + (vector,) * 2,
        out_specs=(both, both) + (weight,) * 6 + (vector,) * 2,
        check_vma=False,
    )
```

```python
import functools
import math

import jax
import jax.numpy as jnp
from jax import lax
from jax.experimental import pallas as pl
from jax.experimental.pallas import tpu as pltpu
from jax.sharding import PartitionSpec as P

HEADS = 5
EPSILON = 1e-06
MASKED = -1000000000.0
F32 = jnp.float32
BF16 = jnp.bfloat16

PARTS_W = 8
PARTS_N = 4
SLOTS = 16
TILE = 32
CHUNK = 256
PAD = 40
UNROLL = 4
RUN = 160
REST = RUN - 128


def dot_nn(left, right):
    return jnp.dot(left, right, preferred_element_type=F32)


def dot_nt(left, right):
    return lax.dot_general(left, right, (((1,), (1,)), ((), ())), preferred_element_type=F32)


def dot_tn(left, right):
    return lax.dot_general(left, right, (((0,), (0,)), ((), ())), preferred_element_type=F32)


def lanes(*parts):
    return jnp.concatenate(parts, axis=1)


def rows_of(*parts):
    return jnp.concatenate(parts, axis=0)


def my_index(tuned):
    if not tuned:
        return jnp.int32(0)
    return lax.axis_index("wide") * PARTS_N + lax.axis_index("narrow")


def slot_of(device, me):
    delta = device ^ me
    return ((delta >> 1) & 3) * 4 + (delta >> 3)


def round_slot(device, me):
    delta = device ^ me
    first, second = (delta >> 1) & 1, (delta >> 2) & 1
    if device & 1:
        first, second = second, first
    return second * 8 + first * 4 + (delta >> 3)


def normalise(values):
    centre = values - jnp.mean(values, axis=-1, keepdims=True)
    inverse = lax.rsqrt(jnp.mean(centre * centre, axis=-1, keepdims=True) + EPSILON)
    return centre * inverse, inverse


def normalise_back(grad, normed, inverse, gain):
    scaled = grad * gain
    first = jnp.mean(scaled, axis=-1, keepdims=True)
    second = jnp.mean(scaled * normed, axis=-1, keepdims=True)
    return (scaled - first - normed * second) * inverse


def column_sum(values):
    return jnp.sum(values, axis=0, keepdims=True)


def piece_of(own_ref, other_ref, device, me, first=0, last=5):
    slot = round_slot(device, me)
    mine = ((device ^ me) & 1) == 0
    at = pl.ds(128 * first, 128 * (last - first))
    return jnp.where(mine, own_ref[slot, :, at].astype(F32), other_ref[slot, :, at].astype(F32))


def token_geometry(geo_ref, capacity, width):
    row0, row1, col0, col1 = (geo_ref[k] for k in range(4))
    area0, area1 = row0 * col0, row1 * col1
    position = lax.broadcasted_iota(jnp.int32, (capacity, width), 0)
    first = position < area0
    second = jnp.logical_and(position >= area0, position < area0 + area1)
    widths = jnp.maximum(jnp.where(second, col1, col0), 2)
    heights = jnp.where(second, row1, row0)
    local = position - jnp.where(second, area0, 0)
    row = ((local.astype(F32) + 0.5) / widths.astype(F32)).astype(jnp.int32)
    col = local - row * widths
    return first, second, row, col, heights, widths


def pack_kernel(*refs):
    sources, (ab_ref, v_ref), held, semaphores = refs[:8], refs[8:10], refs[10:18], refs[18]
    copies = [pltpu.make_async_copy(source, ref, semaphores.at[i]) for i, (source, ref) in enumerate(zip(sources, held))]
    for copy in copies:
        copy.start()
    for copy in copies:
        copy.wait()
    q_ref, kv_ref, red_ref, proj_ref, up_ref, down_ref, vm_ref, vh_ref = held
    cw = q_ref.shape[0]

    def wider(ref):
        return ref[...].astype(F32)

    kv = wider(kv_ref).T
    ab_ref[0] = lanes(wider(red_ref), wider(q_ref), kv[:cw], kv[cw:], wider(proj_ref)).astype(BF16)
    up, down = wider(up_ref), wider(down_ref)
    columns = (down[:, :RUN], down[:, RUN:], up[:cw], up[cw:])
    ab_ref[1] = lanes(*[c[:, :128] for c in columns], *[c[:, 128:] for c in columns]).astype(BF16)
    v_ref[0] = jnp.zeros_like(v_ref[0])
    both = lanes(wider(vm_ref), wider(vh_ref))
    v_ref[0, : both.shape[0], : both.shape[1]] = both.astype(BF16)


def pack(arguments, piece, vpiece):
    vmem = pl.BlockSpec(memory_space=pltpu.VMEM)
    return pl.pallas_call(
        pack_kernel,
        out_shape=[jax.ShapeDtypeStruct(shape, BF16) for shape in ((2,) + piece, (1,) + vpiece)],
        in_specs=[pl.BlockSpec(memory_space=pl.ANY)] * len(arguments),
        out_specs=[vmem] * 2,
        scratch_shapes=[pltpu.VMEM(v.shape, v.dtype) for v in arguments] + [pltpu.SemaphoreType.DMA((len(arguments),))],
        compiler_params=pltpu.CompilerParams(vmem_limit_bytes=60 * 2**20),
    )(*arguments)


def prepare_kernel(
    rows_hbm, cols_hbm, tok_hbm, x_ref, n1_ref, r1_ref, chosen_ref, live_ref, geo_ref,
    rows_ref, cols_ref, tok_ref, semaphores,
):
    copies = [
        pltpu.make_async_copy(source, target, semaphores.at[i])
        for i, (source, target) in enumerate(((rows_hbm, rows_ref), (cols_hbm, cols_ref), (tok_hbm, tok_ref)))
    ]
    for copy in copies:
        copy.start()
    for copy in copies:
        copy.wait()
    capacity = tok_ref.shape[1]
    for j in range(2):
        geo_ref[j] = rows_ref[j]
        geo_ref[2 + j] = cols_ref[j]
    tokens = tok_ref[...].astype(F32).T
    x_ref[...] = tokens
    normed, inverse = normalise(tokens)
    n1_ref[...] = normed
    r1_ref[...] = inverse
    chosen_ref[...] = one_hot(rows_ref, cols_ref, capacity)
    area0, area1 = rows_ref[0] * cols_ref[0], rows_ref[1] * cols_ref[1]
    quarter0, quarter1 = area0 // 4, area1 // 4
    token = lax.broadcasted_iota(jnp.int32, live_ref.shape, 0)
    key = lax.broadcasted_iota(jnp.int32, live_ref.shape, 1)
    live = ((token < area0) & (key < quarter0)) | (
        (token >= area0) & (token < area0 + area1) & (key >= quarter0) & (key < quarter0 + quarter1)
    )
    live_ref[...] = jnp.where(live, 1.0, 0.0)


def prepare(img_rows, img_cols, tokens):
    width, capacity = tokens.shape
    keys = capacity // 4
    vmem, smem = (pl.BlockSpec(memory_space=space) for space in (pltpu.VMEM, pltpu.SMEM))
    outputs = (
        ((capacity, width), F32), ((capacity, width), F32), ((capacity, 1), F32), ((capacity, capacity), BF16),
        ((capacity, keys), F32), ((4,), jnp.int32),
    )
    return pl.pallas_call(
        prepare_kernel,
        out_shape=[jax.ShapeDtypeStruct(shape, kind) for shape, kind in outputs],
        in_specs=[pl.BlockSpec(memory_space=pl.ANY)] * 3,
        out_specs=[vmem] * 5 + [smem],
        scratch_shapes=[
            pltpu.SMEM((2,), jnp.int32), pltpu.SMEM((2,), jnp.int32), pltpu.VMEM((width, capacity), BF16),
            pltpu.SemaphoreType.DMA((3,)),
        ],
        compiler_params=pltpu.CompilerParams(vmem_limit_bytes=60 * 2**20),
        cost_estimate=pl.CostEstimate(flops=2 * 10**9, bytes_accessed=0, transcendentals=0),
    )(img_rows, img_cols, tokens)


def attend_kernel(
    tuned,
    x_ref, n1_ref, chosen_ref, live_ref, own_ref, oth_ref, v0_ref, v1_ref, v2_ref, v3_ref,
    x2_ref, h1_ref, patch_ref, nk_ref, rk_ref, kn_ref, q_ref, kb_ref, vb_ref,
    p_ref, o_ref, wr_ref, wq_ref, wkv_ref, wp_ref, mv_ref, hv_ref,
    score_ref,
):
    me = my_index(tuned)
    capacity, width = x_ref.shape
    cw, rn = width // PARTS_W, width // PARTS_N
    keys = capacity // 4
    dim = width // HEADS

    held = [ref[0].astype(F32) for ref in (v0_ref, v1_ref, v2_ref, v3_ref)]
    odd = (me & 1) == 1
    held = [jnp.where(odd, held[k ^ 1], held[k]) for k in range(4)]
    odd = (me & 2) == 2
    pieces = [jnp.where(odd, held[k ^ 2], held[k]) for k in range(4)]
    mv = lanes(*[p[:, :rn] for p in pieces])
    mv_ref[...] = mv
    runs = [p[:, rn + e * RUN : rn + (e + 1) * RUN] for p in pieces for e in range(2)]
    hv_ref[...] = lanes(*[r[:, :128] for r in runs], *[r[:, 128:] for r in runs])

    for pair in range(PARTS_W // 2):
        got = [
            [piece_of(own_ref, oth_ref, w * PARTS_N + n, me) for n in range(PARTS_N)]
            for w in (2 * pair, 2 * pair + 1)
        ]
        at = pl.ds(pair * 2 * cw, 2 * cw)
        for n in range(PARTS_N):
            wr_ref[n, at, :] = rows_of(got[0][n][:, :width], got[1][n][:, :width]).astype(BF16)

        def unit(w, k):
            return lanes(*[got[w][n][:, width + k * rn : width + (k + 1) * rn] for n in range(PARTS_N)])

        wq_ref[at, :] = rows_of(unit(0, 0), unit(1, 0)).astype(BF16)
        wkv_ref[pl.ds(pair * 4 * cw, 4 * cw), :] = rows_of(
            unit(0, 1), unit(0, 2), unit(1, 1), unit(1, 2)
        ).astype(BF16)
        wp_ref[at, :] = rows_of(unit(0, 3), unit(1, 3)).astype(BF16)

    h1 = (n1_ref[...] * mv[0:1] + mv[1:2]).astype(BF16)
    h1_ref[...] = h1
    q = (dot_nt(h1, wq_ref[...]) + mv[2:3]).astype(BF16)
    q_ref[...] = q

    patches = dot_nn(chosen_ref[...], h1).astype(BF16)
    patch_ref[...] = patches
    reduced = mv[4:5]
    for n in range(4):
        reduced = reduced + dot_nt(patches[n * keys : (n + 1) * keys], wr_ref[n])
    nk, rk = normalise(reduced)
    nk_ref[...] = nk
    rk_ref[...] = rk
    kn = (nk * mv[5:6] + mv[6:7]).astype(BF16)
    kn_ref[...] = kn
    kv = dot_nt(kn, wkv_ref[...])
    k = kv[:, :width].astype(BF16).astype(F32)
    v = (kv[:, width:] + mv[3:4]).astype(BF16).astype(F32)
    lane = lax.broadcasted_iota(jnp.int32, (keys, width), 1)
    for h in range(HEADS):
        inside = (lane >= h * dim) & (lane < (h + 1) * dim)
        at = pl.ds(h * keys, keys)
        kb_ref[at, :] = jnp.where(inside, k, 0.0).astype(BF16)
        vb_ref[at, :] = jnp.where(inside, v, 0.0).astype(BF16)

    score_ref[...] = dot_nt(q, kb_ref[...]) * dim ** (-0.5)
    def soften(i, carry):
        at = pl.ds(pl.multiple_of(i * 64, 64), 64)
        live = live_ref[at, :] > 0.5
        for h in range(HEADS):
            lane_at = pl.ds(h * keys, keys)
            s = jnp.where(live, score_ref[at, lane_at], MASKED)
            e = jnp.exp(s - jnp.max(s, axis=-1, keepdims=True))
            p_ref[at, lane_at] = e / jnp.sum(e, axis=-1, keepdims=True)
        return carry

    lax.fori_loop(0, capacity // 64, soften, 0)
    o = dot_nn(p_ref[...].astype(BF16), vb_ref[...]).astype(BF16)
    o_ref[...] = o
    x2_ref[...] = x_ref[...] + dot_nt(o, wp_ref[...]) + mv[7:8]


def one_hot(rows_ref, cols_ref, capacity):
    row0, row1, col0, col1 = rows_ref[0], rows_ref[1], cols_ref[0], cols_ref[1]
    area0, area1 = row0 * col0, row1 * col1
    quarter0, quarter1 = area0 // 4, area1 // 4
    keys = capacity // 4
    index = lax.broadcasted_iota(jnp.int32, (capacity, 128), 0)
    tap = index // keys
    key = index - tap * keys
    first = key < quarter0
    second = jnp.logical_and(key >= quarter0, key < quarter0 + quarter1)
    width = jnp.maximum(jnp.where(second, col1, col0), 2)
    half = width // 2
    local = key - jnp.where(second, quarter0, 0)
    row = ((local.astype(F32) + 0.5) / half.astype(F32)).astype(jnp.int32)
    col = local - row * half
    token = jnp.where(second, area0, 0) + (2 * row + tap // 2) * width + 2 * col + tap % 2
    token = jnp.where(first | second, token, -1)
    lane = lax.broadcasted_iota(jnp.int32, (capacity, 128), 1)
    return lanes(
        *[jnp.where(token == lane + t * 128, 1.0, 0.0).astype(BF16) for t in range(capacity // 128)]
    )


def prepare_two_kernel(
    geo_ref, cot_ref, x2_ref, mv_ref, n2_ref, r2_ref, h2_ref, h2t_ref, gy_ref, gyt_ref, mask_ref
):
    width, capacity = cot_ref.shape
    normed, inverse = normalise(x2_ref[...])
    n2_ref[...] = normed
    r2_ref[...] = inverse
    h2 = normed * mv_ref[8:9, :] + mv_ref[9:10, :]
    h2_ref[...] = h2.astype(BF16)
    h2t_ref[...] = h2.T.astype(BF16)
    area = geo_ref[0] * geo_ref[2] + geo_ref[1] * geo_ref[3]
    position = lax.broadcasted_iota(jnp.int32, (width, capacity), 1)
    gyt = jnp.where(position < area, cot_ref[...].astype(F32), 0.0)
    gyt_ref[...] = gyt.astype(BF16)
    gy_ref[...] = gyt.T.astype(BF16)
    first, second, row, col, heights, widths = token_geometry(geo_ref, capacity, 128)
    live = first | second
    conditions = (
        live & (col > 0),
        live & (col < widths - 1),
        first & (row > 0),
        second & (row > 0),
        first & (row < heights - 1),
        second & (row < heights - 1),
        live,
    )
    for k, condition in enumerate(conditions):
        mask_ref[k] = jnp.where(condition, 1.0, 0.0)


def ffn_kernel(
    tuned,
    geo_ref, n2_ref, r2_ref, h2_ref, h2t_ref, gy_ref, gyt_ref, mask_ref, own_ref, oth_ref, mv_ref, hv_ref,
    gown_ref, gsend_ref, mix_ref, dx2_ref, mg_ref, hg_ref,
    wu_ref, wd_ref, f_ref, gm_ref, gp_ref, dc_ref, ul_ref, ur_ref, g0_ref, slope_ref, act_ref, u0_ref, df_ref, da_ref,
    dh2_ref, upg_ref, dng_ref,
):
    me = my_index(tuned)
    capacity, width = n2_ref.shape
    hidden = hv_ref.shape[1]
    cw, rn = width // PARTS_W, width // PARTS_N
    tiles = capacity // TILE
    tails = 128 * PARTS_W

    for pair in range(PARTS_W // 2):
        at = pl.ds(pair * 2 * cw, 2 * cw)
        got = [
            rows_of(*[piece_of(own_ref, oth_ref, w * PARTS_N + n, me, 0, 5) for w in (2 * pair, 2 * pair + 1)])
            for n in range(PARTS_N)
        ]
        for n in range(PARTS_N):
            wd_ref[at, pl.ds(256 * n, 256)] = got[n][:, :256].astype(BF16)
        wd_ref[at, pl.ds(tails, 2 * REST * PARTS_N)] = lanes(*[g[:, 512 : 512 + 2 * REST] for g in got]).astype(BF16)
    for n in range(PARTS_N):
        at = pl.ds(n * rn, rn)
        ends = []
        for w in range(PARTS_W):
            got = piece_of(own_ref, oth_ref, w * PARTS_N + n, me, 2, 5)
            wu_ref[at, pl.ds(128 * w, 128)] = rows_of(got[:, :128], got[:, 128:256]).astype(BF16)
            ends.append(rows_of(got[:, 256 + 2 * REST : 256 + 3 * REST], got[:, 256 + 3 * REST :]))
        wu_ref[at, pl.ds(tails, REST * PARTS_W)] = lanes(*ends).astype(BF16)

    w0, w1 = geo_ref[2], geo_ref[3]

    for ref in (f_ref, gm_ref, gp_ref, dc_ref, ul_ref, ur_ref):
        ref[:, :PAD, :] = jnp.zeros((CHUNK // 128, PAD, 128), F32)
        ref[:, PAD + capacity :, :] = jnp.zeros((CHUNK // 128, PAD, 128), F32)

    mix_ref[...] = jnp.zeros_like(mix_ref)
    dh2_ref[...] = jnp.zeros_like(dh2_ref)

    def fold(values):
        return jnp.sum(values.reshape(TILE // 8, 8, 128), axis=0)

    halves = CHUNK // 128

    def chunk_step(c, carry):
        at_c = pl.ds(pl.multiple_of(c * CHUNK, CHUNK), CHUNK)

        def vector(k, j):
            return hv_ref[k : k + 1, pl.ds(pl.multiple_of(c * CHUNK + j * 128, 128), 128)]

        def put_vector(k, j, value):
            hg_ref[k : k + 1, pl.ds(pl.multiple_of(c * CHUNK + j * 128, 128), 128)] = value

        first_layer = dot_nn(h2_ref[...], wu_ref[:, at_c])
        for j in range(halves):
            f_ref[j, pl.ds(PAD, capacity), :] = first_layer[:, j * 128 : (j + 1) * 128] + vector(0, j)

        def taps_of(j, r, at):
            here = f_ref[j, pl.ds(PAD + r, TILE), :]
            left = f_ref[j, pl.ds(PAD + r - 1, TILE), :] * mask_ref[0, at, :]
            right = f_ref[j, pl.ds(PAD + r + 1, TILE), :] * mask_ref[1, at, :]
            return left, here, right

        def column_taps(i, carry):
            r = pl.multiple_of(i * TILE, TILE)
            at = pl.ds(r, TILE)
            for j in range(halves):
                left, here, right = taps_of(j, r, at)
                v = [vector(k, j) for k in range(11)]
                gm_ref[j, pl.ds(PAD + r, TILE), :] = v[2] * left + v[3] * here + v[4] * right
                g0_ref[j, at, :] = v[1] + v[5] * left + v[6] * here + v[7] * right
                gp_ref[j, pl.ds(PAD + r, TILE), :] = v[8] * left + v[9] * here + v[10] * right
            return carry

        lax.fori_loop(0, tiles, column_taps, 0, unroll=UNROLL)

        def activate(i, carry):
            r = pl.multiple_of(i * TILE, TILE)
            at = pl.ds(r, TILE)
            for j in range(halves):
                conv = (
                    g0_ref[j, at, :]
                    + mask_ref[2, at, :] * gm_ref[j, pl.ds(PAD + r - w0, TILE), :]
                    + mask_ref[3, at, :] * gm_ref[j, pl.ds(PAD + r - w1, TILE), :]
                    + mask_ref[4, at, :] * gp_ref[j, pl.ds(PAD + r + w0, TILE), :]
                    + mask_ref[5, at, :] * gp_ref[j, pl.ds(PAD + r + w1, TILE), :]
                )
                half = 0.5 * (1.0 + lax.erf(conv * 2.0 ** (-0.5)))
                lane_at = pl.ds(j * 128, 128)
                act_ref[at, lane_at] = (conv * half).astype(BF16)
                slope = half + conv * jnp.exp(-0.5 * conv * conv) * (2.0 * math.pi) ** (-0.5)
                slope_ref[at, lane_at] = slope
            return carry

        lax.fori_loop(0, tiles, activate, 0, unroll=UNROLL)
        act = act_ref[...]
        mix_ref[...] += dot_nt(act, wd_ref[:, at_c])
        dng_ref[:, at_c] = dot_nn(gyt_ref[...], act)
        da_ref[...] = dot_nn(gy_ref[...], wd_ref[:, at_c])

        def into_conv(i, carry):
            r = pl.multiple_of(i * TILE, TILE)
            at = pl.ds(r, TILE)
            totals = []
            for j in range(halves):
                value = da_ref[at, pl.ds(j * 128, 128)] * slope_ref[at, pl.ds(j * 128, 128)]
                dc_ref[j, pl.ds(PAD + r, TILE), :] = value
                totals.append(carry[j] + fold(value))
            return tuple(totals)

        zero = jnp.zeros((8, 128), F32)
        totals = lax.fori_loop(0, tiles, into_conv, (zero,) * halves, unroll=UNROLL)
        for j in range(halves):
            put_vector(1, j, column_sum(totals[j]))

        for j in range(halves):
            v = [vector(k, j) for k in range(11)]

            def tap_back(i, carry, j=j, v=v):
                r = pl.multiple_of(i * TILE, TILE)
                at = pl.ds(r, TILE)
                left, here, right = taps_of(j, r, at)
                below = (
                    mask_ref[4, at, :] * dc_ref[j, pl.ds(PAD + r + w0, TILE), :]
                    + mask_ref[5, at, :] * dc_ref[j, pl.ds(PAD + r + w1, TILE), :]
                )
                level = dc_ref[j, pl.ds(PAD + r, TILE), :]
                above = (
                    mask_ref[2, at, :] * dc_ref[j, pl.ds(PAD + r - w0, TILE), :]
                    + mask_ref[3, at, :] * dc_ref[j, pl.ds(PAD + r - w1, TILE), :]
                )
                ul_ref[j, pl.ds(PAD + r, TILE), :] = v[2] * below + v[5] * level + v[8] * above
                u0_ref[j, at, :] = v[3] * below + v[6] * level + v[9] * above
                ur_ref[j, pl.ds(PAD + r, TILE), :] = v[4] * below + v[7] * level + v[10] * above
                grads = [fold(d * f) for d in (below, level, above) for f in (left, here, right)]
                return tuple(a + b for a, b in zip(carry, grads))

            sums = lax.fori_loop(0, tiles, tap_back, (zero,) * 9, unroll=UNROLL)
            for k in range(9):
                put_vector(2 + k, j, column_sum(sums[k]))

        def spread_back(i, carry):
            r = pl.multiple_of(i * TILE, TILE)
            at = pl.ds(r, TILE)
            totals = []
            for j in range(halves):
                value = (
                    u0_ref[j, at, :]
                    + mask_ref[0, at, :] * ur_ref[j, pl.ds(PAD + r - 1, TILE), :]
                    + mask_ref[1, at, :] * ul_ref[j, pl.ds(PAD + r + 1, TILE), :]
                ).astype(BF16)
                df_ref[at, pl.ds(j * 128, 128)] = value
                totals.append(carry[j] + fold(value.astype(F32)))
            return tuple(totals)

        totals = lax.fori_loop(0, tiles, spread_back, (zero,) * halves, unroll=UNROLL)
        for j in range(halves):
            put_vector(0, j, column_sum(totals[j]))
        df = df_ref[...]
        upg_ref[:, at_c] = dot_nn(h2t_ref[...], df)
        dh2_ref[...] += dot_nt(df, wu_ref[:, at_c])
        return carry

    lax.fori_loop(0, hidden // CHUNK, chunk_step, 0)
    hg_ref[11:, :] = jnp.zeros((hg_ref.shape[0] - 11, hidden), F32)

    def value_of(w, n):
        down = pl.ds(w * cw, cw)
        up = [pl.ds(n * rn + e * cw, cw) for e in range(2)]
        return lanes(
            dng_ref[down, pl.ds(256 * n, 256)],
            *[upg_ref[e, pl.ds(128 * w, 128)] for e in up],
            dng_ref[down, pl.ds(tails + 2 * REST * n, 2 * REST)],
            *[upg_ref[e, pl.ds(tails + REST * w, REST)] for e in up],
        )

    store_pieces(gown_ref, gsend_ref, me, value_of)

    def finish(i, carry):
        at = pl.ds(pl.multiple_of(i * 64, 64), 64)
        gy = gy_ref[at, :].astype(F32)
        grad, normed = dh2_ref[at, :], n2_ref[at, :]
        dx2_ref[at, :] = gy + normalise_back(grad, normed, r2_ref[at, :], mv_ref[8:9, :])
        return tuple(a + column_sum(b) for a, b in zip(carry, (grad * normed, grad, gy)))

    zero = jnp.zeros((1, width), F32)
    sums = lax.fori_loop(0, capacity // 64, finish, (zero, zero, zero))
    mg_ref[...] = jnp.zeros_like(mg_ref)
    for k in range(3):
        mg_ref[8 + k : 9 + k, :] = sums[k]


def store_pieces(own_ref, send_ref, me, value_of):
    even = (me & 1) == 0
    for w in range(PARTS_W):
        for x in range(PARTS_N // 2):
            first, second = value_of(w, 2 * x), value_of(w, 2 * x + 1)
            slot = slot_of(w * PARTS_N + 2 * x, me)
            own_ref[slot] = jnp.where(even, first, second).astype(BF16)
            send_ref[slot] = jnp.where(even, second, first).astype(BF16)


def score_back_kernel(dx2_ref, vb_ref, p_ref, o_ref, wp_ref, gp_ref, dob_ref, ds_ref, bp_ref, dp_ref):
    capacity = dx2_ref.shape[0]
    keys = capacity // 4
    datt = dx2_ref[...].astype(BF16)
    bp_ref[...] = column_sum(datt.astype(F32))
    gp_ref[...] = dot_tn(datt, o_ref[...])
    dob = dot_nn(datt, wp_ref[...]).astype(BF16)
    dob_ref[...] = dob
    dp_ref[...] = dot_nt(dob, vb_ref[...])

    def soften_back(i, carry):
        at = pl.ds(pl.multiple_of(i * 64, 64), 64)
        for h in range(HEADS):
            lane_at = pl.ds(h * keys, keys)
            p = p_ref[at, lane_at]
            dp = dp_ref[at, lane_at]
            row = jnp.sum(p * dp, axis=-1, keepdims=True)
            ds_ref[at, lane_at] = (p * (dp - row)).astype(BF16)
        return carry

    lax.fori_loop(0, capacity // 64, soften_back, 0)


def attend_back_kernel(
    tuned,
    dob_ref, ds_ref, gp_ref, h1_ref, patch_ref, nk_ref, rk_ref, kn_ref, q_ref, kb_ref, p_ref,
    wr_ref, wkv_ref, mv_ref,
    gown_ref, gsend_ref, dq_ref, dpatch_ref, vk_ref,
    gr_ref, gq_ref, gkv_ref,
):
    me = my_index(tuned)
    capacity, width = h1_ref.shape
    cw, rn = width // PARTS_W, width // PARTS_N
    keys = capacity // 4
    dim = width // HEADS
    scale = dim ** (-0.5)

    ds = ds_ref[...]
    dq = (dot_nn(ds, kb_ref[...]) * scale).astype(BF16)
    dq_ref[...] = dq
    dk_all = dot_tn(ds, q_ref[...])
    dv_all = dot_tn(p_ref[...].astype(BF16), dob_ref[...])
    lane = lax.broadcasted_iota(jnp.int32, (keys, width), 1)
    dk = jnp.zeros((keys, width), F32)
    dv = jnp.zeros((keys, width), F32)
    for h in range(HEADS):
        inside = (lane >= h * dim) & (lane < (h + 1) * dim)
        dk = jnp.where(inside, dk_all[h * keys : (h + 1) * keys], dk)
        dv = jnp.where(inside, dv_all[h * keys : (h + 1) * keys], dv)
    dk = (dk * scale).astype(BF16)
    dv = dv.astype(BF16)
    gq_ref[...] = dot_tn(dq, h1_ref[...])
    kn = kn_ref[...]
    gkv_ref[pl.ds(0, width), :] = dot_tn(dk, kn)
    gkv_ref[pl.ds(width, width), :] = dot_tn(dv, kn)
    dkn = dot_nn(dk, wkv_ref[pl.ds(0, width), :]) + dot_nn(dv, wkv_ref[pl.ds(width, width), :])
    nk = nk_ref[...]
    dsr = normalise_back(dkn, nk, rk_ref[...], mv_ref[5:6, :]).astype(BF16)
    vk_ref[...] = rows_of(
        column_sum(dq.astype(F32)),
        column_sum(dv.astype(F32)),
        column_sum(dsr.astype(F32)),
        column_sum(dkn * nk),
        column_sum(dkn),
        jnp.zeros((3, width), F32),
    )
    for n in range(4):
        at = pl.ds(n * keys, keys)
        gr_ref[n] = dot_tn(dsr, patch_ref[at, :])
        dpatch_ref[at, :] = dot_nn(dsr, wr_ref[n])

    def value_of(w, n):
        at, lane_at = pl.ds(w * cw, cw), pl.ds(n * rn, rn)
        return lanes(
            gr_ref[n, at, :],
            gq_ref[at, lane_at],
            gkv_ref[pl.ds(2 * w * cw, cw), lane_at],
            gkv_ref[pl.ds(2 * w * cw + cw, cw), lane_at],
            gp_ref[at, lane_at],
        )

    store_pieces(gown_ref, gsend_ref, me, value_of)


def token_back_kernel(
    tuned,
    dx2_ref, dq_ref, dpatch_ref, n1_ref, r1_ref, chosen_ref, wq_ref, mv_ref, mg_ref, hg_ref, vk_ref, bp_ref,
    x2_ref, mix_ref, mask_ref,
    mixed_ref, tg_ref, vown_ref, vsend_ref,
):
    me = my_index(tuned)
    capacity, width = dx2_ref.shape
    rn = width // PARTS_N
    occupied = mask_ref[6]
    occupied = lanes(*([occupied] * (width // 128)), occupied[:, : width % 128])
    mixed_ref[...] = ((x2_ref[...] + mix_ref[...] + mv_ref[10:11, :]) * occupied).T.astype(BF16)
    chosen = chosen_ref[...]
    high = dpatch_ref[...].astype(BF16)
    low = (dpatch_ref[...] - high.astype(F32)).astype(BF16)
    dh1 = dot_nn(dq_ref[...], wq_ref[...]) + dot_tn(chosen, high) + dot_tn(chosen, low)
    n1 = n1_ref[...]
    vk = vk_ref[...]
    token_grad = dx2_ref[...] + normalise_back(dh1, n1, r1_ref[...], mv_ref[0:1, :])
    tg_ref[...] = token_grad.T.astype(BF16)
    sums = rows_of(column_sum(dh1 * n1), column_sum(dh1), vk[0:5], bp_ref[...], mg_ref[8:16, :])
    hg = hg_ref[...]
    spare = jnp.zeros((16, 3 * rn), F32)
    value = []
    for n in range(PARTS_N):
        parts = []
        for w in (2 * n, 2 * n + 1):
            parts += [hg[:, 128 * w : 128 * (w + 1)], hg[:, 1024 + REST * w : 1024 + REST * (w + 1)]]
        value.append(lanes(sums[:, n * rn : (n + 1) * rn], *parts, spare))
    even = (me & 1) == 0
    for x in range(2):
        slot = x ^ ((me >> 1) & 1)
        vown_ref[slot] = jnp.where(even, value[2 * x], value[2 * x + 1]).astype(BF16)
        vsend_ref[slot] = jnp.where(even, value[2 * x + 1], value[2 * x]).astype(BF16)


def total_of(refs):
    value = refs[0][...].astype(F32)
    for ref in refs[1:]:
        value = value + ref[...].astype(F32)
    return value


def core_sum_kernel(own_ref, got_ref, *out_refs):
    for k, ref in enumerate(out_refs):
        at = slice(4 * k, 4 * k + 4)
        ref[...] = (own_ref[at].astype(F32) + got_ref[at].astype(F32)).astype(BF16)


def core_sum_vector_kernel(own_ref, got_ref, vown_ref, vgot_ref, *out_refs):
    cw = own_ref.shape[1]
    vector = [(vown_ref[x].astype(F32) + vgot_ref[x].astype(F32)).astype(BF16) for x in range(2)]
    for k, ref in enumerate(out_refs):
        parts = [own_ref[4 * k + j].astype(F32) + got_ref[4 * k + j].astype(F32) for j in range(4)]
        ref[pl.ds(0, 4 * cw), :] = rows_of(*parts).astype(BF16)
        ref[pl.ds(4 * cw, vector[0].shape[0]), :] = vector[k & 1]


def plane_sum_kernel(a_ref, b_ref, c_ref, d_ref, *out_refs):
    total = total_of((a_ref, b_ref, c_ref, d_ref)).astype(BF16)
    for k, ref in enumerate(out_refs):
        ref[0] = total[k]


def plane_sum_vector_kernel(cw, a_ref, b_ref, c_ref, d_ref, *out_refs):
    total = total_of((a_ref, b_ref, c_ref, d_ref))
    for k, ref in enumerate(out_refs):
        ref[...] = rows_of(total[k * cw : (k + 1) * cw], total[4 * cw :]).astype(BF16)


def finish_ffn_kernel(a_ref, b_ref, c_ref, d_ref, up_ref, down_ref):
    total = total_of((a_ref, b_ref, c_ref, d_ref))[0]
    columns = [
        lanes(total[:, 128 * k : 128 * (k + 1)], total[:, 512 + REST * k : 512 + REST * (k + 1)]) for k in range(4)
    ]
    down_ref[...] = lanes(*columns[:2])
    up_ref[...] = rows_of(*columns[2:])


def finish_attend_kernel(a_ref, b_ref, c_ref, d_ref, q_ref, kv_ref, red_ref, proj_ref, vm_ref, vh_ref):
    total = total_of((a_ref, b_ref, c_ref, d_ref))
    cw, width = red_ref.shape
    rn = q_ref.shape[1]
    red_ref[...] = total[:cw, :width]
    unit = [total[:cw, width + k * rn : width + (k + 1) * rn] for k in range(4)]
    q_ref[...] = unit[0]
    kv_ref[...] = rows_of(unit[1], unit[2]).T
    proj_ref[...] = unit[3]
    vm_ref[...] = total[cw : cw + vm_ref.shape[0], :rn]
    vh_ref[...] = total[cw : cw + vh_ref.shape[0], rn : rn + width]


def call(kernel, inputs, outputs, scratch=(), scalars=0, limit=40, flops=0, moved=0):
    vmem = pl.BlockSpec(memory_space=pltpu.VMEM)
    smem = pl.BlockSpec(memory_space=pltpu.SMEM)
    return pl.pallas_call(
        kernel,
        out_shape=[jax.ShapeDtypeStruct(shape, kind) for shape, kind in outputs],
        in_specs=[smem] * scalars + [vmem] * (len(inputs) - scalars),
        out_specs=[vmem] * len(outputs),
        scratch_shapes=[pltpu.VMEM(shape, kind) for shape, kind in scratch],
        compiler_params=pltpu.CompilerParams(vmem_limit_bytes=limit * 2**20),
        cost_estimate=pl.CostEstimate(flops=flops, bytes_accessed=moved, transcendentals=0),
    )(*inputs)


def after(value, *others):
    return lax.optimization_barrier((value, *others))[0]


def on_device(
    mesh_shape,
    tokens, cotangent, img_rows, img_cols,
    q_weight, kv_weight, reduce_weight, proj_weight, up_weight, down_weight, vec_model, vec_hidden,
):
    wide, narrow = mesh_shape
    tuned = (wide, narrow) == (PARTS_W, PARTS_N)
    capacity, width = tokens.shape
    hidden = vec_hidden.shape[1] * narrow
    cw, rn = width // PARTS_W, width // PARTS_N
    keys = capacity // 4
    piece = (cw, 2 * width)
    vpiece = (16, 2 * width)

    def swap(value, mask, other=None):
        masks = (mask, mask if other is None else other)
        pairs = [(i, i ^ masks[i & 1]) for i in range(wide * narrow)]
        return lax.ppermute(value, ("wide", "narrow"), pairs)

    tokens_f32 = ((capacity, width), F32)
    tokens_low = ((capacity, width), BF16)
    x, n1, r1, chosen, live, geo = prepare(img_rows, img_cols, tokens.T)
    if tuned:
        packed, pack_v = pack(
            (
                q_weight.T, kv_weight, reduce_weight.T, proj_weight.T, up_weight, down_weight.T,
                vec_model, vec_hidden,
            ),
            piece, vpiece,
        )
        line = [swap(packed, m) for m in (8, 16, 24)]
        vecs = [pack_v] + [swap(pack_v, m) for m in (1, 2, 3)]
        line = lax.optimization_barrier((*line, x, n1, chosen))[:3]
        near_a, near_b = (jnp.concatenate([v[k : k + 1] for v in (packed, *line)], axis=0) for k in range(2))
        half_a = jnp.concatenate([near_a, swap(near_a, 2, 4)], axis=0)
        half_b = jnp.concatenate([near_b, swap(near_b, 2, 4)], axis=0)
        own_a = jnp.concatenate([half_a, swap(half_a, 4, 2)], axis=0)
        own_a, half_b, *vecs = lax.optimization_barrier((own_a, half_b, *vecs))
        oth_a = swap(own_a, 1)
        rest_b = swap(half_b, 4, 2)
    else:
        own_a, oth_a, own_b, oth_b, vecs = gather_plain(
            q_weight, kv_weight, reduce_weight, proj_weight, up_weight, down_weight, vec_model, vec_hidden
        )

    square = (width, width)
    (
        x2, h1, patches, nk, rk, kn, q, kb, vb, p, o, wr, wq, wkv, wp, mv, hv,
    ) = call(
        functools.partial(attend_kernel, tuned),
        (x, n1, chosen, live, own_a, oth_a, *vecs),
        (
            tokens_f32, tokens_low,
            ((capacity, width), BF16), ((keys, width), F32), ((keys, 1), F32), ((keys, width), BF16),
            ((capacity, width), BF16), ((HEADS * keys, width), BF16), ((HEADS * keys, width), BF16),
            ((capacity, HEADS * keys), F32), ((capacity, width), BF16),
            ((4,) + square, BF16), (square, BF16), ((2 * width, width), BF16), (square, BF16),
            ((16, width), F32), ((16, hidden), F32),
        ),
        scratch=(((capacity, HEADS * keys), F32),),
        flops=8 * 10**9,
    )

    if tuned:
        own_b = jnp.concatenate([half_b, after(rest_b, x2)], axis=0)
        oth_b = swap(own_b, 1)
    padded = ((CHUNK // 128, capacity + 2 * PAD, 128), F32)
    halved = ((CHUNK // 128, capacity, 128), F32)
    chunked = ((capacity, CHUNK), F32)
    n2, r2, h2, h2t, gy, gyt, masks = call(
        prepare_two_kernel,
        (geo, cotangent.T, x2, mv),
        (
            tokens_f32, ((capacity, 1), F32), tokens_low, ((width, capacity), BF16),
            tokens_low, ((width, capacity), BF16), ((7, capacity, 128), F32),
        ),
        scalars=1,
        flops=2 * 10**9,
    )
    gown_b, gsend_b, mix, dx2, mg, hg = call(
        functools.partial(ffn_kernel, tuned),
        (geo, n2, r2, h2, h2t, gy, gyt, masks, own_b, oth_b, mv, hv),
        (
            ((SLOTS,) + piece, BF16), ((SLOTS,) + piece, BF16),
            tokens_f32, tokens_f32, ((16, width), F32), ((16, hidden), F32),
        ),
        scratch=(
            ((width, hidden), BF16), ((width, hidden), BF16),
            padded, padded, padded, padded, padded, padded,
            halved, chunked, ((capacity, CHUNK), BF16), halved, ((capacity, CHUNK), BF16), chunked,
            tokens_f32, ((width, hidden), F32), ((width, hidden), F32),
        ),
        scalars=1,
        flops=33 * 10**9,
    )

    if tuned:
        got_b = swap(gsend_b, 1)
    gp, dob, ds, bp = call(
        score_back_kernel,
        (dx2, vb, p, o, wp),
        (
            (square, F32), ((capacity, width), BF16), ((capacity, HEADS * keys), BF16), ((1, width), F32),
        ),
        scratch=(((capacity, HEADS * keys), F32),),
        flops=25 * 10**8,
    )
    four = (4,) + piece
    if tuned:
        got_b = after(got_b, ds)
        half_b = call(core_sum_kernel, (gown_b, got_b), ((four, BF16),) * 4)
        plane_b = [swap(half_b[k], 2 * k) for k in (1, 2, 3)]
        ds = after(ds, half_b[1])
    gown_a, gsend_a, dq, dpatch, vk = call(
        functools.partial(attend_back_kernel, tuned),
        (dob, ds, gp, h1, patches, nk, rk, kn, q, kb, p, wr, wkv, mv),
        (
            ((SLOTS,) + piece, BF16), ((SLOTS,) + piece, BF16), ((capacity, width), BF16), ((capacity, width), F32),
            ((8, width), F32),
        ),
        scratch=(((4,) + square, F32), (square, F32), ((2 * width, width), F32)),
        flops=0,
    )
    if tuned:
        got_a = swap(gsend_a, 1)
        near_b = call(plane_sum_kernel, (half_b[0], *plane_b), (((1,) + piece, BF16),) * 4, flops=2 * 10**10)
        line_b = [swap(near_b[k], 8 * k) for k in (1, 2, 3)]
    mixed, token_grad, vown, vsend = call(
        functools.partial(token_back_kernel, tuned),
        (dx2, dq, dpatch, n1, r1, chosen, wq, mv, mg, hg, vk, bp, x2, mix, masks),
        (((width, capacity), BF16), ((width, capacity), BF16), ((2,) + vpiece, BF16), ((2,) + vpiece, BF16)),
    )

    if not tuned:
        grads = scatter_plain(mesh_shape, width, gown_a, gsend_a, gown_b, gsend_b, vown, vsend)
        return (mixed.T, token_grad.T) + grads

    gown_a = after(gown_a, near_b[1])
    joined = ((4 * cw + 16, 2 * width), BF16)
    half_a = call(core_sum_vector_kernel, (gown_a, got_a, vown, swap(vsend, 1)), (joined,) * 4)
    plane_a = [swap(half_a[k], 2 * k) for k in (1, 2, 3)]
    plane_a = lax.optimization_barrier((*plane_a, *line_b))[:3]
    near_a = call(
        functools.partial(plane_sum_vector_kernel, cw), (half_a[0], *plane_a), (((cw + 16, 2 * width), BF16),) * 4
    )
    line_a = [swap(near_a[k], 8 * k) for k in (1, 2, 3)]
    up_grad, down_grad = call(
        finish_ffn_kernel, (near_b[0], *line_b), (((rn, 4 * cw), F32), ((cw, width), F32))
    )
    q_grad, kv_grad, reduce_grad, proj_grad, vm_grad, vh_grad = call(
        finish_attend_kernel,
        (near_a[0], *line_a),
        (
            ((cw, rn), F32), ((rn, 2 * cw), F32), ((cw, width), F32), ((cw, rn), F32),
            ((11, rn), F32), ((11, width), F32),
        ),
    )
    return (
        mixed.T, token_grad.T, q_grad.T, kv_grad, reduce_grad.T, proj_grad.T, up_grad, down_grad.T, vm_grad, vh_grad,
    )


def gather_plain(q, kv, reduce, proj, up, down, vec_model, vec_hidden):
    def whole(value):
        rows = lax.all_gather(value, "narrow", axis=0, tiled=True)
        return lax.all_gather(rows, "wide", axis=1, tiled=True).T

    q, kv, reduce, proj, up, down = (whole(v) for v in (q, kv, reduce, proj, up, down))
    width = q.shape[0]
    cw, rn = width // PARTS_W, width // PARTS_N

    def pieces(turned, blocks):
        split = turned.reshape(PARTS_W, blocks, cw, PARTS_N, -1)
        return split.transpose(0, 3, 2, 1, 4).reshape(PARTS_W, PARTS_N, cw, -1)

    def slots(value):
        value = value.reshape(4, 2, 2, 2, cw, -1)
        even = value[:, :, :, 0].transpose(1, 2, 0, 3, 4)
        odd = value[:, :, :, 1].transpose(2, 1, 0, 3, 4)
        return even.reshape(SLOTS, cw, -1), odd.reshape(SLOTS, cw, -1)

    a = jnp.concatenate([pieces(reduce, 1), pieces(q, 1), pieces(kv, 2), pieces(proj, 1)], axis=-1)
    columns = pieces(down, 1).reshape(PARTS_W, PARTS_N, cw, 2, RUN)
    columns = [columns[..., e, :] for e in range(2)]
    halves = up.T.reshape(PARTS_N, 2, cw, PARTS_W, RUN).transpose(1, 3, 0, 2, 4)
    columns += [halves[0], halves[1]]
    b = jnp.concatenate([c[..., :128] for c in columns] + [c[..., 128:] for c in columns], axis=-1)
    vm = lax.all_gather(vec_model, "narrow", axis=1, tiled=True)
    vh = lax.all_gather(vec_hidden, "narrow", axis=1, tiled=True)
    both = jnp.concatenate([vm.reshape(11, PARTS_N, rn), vh.reshape(11, PARTS_N, width)], axis=-1)
    vecs = jnp.pad(both.transpose(1, 0, 2), ((0, 0), (0, 5), (0, 3 * rn)))
    return (*slots(a), *slots(b), [vecs[n : n + 1] for n in range(PARTS_N)])


def scatter_plain(mesh_shape, width, gown_a, gsend_a, gown_b, gsend_b, vown, vsend):
    cw, rn = width // PARTS_W, width // PARTS_N

    def devices(own, send):
        both = jnp.stack([own, send]).reshape(2, 4, 4, cw, -1).transpose(2, 1, 0, 3, 4)
        return both.reshape(PARTS_W, PARTS_N, cw, -1)

    def natural(value, blocks):
        split = value.reshape(PARTS_W, PARTS_N, cw, blocks, -1).transpose(0, 3, 2, 1, 4)
        return split.reshape(PARTS_W * blocks * cw, -1).T

    def share(value):
        columns = lax.psum_scatter(value.astype(BF16), "wide", scatter_dimension=1, tiled=True)
        return lax.psum_scatter(columns, "narrow", scatter_dimension=0, tiled=True).astype(F32)

    a = devices(gown_a, gsend_a)
    b = devices(gown_b, gsend_b)
    reduce = natural(a[..., :width], 1)
    q = natural(a[..., width : width + rn], 1)
    kv = natural(a[..., width + rn : width + 3 * rn], 2)
    proj = natural(a[..., width + 3 * rn :], 1)
    columns = [
        jnp.concatenate([b[..., 128 * k : 128 * (k + 1)], b[..., 512 + REST * k : 512 + REST * (k + 1)]], axis=-1)
        for k in range(4)
    ]
    down = natural(jnp.concatenate(columns[:2], axis=-1), 1)
    up = jnp.stack(columns[2:]).transpose(2, 0, 3, 1, 4).reshape(width, -1)
    vectors = jnp.stack([vown, vsend], axis=1).reshape(PARTS_N, 16, -1)[:, :11].transpose(1, 0, 2)
    vm = vectors[..., :rn].reshape(11, width)
    vh = vectors[..., rn : rn + width].reshape(11, PARTS_N * width)

    def share_vector(value):
        total = lax.psum(value.astype(BF16), "wide")
        return lax.psum_scatter(total, "narrow", scatter_dimension=1, tiled=True).astype(F32)

    return tuple(share(v) for v in (q, kv, reduce, proj, up, down)) + (share_vector(vm), share_vector(vh))


def solution(mesh):
    both, rows, weight, vector = P(("wide", "narrow"), None), P(("wide", "narrow")), P("narrow", "wide"), P(None, "narrow")
    return jax.shard_map(
        functools.partial(on_device, (mesh.shape["wide"], mesh.shape["narrow"])),
        mesh=mesh,
        in_specs=(both, both, rows, rows) + (weight,) * 6 + (vector,) * 2,
        out_specs=(both, both) + (weight,) * 6 + (vector,) * 2,
        check_vma=False,
    )
```

```python
import functools
import math

import jax
import jax.numpy as jnp
from jax import lax
from jax.experimental import pallas as pl
from jax.experimental.pallas import tpu as pltpu
from jax.sharding import PartitionSpec as P

HEADS = 5
EPSILON = 1e-06
MASKED = -1000000000.0
F32 = jnp.float32
BF16 = jnp.bfloat16

PARTS_W = 8
PARTS_N = 4
SLOTS = 16
TILE = 32
CHUNK = 256
PAD = 40
MROWS = 512
RUN = 160
REST = RUN - 128


def dot_nn(left, right):
    return jnp.dot(left, right, preferred_element_type=F32)


def dot_nt(left, right):
    return lax.dot_general(left, right, (((1,), (1,)), ((), ())), preferred_element_type=F32)


def dot_tn(left, right):
    return lax.dot_general(left, right, (((0,), (0,)), ((), ())), preferred_element_type=F32)


def lanes(*parts):
    return jnp.concatenate(parts, axis=1)


def rows_of(*parts):
    return jnp.concatenate(parts, axis=0)


def my_index(tuned):
    if not tuned:
        return jnp.int32(0)
    return lax.axis_index("wide") * PARTS_N + lax.axis_index("narrow")


def round_slot(device, me):
    delta = device ^ me
    first, second = (delta >> 1) & 1, (delta >> 2) & 1
    if device & 1:
        first, second = second, first
    return second * 8 + first * 4 + (delta >> 3)


def mixed_slot(device, me):
    delta = device ^ me
    plane = [(delta >> 1) & 1, (delta >> 2) & 1]
    line = [(delta >> 4) & 1, (delta >> 3) & 1]
    if device & 1:
        plane = plane[::-1]
    return plane[1] * 8 + line[1] * 4 + line[0] * 2 + plane[0]


def normalise(values):
    centre = values - jnp.mean(values, axis=-1, keepdims=True)
    inverse = lax.rsqrt(jnp.mean(centre * centre, axis=-1, keepdims=True) + EPSILON)
    return centre * inverse, inverse


def normalise_back(grad, normed, inverse, gain):
    scaled = grad * gain
    first = jnp.mean(scaled, axis=-1, keepdims=True)
    second = jnp.mean(scaled * normed, axis=-1, keepdims=True)
    return (scaled - first - normed * second) * inverse


def column_sum(values):
    return jnp.sum(values, axis=0, keepdims=True)


def piece_of(own_ref, other_ref, device, me, first=0, last=5, order=round_slot):
    slot = order(device, me)
    mine = ((device ^ me) & 1) == 0
    at = pl.ds(128 * first, 128 * (last - first))
    return jnp.where(mine, own_ref[slot, :, at].astype(F32), other_ref[slot, :, at].astype(F32))


def token_geometry(geo_ref, capacity, width):
    row0, row1, col0, col1 = (geo_ref[k] for k in range(4))
    area0, area1 = row0 * col0, row1 * col1
    position = lax.broadcasted_iota(jnp.int32, (capacity, width), 0)
    first = position < area0
    second = jnp.logical_and(position >= area0, position < area0 + area1)
    widths = jnp.maximum(jnp.where(second, col1, col0), 2)
    heights = jnp.where(second, row1, row0)
    local = position - jnp.where(second, area0, 0)
    row = ((local.astype(F32) + 0.5) / widths.astype(F32)).astype(jnp.int32)
    col = local - row * widths
    return first, second, row, col, heights, widths


def pack_kernel(*refs):
    sources, (a_ref, b_ref, v_ref), held, semaphores = refs[:8], refs[8:11], refs[11:19], refs[19]
    copies = [pltpu.make_async_copy(source, ref, semaphores.at[i]) for i, (source, ref) in enumerate(zip(sources, held))]
    for copy in copies:
        copy.start()
    for copy in copies:
        copy.wait()
    q_ref, kv_ref, red_ref, proj_ref, up_ref, down_ref, vm_ref, vh_ref = held
    cw = q_ref.shape[0]

    def wider(ref):
        return ref[...].astype(F32)

    kv = wider(kv_ref).T
    a_ref[0] = lanes(wider(red_ref), wider(q_ref), kv[:cw], kv[cw:], wider(proj_ref)).astype(BF16)
    up, down = wider(up_ref), wider(down_ref)
    columns = (down[:, :RUN], down[:, RUN:], up[:cw], up[cw:])
    b_ref[0] = lanes(*[c[:, :128] for c in columns], *[c[:, 128:] for c in columns]).astype(BF16)
    v_ref[0] = jnp.zeros_like(v_ref[0])
    both = lanes(wider(vm_ref), wider(vh_ref))
    v_ref[0, : both.shape[0], : both.shape[1]] = both.astype(BF16)


def pack(arguments, piece, vpiece):
    vmem = pl.BlockSpec(memory_space=pltpu.VMEM)
    return pl.pallas_call(
        pack_kernel,
        out_shape=[jax.ShapeDtypeStruct((1,) + shape, BF16) for shape in (piece, piece, vpiece)],
        in_specs=[pl.BlockSpec(memory_space=pl.ANY)] * len(arguments),
        out_specs=[vmem] * 3,
        scratch_shapes=[pltpu.VMEM(v.shape, v.dtype) for v in arguments] + [pltpu.SemaphoreType.DMA((len(arguments),))],
        compiler_params=pltpu.CompilerParams(vmem_limit_bytes=60 * 2**20),
    )(*arguments)


def prepare_kernel(
    rows_hbm, cols_hbm, tok_hbm, x_ref, n1_ref, r1_ref, chosen_ref, live_ref, geo_ref,
    rows_ref, cols_ref, tok_ref, semaphores,
):
    copies = [
        pltpu.make_async_copy(source, target, semaphores.at[i])
        for i, (source, target) in enumerate(((rows_hbm, rows_ref), (cols_hbm, cols_ref), (tok_hbm, tok_ref)))
    ]
    for copy in copies:
        copy.start()
    for copy in copies:
        copy.wait()
    capacity = tok_ref.shape[1]
    for j in range(2):
        geo_ref[j] = rows_ref[j]
        geo_ref[2 + j] = cols_ref[j]
    tokens = tok_ref[...].astype(F32).T
    x_ref[...] = tokens
    normed, inverse = normalise(tokens)
    n1_ref[...] = normed
    r1_ref[...] = inverse
    chosen_ref[...] = one_hot(rows_ref, cols_ref, capacity)
    area0, area1 = rows_ref[0] * cols_ref[0], rows_ref[1] * cols_ref[1]
    quarter0, quarter1 = area0 // 4, area1 // 4
    token = lax.broadcasted_iota(jnp.int32, live_ref.shape, 0)
    key = lax.broadcasted_iota(jnp.int32, live_ref.shape, 1)
    live = ((token < area0) & (key < quarter0)) | (
        (token >= area0) & (token < area0 + area1) & (key >= quarter0) & (key < quarter0 + quarter1)
    )
    live_ref[...] = jnp.where(live, 1.0, 0.0)


def prepare(img_rows, img_cols, tokens):
    width, capacity = tokens.shape
    keys = capacity // 4
    vmem, smem = (pl.BlockSpec(memory_space=space) for space in (pltpu.VMEM, pltpu.SMEM))
    outputs = (
        ((capacity, width), F32), ((capacity, width), F32), ((capacity, 1), F32), ((capacity, capacity), BF16),
        ((capacity, keys), F32), ((4,), jnp.int32),
    )
    return pl.pallas_call(
        prepare_kernel,
        out_shape=[jax.ShapeDtypeStruct(shape, kind) for shape, kind in outputs],
        in_specs=[pl.BlockSpec(memory_space=pl.ANY)] * 3,
        out_specs=[vmem] * 5 + [smem],
        scratch_shapes=[
            pltpu.SMEM((2,), jnp.int32), pltpu.SMEM((2,), jnp.int32), pltpu.VMEM((width, capacity), BF16),
            pltpu.SemaphoreType.DMA((3,)),
        ],
        compiler_params=pltpu.CompilerParams(vmem_limit_bytes=60 * 2**20),
        cost_estimate=pl.CostEstimate(flops=2 * 10**9, bytes_accessed=0, transcendentals=0),
    )(img_rows, img_cols, tokens)


def attend_kernel(
    tuned,
    x_ref, n1_ref, chosen_ref, live_ref, own_ref, oth_ref, vec_ref,
    x2_ref, h1_ref, patch_ref, nk_ref, rk_ref, kn_ref, q_ref, kb_ref, vb_ref,
    p_ref, o_ref, wr_ref, wq_ref, wkv_ref, wp_ref, mv_ref, hv_ref,
    score_ref,
):
    me = my_index(tuned)
    capacity, width = x_ref.shape
    cw, rn = width // PARTS_W, width // PARTS_N
    keys = capacity // 4
    dim = width // HEADS

    pieces = [vec_ref[n ^ (me & 3)].astype(F32) for n in range(PARTS_N)]
    mv = lanes(*[p[:, :rn] for p in pieces])
    mv_ref[...] = mv
    runs = [p[:, rn + e * RUN : rn + (e + 1) * RUN] for p in pieces for e in range(2)]
    hv_ref[...] = lanes(*[r[:, :128] for r in runs], *[r[:, 128:] for r in runs])

    for pair in range(PARTS_W // 2):
        got = [
            [piece_of(own_ref, oth_ref, w * PARTS_N + n, me) for n in range(PARTS_N)]
            for w in (2 * pair, 2 * pair + 1)
        ]
        at = pl.ds(pair * 2 * cw, 2 * cw)
        for n in range(PARTS_N):
            wr_ref[n, at, :] = rows_of(got[0][n][:, :width], got[1][n][:, :width]).astype(BF16)

        def unit(w, k):
            return lanes(*[got[w][n][:, width + k * rn : width + (k + 1) * rn] for n in range(PARTS_N)])

        wq_ref[at, :] = rows_of(unit(0, 0), unit(1, 0)).astype(BF16)
        wkv_ref[pl.ds(pair * 4 * cw, 4 * cw), :] = rows_of(
            unit(0, 1), unit(0, 2), unit(1, 1), unit(1, 2)
        ).astype(BF16)
        wp_ref[at, :] = rows_of(unit(0, 3), unit(1, 3)).astype(BF16)

    h1 = (n1_ref[...] * mv[0:1] + mv[1:2]).astype(BF16)
    h1_ref[...] = h1
    q = (dot_nt(h1, wq_ref[...]) + mv[2:3]).astype(BF16)
    q_ref[...] = q

    patches = dot_nn(chosen_ref[...], h1).astype(BF16)
    patch_ref[...] = patches
    reduced = mv[4:5]
    for n in range(4):
        reduced = reduced + dot_nt(patches[n * keys : (n + 1) * keys], wr_ref[n])
    nk, rk = normalise(reduced)
    nk_ref[...] = nk
    rk_ref[...] = rk
    kn = (nk * mv[5:6] + mv[6:7]).astype(BF16)
    kn_ref[...] = kn
    kv = dot_nt(kn, wkv_ref[...])
    k = kv[:, :width].astype(BF16).astype(F32)
    v = (kv[:, width:] + mv[3:4]).astype(BF16).astype(F32)
    lane = lax.broadcasted_iota(jnp.int32, (keys, width), 1)
    for h in range(HEADS):
        inside = (lane >= h * dim) & (lane < (h + 1) * dim)
        at = pl.ds(h * keys, keys)
        kb_ref[at, :] = jnp.where(inside, k, 0.0).astype(BF16)
        vb_ref[at, :] = jnp.where(inside, v, 0.0).astype(BF16)

    score_ref[...] = dot_nt(q, kb_ref[...]) * dim ** (-0.5)
    def soften(i, carry):
        at = pl.ds(pl.multiple_of(i * 64, 64), 64)
        live = live_ref[at, :] > 0.5
        for h in range(HEADS):
            lane_at = pl.ds(h * keys, keys)
            s = jnp.where(live, score_ref[at, lane_at], MASKED)
            e = jnp.exp(s - jnp.max(s, axis=-1, keepdims=True))
            p_ref[at, lane_at] = e / jnp.sum(e, axis=-1, keepdims=True)
        return carry

    lax.fori_loop(0, capacity // 64, soften, 0)
    o = dot_nn(p_ref[...].astype(BF16), vb_ref[...]).astype(BF16)
    o_ref[...] = o
    x2_ref[...] = x_ref[...] + dot_nt(o, wp_ref[...]) + mv[7:8]


def one_hot(rows_ref, cols_ref, capacity):
    row0, row1, col0, col1 = rows_ref[0], rows_ref[1], cols_ref[0], cols_ref[1]
    area0, area1 = row0 * col0, row1 * col1
    quarter0, quarter1 = area0 // 4, area1 // 4
    keys = capacity // 4
    index = lax.broadcasted_iota(jnp.int32, (capacity, 128), 0)
    tap = index // keys
    key = index - tap * keys
    first = key < quarter0
    second = jnp.logical_and(key >= quarter0, key < quarter0 + quarter1)
    width = jnp.maximum(jnp.where(second, col1, col0), 2)
    half = width // 2
    local = key - jnp.where(second, quarter0, 0)
    row = ((local.astype(F32) + 0.5) / half.astype(F32)).astype(jnp.int32)
    col = local - row * half
    token = jnp.where(second, area0, 0) + (2 * row + tap // 2) * width + 2 * col + tap % 2
    token = jnp.where(first | second, token, -1)
    lane = lax.broadcasted_iota(jnp.int32, (capacity, 128), 1)
    return lanes(
        *[jnp.where(token == lane + t * 128, 1.0, 0.0).astype(BF16) for t in range(capacity // 128)]
    )


def prepare_two_kernel(
    geo_ref, cot_ref, x2_ref, mv_ref, n2_ref, r2_ref, h2_ref, h2t_ref, gy_ref, gyt_ref, mask_ref
):
    width, capacity = cot_ref.shape
    normed, inverse = normalise(x2_ref[...])
    n2_ref[...] = normed
    r2_ref[...] = inverse
    h2 = normed * mv_ref[8:9, :] + mv_ref[9:10, :]
    h2_ref[...] = h2.astype(BF16)
    h2t_ref[...] = h2.T.astype(BF16)
    area = geo_ref[0] * geo_ref[2] + geo_ref[1] * geo_ref[3]
    position = lax.broadcasted_iota(jnp.int32, (width, capacity), 1)
    gyt = jnp.where(position < area, cot_ref[...].astype(F32), 0.0)
    gyt_ref[...] = gyt.astype(BF16)
    gy_ref[...] = gyt.T.astype(BF16)
    first, second, row, col, heights, widths = token_geometry(geo_ref, capacity, 128)
    live = first | second
    conditions = (
        live & (col > 0),
        live & (col < widths - 1),
        first & (row > 0),
        second & (row > 0),
        first & (row < heights - 1),
        second & (row < heights - 1),
        live,
    )
    for k, condition in enumerate(conditions):
        mask_ref[k] = jnp.where(condition, 1.0, 0.0)


def ffn_kernel(
    tuned,
    geo_ref, n2_ref, r2_ref, h2_ref, h2t_ref, gy_ref, gyt_ref, mask_ref, own_ref, oth_ref, mv_ref, hv_ref,
    gown_ref, gsend_ref, mix_ref, dx2_ref, mg_ref, hg_ref,
    wu_ref, wd_ref, f_ref, gm_ref, gp_ref, dc_ref, ul_ref, ur_ref, g0_ref, slope_ref, act_ref, u0_ref, df_ref, da_ref,
    dh2_ref, upg_ref, dng_ref,
):
    me = my_index(tuned)
    capacity, width = n2_ref.shape
    hidden = hv_ref.shape[1]
    cw, rn = width // PARTS_W, width // PARTS_N
    tiles = capacity // TILE
    tails = 128 * PARTS_W

    for pair in range(PARTS_W // 2):
        at = pl.ds(pair * 2 * cw, 2 * cw)
        got = [
            rows_of(*[piece_of(own_ref, oth_ref, w * PARTS_N + n, me, 0, 5, mixed_slot) for w in (2 * pair, 2 * pair + 1)])
            for n in range(PARTS_N)
        ]
        for n in range(PARTS_N):
            wd_ref[at, pl.ds(256 * n, 256)] = got[n][:, :256].astype(BF16)
        wd_ref[at, pl.ds(tails, 2 * REST * PARTS_N)] = lanes(*[g[:, 512 : 512 + 2 * REST] for g in got]).astype(BF16)
    for n in range(PARTS_N):
        at = pl.ds(n * rn, rn)
        ends = []
        for w in range(PARTS_W):
            got = piece_of(own_ref, oth_ref, w * PARTS_N + n, me, 2, 5, mixed_slot)
            wu_ref[at, pl.ds(128 * w, 128)] = rows_of(got[:, :128], got[:, 128:256]).astype(BF16)
            ends.append(rows_of(got[:, 256 + 2 * REST : 256 + 3 * REST], got[:, 256 + 3 * REST :]))
        wu_ref[at, pl.ds(tails, REST * PARTS_W)] = lanes(*ends).astype(BF16)

    w0, w1 = geo_ref[2], geo_ref[3]

    for ref in (f_ref, gm_ref, gp_ref, dc_ref, ul_ref, ur_ref):
        ref[:, :PAD, :] = jnp.zeros((CHUNK // 128, PAD, 128), F32)
        ref[:, PAD + capacity :, :] = jnp.zeros((CHUNK // 128, PAD, 128), F32)

    mix_ref[...] = jnp.zeros_like(mix_ref)
    dh2_ref[...] = jnp.zeros_like(dh2_ref)

    def fold(values):
        return jnp.sum(values.reshape(TILE // 8, 8, 128), axis=0)

    halves = CHUNK // 128
    chunks = hidden // CHUNK
    zero = jnp.zeros((8, 128), F32)

    def columns(c):
        return pl.ds(pl.multiple_of(c * CHUNK, CHUNK), CHUNK)

    def vector(c, k, j):
        return hv_ref[k : k + 1, pl.ds(pl.multiple_of(c * CHUNK + j * 128, 128), 128)]

    def put_vector(c, k, j, value):
        hg_ref[k : k + 1, pl.ds(pl.multiple_of(c * CHUNK + j * 128, 128), 128)] = value

    def first_layer(c, at):
        value = dot_nn(h2_ref[at, :], wu_ref[:, columns(c)])
        for j in range(halves):
            f_ref[j, pl.ds(PAD + at.start, at.size), :] = value[:, j * 128 : (j + 1) * 128] + vector(c, 0, j)

    def act_grad(c, at):
        da_ref[at, :] = dot_nn(gy_ref[at, :], wd_ref[:, columns(c)])

    def second_layer(c, at):
        mix_ref[at, :] += dot_nt(act_ref[at, :], wd_ref[:, columns(c)])

    def down_grad(c, at):
        dng_ref[at, columns(c)] = dot_nn(gyt_ref[at, :], act_ref[...])

    def up_grad(c, at):
        upg_ref[at, columns(c)] = dot_nn(h2t_ref[at, :], df_ref[...])

    def h2_grad(c, at):
        dh2_ref[at, :] += dot_nt(df_ref[at, :], wu_ref[:, columns(c)])

    def tasks(product, c, rows, size):
        return [functools.partial(product, c, pl.ds(r, min(size, rows - r))) for r in range(0, rows, size)]

    def interleave(steps, products):
        done = 0
        for i, step in enumerate(steps):
            step()
            while done < len(products) and done * len(steps) < (i + 1) * len(products):
                products[done]()
                done += 1

    def chunk_step(c, carry):
        before = jnp.maximum(c - 1, 0)
        following = jnp.minimum(c + 1, chunks - 1)
        v = [[vector(c, k, j) for k in range(11)] for j in range(halves)]

        def taps_of(j, r, at):
            here = f_ref[j, pl.ds(PAD + r, TILE), :]
            left = f_ref[j, pl.ds(PAD + r - 1, TILE), :] * mask_ref[0, at, :]
            right = f_ref[j, pl.ds(PAD + r + 1, TILE), :] * mask_ref[1, at, :]
            return left, here, right

        def column_taps(r, j):
            at = pl.ds(r, TILE)
            left, here, right = taps_of(j, r, at)
            u = v[j]
            gm_ref[j, pl.ds(PAD + r, TILE), :] = u[2] * left + u[3] * here + u[4] * right
            g0_ref[j, at, :] = u[1] + u[5] * left + u[6] * here + u[7] * right
            gp_ref[j, pl.ds(PAD + r, TILE), :] = u[8] * left + u[9] * here + u[10] * right

        def activate(r, j):
            at = pl.ds(r, TILE)
            conv = (
                g0_ref[j, at, :]
                + mask_ref[2, at, :] * gm_ref[j, pl.ds(PAD + r - w0, TILE), :]
                + mask_ref[3, at, :] * gm_ref[j, pl.ds(PAD + r - w1, TILE), :]
                + mask_ref[4, at, :] * gp_ref[j, pl.ds(PAD + r + w0, TILE), :]
                + mask_ref[5, at, :] * gp_ref[j, pl.ds(PAD + r + w1, TILE), :]
            )
            half = 0.5 * (1.0 + lax.erf(conv * 2.0 ** (-0.5)))
            lane_at = pl.ds(j * 128, 128)
            act_ref[at, lane_at] = (conv * half).astype(BF16)
            slope_ref[at, lane_at] = half + conv * jnp.exp(-0.5 * conv * conv) * (2.0 * math.pi) ** (-0.5)

        conv_sums = [zero] * halves

        def into_conv(r, j):
            at, lane_at = pl.ds(r, TILE), pl.ds(j * 128, 128)
            value = da_ref[at, lane_at] * slope_ref[at, lane_at]
            dc_ref[j, pl.ds(PAD + r, TILE), :] = value
            conv_sums[j] = conv_sums[j] + fold(value)

        tap_sums = [[zero] * 9 for _ in range(halves)]

        def tap_back(r, j):
            at = pl.ds(r, TILE)
            left, here, right = taps_of(j, r, at)
            u = v[j]
            below = (
                mask_ref[4, at, :] * dc_ref[j, pl.ds(PAD + r + w0, TILE), :]
                + mask_ref[5, at, :] * dc_ref[j, pl.ds(PAD + r + w1, TILE), :]
            )
            level = dc_ref[j, pl.ds(PAD + r, TILE), :]
            above = (
                mask_ref[2, at, :] * dc_ref[j, pl.ds(PAD + r - w0, TILE), :]
                + mask_ref[3, at, :] * dc_ref[j, pl.ds(PAD + r - w1, TILE), :]
            )
            ul_ref[j, pl.ds(PAD + r, TILE), :] = u[2] * below + u[5] * level + u[8] * above
            u0_ref[j, at, :] = u[3] * below + u[6] * level + u[9] * above
            ur_ref[j, pl.ds(PAD + r, TILE), :] = u[4] * below + u[7] * level + u[10] * above
            grads = [fold(d * f) for d in (below, level, above) for f in (left, here, right)]
            tap_sums[j] = [a + b for a, b in zip(tap_sums[j], grads)]

        up_sums = [zero] * halves

        def spread_back(r, j):
            at = pl.ds(r, TILE)
            value = (
                u0_ref[j, at, :]
                + mask_ref[0, at, :] * ur_ref[j, pl.ds(PAD + r - 1, TILE), :]
                + mask_ref[1, at, :] * ul_ref[j, pl.ds(PAD + r + 1, TILE), :]
            ).astype(BF16)
            df_ref[at, pl.ds(j * 128, 128)] = value
            up_sums[j] = up_sums[j] + fold(value.astype(F32))

        def steps(step):
            return [functools.partial(step, r, j) for j in range(halves) for r in range(0, capacity, TILE)]

        interleave(
            steps(column_taps) + steps(activate),
            tasks(act_grad, c, capacity, MROWS) + tasks(up_grad, before, width, MROWS)
            + tasks(h2_grad, before, capacity, MROWS),
        )
        interleave(
            steps(into_conv) + steps(tap_back),
            tasks(second_layer, c, capacity, MROWS) + tasks(down_grad, c, width, MROWS),
        )
        interleave(steps(spread_back), tasks(first_layer, following, capacity, MROWS))
        for j in range(halves):
            put_vector(c, 0, j, column_sum(up_sums[j]))
            put_vector(c, 1, j, column_sum(conv_sums[j]))
            for k in range(9):
                put_vector(c, 2 + k, j, column_sum(tap_sums[j][k]))
        return carry

    df_ref[...] = jnp.zeros_like(df_ref)
    first_layer(0, pl.ds(0, capacity))
    lax.fori_loop(0, chunks, chunk_step, 0)
    up_grad(chunks - 1, pl.ds(0, width))
    h2_grad(chunks - 1, pl.ds(0, capacity))
    hg_ref[11:, :] = jnp.zeros((hg_ref.shape[0] - 11, hidden), F32)

    def value_of(w, n):
        down = pl.ds(w * cw, cw)
        up = [pl.ds(n * rn + e * cw, cw) for e in range(2)]
        return lanes(
            dng_ref[down, pl.ds(256 * n, 256)],
            *[upg_ref[e, pl.ds(128 * w, 128)] for e in up],
            dng_ref[down, pl.ds(tails + 2 * REST * n, 2 * REST)],
            *[upg_ref[e, pl.ds(tails + REST * w, REST)] for e in up],
        )

    store_pieces(gown_ref, gsend_ref, me, value_of, mixed_slot)

    def finish(i, carry):
        at = pl.ds(pl.multiple_of(i * 64, 64), 64)
        gy = gy_ref[at, :].astype(F32)
        grad, normed = dh2_ref[at, :], n2_ref[at, :]
        dx2_ref[at, :] = gy + normalise_back(grad, normed, r2_ref[at, :], mv_ref[8:9, :])
        return tuple(a + column_sum(b) for a, b in zip(carry, (grad * normed, grad, gy)))

    zero = jnp.zeros((1, width), F32)
    sums = lax.fori_loop(0, capacity // 64, finish, (zero, zero, zero))
    mg_ref[...] = jnp.zeros_like(mg_ref)
    for k in range(3):
        mg_ref[8 + k : 9 + k, :] = sums[k]


def store_pieces(own_ref, send_ref, me, value_of, order):
    even = (me & 1) == 0
    for w in range(PARTS_W):
        for x in range(PARTS_N // 2):
            first, second = value_of(w, 2 * x), value_of(w, 2 * x + 1)
            slot0, slot1 = (order(w * PARTS_N + 2 * x + c, me) for c in range(2))
            own_ref[jnp.where(even, slot0, slot1)] = jnp.where(even, first, second).astype(BF16)
            send_ref[jnp.where(even, slot1, slot0)] = jnp.where(even, second, first).astype(BF16)


def score_back_kernel(dx2_ref, vb_ref, p_ref, o_ref, wp_ref, gp_ref, dob_ref, ds_ref, bp_ref, dp_ref):
    capacity = dx2_ref.shape[0]
    keys = capacity // 4
    datt = dx2_ref[...].astype(BF16)
    bp_ref[...] = column_sum(datt.astype(F32))
    gp_ref[...] = dot_tn(datt, o_ref[...])
    dob = dot_nn(datt, wp_ref[...]).astype(BF16)
    dob_ref[...] = dob
    dp_ref[...] = dot_nt(dob, vb_ref[...])

    def soften_back(i, carry):
        at = pl.ds(pl.multiple_of(i * 64, 64), 64)
        for h in range(HEADS):
            lane_at = pl.ds(h * keys, keys)
            p = p_ref[at, lane_at]
            dp = dp_ref[at, lane_at]
            row = jnp.sum(p * dp, axis=-1, keepdims=True)
            ds_ref[at, lane_at] = (p * (dp - row)).astype(BF16)
        return carry

    lax.fori_loop(0, capacity // 64, soften_back, 0)


def attend_back_kernel(
    tuned,
    dob_ref, ds_ref, gp_ref, h1_ref, patch_ref, nk_ref, rk_ref, kn_ref, q_ref, kb_ref, p_ref,
    wr_ref, wkv_ref, mv_ref,
    gown_ref, gsend_ref, dq_ref, dpatch_ref, vk_ref,
    gr_ref, gq_ref, gkv_ref,
):
    me = my_index(tuned)
    capacity, width = h1_ref.shape
    cw, rn = width // PARTS_W, width // PARTS_N
    keys = capacity // 4
    dim = width // HEADS
    scale = dim ** (-0.5)

    ds = ds_ref[...]
    dq = (dot_nn(ds, kb_ref[...]) * scale).astype(BF16)
    dq_ref[...] = dq
    dk_all = dot_tn(ds, q_ref[...])
    dv_all = dot_tn(p_ref[...].astype(BF16), dob_ref[...])
    lane = lax.broadcasted_iota(jnp.int32, (keys, width), 1)
    dk = jnp.zeros((keys, width), F32)
    dv = jnp.zeros((keys, width), F32)
    for h in range(HEADS):
        inside = (lane >= h * dim) & (lane < (h + 1) * dim)
        dk = jnp.where(inside, dk_all[h * keys : (h + 1) * keys], dk)
        dv = jnp.where(inside, dv_all[h * keys : (h + 1) * keys], dv)
    dk = (dk * scale).astype(BF16)
    dv = dv.astype(BF16)
    gq_ref[...] = dot_tn(dq, h1_ref[...])
    kn = kn_ref[...]
    gkv_ref[pl.ds(0, width), :] = dot_tn(dk, kn)
    gkv_ref[pl.ds(width, width), :] = dot_tn(dv, kn)
    dkn = dot_nn(dk, wkv_ref[pl.ds(0, width), :]) + dot_nn(dv, wkv_ref[pl.ds(width, width), :])
    nk = nk_ref[...]
    dsr = normalise_back(dkn, nk, rk_ref[...], mv_ref[5:6, :]).astype(BF16)
    vk_ref[...] = rows_of(
        column_sum(dq.astype(F32)),
        column_sum(dv.astype(F32)),
        column_sum(dsr.astype(F32)),
        column_sum(dkn * nk),
        column_sum(dkn),
        jnp.zeros((3, width), F32),
    )
    for n in range(4):
        at = pl.ds(n * keys, keys)
        gr_ref[n] = dot_tn(dsr, patch_ref[at, :])
        dpatch_ref[at, :] = dot_nn(dsr, wr_ref[n])

    def value_of(w, n):
        at, lane_at = pl.ds(w * cw, cw), pl.ds(n * rn, rn)
        return lanes(
            gr_ref[n, at, :],
            gq_ref[at, lane_at],
            gkv_ref[pl.ds(2 * w * cw, cw), lane_at],
            gkv_ref[pl.ds(2 * w * cw + cw, cw), lane_at],
            gp_ref[at, lane_at],
        )

    store_pieces(gown_ref, gsend_ref, me, value_of, round_slot)


def fold_rows(value, unit):
    rest = value[8:]
    beside = lanes(rest[:, : 3 * unit], jnp.zeros((8, 256 - 3 * unit), F32))
    below = lanes(rest[:, 3 * unit :], jnp.zeros((8, 256 - 2 * unit), F32))
    return lanes(value[:8], (beside + pltpu.roll(below, 3, 0))[:, : 3 * unit])


def unfold_rows(value, unit):
    beside = lanes(value[:, 5 * unit :], jnp.zeros((8, 256 - 3 * unit), F32))
    below = pltpu.roll(beside, 5, 0)
    return rows_of(value[:, : 5 * unit], lanes(beside[:, : 3 * unit], below[:, : 2 * unit]))


def token_back_kernel(
    tuned,
    dx2_ref, dq_ref, dpatch_ref, n1_ref, r1_ref, chosen_ref, wq_ref, mv_ref, mg_ref, hg_ref, vk_ref, bp_ref,
    x2_ref, mix_ref, mask_ref,
    mixed_ref, tg_ref, vown_ref, vsend_ref,
):
    me = my_index(tuned)
    capacity, width = dx2_ref.shape
    rn = width // PARTS_N
    occupied = mask_ref[6]
    occupied = lanes(*([occupied] * (width // 128)), occupied[:, : width % 128])
    mixed_ref[...] = ((x2_ref[...] + mix_ref[...] + mv_ref[10:11, :]) * occupied).T.astype(BF16)
    chosen = chosen_ref[...]
    high = dpatch_ref[...].astype(BF16)
    low = (dpatch_ref[...] - high.astype(F32)).astype(BF16)
    dh1 = dot_nn(dq_ref[...], wq_ref[...]) + dot_tn(chosen, high) + dot_tn(chosen, low)
    n1 = n1_ref[...]
    vk = vk_ref[...]
    token_grad = dx2_ref[...] + normalise_back(dh1, n1, r1_ref[...], mv_ref[0:1, :])
    tg_ref[...] = token_grad.T.astype(BF16)
    sums = rows_of(column_sum(dh1 * n1), column_sum(dh1), vk[0:5], bp_ref[...], mg_ref[8:16, :])
    hg = hg_ref[...]
    value = []
    for n in range(PARTS_N):
        parts = []
        for w in (2 * n, 2 * n + 1):
            parts += [hg[:, 128 * w : 128 * (w + 1)], hg[:, 1024 + REST * w : 1024 + REST * (w + 1)]]
        value.append(fold_rows(lanes(sums[:, n * rn : (n + 1) * rn], *parts), rn))
    even = (me & 1) == 0
    for x in range(2):
        slot = x ^ ((me >> 1) & 1)
        vown_ref[slot] = jnp.where(even, value[2 * x], value[2 * x + 1]).astype(BF16)
        vsend_ref[slot] = jnp.where(even, value[2 * x + 1], value[2 * x]).astype(BF16)


def total_of(refs):
    value = refs[0][...].astype(F32)
    for ref in refs[1:]:
        value = value + ref[...].astype(F32)
    return value


def halve_kernel(keep_ref, got_ref, low_ref, high_ref):
    half = low_ref.shape[0]
    low_ref[...] = (keep_ref[:half].astype(F32) + got_ref[:half].astype(F32)).astype(BF16)
    high_ref[...] = (keep_ref[half:].astype(F32) + got_ref[half:].astype(F32)).astype(BF16)


def halve_core_kernel(keep_ref, got_ref, vkeep_ref, vgot_ref, low_ref, vlow_ref, send_ref):
    half = low_ref.shape[0]
    low_ref[...] = (keep_ref[:half].astype(F32) + got_ref[:half].astype(F32)).astype(BF16)
    parts = [keep_ref[half + k].astype(F32) + got_ref[half + k].astype(F32) for k in range(half)]
    vector = total_of((vkeep_ref, vgot_ref))
    vlow_ref[...] = vector.astype(BF16)
    send_ref[...] = rows_of(*parts, vector[0], vector[1]).astype(BF16)


def halve_round_kernel(tuned, keep_ref, vkeep_ref, got_ref, low_ref, vlow_ref, send_ref):
    half, cw = low_ref.shape[:2]
    rows = vkeep_ref.shape[1]
    got = got_ref[...].astype(F32)
    parts = [keep_ref[k].astype(F32) + got[k * cw : (k + 1) * cw] for k in range(2 * half)]
    for k in range(half):
        low_ref[k] = parts[k].astype(BF16)
    got0, got1 = (got[2 * half * cw + k * rows : 2 * half * cw + (k + 1) * rows] for k in range(2))
    keep0, keep1 = vkeep_ref[0].astype(F32), vkeep_ref[1].astype(F32)
    even = (my_index(tuned) & 1) == 0
    low = keep0 + jnp.where(even, got0, got1)
    vlow_ref[0] = low.astype(BF16)
    send_ref[...] = rows_of(*parts[half:], jnp.where(even, keep1 + got1, low)).astype(BF16)


def quarter_vector_kernel(keep_ref, vkeep_ref, got_ref, *out_refs):
    cw = keep_ref.shape[1]
    got = got_ref[...].astype(F32)
    vector = vkeep_ref[0].astype(F32) + got[4 * cw :]
    for k, ref in enumerate(out_refs):
        ref[...] = rows_of(keep_ref[k].astype(F32) + got[k * cw : (k + 1) * cw], vector).astype(BF16)


def finish_ffn_kernel(a_ref, b_ref, up_ref, down_ref):
    total = total_of((a_ref, b_ref))[0]
    columns = [
        lanes(total[:, 128 * k : 128 * (k + 1)], total[:, 512 + REST * k : 512 + REST * (k + 1)]) for k in range(4)
    ]
    down_ref[...] = lanes(*columns[:2])
    up_ref[...] = rows_of(*columns[2:])


def finish_attend_kernel(a_ref, b_ref, c_ref, d_ref, q_ref, kv_ref, red_ref, proj_ref, vm_ref, vh_ref):
    total = total_of((a_ref, b_ref, c_ref, d_ref))
    cw, width = red_ref.shape
    rn = q_ref.shape[1]
    red_ref[...] = total[:cw, :width]
    unit = [total[:cw, width + k * rn : width + (k + 1) * rn] for k in range(4)]
    q_ref[...] = unit[0]
    kv_ref[...] = rows_of(unit[1], unit[2]).T
    proj_ref[...] = unit[3]
    vector = unfold_rows(total[cw:], rn)
    vm_ref[...] = vector[: vm_ref.shape[0], :rn]
    vh_ref[...] = vector[: vh_ref.shape[0], rn:]


def call(kernel, inputs, outputs, scratch=(), scalars=0, limit=40, flops=0, moved=0):
    vmem = pl.BlockSpec(memory_space=pltpu.VMEM)
    smem = pl.BlockSpec(memory_space=pltpu.SMEM)
    return pl.pallas_call(
        kernel,
        out_shape=[jax.ShapeDtypeStruct(shape, kind) for shape, kind in outputs],
        in_specs=[smem] * scalars + [vmem] * (len(inputs) - scalars),
        out_specs=[vmem] * len(outputs),
        scratch_shapes=[pltpu.VMEM(shape, kind) for shape, kind in scratch],
        compiler_params=pltpu.CompilerParams(vmem_limit_bytes=limit * 2**20),
        cost_estimate=pl.CostEstimate(flops=flops, bytes_accessed=moved, transcendentals=0),
    )(*inputs)


def after(value, *others):
    return lax.optimization_barrier((value, *others))[0]


def on_device(
    mesh_shape,
    tokens, cotangent, img_rows, img_cols,
    q_weight, kv_weight, reduce_weight, proj_weight, up_weight, down_weight, vec_model, vec_hidden,
):
    wide, narrow = mesh_shape
    tuned = (wide, narrow) == (PARTS_W, PARTS_N)
    capacity, width = tokens.shape
    hidden = vec_hidden.shape[1] * narrow
    cw, rn = width // PARTS_W, width // PARTS_N
    keys = capacity // 4
    piece = (cw, 2 * width)
    vpiece, gpiece = (16, 2 * width), (8, 2 * width)

    def swap(value, mask, other=None):
        masks = (mask, mask if other is None else other)
        pairs = [(i, i ^ masks[i & 1]) for i in range(wide * narrow)]
        return lax.ppermute(value, ("wide", "narrow"), pairs)

    tokens_f32 = ((capacity, width), F32)
    tokens_low = ((capacity, width), BF16)
    x, n1, r1, chosen, live, geo = prepare(img_rows, img_cols, tokens.T)
    if tuned:
        pack_a, pack_b, pack_v = pack(
            (
                q_weight.T, kv_weight, reduce_weight.T, proj_weight.T, up_weight, down_weight.T,
                vec_model, vec_hidden,
            ),
            piece, vpiece,
        )
        def join(*parts):
            return jnp.concatenate(parts, axis=0)

        line_a = [swap(pack_a, m) for m in (8, 16, 24)]
        got_b, got_v = swap(pack_b, 2, 4), swap(pack_v, 1)
        *line_a, got_b, got_v = lax.optimization_barrier((*line_a, got_b, got_v, x, n1, chosen))[:5]
        buf_a, buf_b, vecs = join(pack_a, *line_a), join(pack_b, got_b), join(pack_v, got_v)
        buf_a, buf_b = join(buf_a, swap(buf_a, 2, 4)), join(buf_b, swap(buf_b, 16))
        got = lax.optimization_barrier((swap(buf_a, 4, 2), swap(buf_b, 8), swap(vecs, 2)))
        own_a, half_b, vecs = (join(v, g) for v, g in zip((buf_a, buf_b, vecs), got))
        oth_a = swap(own_a, 1)
        rest_b = swap(half_b, 4, 2)
    else:
        own_a, oth_a, own_b, oth_b, vecs = gather_plain(
            q_weight, kv_weight, reduce_weight, proj_weight, up_weight, down_weight, vec_model, vec_hidden
        )

    square = (width, width)
    (
        x2, h1, patches, nk, rk, kn, q, kb, vb, p, o, wr, wq, wkv, wp, mv, hv,
    ) = call(
        functools.partial(attend_kernel, tuned),
        (x, n1, chosen, live, own_a, oth_a, vecs),
        (
            tokens_f32, tokens_low,
            ((capacity, width), BF16), ((keys, width), F32), ((keys, 1), F32), ((keys, width), BF16),
            ((capacity, width), BF16), ((HEADS * keys, width), BF16), ((HEADS * keys, width), BF16),
            ((capacity, HEADS * keys), F32), ((capacity, width), BF16),
            ((4,) + square, BF16), (square, BF16), ((2 * width, width), BF16), (square, BF16),
            ((16, width), F32), ((16, hidden), F32),
        ),
        scratch=(((capacity, HEADS * keys), F32),),
        flops=8 * 10**9,
    )

    if tuned:
        own_b = jnp.concatenate([half_b, after(rest_b, x2)], axis=0)
        oth_b = swap(own_b, 1)
    padded = ((CHUNK // 128, capacity + 2 * PAD, 128), F32)
    halved = ((CHUNK // 128, capacity, 128), F32)
    chunked = ((capacity, CHUNK), F32)
    n2, r2, h2, h2t, gy, gyt, masks = call(
        prepare_two_kernel,
        (geo, cotangent.T, x2, mv),
        (
            tokens_f32, ((capacity, 1), F32), tokens_low, ((width, capacity), BF16),
            tokens_low, ((width, capacity), BF16), ((7, capacity, 128), F32),
        ),
        scalars=1,
        flops=2 * 10**9,
    )
    gown_b, gsend_b, mix, dx2, mg, hg = call(
        functools.partial(ffn_kernel, tuned),
        (geo, n2, r2, h2, h2t, gy, gyt, masks, own_b, oth_b, mv, hv),
        (
            ((SLOTS,) + piece, BF16), ((SLOTS,) + piece, BF16),
            tokens_f32, tokens_f32, ((16, width), F32), ((16, hidden), F32),
        ),
        scratch=(
            ((width, hidden), BF16), ((width, hidden), BF16),
            padded, padded, padded, padded, padded, padded,
            halved, chunked, ((capacity, CHUNK), BF16), halved, ((capacity, CHUNK), BF16), chunked,
            tokens_f32, ((width, hidden), F32), ((width, hidden), F32),
        ),
        scalars=1,
        flops=33 * 10**9,
    )

    if tuned:
        got_b = swap(gsend_b, 1)
    gp, dob, ds, bp = call(
        score_back_kernel,
        (dx2, vb, p, o, wp),
        (
            (square, F32), ((capacity, width), BF16), ((capacity, HEADS * keys), BF16), ((1, width), F32),
        ),
        scratch=(((capacity, HEADS * keys), F32),),
        flops=25 * 10**8,
    )
    def halve(keep, got, flops=0):
        shape = ((keep.shape[0] // 2,) + piece, BF16)
        return call(halve_kernel, (keep, got), (shape, shape), flops=flops)

    if tuned:
        got_b = after(got_b, ds)
        low_b, high_b = halve(gown_b, got_b)
        ds = after(ds, high_b)
        got_b = swap(high_b, 4, 2)
    gown_a, gsend_a, dq, dpatch, vk = call(
        functools.partial(attend_back_kernel, tuned),
        (dob, ds, gp, h1, patches, nk, rk, kn, q, kb, p, wr, wkv, mv),
        (
            ((SLOTS,) + piece, BF16), ((SLOTS,) + piece, BF16), ((capacity, width), BF16), ((capacity, width), F32),
            ((8, width), F32),
        ),
        scratch=(((4,) + square, F32), (square, F32), ((2 * width, width), F32)),
        flops=0,
    )
    if tuned:
        got_a = swap(gsend_a, 1)
        low_b, high_b = halve(low_b, got_b, flops=2 * 10**10)
        gown_a = after(gown_a, high_b)
    mixed, token_grad, vown, vsend = call(
        functools.partial(token_back_kernel, tuned),
        (dx2, dq, dpatch, n1, r1, chosen, wq, mv, mg, hg, vk, bp, x2, mix, masks),
        (((width, capacity), BF16), ((width, capacity), BF16), ((2,) + gpiece, BF16), ((2,) + gpiece, BF16)),
    )

    if not tuned:
        grads = scatter_plain(mesh_shape, width, gown_a, gsend_a, gown_b, gsend_b, vown, vsend)
        return (mixed.T, token_grad.T) + grads

    vrows = gpiece[0]
    low_a, vlow, high_a = call(
        halve_core_kernel,
        (gown_a, got_a, vown, swap(vsend, 1)),
        (((8,) + piece, BF16), ((2,) + gpiece, BF16), ((8 * cw + 2 * vrows, 2 * width), BF16)),
    )
    got_a, got_b = lax.optimization_barrier((swap(high_a, 4, 2), swap(high_b, 8)))
    low_a, vlow, high_a = call(
        functools.partial(halve_round_kernel, tuned),
        (low_a, vlow, got_a),
        (((4,) + piece, BF16), ((1,) + gpiece, BF16), ((4 * cw + vrows, 2 * width), BF16)),
    )
    low_b, high_b = halve(low_b, got_b)
    got_a, got_b = swap(high_a, 2, 4), swap(high_b, 16)
    near_a = list(call(quarter_vector_kernel, (low_a, vlow, got_a), (((cw + vrows, 2 * width), BF16),) * 4))
    near_a[1], got_b = lax.optimization_barrier((near_a[1], got_b))
    line_a = [swap(near_a[k], 8 * k) for k in (1, 2, 3)]
    low_b, high_b = halve(low_b, got_b)
    up_grad, down_grad = call(
        finish_ffn_kernel, (low_b, swap(high_b, 2, 4)), (((rn, 4 * cw), F32), ((cw, width), F32))
    )
    q_grad, kv_grad, reduce_grad, proj_grad, vm_grad, vh_grad = call(
        finish_attend_kernel,
        (near_a[0], *line_a),
        (
            ((cw, rn), F32), ((rn, 2 * cw), F32), ((cw, width), F32), ((cw, rn), F32),
            ((11, rn), F32), ((11, width), F32),
        ),
    )
    return (
        mixed.T, token_grad.T, q_grad.T, kv_grad, reduce_grad.T, proj_grad.T, up_grad, down_grad.T, vm_grad, vh_grad,
    )


def gather_plain(q, kv, reduce, proj, up, down, vec_model, vec_hidden):
    def whole(value):
        rows = lax.all_gather(value, "narrow", axis=0, tiled=True)
        return lax.all_gather(rows, "wide", axis=1, tiled=True).T

    q, kv, reduce, proj, up, down = (whole(v) for v in (q, kv, reduce, proj, up, down))
    width = q.shape[0]
    cw, rn = width // PARTS_W, width // PARTS_N

    def pieces(turned, blocks):
        split = turned.reshape(PARTS_W, blocks, cw, PARTS_N, -1)
        return split.transpose(0, 3, 2, 1, 4).reshape(PARTS_W, PARTS_N, cw, -1)

    def slots(value, mixed=False):
        value = value.reshape(2, 2, 2, 2, 2, cw, -1)
        orders = ((2, 1, 0, 3), (3, 1, 0, 2)) if mixed else ((2, 3, 0, 1), (3, 2, 0, 1))
        return tuple(
            value[:, :, :, :, core].transpose(*order, 4, 5).reshape(SLOTS, cw, -1) for core, order in enumerate(orders)
        )

    a = jnp.concatenate([pieces(reduce, 1), pieces(q, 1), pieces(kv, 2), pieces(proj, 1)], axis=-1)
    columns = pieces(down, 1).reshape(PARTS_W, PARTS_N, cw, 2, RUN)
    columns = [columns[..., e, :] for e in range(2)]
    halves = up.T.reshape(PARTS_N, 2, cw, PARTS_W, RUN).transpose(1, 3, 0, 2, 4)
    columns += [halves[0], halves[1]]
    b = jnp.concatenate([c[..., :128] for c in columns] + [c[..., 128:] for c in columns], axis=-1)
    vm = lax.all_gather(vec_model, "narrow", axis=1, tiled=True)
    vh = lax.all_gather(vec_hidden, "narrow", axis=1, tiled=True)
    both = jnp.concatenate([vm.reshape(11, PARTS_N, rn), vh.reshape(11, PARTS_N, width)], axis=-1)
    vecs = jnp.pad(both.transpose(1, 0, 2), ((0, 0), (0, 5), (0, 3 * rn)))
    return (*slots(a), *slots(b, True), vecs)


def scatter_plain(mesh_shape, width, gown_a, gsend_a, gown_b, gsend_b, vown, vsend):
    cw, rn = width // PARTS_W, width // PARTS_N

    def devices(own, send, mixed=False):
        orders = ((2, 1, 0, 3), (3, 1, 0, 2)) if mixed else ((2, 3, 0, 1), (3, 2, 0, 1))
        parts = []
        for value, order in zip((own, send), orders):
            back = sorted(range(4), key=lambda k: order[k])
            parts.append(value.reshape(2, 2, 2, 2, cw, -1).transpose(*back, 4, 5))
        return jnp.stack(parts, axis=4).reshape(PARTS_W, PARTS_N, cw, -1)

    def natural(value, blocks):
        split = value.reshape(PARTS_W, PARTS_N, cw, blocks, -1).transpose(0, 3, 2, 1, 4)
        return split.reshape(PARTS_W * blocks * cw, -1).T

    def share(value):
        columns = lax.psum_scatter(value.astype(BF16), "wide", scatter_dimension=1, tiled=True)
        return lax.psum_scatter(columns, "narrow", scatter_dimension=0, tiled=True).astype(F32)

    a = devices(gown_a, gsend_a)
    b = devices(gown_b, gsend_b, True)
    reduce = natural(a[..., :width], 1)
    q = natural(a[..., width : width + rn], 1)
    kv = natural(a[..., width + rn : width + 3 * rn], 2)
    proj = natural(a[..., width + 3 * rn :], 1)
    columns = [
        jnp.concatenate([b[..., 128 * k : 128 * (k + 1)], b[..., 512 + REST * k : 512 + REST * (k + 1)]], axis=-1)
        for k in range(4)
    ]
    down = natural(jnp.concatenate(columns[:2], axis=-1), 1)
    up = jnp.stack(columns[2:]).transpose(2, 0, 3, 1, 4).reshape(width, -1)
    vectors = jnp.stack([vown, vsend], axis=1).reshape(PARTS_N, 8, -1)
    beside = vectors[..., 5 * rn :]
    beside = jnp.concatenate([beside[:, :3], beside[:, 3:6, : 2 * rn]], axis=-1)
    vectors = jnp.concatenate([vectors[..., : 5 * rn], beside], axis=1).transpose(1, 0, 2)
    vm = vectors[..., :rn].reshape(11, width)
    vh = vectors[..., rn : rn + width].reshape(11, PARTS_N * width)

    def share_vector(value):
        total = lax.psum(value.astype(BF16), "wide")
        return lax.psum_scatter(total, "narrow", scatter_dimension=1, tiled=True).astype(F32)

    return tuple(share(v) for v in (q, kv, reduce, proj, up, down)) + (share_vector(vm), share_vector(vh))


def solution(mesh):
    both, rows, weight, vector = P(("wide", "narrow"), None), P(("wide", "narrow")), P("narrow", "wide"), P(None, "narrow")
    return jax.shard_map(
        functools.partial(on_device, (mesh.shape["wide"], mesh.shape["narrow"])),
        mesh=mesh,
        in_specs=(both, both, rows, rows) + (weight,) * 6 + (vector,) * 2,
        out_specs=(both, both) + (weight,) * 6 + (vector,) * 2,
        check_vma=False,
    )
```

```python
import functools
import math

import jax
import jax.numpy as jnp
from jax import lax
from jax.experimental import pallas as pl
from jax.experimental.pallas import tpu as pltpu
from jax.sharding import PartitionSpec as P

HEADS = 5
EPSILON = 1e-06
MASKED = -1000000000.0
F32 = jnp.float32
BF16 = jnp.bfloat16

PARTS_W = 8
PARTS_N = 4
SLOTS = 16
TILE = 32
CHUNK = 256
PAD = 40
MROWS = 512
RUN = 160
REST = RUN - 128


def dot_nn(left, right):
    return jnp.dot(left, right, preferred_element_type=F32)


def dot_nt(left, right):
    return lax.dot_general(left, right, (((1,), (1,)), ((), ())), preferred_element_type=F32)


def dot_tn(left, right):
    return lax.dot_general(left, right, (((0,), (0,)), ((), ())), preferred_element_type=F32)


def lanes(*parts):
    return jnp.concatenate(parts, axis=1)


def rows_of(*parts):
    return jnp.concatenate(parts, axis=0)


def my_index(tuned):
    if not tuned:
        return jnp.int32(0)
    return lax.axis_index("wide") * PARTS_N + lax.axis_index("narrow")


def round_slot(device, me):
    delta = device ^ me
    first, second = (delta >> 1) & 1, (delta >> 2) & 1
    if device & 1:
        first, second = second, first
    return second * 8 + first * 4 + (delta >> 3)


def mixed_slot(device, me):
    delta = device ^ me
    x, y = (delta >> 1) & 1, (delta >> 2) & 1
    odd = (device & 1) == 1
    first, second = jnp.where(odd, y, x), jnp.where(odd, x, y)
    return second * 8 + ((delta >> 3) & 1) * 4 + ((delta >> 4) & 1) * 2 + first


def normalise(values):
    centre = values - jnp.mean(values, axis=-1, keepdims=True)
    inverse = lax.rsqrt(jnp.mean(centre * centre, axis=-1, keepdims=True) + EPSILON)
    return centre * inverse, inverse


def normalise_back(grad, normed, inverse, gain):
    scaled = grad * gain
    first = jnp.mean(scaled, axis=-1, keepdims=True)
    second = jnp.mean(scaled * normed, axis=-1, keepdims=True)
    return (scaled - first - normed * second) * inverse


def column_sum(values):
    return jnp.sum(values, axis=0, keepdims=True)


def piece_of(own_ref, other_ref, device, me, first=0, last=5, order=round_slot):
    slot = order(device, me)
    mine = ((device ^ me) & 1) == 0
    at = pl.ds(128 * first, 128 * (last - first))
    return jnp.where(mine, own_ref[slot, :, at].astype(F32), other_ref[slot, :, at].astype(F32))


def token_geometry(geo_ref, capacity, width):
    row0, row1, col0, col1 = (geo_ref[k] for k in range(4))
    area0, area1 = row0 * col0, row1 * col1
    position = lax.broadcasted_iota(jnp.int32, (capacity, width), 0)
    first = position < area0
    second = jnp.logical_and(position >= area0, position < area0 + area1)
    widths = jnp.maximum(jnp.where(second, col1, col0), 2)
    heights = jnp.where(second, row1, row0)
    local = position - jnp.where(second, area0, 0)
    row = ((local.astype(F32) + 0.5) / widths.astype(F32)).astype(jnp.int32)
    col = local - row * widths
    return first, second, row, col, heights, widths


def pack_kernel(*refs):
    sources, (a_ref, b_ref, v_ref), held, semaphores = refs[:8], refs[8:11], refs[11:19], refs[19]
    copies = [pltpu.make_async_copy(source, ref, semaphores.at[i]) for i, (source, ref) in enumerate(zip(sources, held))]
    for copy in copies:
        copy.start()
    for copy in copies:
        copy.wait()
    q_ref, kv_ref, red_ref, proj_ref, up_ref, down_ref, vm_ref, vh_ref = held
    cw = q_ref.shape[0]

    def wider(ref):
        return ref[...].astype(F32)

    kv = wider(kv_ref).T
    a_ref[0] = lanes(wider(red_ref), wider(q_ref), kv[:cw], kv[cw:], wider(proj_ref)).astype(BF16)
    up, down = wider(up_ref), wider(down_ref)
    columns = (down[:, :RUN], down[:, RUN:], up[:cw], up[cw:])
    b_ref[0] = lanes(*[c[:, :128] for c in columns], *[c[:, 128:] for c in columns]).astype(BF16)
    v_ref[0] = jnp.zeros_like(v_ref[0])
    both = lanes(wider(vm_ref), wider(vh_ref))
    v_ref[0, : both.shape[0], : both.shape[1]] = both.astype(BF16)


def pack(arguments, piece, vpiece):
    vmem = pl.BlockSpec(memory_space=pltpu.VMEM)
    return pl.pallas_call(
        pack_kernel,
        out_shape=[jax.ShapeDtypeStruct((1,) + shape, BF16) for shape in (piece, piece, vpiece)],
        in_specs=[pl.BlockSpec(memory_space=pl.ANY)] * len(arguments),
        out_specs=[vmem] * 3,
        scratch_shapes=[pltpu.VMEM(v.shape, v.dtype) for v in arguments] + [pltpu.SemaphoreType.DMA((len(arguments),))],
        compiler_params=pltpu.CompilerParams(vmem_limit_bytes=60 * 2**20),
    )(*arguments)


def prepare_kernel(
    rows_hbm, cols_hbm, tok_hbm, x_ref, n1_ref, r1_ref, chosen_ref, live_ref, geo_ref,
    rows_ref, cols_ref, tok_ref, semaphores,
):
    copies = [
        pltpu.make_async_copy(source, target, semaphores.at[i])
        for i, (source, target) in enumerate(((rows_hbm, rows_ref), (cols_hbm, cols_ref), (tok_hbm, tok_ref)))
    ]
    for copy in copies:
        copy.start()
    for copy in copies:
        copy.wait()
    capacity = tok_ref.shape[1]
    for j in range(2):
        geo_ref[j] = rows_ref[j]
        geo_ref[2 + j] = cols_ref[j]
    tokens = tok_ref[...].astype(F32).T
    x_ref[...] = tokens
    normed, inverse = normalise(tokens)
    n1_ref[...] = normed
    r1_ref[...] = inverse
    chosen_ref[...] = one_hot(rows_ref, cols_ref, capacity)
    area0, area1 = rows_ref[0] * cols_ref[0], rows_ref[1] * cols_ref[1]
    quarter0, quarter1 = area0 // 4, area1 // 4
    token = lax.broadcasted_iota(jnp.int32, live_ref.shape, 0)
    key = lax.broadcasted_iota(jnp.int32, live_ref.shape, 1)
    live = ((token < area0) & (key < quarter0)) | (
        (token >= area0) & (token < area0 + area1) & (key >= quarter0) & (key < quarter0 + quarter1)
    )
    live_ref[...] = jnp.where(live, 1.0, 0.0)


def prepare(img_rows, img_cols, tokens):
    width, capacity = tokens.shape
    keys = capacity // 4
    vmem, smem = (pl.BlockSpec(memory_space=space) for space in (pltpu.VMEM, pltpu.SMEM))
    outputs = (
        ((capacity, width), F32), ((capacity, width), F32), ((capacity, 1), F32), ((capacity, capacity), BF16),
        ((capacity, keys), F32), ((4,), jnp.int32),
    )
    return pl.pallas_call(
        prepare_kernel,
        out_shape=[jax.ShapeDtypeStruct(shape, kind) for shape, kind in outputs],
        in_specs=[pl.BlockSpec(memory_space=pl.ANY)] * 3,
        out_specs=[vmem] * 5 + [smem],
        scratch_shapes=[
            pltpu.SMEM((2,), jnp.int32), pltpu.SMEM((2,), jnp.int32), pltpu.VMEM((width, capacity), BF16),
            pltpu.SemaphoreType.DMA((3,)),
        ],
        compiler_params=pltpu.CompilerParams(vmem_limit_bytes=60 * 2**20),
        cost_estimate=pl.CostEstimate(flops=2 * 10**9, bytes_accessed=0, transcendentals=0),
    )(img_rows, img_cols, tokens)


def attend_kernel(
    tuned,
    geo_ref, cot_ref, x_ref, n1_ref, chosen_ref, live_ref, own_ref, oth_ref, vec_ref,
    x2_ref, h1_ref, patch_ref, nk_ref, rk_ref, kn_ref, q_ref, kb_ref, vb_ref,
    p_ref, o_ref, wr_ref, wq_ref, wkv_ref, wp_ref, mv_ref, hv_ref, gy_ref, gyt_ref, mask_ref,
    score_ref,
):
    me = my_index(tuned)
    capacity, width = x_ref.shape
    cw, rn = width // PARTS_W, width // PARTS_N
    keys = capacity // 4
    dim = width // HEADS

    pieces = [vec_ref[n ^ (me & 3)].astype(F32) for n in range(PARTS_N)]
    mv = lanes(*[p[:, :rn] for p in pieces])
    mv_ref[...] = mv
    runs = [p[:, rn + e * RUN : rn + (e + 1) * RUN] for p in pieces for e in range(2)]
    hv_ref[...] = lanes(*[r[:, :128] for r in runs], *[r[:, 128:] for r in runs])

    for pair in range(PARTS_W // 2):
        got = [
            [piece_of(own_ref, oth_ref, w * PARTS_N + n, me) for n in range(PARTS_N)]
            for w in (2 * pair, 2 * pair + 1)
        ]
        at = pl.ds(pair * 2 * cw, 2 * cw)
        for n in range(PARTS_N):
            wr_ref[n, at, :] = rows_of(got[0][n][:, :width], got[1][n][:, :width]).astype(BF16)

        def unit(w, k):
            return lanes(*[got[w][n][:, width + k * rn : width + (k + 1) * rn] for n in range(PARTS_N)])

        wq_ref[at, :] = rows_of(unit(0, 0), unit(1, 0)).astype(BF16)
        wkv_ref[pl.ds(pair * 4 * cw, 4 * cw), :] = rows_of(
            unit(0, 1), unit(0, 2), unit(1, 1), unit(1, 2)
        ).astype(BF16)
        wp_ref[at, :] = rows_of(unit(0, 3), unit(1, 3)).astype(BF16)

    h1 = (n1_ref[...] * mv[0:1] + mv[1:2]).astype(BF16)
    h1_ref[...] = h1
    q = (dot_nt(h1, wq_ref[...]) + mv[2:3]).astype(BF16)
    q_ref[...] = q

    patches = dot_nn(chosen_ref[...], h1).astype(BF16)
    patch_ref[...] = patches
    reduced = mv[4:5]
    for n in range(4):
        reduced = reduced + dot_nt(patches[n * keys : (n + 1) * keys], wr_ref[n])
    nk, rk = normalise(reduced)
    nk_ref[...] = nk
    rk_ref[...] = rk
    kn = (nk * mv[5:6] + mv[6:7]).astype(BF16)
    kn_ref[...] = kn
    kv = dot_nt(kn, wkv_ref[...])
    k = kv[:, :width].astype(BF16).astype(F32)
    v = (kv[:, width:] + mv[3:4]).astype(BF16).astype(F32)
    lane = lax.broadcasted_iota(jnp.int32, (keys, width), 1)
    for h in range(HEADS):
        inside = (lane >= h * dim) & (lane < (h + 1) * dim)
        at = pl.ds(h * keys, keys)
        kb_ref[at, :] = jnp.where(inside, k, 0.0).astype(BF16)
        vb_ref[at, :] = jnp.where(inside, v, 0.0).astype(BF16)

    score_ref[...] = dot_nt(q, kb_ref[...]) * dim ** (-0.5)
    def soften(i, carry):
        at = pl.ds(pl.multiple_of(i * 64, 64), 64)
        live = live_ref[at, :] > 0.5
        for h in range(HEADS):
            lane_at = pl.ds(h * keys, keys)
            s = jnp.where(live, score_ref[at, lane_at], MASKED)
            e = jnp.exp(s - jnp.max(s, axis=-1, keepdims=True))
            p_ref[at, lane_at] = e / jnp.sum(e, axis=-1, keepdims=True)
        return carry

    lax.fori_loop(0, capacity // 64, soften, 0, unroll=True)
    o = dot_nn(p_ref[...].astype(BF16), vb_ref[...]).astype(BF16)
    o_ref[...] = o
    x2_ref[...] = x_ref[...] + dot_nt(o, wp_ref[...]) + mv[7:8]
    mask_gradient(geo_ref, cot_ref, gy_ref, gyt_ref, mask_ref)


def one_hot(rows_ref, cols_ref, capacity):
    row0, row1, col0, col1 = rows_ref[0], rows_ref[1], cols_ref[0], cols_ref[1]
    area0, area1 = row0 * col0, row1 * col1
    quarter0, quarter1 = area0 // 4, area1 // 4
    keys = capacity // 4
    index = lax.broadcasted_iota(jnp.int32, (capacity, 128), 0)
    tap = index // keys
    key = index - tap * keys
    first = key < quarter0
    second = jnp.logical_and(key >= quarter0, key < quarter0 + quarter1)
    width = jnp.maximum(jnp.where(second, col1, col0), 2)
    half = width // 2
    local = key - jnp.where(second, quarter0, 0)
    row = ((local.astype(F32) + 0.5) / half.astype(F32)).astype(jnp.int32)
    col = local - row * half
    token = jnp.where(second, area0, 0) + (2 * row + tap // 2) * width + 2 * col + tap % 2
    token = jnp.where(first | second, token, -1)
    lane = lax.broadcasted_iota(jnp.int32, (capacity, 128), 1)
    return lanes(
        *[jnp.where(token == lane + t * 128, 1.0, 0.0).astype(BF16) for t in range(capacity // 128)]
    )


def mask_gradient(geo_ref, cot_ref, gy_ref, gyt_ref, mask_ref):
    width, capacity = cot_ref.shape
    area = geo_ref[0] * geo_ref[2] + geo_ref[1] * geo_ref[3]
    position = lax.broadcasted_iota(jnp.int32, (width, capacity), 1)
    gyt = jnp.where(position < area, cot_ref[...].astype(F32), 0.0)
    gyt_ref[...] = gyt.astype(BF16)
    gy_ref[...] = gyt.T.astype(BF16)
    first, second, row, col, heights, widths = token_geometry(geo_ref, capacity, 128)
    live = first | second
    start = lax.broadcasted_iota(jnp.int32, (capacity, 128), 0) // TILE * TILE
    late = start >= geo_ref[0] * geo_ref[2]
    early = jnp.logical_not(late)
    usual = (late & second) | (early & first)
    apart = second & early
    conditions = (
        live & (col > 0),
        live & (col < widths - 1),
        usual & (row > 0),
        usual & (row < heights - 1),
        apart & (row > 0),
        apart & (row < heights - 1),
        live,
    )
    for k, condition in enumerate(conditions):
        mask_ref[k] = jnp.where(condition, 1.0, 0.0)


def place_pieces(ref, core, me, wu_ref, wd_ref):
    cw = ref.shape[1]
    rn = 2 * cw
    tails = 128 * PARTS_W
    for x in range(PARTS_N // 2):
        n = 2 * x + core
        pieces = [ref[mixed_slot(w * PARTS_N + n, me)].astype(F32) for w in range(PARTS_W)]
        lane_at = pl.ds(pl.multiple_of(256 * n, 256), 256)
        for pair in range(PARTS_W // 2):
            value = rows_of(pieces[2 * pair][:, :256], pieces[2 * pair + 1][:, :256])
            wd_ref[pl.ds(pair * 2 * cw, 2 * cw), lane_at] = value.astype(BF16)
        at = pl.ds(pl.multiple_of(rn * n, 16), rn)
        for w, p in enumerate(pieces):
            wu_ref[at, pl.ds(128 * w, 128)] = rows_of(p[:, 256:384], p[:, 384:512]).astype(BF16)
        ends = [rows_of(p[:, 512 + 2 * REST : 512 + 3 * REST], p[:, 512 + 3 * REST :]) for p in pieces]
        wu_ref[at, pl.ds(tails, REST * PARTS_W)] = lanes(*ends).astype(BF16)


def prepare_two_kernel(tuned, x2_ref, mv_ref, own_ref, n2_ref, r2_ref, h2_ref, h2t_ref, wu_ref, wd_ref):
    me = my_index(tuned)
    place_pieces(own_ref, me & 1, me, wu_ref, wd_ref)
    normed, inverse = normalise(x2_ref[...])
    n2_ref[...] = normed
    r2_ref[...] = inverse
    h2 = normed * mv_ref[8:9, :] + mv_ref[9:10, :]
    h2_ref[...] = h2.astype(BF16)
    h2t_ref[...] = h2.T.astype(BF16)


def ffn_kernel(
    tuned,
    geo_ref, h2_ref, h2t_ref, gy_ref, gyt_ref, mask_ref, own_ref, oth_ref, hv_ref, wu_in_ref, wd_in_ref,
    gown_ref, gsend_ref, act_ref, dh2_ref, hg_ref, wu_ref, wd_ref,
    f_ref, gm_ref, gp_ref, dc_ref, ul_ref, ur_ref, g0_ref, slope_ref, u0_ref, df_ref, da_ref,
    upg_ref, dng_ref,
):
    me = my_index(tuned)
    capacity, width = h2_ref.shape
    hidden = hv_ref.shape[1]
    cw, rn = width // PARTS_W, width // PARTS_N
    tiles = capacity // TILE
    tails = 128 * PARTS_W

    place_pieces(oth_ref, 1 - (me & 1), me, wu_ref, wd_ref)
    for pair in range(PARTS_W // 2):
        got = [
            rows_of(*[piece_of(own_ref, oth_ref, w * PARTS_N + n, me, 4, 5, mixed_slot) for w in (2 * pair, 2 * pair + 1)])
            for n in range(PARTS_N)
        ]
        ends = lanes(*[g[:, : 2 * REST] for g in got]).astype(BF16)
        wd_ref[pl.ds(pair * 2 * cw, 2 * cw), pl.ds(tails, 2 * REST * PARTS_N)] = ends

    area, w0, w1 = geo_ref[0] * geo_ref[2], geo_ref[2], geo_ref[3]
    split = pl.multiple_of(jnp.minimum(area // TILE, tiles - 1) * TILE, TILE)

    for ref in (f_ref, gm_ref, gp_ref, dc_ref, ul_ref, ur_ref):
        ref[:, :PAD, :] = jnp.zeros((CHUNK // 128, PAD, 128), F32)
        ref[:, PAD + capacity :, :] = jnp.zeros((CHUNK // 128, PAD, 128), F32)

    dh2_ref[...] = jnp.zeros_like(dh2_ref)

    def fold(values):
        return jnp.sum(values.reshape(TILE // 8, 8, 128), axis=0)

    halves = CHUNK // 128
    chunks = hidden // CHUNK
    zero = jnp.zeros((8, 128), F32)

    def columns(c):
        return pl.ds(pl.multiple_of(c * CHUNK, CHUNK), CHUNK)

    def vector(c, k, j):
        return hv_ref[k : k + 1, pl.ds(pl.multiple_of(c * CHUNK + j * 128, 128), 128)]

    def put_vector(c, k, j, value):
        hg_ref[k : k + 1, pl.ds(pl.multiple_of(c * CHUNK + j * 128, 128), 128)] = value

    def first_layer(c, at):
        value = dot_nn(h2_ref[at, :], wu_ref[:, columns(c)])
        for j in range(halves):
            f_ref[j, pl.ds(PAD + at.start, at.size), :] = value[:, j * 128 : (j + 1) * 128] + vector(c, 0, j)

    def act_grad(c, at):
        da_ref[at, :] = dot_nn(gy_ref[at, :], wd_ref[:, columns(c)])

    def down_grad(c, at):
        dng_ref[at, columns(c)] = dot_nn(gyt_ref[at, :], act_ref[:, columns(c)])

    def up_grad(c, at):
        upg_ref[at, columns(c)] = dot_nn(h2t_ref[at, :], df_ref[...])

    def h2_grad(c, at):
        dh2_ref[at, :] += dot_nt(df_ref[at, :], wu_ref[:, columns(c)])

    def tasks(product, c, rows, size):
        return [functools.partial(product, c, pl.ds(r, min(size, rows - r))) for r in range(0, rows, size)]

    def interleave(steps, products):
        done = 0
        for i, step in enumerate(steps):
            step()
            while done < len(products) and done * len(steps) < (i + 1) * len(products):
                products[done]()
                done += 1

    def chunk_step(c, carry):
        before = jnp.maximum(c - 1, 0)
        following = jnp.minimum(c + 1, chunks - 1)
        v = [[vector(c, k, j) for k in range(11)] for j in range(halves)]

        def taps_of(j, r, mask_left, mask_right):
            here = f_ref[j, pl.ds(PAD + r, TILE), :]
            left = f_ref[j, pl.ds(PAD + r - 1, TILE), :] * mask_left
            right = f_ref[j, pl.ds(PAD + r + 1, TILE), :] * mask_right
            return left, here, right

        def row_length(r):
            return jnp.where(area > r, w0, w1)

        def column_taps(r):
            at = pl.ds(r, TILE)
            masks = mask_ref[0, at, :], mask_ref[1, at, :]
            for j in range(halves):
                left, here, right = taps_of(j, r, *masks)
                u = v[j]
                gm_ref[j, pl.ds(PAD + r, TILE), :] = u[2] * left + u[3] * here + u[4] * right
                g0_ref[j, at, :] = u[1] + u[5] * left + u[6] * here + u[7] * right
                gp_ref[j, pl.ds(PAD + r, TILE), :] = u[8] * left + u[9] * here + u[10] * right

        def column_taps_split():
            at = pl.ds(split, TILE)
            for j in range(halves):
                g0_ref[j, at, :] += (
                    mask_ref[4, at, :] * gm_ref[j, pl.ds(PAD + split - w1, TILE), :]
                    + mask_ref[5, at, :] * gp_ref[j, pl.ds(PAD + split + w1, TILE), :]
                )

        def activate(r):
            at = pl.ds(r, TILE)
            length = row_length(r)
            above, below = mask_ref[2, at, :], mask_ref[3, at, :]
            for j in range(halves):
                conv = (
                    g0_ref[j, at, :]
                    + above * gm_ref[j, pl.ds(PAD + r - length, TILE), :]
                    + below * gp_ref[j, pl.ds(PAD + r + length, TILE), :]
                )
                half = 0.5 * (1.0 + lax.erf(conv * 2.0 ** (-0.5)))
                act_ref[at, pl.ds(pl.multiple_of(c * CHUNK + j * 128, 128), 128)] = (conv * half).astype(BF16)
                slope_ref[at, pl.ds(j * 128, 128)] = half + conv * jnp.exp(-0.5 * conv * conv) * (2.0 * math.pi) ** (-0.5)

        conv_sums = [zero] * halves

        def into_conv(r):
            at = pl.ds(r, TILE)
            for j in range(halves):
                lane_at = pl.ds(j * 128, 128)
                value = da_ref[at, lane_at] * slope_ref[at, lane_at]
                dc_ref[j, pl.ds(PAD + r, TILE), :] = value
                conv_sums[j] = conv_sums[j] + fold(value)

        tap_sums = [[zero] * 9 for _ in range(halves)]

        def tap_back(r):
            at = pl.ds(r, TILE)
            length = row_length(r)
            masks = [mask_ref[k, at, :] for k in range(4)]
            for j in range(halves):
                left, here, right = taps_of(j, r, *masks[:2])
                u = v[j]
                below = masks[3] * dc_ref[j, pl.ds(PAD + r + length, TILE), :]
                level = dc_ref[j, pl.ds(PAD + r, TILE), :]
                above = masks[2] * dc_ref[j, pl.ds(PAD + r - length, TILE), :]
                ul_ref[j, pl.ds(PAD + r, TILE), :] = u[2] * below + u[5] * level + u[8] * above
                u0_ref[j, at, :] = u[3] * below + u[6] * level + u[9] * above
                ur_ref[j, pl.ds(PAD + r, TILE), :] = u[4] * below + u[7] * level + u[10] * above
                grads = [fold(d * f) for d in (below, level, above) for f in (left, here, right)]
                tap_sums[j] = [a + b for a, b in zip(tap_sums[j], grads)]

        def tap_back_split():
            at, padded = pl.ds(split, TILE), pl.ds(PAD + split, TILE)
            masks = [mask_ref[k, at, :] for k in (0, 1, 4, 5)]
            for j in range(halves):
                left, here, right = taps_of(j, split, *masks[:2])
                u = v[j]
                below = masks[3] * dc_ref[j, pl.ds(PAD + split + w1, TILE), :]
                above = masks[2] * dc_ref[j, pl.ds(PAD + split - w1, TILE), :]
                ul_ref[j, padded, :] += u[2] * below + u[8] * above
                u0_ref[j, at, :] += u[3] * below + u[9] * above
                ur_ref[j, padded, :] += u[4] * below + u[10] * above
                grads = [fold(d * f) for d in (below, above) for f in (left, here, right)]
                tap_sums[j] = [a + b for a, b in zip(tap_sums[j], grads[:3] + [zero] * 3 + grads[3:])]

        up_sums = [zero] * halves

        def spread_back(r):
            at = pl.ds(r, TILE)
            mask_left, mask_right = mask_ref[0, at, :], mask_ref[1, at, :]
            for j in range(halves):
                value = (
                    u0_ref[j, at, :]
                    + mask_left * ur_ref[j, pl.ds(PAD + r - 1, TILE), :]
                    + mask_right * ul_ref[j, pl.ds(PAD + r + 1, TILE), :]
                ).astype(BF16)
                df_ref[at, pl.ds(j * 128, 128)] = value
                up_sums[j] = up_sums[j] + fold(value.astype(F32))

        def steps(step):
            return [functools.partial(step, r) for r in range(0, capacity, TILE)]

        interleave(
            steps(column_taps) + [column_taps_split] + steps(activate),
            tasks(act_grad, c, capacity, MROWS) + tasks(up_grad, before, width, MROWS)
            + tasks(h2_grad, before, capacity, MROWS),
        )
        interleave(
            steps(into_conv) + steps(tap_back) + [tap_back_split],
            tasks(down_grad, c, width, MROWS),
        )
        interleave(steps(spread_back), tasks(first_layer, following, capacity, MROWS))
        for j in range(halves):
            put_vector(c, 0, j, column_sum(up_sums[j]))
            put_vector(c, 1, j, column_sum(conv_sums[j]))
            for k in range(9):
                put_vector(c, 2 + k, j, column_sum(tap_sums[j][k]))
        return carry

    df_ref[...] = jnp.zeros_like(df_ref)
    first_layer(0, pl.ds(0, capacity))
    lax.fori_loop(0, chunks, chunk_step, 0)
    up_grad(chunks - 1, pl.ds(0, width))
    h2_grad(chunks - 1, pl.ds(0, capacity))
    hg_ref[11:, :] = jnp.zeros((hg_ref.shape[0] - 11, hidden), F32)

    def value_of(w, n):
        down = pl.ds(w * cw, cw)
        up = [pl.ds(n * rn + e * cw, cw) for e in range(2)]
        return lanes(
            dng_ref[down, pl.ds(256 * n, 256)],
            *[upg_ref[e, pl.ds(128 * w, 128)] for e in up],
            dng_ref[down, pl.ds(tails + 2 * REST * n, 2 * REST)],
            *[upg_ref[e, pl.ds(tails + REST * w, REST)] for e in up],
        )

    store_pieces(gown_ref, gsend_ref, me, value_of, mixed_slot)


def store_pieces(own_ref, send_ref, me, value_of, order):
    even = (me & 1) == 0
    for w in range(PARTS_W):
        for x in range(PARTS_N // 2):
            first, second = value_of(w, 2 * x), value_of(w, 2 * x + 1)
            slot0, slot1 = (order(w * PARTS_N + 2 * x + c, me) for c in range(2))
            own_ref[jnp.where(even, slot0, slot1)] = jnp.where(even, first, second).astype(BF16)
            send_ref[jnp.where(even, slot1, slot0)] = jnp.where(even, second, first).astype(BF16)


def score_back_kernel(
    dh2_ref, n2_ref, r2_ref, gy_ref, mv_ref, vb_ref, p_ref, o_ref, wp_ref,
    gp_ref, dob_ref, ds_ref, bp_ref, dx2_ref, mg_ref,
    dp_ref,
):
    capacity, width = dh2_ref.shape
    keys = capacity // 4

    def norm_back(i, carry):
        at = pl.ds(pl.multiple_of(i * 64, 64), 64)
        gy = gy_ref[at, :].astype(F32)
        grad, normed = dh2_ref[at, :], n2_ref[at, :]
        dx2_ref[at, :] = gy + normalise_back(grad, normed, r2_ref[at, :], mv_ref[8:9, :])
        return tuple(a + column_sum(b) for a, b in zip(carry, (grad * normed, grad, gy)))

    zero = jnp.zeros((1, width), F32)
    sums = lax.fori_loop(0, capacity // 64, norm_back, (zero, zero, zero), unroll=True)
    mg_ref[...] = jnp.zeros_like(mg_ref)
    for k in range(3):
        mg_ref[8 + k : 9 + k, :] = sums[k]

    datt = dx2_ref[...].astype(BF16)
    bp_ref[...] = column_sum(datt.astype(F32))
    gp_ref[...] = dot_tn(datt, o_ref[...])
    dob = dot_nn(datt, wp_ref[...]).astype(BF16)
    dob_ref[...] = dob
    dp_ref[...] = dot_nt(dob, vb_ref[...])

    def soften_back(i, carry):
        at = pl.ds(pl.multiple_of(i * 64, 64), 64)
        for h in range(HEADS):
            lane_at = pl.ds(h * keys, keys)
            p = p_ref[at, lane_at]
            dp = dp_ref[at, lane_at]
            row = jnp.sum(p * dp, axis=-1, keepdims=True)
            ds_ref[at, lane_at] = (p * (dp - row)).astype(BF16)
        return carry

    lax.fori_loop(0, capacity // 64, soften_back, 0, unroll=True)


def attend_back_kernel(
    tuned,
    dob_ref, ds_ref, gp_ref, h1_ref, patch_ref, nk_ref, rk_ref, kn_ref, q_ref, kb_ref, p_ref,
    wr_ref, wkv_ref, mv_ref,
    gown_ref, gsend_ref, dq_ref, dpatch_ref, vk_ref,
    gr_ref, gq_ref, gkv_ref,
):
    me = my_index(tuned)
    capacity, width = h1_ref.shape
    cw, rn = width // PARTS_W, width // PARTS_N
    keys = capacity // 4
    dim = width // HEADS
    scale = dim ** (-0.5)

    ds = ds_ref[...]
    dq = (dot_nn(ds, kb_ref[...]) * scale).astype(BF16)
    dq_ref[...] = dq
    dk_all = dot_tn(ds, q_ref[...])
    dv_all = dot_tn(p_ref[...].astype(BF16), dob_ref[...])
    lane = lax.broadcasted_iota(jnp.int32, (keys, width), 1)
    dk = jnp.zeros((keys, width), F32)
    dv = jnp.zeros((keys, width), F32)
    for h in range(HEADS):
        inside = (lane >= h * dim) & (lane < (h + 1) * dim)
        dk = jnp.where(inside, dk_all[h * keys : (h + 1) * keys], dk)
        dv = jnp.where(inside, dv_all[h * keys : (h + 1) * keys], dv)
    dk = (dk * scale).astype(BF16)
    dv = dv.astype(BF16)
    gq_ref[...] = dot_tn(dq, h1_ref[...])
    kn = kn_ref[...]
    gkv_ref[pl.ds(0, width), :] = dot_tn(dk, kn)
    gkv_ref[pl.ds(width, width), :] = dot_tn(dv, kn)
    dkn = dot_nn(dk, wkv_ref[pl.ds(0, width), :]) + dot_nn(dv, wkv_ref[pl.ds(width, width), :])
    nk = nk_ref[...]
    dsr = normalise_back(dkn, nk, rk_ref[...], mv_ref[5:6, :]).astype(BF16)
    vk_ref[...] = rows_of(
        column_sum(dq.astype(F32)),
        column_sum(dv.astype(F32)),
        column_sum(dsr.astype(F32)),
        column_sum(dkn * nk),
        column_sum(dkn),
        jnp.zeros((3, width), F32),
    )
    for n in range(4):
        at = pl.ds(n * keys, keys)
        gr_ref[n] = dot_tn(dsr, patch_ref[at, :])
        dpatch_ref[at, :] = dot_nn(dsr, wr_ref[n])

    def value_of(w, n):
        at, lane_at = pl.ds(w * cw, cw), pl.ds(n * rn, rn)
        return lanes(
            gr_ref[n, at, :],
            gq_ref[at, lane_at],
            gkv_ref[pl.ds(2 * w * cw, cw), lane_at],
            gkv_ref[pl.ds(2 * w * cw + cw, cw), lane_at],
            gp_ref[at, lane_at],
        )

    store_pieces(gown_ref, gsend_ref, me, value_of, round_slot)


def mixed_kernel(x2_ref, act_ref, wd_ref, mv_ref, mask_ref, mixed_ref):
    width = x2_ref.shape[1]
    occupied = mask_ref[6]
    occupied = lanes(*([occupied] * (width // 128)), occupied[:, : width % 128])
    mixed = x2_ref[...] + dot_nt(act_ref[...], wd_ref[...]) + mv_ref[10:11, :]
    mixed_ref[...] = (mixed * occupied).T.astype(BF16)


def fold_rows(value, unit):
    rest = value[8:]
    beside = lanes(rest[:, : 3 * unit], jnp.zeros((8, 256 - 3 * unit), F32))
    below = lanes(rest[:, 3 * unit :], jnp.zeros((8, 256 - 2 * unit), F32))
    return lanes(value[:8], (beside + pltpu.roll(below, 3, 0))[:, : 3 * unit])


def unfold_rows(value, unit):
    beside = lanes(value[:, 5 * unit :], jnp.zeros((8, 256 - 3 * unit), F32))
    below = pltpu.roll(beside, 5, 0)
    return rows_of(value[:, : 5 * unit], lanes(beside[:, : 3 * unit], below[:, : 2 * unit]))


def token_back_kernel(
    tuned,
    dx2_ref, dq_ref, dpatch_ref, n1_ref, r1_ref, chosen_ref, wq_ref, mv_ref, mg_ref, hg_ref, vk_ref, bp_ref,
    tg_ref, vown_ref, vsend_ref,
):
    me = my_index(tuned)
    capacity, width = dx2_ref.shape
    rn = width // PARTS_N
    chosen = chosen_ref[...]
    high = dpatch_ref[...].astype(BF16)
    low = (dpatch_ref[...] - high.astype(F32)).astype(BF16)
    dh1 = dot_nn(dq_ref[...], wq_ref[...]) + dot_tn(chosen, high) + dot_tn(chosen, low)
    n1 = n1_ref[...]
    vk = vk_ref[...]
    token_grad = dx2_ref[...] + normalise_back(dh1, n1, r1_ref[...], mv_ref[0:1, :])
    tg_ref[...] = token_grad.T.astype(BF16)
    sums = rows_of(column_sum(dh1 * n1), column_sum(dh1), vk[0:5], bp_ref[...], mg_ref[8:16, :])
    hg = hg_ref[...]
    value = []
    for n in range(PARTS_N):
        parts = []
        for w in (2 * n, 2 * n + 1):
            parts += [hg[:, 128 * w : 128 * (w + 1)], hg[:, 1024 + REST * w : 1024 + REST * (w + 1)]]
        value.append(fold_rows(lanes(sums[:, n * rn : (n + 1) * rn], *parts), rn))
    even = (me & 1) == 0
    for x in range(2):
        slot = x ^ ((me >> 1) & 1)
        vown_ref[slot] = jnp.where(even, value[2 * x], value[2 * x + 1]).astype(BF16)
        vsend_ref[slot] = jnp.where(even, value[2 * x + 1], value[2 * x]).astype(BF16)


def total_of(refs):
    value = refs[0][...].astype(F32)
    for ref in refs[1:]:
        value = value + ref[...].astype(F32)
    return value


def halve_kernel(keep_ref, got_ref, low_ref, high_ref):
    half = low_ref.shape[0]
    low_ref[...] = (keep_ref[:half].astype(F32) + got_ref[:half].astype(F32)).astype(BF16)
    high_ref[...] = (keep_ref[half:].astype(F32) + got_ref[half:].astype(F32)).astype(BF16)


def halve_core_kernel(keep_ref, got_ref, vkeep_ref, vgot_ref, low_ref, vlow_ref, send_ref):
    half = low_ref.shape[0]
    low_ref[...] = (keep_ref[:half].astype(F32) + got_ref[:half].astype(F32)).astype(BF16)
    parts = [keep_ref[half + k].astype(F32) + got_ref[half + k].astype(F32) for k in range(half)]
    vector = total_of((vkeep_ref, vgot_ref))
    vlow_ref[...] = vector.astype(BF16)
    send_ref[...] = rows_of(*parts, vector[0], vector[1]).astype(BF16)


def halve_round_kernel(tuned, keep_ref, vkeep_ref, got_ref, low_ref, vlow_ref, send_ref):
    half, cw = low_ref.shape[:2]
    rows = vkeep_ref.shape[1]
    got = got_ref[...].astype(F32)
    parts = [keep_ref[k].astype(F32) + got[k * cw : (k + 1) * cw] for k in range(2 * half)]
    for k in range(half):
        low_ref[k] = parts[k].astype(BF16)
    got0, got1 = (got[2 * half * cw + k * rows : 2 * half * cw + (k + 1) * rows] for k in range(2))
    keep0, keep1 = vkeep_ref[0].astype(F32), vkeep_ref[1].astype(F32)
    even = (my_index(tuned) & 1) == 0
    low = keep0 + jnp.where(even, got0, got1)
    vlow_ref[0] = low.astype(BF16)
    send_ref[...] = rows_of(*parts[half:], jnp.where(even, keep1 + got1, low)).astype(BF16)


def quarter_vector_kernel(keep_ref, vkeep_ref, got_ref, *out_refs):
    cw = keep_ref.shape[1]
    got = got_ref[...].astype(F32)
    vector = vkeep_ref[0].astype(F32) + got[4 * cw :]
    for k, ref in enumerate(out_refs):
        ref[...] = rows_of(keep_ref[k].astype(F32) + got[k * cw : (k + 1) * cw], vector).astype(BF16)


def finish_kernel(
    a_ref, b_ref, c_ref, d_ref, ffn_ref, ffn_got_ref,
    q_ref, kv_ref, red_ref, proj_ref, up_ref, down_ref, vm_ref, vh_ref,
):
    total = total_of((a_ref, b_ref, c_ref, d_ref))
    cw, width = red_ref.shape
    rn = q_ref.shape[1]
    red_ref[...] = total[:cw, :width]
    unit = [total[:cw, width + k * rn : width + (k + 1) * rn] for k in range(4)]
    q_ref[...] = unit[0]
    kv_ref[...] = rows_of(unit[1], unit[2]).T
    proj_ref[...] = unit[3]
    vector = unfold_rows(total[cw:], rn)
    vm_ref[...] = vector[: vm_ref.shape[0], :rn]
    vh_ref[...] = vector[: vh_ref.shape[0], rn:]
    total = total_of((ffn_ref, ffn_got_ref))[0]
    columns = [
        lanes(total[:, 128 * k : 128 * (k + 1)], total[:, 512 + REST * k : 512 + REST * (k + 1)]) for k in range(4)
    ]
    down_ref[...] = lanes(*columns[:2])
    up_ref[...] = rows_of(*columns[2:])


def call(kernel, inputs, outputs, scratch=(), scalars=0, limit=40, flops=0, moved=0, aliases={}):
    vmem = pl.BlockSpec(memory_space=pltpu.VMEM)
    smem = pl.BlockSpec(memory_space=pltpu.SMEM)
    return pl.pallas_call(
        kernel,
        out_shape=[jax.ShapeDtypeStruct(shape, kind) for shape, kind in outputs],
        in_specs=[smem] * scalars + [vmem] * (len(inputs) - scalars),
        out_specs=[vmem] * len(outputs),
        scratch_shapes=[pltpu.VMEM(shape, kind) for shape, kind in scratch],
        input_output_aliases=aliases,
        compiler_params=pltpu.CompilerParams(vmem_limit_bytes=limit * 2**20),
        cost_estimate=pl.CostEstimate(flops=flops, bytes_accessed=moved, transcendentals=0),
    )(*inputs)


def after(value, *others):
    return lax.optimization_barrier((value, *others))[0]


def on_device(
    mesh_shape,
    tokens, cotangent, img_rows, img_cols,
    q_weight, kv_weight, reduce_weight, proj_weight, up_weight, down_weight, vec_model, vec_hidden,
):
    wide, narrow = mesh_shape
    tuned = (wide, narrow) == (PARTS_W, PARTS_N)
    capacity, width = tokens.shape
    hidden = vec_hidden.shape[1] * narrow
    cw, rn = width // PARTS_W, width // PARTS_N
    keys = capacity // 4
    piece = (cw, 2 * width)
    vpiece, gpiece = (16, 2 * width), (8, 2 * width)

    def join(*parts):
        return jnp.concatenate(parts, axis=0)

    def swap(value, mask, other=None):
        masks = (mask, mask if other is None else other)
        pairs = [(i, i ^ masks[i & 1]) for i in range(wide * narrow)]
        return lax.ppermute(value, ("wide", "narrow"), pairs)

    tokens_f32 = ((capacity, width), F32)
    tokens_low = ((capacity, width), BF16)
    x, n1, r1, chosen, live, geo = prepare(img_rows, img_cols, tokens.T)
    if tuned:
        pack_a, pack_b, pack_v = pack(
            (
                q_weight.T, kv_weight, reduce_weight.T, proj_weight.T, up_weight, down_weight.T,
                vec_model, vec_hidden,
            ),
            piece, vpiece,
        )
        line_a = [swap(pack_a, m) for m in (8, 16, 24)]
        got_b, got_v = swap(pack_b, 2, 4), swap(pack_v, 1)
        *line_a, got_b, got_v = lax.optimization_barrier((*line_a, got_b, got_v, x, n1, chosen))[:5]
        buf_a, buf_b, vecs = join(pack_a, *line_a), join(pack_b, got_b), join(pack_v, got_v)
        buf_a, buf_b = join(buf_a, swap(buf_a, 2, 4)), join(buf_b, swap(buf_b, 16))
        got = lax.optimization_barrier((swap(buf_a, 4, 2), swap(buf_b, 8), swap(vecs, 2)))
        own_a, half_b, vecs = (join(v, g) for v, g in zip((buf_a, buf_b, vecs), got))
        oth_a = swap(own_a, 1)
        rest_b = swap(half_b, 4, 2)
    else:
        own_a, oth_a, own_b, oth_b, vecs = gather_plain(
            q_weight, kv_weight, reduce_weight, proj_weight, up_weight, down_weight, vec_model, vec_hidden
        )

    square = (width, width)
    (
        x2, h1, patches, nk, rk, kn, q, kb, vb, p, o, wr, wq, wkv, wp, mv, hv, gy, gyt, masks,
    ) = call(
        functools.partial(attend_kernel, tuned),
        (geo, cotangent.T, x, n1, chosen, live, own_a, oth_a, vecs),
        (
            tokens_f32, tokens_low,
            ((capacity, width), BF16), ((keys, width), F32), ((keys, 1), F32), ((keys, width), BF16),
            ((capacity, width), BF16), ((HEADS * keys, width), BF16), ((HEADS * keys, width), BF16),
            ((capacity, HEADS * keys), F32), ((capacity, width), BF16),
            ((4,) + square, BF16), (square, BF16), ((2 * width, width), BF16), (square, BF16),
            ((16, width), F32), ((16, hidden), F32),
            tokens_low, ((width, capacity), BF16), ((7, capacity, 128), F32),
        ),
        scratch=(((capacity, HEADS * keys), F32),),
        scalars=1,
        flops=8 * 10**9,
    )

    if tuned:
        own_b = join(half_b, after(rest_b, x2))
        oth_b = swap(own_b, 1)
    padded = ((CHUNK // 128, capacity + 2 * PAD, 128), F32)
    halved = ((CHUNK // 128, capacity, 128), F32)
    chunked = ((capacity, CHUNK), F32)
    n2, r2, h2, h2t, wu, wd = call(
        functools.partial(prepare_two_kernel, tuned),
        (x2, mv, own_b),
        (
            tokens_f32, ((capacity, 1), F32), tokens_low, ((width, capacity), BF16),
            ((width, hidden), BF16), ((width, hidden), BF16),
        ),
        flops=10**9,
    )
    gown_b, gsend_b, act, dh2, hg, wu, wd = call(
        functools.partial(ffn_kernel, tuned),
        (geo, h2, h2t, gy, gyt, masks, own_b, oth_b, hv, wu, wd),
        (
            ((SLOTS,) + piece, BF16), ((SLOTS,) + piece, BF16),
            ((capacity, hidden), BF16), tokens_f32, ((16, hidden), F32),
            ((width, hidden), BF16), ((width, hidden), BF16),
        ),
        aliases={9: 5, 10: 6},
        scratch=(
            padded, padded, padded, padded, padded, padded,
            halved, chunked, halved, ((capacity, CHUNK), BF16), chunked,
            ((width, hidden), F32), ((width, hidden), F32),
        ),
        scalars=1,
        flops=33 * 10**9,
    )

    if tuned:
        got_b = swap(gsend_b, 1)
    gp, dob, ds, bp, dx2, mg = call(
        score_back_kernel,
        (dh2, n2, r2, gy, mv, vb, p, o, wp),
        (
            (square, F32), ((capacity, width), BF16), ((capacity, HEADS * keys), BF16), ((1, width), F32),
            tokens_f32, ((16, width), F32),
        ),
        scratch=(((capacity, HEADS * keys), F32),),
        flops=25 * 10**8,
    )
    def halve(keep, got, flops=0):
        shape = ((keep.shape[0] // 2,) + piece, BF16)
        return call(halve_kernel, (keep, got), (shape, shape), flops=flops)

    if tuned:
        got_b = after(got_b, ds)
        low_b, high_b = halve(gown_b, got_b)
        ds = after(ds, high_b)
        got_b = swap(high_b, 4, 2)
    gown_a, gsend_a, dq, dpatch, vk = call(
        functools.partial(attend_back_kernel, tuned),
        (dob, ds, gp, h1, patches, nk, rk, kn, q, kb, p, wr, wkv, mv),
        (
            ((SLOTS,) + piece, BF16), ((SLOTS,) + piece, BF16), ((capacity, width), BF16), ((capacity, width), F32),
            ((8, width), F32),
        ),
        scratch=(((4,) + square, F32), (square, F32), ((2 * width, width), F32)),
        flops=0,
    )
    if tuned:
        got_a = swap(gsend_a, 1)
        low_b, high_b = halve(low_b, got_b, flops=7 * 10**9)
        gown_a = after(gown_a, high_b)
    (mixed,) = call(mixed_kernel, (x2, act, wd, mv, masks), (((width, capacity), BF16),), flops=10**9)
    token_grad, vown, vsend = call(
        functools.partial(token_back_kernel, tuned),
        (dx2, dq, dpatch, n1, r1, chosen, wq, mv, mg, hg, vk, bp),
        (((width, capacity), BF16), ((2,) + gpiece, BF16), ((2,) + gpiece, BF16)),
    )

    if not tuned:
        grads = scatter_plain(mesh_shape, width, gown_a, gsend_a, gown_b, gsend_b, vown, vsend)
        return (mixed.T, token_grad.T) + grads

    vrows = gpiece[0]
    low_a, vlow, high_a = call(
        halve_core_kernel,
        (gown_a, got_a, vown, swap(vsend, 1)),
        (((8,) + piece, BF16), ((2,) + gpiece, BF16), ((8 * cw + 2 * vrows, 2 * width), BF16)),
    )
    got_a, got_b, mixed = lax.optimization_barrier((swap(high_a, 4, 2), swap(high_b, 8), mixed))
    low_a, vlow, high_a = call(
        functools.partial(halve_round_kernel, tuned),
        (low_a, vlow, got_a),
        (((4,) + piece, BF16), ((1,) + gpiece, BF16), ((4 * cw + vrows, 2 * width), BF16)),
    )
    low_b, high_b = halve(low_b, got_b)
    got_a, got_b = swap(high_a, 2, 4), swap(high_b, 16)
    near_a = list(call(quarter_vector_kernel, (low_a, vlow, got_a), (((cw + vrows, 2 * width), BF16),) * 4))
    line_a = [swap(near_a[k], 8 * k) for k in (1, 2, 3)]
    low_b, high_b = halve(low_b, got_b)
    q_grad, kv_grad, reduce_grad, proj_grad, up_grad, down_grad, vm_grad, vh_grad = call(
        finish_kernel,
        (near_a[0], *line_a, low_b, swap(high_b, 2, 4)),
        (
            ((cw, rn), F32), ((rn, 2 * cw), F32), ((cw, width), F32), ((cw, rn), F32),
            ((rn, 4 * cw), F32), ((cw, width), F32), ((11, rn), F32), ((11, width), F32),
        ),
    )
    return (
        mixed.T, token_grad.T, q_grad.T, kv_grad, reduce_grad.T, proj_grad.T, up_grad, down_grad.T, vm_grad, vh_grad,
    )


def gather_plain(q, kv, reduce, proj, up, down, vec_model, vec_hidden):
    def whole(value):
        rows = lax.all_gather(value, "narrow", axis=0, tiled=True)
        return lax.all_gather(rows, "wide", axis=1, tiled=True).T

    q, kv, reduce, proj, up, down = (whole(v) for v in (q, kv, reduce, proj, up, down))
    width = q.shape[0]
    cw, rn = width // PARTS_W, width // PARTS_N

    def pieces(turned, blocks):
        split = turned.reshape(PARTS_W, blocks, cw, PARTS_N, -1)
        return split.transpose(0, 3, 2, 1, 4).reshape(PARTS_W, PARTS_N, cw, -1)

    def slots(value, mixed=False):
        value = value.reshape(2, 2, 2, 2, 2, cw, -1)
        orders = ((2, 1, 0, 3), (3, 1, 0, 2)) if mixed else ((2, 3, 0, 1), (3, 2, 0, 1))
        return tuple(
            value[:, :, :, :, core].transpose(*order, 4, 5).reshape(SLOTS, cw, -1) for core, order in enumerate(orders)
        )

    a = jnp.concatenate([pieces(reduce, 1), pieces(q, 1), pieces(kv, 2), pieces(proj, 1)], axis=-1)
    columns = pieces(down, 1).reshape(PARTS_W, PARTS_N, cw, 2, RUN)
    columns = [columns[..., e, :] for e in range(2)]
    halves = up.T.reshape(PARTS_N, 2, cw, PARTS_W, RUN).transpose(1, 3, 0, 2, 4)
    columns += [halves[0], halves[1]]
    b = jnp.concatenate([c[..., :128] for c in columns] + [c[..., 128:] for c in columns], axis=-1)
    vm = lax.all_gather(vec_model, "narrow", axis=1, tiled=True)
    vh = lax.all_gather(vec_hidden, "narrow", axis=1, tiled=True)
    both = jnp.concatenate([vm.reshape(11, PARTS_N, rn), vh.reshape(11, PARTS_N, width)], axis=-1)
    vecs = jnp.pad(both.transpose(1, 0, 2), ((0, 0), (0, 5), (0, 3 * rn)))
    return (*slots(a), *slots(b, True), vecs)


def scatter_plain(mesh_shape, width, gown_a, gsend_a, gown_b, gsend_b, vown, vsend):
    cw, rn = width // PARTS_W, width // PARTS_N

    def devices(own, send, mixed=False):
        orders = ((2, 1, 0, 3), (3, 1, 0, 2)) if mixed else ((2, 3, 0, 1), (3, 2, 0, 1))
        parts = []
        for value, order in zip((own, send), orders):
            back = sorted(range(4), key=lambda k: order[k])
            parts.append(value.reshape(2, 2, 2, 2, cw, -1).transpose(*back, 4, 5))
        return jnp.stack(parts, axis=4).reshape(PARTS_W, PARTS_N, cw, -1)

    def natural(value, blocks):
        split = value.reshape(PARTS_W, PARTS_N, cw, blocks, -1).transpose(0, 3, 2, 1, 4)
        return split.reshape(PARTS_W * blocks * cw, -1).T

    def share(value):
        columns = lax.psum_scatter(value.astype(BF16), "wide", scatter_dimension=1, tiled=True)
        return lax.psum_scatter(columns, "narrow", scatter_dimension=0, tiled=True).astype(F32)

    a = devices(gown_a, gsend_a)
    b = devices(gown_b, gsend_b, True)
    reduce = natural(a[..., :width], 1)
    q = natural(a[..., width : width + rn], 1)
    kv = natural(a[..., width + rn : width + 3 * rn], 2)
    proj = natural(a[..., width + 3 * rn :], 1)
    columns = [
        jnp.concatenate([b[..., 128 * k : 128 * (k + 1)], b[..., 512 + REST * k : 512 + REST * (k + 1)]], axis=-1)
        for k in range(4)
    ]
    down = natural(jnp.concatenate(columns[:2], axis=-1), 1)
    up = jnp.stack(columns[2:]).transpose(2, 0, 3, 1, 4).reshape(width, -1)
    vectors = jnp.stack([vown, vsend], axis=1).reshape(PARTS_N, 8, -1)
    beside = vectors[..., 5 * rn :]
    beside = jnp.concatenate([beside[:, :3], beside[:, 3:6, : 2 * rn]], axis=-1)
    vectors = jnp.concatenate([vectors[..., : 5 * rn], beside], axis=1).transpose(1, 0, 2)
    vm = vectors[..., :rn].reshape(11, width)
    vh = vectors[..., rn : rn + width].reshape(11, PARTS_N * width)

    def share_vector(value):
        total = lax.psum(value.astype(BF16), "wide")
        return lax.psum_scatter(total, "narrow", scatter_dimension=1, tiled=True).astype(F32)

    return tuple(share(v) for v in (q, kv, reduce, proj, up, down)) + (share_vector(vm), share_vector(vh))


def solution(mesh):
    both, rows, weight, vector = P(("wide", "narrow"), None), P(("wide", "narrow")), P("narrow", "wide"), P(None, "narrow")
    return jax.shard_map(
        functools.partial(on_device, (mesh.shape["wide"], mesh.shape["narrow"])),
        mesh=mesh,
        in_specs=(both, both, rows, rows) + (weight,) * 6 + (vector,) * 2,
        out_specs=(both, both) + (weight,) * 6 + (vector,) * 2,
        check_vma=False,
    )
```

```python
import functools
import math

import jax
import jax.numpy as jnp
from jax import lax
from jax.experimental import pallas as pl
from jax.experimental.pallas import tpu as pltpu
from jax.sharding import PartitionSpec as P

HEADS = 5
EPSILON = 1e-06
MASKED = -1000000000.0
F32 = jnp.float32
BF16 = jnp.bfloat16

PARTS_W = 8
PARTS_N = 4
SLOTS = 16
TILE = 32
CHUNK = 256
PAD = 40
MROWS = 512
RUN = 160
REST = RUN - 128


def dot_nn(left, right):
    return jnp.dot(left, right, preferred_element_type=F32)


def dot_nt(left, right):
    return lax.dot_general(left, right, (((1,), (1,)), ((), ())), preferred_element_type=F32)


def dot_tn(left, right):
    return lax.dot_general(left, right, (((0,), (0,)), ((), ())), preferred_element_type=F32)


def lanes(*parts):
    return jnp.concatenate(parts, axis=1)


def rows_of(*parts):
    return jnp.concatenate(parts, axis=0)


def my_index(tuned):
    if not tuned:
        return jnp.int32(0)
    return lax.axis_index("wide") * PARTS_N + lax.axis_index("narrow")


def round_slot(device, me):
    delta = device ^ me
    first, second = (delta >> 1) & 1, (delta >> 2) & 1
    if device & 1:
        first, second = second, first
    return second * 8 + first * 4 + (delta >> 3)


def mixed_slot(device, me):
    delta = device ^ me
    x, y = (delta >> 1) & 1, (delta >> 2) & 1
    odd = (device & 1) == 1
    first, second = jnp.where(odd, y, x), jnp.where(odd, x, y)
    return second * 8 + ((delta >> 3) & 1) * 4 + ((delta >> 4) & 1) * 2 + first


def normalise(values):
    centre = values - jnp.mean(values, axis=-1, keepdims=True)
    inverse = lax.rsqrt(jnp.mean(centre * centre, axis=-1, keepdims=True) + EPSILON)
    return centre * inverse, inverse


def normalise_back(grad, normed, inverse, gain):
    scaled = grad * gain
    first = jnp.mean(scaled, axis=-1, keepdims=True)
    second = jnp.mean(scaled * normed, axis=-1, keepdims=True)
    return (scaled - first - normed * second) * inverse


def column_sum(values):
    return jnp.sum(values, axis=0, keepdims=True)


def piece_of(own_ref, other_ref, device, me, first=0, last=5, order=round_slot):
    slot = order(device, me)
    mine = ((device ^ me) & 1) == 0
    at = pl.ds(128 * first, 128 * (last - first))
    return jnp.where(mine, own_ref[slot, :, at].astype(F32), other_ref[slot, :, at].astype(F32))


def token_geometry(geo_ref, capacity, width):
    row0, row1, col0, col1 = (geo_ref[k] for k in range(4))
    area0, area1 = row0 * col0, row1 * col1
    position = lax.broadcasted_iota(jnp.int32, (capacity, width), 0)
    first = position < area0
    second = jnp.logical_and(position >= area0, position < area0 + area1)
    widths = jnp.maximum(jnp.where(second, col1, col0), 2)
    heights = jnp.where(second, row1, row0)
    local = position - jnp.where(second, area0, 0)
    row = ((local.astype(F32) + 0.5) / widths.astype(F32)).astype(jnp.int32)
    col = local - row * widths
    return first, second, row, col, heights, widths


def pack_kernel(*refs):
    sources, (a_ref, b_ref, v_ref), held, semaphores = refs[:8], refs[8:11], refs[11:19], refs[19]
    copies = [pltpu.make_async_copy(source, ref, semaphores.at[i]) for i, (source, ref) in enumerate(zip(sources, held))]
    for copy in copies:
        copy.start()
    for copy in copies:
        copy.wait()
    q_ref, kv_ref, red_ref, proj_ref, up_ref, down_ref, vm_ref, vh_ref = held
    cw = q_ref.shape[0]

    def wider(ref):
        return ref[...].astype(F32)

    kv = wider(kv_ref).T
    a_ref[0] = lanes(wider(red_ref), wider(q_ref), kv[:cw], kv[cw:], wider(proj_ref)).astype(BF16)
    up, down = wider(up_ref), wider(down_ref)
    columns = (down[:, :RUN], down[:, RUN:], up[:cw], up[cw:])
    b_ref[0] = lanes(*[c[:, :128] for c in columns], *[c[:, 128:] for c in columns]).astype(BF16)
    v_ref[0] = jnp.zeros_like(v_ref[0])
    both = lanes(wider(vm_ref), wider(vh_ref))
    v_ref[0, : both.shape[0], : both.shape[1]] = both.astype(BF16)


def pack(arguments, piece, vpiece):
    vmem = pl.BlockSpec(memory_space=pltpu.VMEM)
    return pl.pallas_call(
        pack_kernel,
        out_shape=[jax.ShapeDtypeStruct((1,) + shape, BF16) for shape in (piece, piece, vpiece)],
        in_specs=[pl.BlockSpec(memory_space=pl.ANY)] * len(arguments),
        out_specs=[vmem] * 3,
        scratch_shapes=[pltpu.VMEM(v.shape, v.dtype) for v in arguments] + [pltpu.SemaphoreType.DMA((len(arguments),))],
        compiler_params=pltpu.CompilerParams(vmem_limit_bytes=60 * 2**20),
    )(*arguments)


def prepare_kernel(
    rows_hbm, cols_hbm, tok_hbm, x_ref, n1_ref, r1_ref, chosen_ref, live_ref, geo_ref,
    rows_ref, cols_ref, tok_ref, semaphores,
):
    copies = [
        pltpu.make_async_copy(source, target, semaphores.at[i])
        for i, (source, target) in enumerate(((rows_hbm, rows_ref), (cols_hbm, cols_ref), (tok_hbm, tok_ref)))
    ]
    for copy in copies:
        copy.start()
    for copy in copies:
        copy.wait()
    capacity = tok_ref.shape[1]
    for j in range(2):
        geo_ref[j] = rows_ref[j]
        geo_ref[2 + j] = cols_ref[j]
    tokens = tok_ref[...].astype(F32).T
    x_ref[...] = tokens
    normed, inverse = normalise(tokens)
    n1_ref[...] = normed
    r1_ref[...] = inverse
    chosen_ref[...] = one_hot(rows_ref, cols_ref, capacity)
    area0, area1 = rows_ref[0] * cols_ref[0], rows_ref[1] * cols_ref[1]
    quarter0, quarter1 = area0 // 4, area1 // 4
    token = lax.broadcasted_iota(jnp.int32, live_ref.shape, 0)
    key = lax.broadcasted_iota(jnp.int32, live_ref.shape, 1)
    live = ((token < area0) & (key < quarter0)) | (
        (token >= area0) & (token < area0 + area1) & (key >= quarter0) & (key < quarter0 + quarter1)
    )
    live_ref[...] = jnp.where(live, 1.0, 0.0)


def prepare(img_rows, img_cols, tokens):
    width, capacity = tokens.shape
    keys = capacity // 4
    vmem, smem = (pl.BlockSpec(memory_space=space) for space in (pltpu.VMEM, pltpu.SMEM))
    outputs = (
        ((capacity, width), F32), ((capacity, width), F32), ((capacity, 1), F32), ((capacity, capacity), BF16),
        ((capacity, keys), F32), ((4,), jnp.int32),
    )
    return pl.pallas_call(
        prepare_kernel,
        out_shape=[jax.ShapeDtypeStruct(shape, kind) for shape, kind in outputs],
        in_specs=[pl.BlockSpec(memory_space=pl.ANY)] * 3,
        out_specs=[vmem] * 5 + [smem],
        scratch_shapes=[
            pltpu.SMEM((2,), jnp.int32), pltpu.SMEM((2,), jnp.int32), pltpu.VMEM((width, capacity), BF16),
            pltpu.SemaphoreType.DMA((3,)),
        ],
        compiler_params=pltpu.CompilerParams(vmem_limit_bytes=60 * 2**20),
        cost_estimate=pl.CostEstimate(flops=2 * 10**9, bytes_accessed=0, transcendentals=0),
    )(img_rows, img_cols, tokens)


def attend_kernel(
    tuned,
    geo_ref, cot_ref, x_ref, n1_ref, chosen_ref, live_ref, own_ref, oth_ref, vec_ref,
    x2_ref, h1_ref, patch_ref, nk_ref, rk_ref, kn_ref, q_ref, kb_ref, vb_ref,
    p_ref, o_ref, wr_ref, wq_ref, wkv_ref, wp_ref, mv_ref, hv_ref, gy_ref, gyt_ref, mask_ref,
    score_ref,
):
    me = my_index(tuned)
    capacity, width = x_ref.shape
    cw, rn = width // PARTS_W, width // PARTS_N
    keys = capacity // 4
    dim = width // HEADS

    pieces = [vec_ref[n ^ (me & 3)].astype(F32) for n in range(PARTS_N)]
    mv = lanes(*[p[:, :rn] for p in pieces])
    mv_ref[...] = mv
    runs = [p[:, rn + e * RUN : rn + (e + 1) * RUN] for p in pieces for e in range(2)]
    hv_ref[...] = lanes(*[r[:, :128] for r in runs], *[r[:, 128:] for r in runs])

    for pair in range(PARTS_W // 2):
        got = [
            [piece_of(own_ref, oth_ref, w * PARTS_N + n, me) for n in range(PARTS_N)]
            for w in (2 * pair, 2 * pair + 1)
        ]
        at = pl.ds(pair * 2 * cw, 2 * cw)
        for n in range(PARTS_N):
            wr_ref[n, at, :] = rows_of(got[0][n][:, :width], got[1][n][:, :width]).astype(BF16)

        def unit(w, k):
            return lanes(*[got[w][n][:, width + k * rn : width + (k + 1) * rn] for n in range(PARTS_N)])

        wq_ref[at, :] = rows_of(unit(0, 0), unit(1, 0)).astype(BF16)
        wkv_ref[pl.ds(pair * 4 * cw, 4 * cw), :] = rows_of(
            unit(0, 1), unit(0, 2), unit(1, 1), unit(1, 2)
        ).astype(BF16)
        wp_ref[at, :] = rows_of(unit(0, 3), unit(1, 3)).astype(BF16)

    h1 = (n1_ref[...] * mv[0:1] + mv[1:2]).astype(BF16)
    h1_ref[...] = h1
    q = (dot_nt(h1, wq_ref[...]) + mv[2:3]).astype(BF16)
    q_ref[...] = q

    patches = dot_nn(chosen_ref[...], h1).astype(BF16)
    patch_ref[...] = patches
    reduced = mv[4:5]
    for n in range(4):
        reduced = reduced + dot_nt(patches[n * keys : (n + 1) * keys], wr_ref[n])
    nk, rk = normalise(reduced)
    nk_ref[...] = nk
    rk_ref[...] = rk
    kn = (nk * mv[5:6] + mv[6:7]).astype(BF16)
    kn_ref[...] = kn
    kv = dot_nt(kn, wkv_ref[...])
    k = kv[:, :width].astype(BF16).astype(F32)
    v = (kv[:, width:] + mv[3:4]).astype(BF16).astype(F32)
    lane = lax.broadcasted_iota(jnp.int32, (keys, width), 1)
    for h in range(HEADS):
        inside = (lane >= h * dim) & (lane < (h + 1) * dim)
        at = pl.ds(h * keys, keys)
        kb_ref[at, :] = jnp.where(inside, k, 0.0).astype(BF16)
        vb_ref[at, :] = jnp.where(inside, v, 0.0).astype(BF16)

    score_ref[...] = dot_nt(q, kb_ref[...]) * dim ** (-0.5)
    def soften(i, carry):
        at = pl.ds(pl.multiple_of(i * 64, 64), 64)
        live = live_ref[at, :] > 0.5
        for h in range(HEADS):
            lane_at = pl.ds(h * keys, keys)
            s = jnp.where(live, score_ref[at, lane_at], MASKED)
            e = jnp.exp(s - jnp.max(s, axis=-1, keepdims=True))
            p_ref[at, lane_at] = e / jnp.sum(e, axis=-1, keepdims=True)
        return carry

    lax.fori_loop(0, capacity // 64, soften, 0, unroll=True)
    o = dot_nn(p_ref[...].astype(BF16), vb_ref[...]).astype(BF16)
    o_ref[...] = o
    x2_ref[...] = x_ref[...] + dot_nt(o, wp_ref[...]) + mv[7:8]
    mask_gradient(geo_ref, cot_ref, gy_ref, gyt_ref, mask_ref)


def one_hot(rows_ref, cols_ref, capacity):
    row0, row1, col0, col1 = rows_ref[0], rows_ref[1], cols_ref[0], cols_ref[1]
    area0, area1 = row0 * col0, row1 * col1
    quarter0, quarter1 = area0 // 4, area1 // 4
    keys = capacity // 4
    index = lax.broadcasted_iota(jnp.int32, (capacity, 128), 0)
    tap = index // keys
    key = index - tap * keys
    first = key < quarter0
    second = jnp.logical_and(key >= quarter0, key < quarter0 + quarter1)
    width = jnp.maximum(jnp.where(second, col1, col0), 2)
    half = width // 2
    local = key - jnp.where(second, quarter0, 0)
    row = ((local.astype(F32) + 0.5) / half.astype(F32)).astype(jnp.int32)
    col = local - row * half
    token = jnp.where(second, area0, 0) + (2 * row + tap // 2) * width + 2 * col + tap % 2
    token = jnp.where(first | second, token, -1)
    lane = lax.broadcasted_iota(jnp.int32, (capacity, 128), 1)
    return lanes(
        *[jnp.where(token == lane + t * 128, 1.0, 0.0).astype(BF16) for t in range(capacity // 128)]
    )


def mask_gradient(geo_ref, cot_ref, gy_ref, gyt_ref, mask_ref):
    width, capacity = cot_ref.shape
    area = geo_ref[0] * geo_ref[2] + geo_ref[1] * geo_ref[3]
    position = lax.broadcasted_iota(jnp.int32, (width, capacity), 1)
    gyt = jnp.where(position < area, cot_ref[...].astype(F32), 0.0)
    gyt_ref[...] = gyt.astype(BF16)
    gy_ref[...] = gyt.T.astype(BF16)
    first, second, row, col, heights, widths = token_geometry(geo_ref, capacity, 128)
    live = first | second
    start = lax.broadcasted_iota(jnp.int32, (capacity, 128), 0) // TILE * TILE
    late = start >= geo_ref[0] * geo_ref[2]
    early = jnp.logical_not(late)
    usual = (late & second) | (early & first)
    apart = second & early
    conditions = (
        live & (col > 0),
        live & (col < widths - 1),
        usual & (row > 0),
        usual & (row < heights - 1),
        apart & (row > 0),
        apart & (row < heights - 1),
        live,
    )
    for k, condition in enumerate(conditions):
        mask_ref[k] = jnp.where(condition, 1.0, 0.0)


def place_pieces(ref, core, me, wu_ref, wd_ref):
    cw = ref.shape[1]
    rn = 2 * cw
    tails = 128 * PARTS_W
    for x in range(PARTS_N // 2):
        n = 2 * x + core
        pieces = [ref[mixed_slot(w * PARTS_N + n, me)].astype(F32) for w in range(PARTS_W)]
        lane_at = pl.ds(pl.multiple_of(256 * n, 256), 256)
        for pair in range(PARTS_W // 2):
            value = rows_of(pieces[2 * pair][:, :256], pieces[2 * pair + 1][:, :256])
            wd_ref[pl.ds(pair * 2 * cw, 2 * cw), lane_at] = value.astype(BF16)
        at = pl.ds(pl.multiple_of(rn * n, 16), rn)
        for w, p in enumerate(pieces):
            wu_ref[at, pl.ds(128 * w, 128)] = rows_of(p[:, 256:384], p[:, 384:512]).astype(BF16)
        ends = [rows_of(p[:, 512 + 2 * REST : 512 + 3 * REST], p[:, 512 + 3 * REST :]) for p in pieces]
        wu_ref[at, pl.ds(tails, REST * PARTS_W)] = lanes(*ends).astype(BF16)


def prepare_two_kernel(tuned, x2_ref, mv_ref, own_ref, n2_ref, r2_ref, h2_ref, h2t_ref, wu_ref, wd_ref):
    me = my_index(tuned)
    place_pieces(own_ref, me & 1, me, wu_ref, wd_ref)
    normed, inverse = normalise(x2_ref[...])
    n2_ref[...] = normed
    r2_ref[...] = inverse
    h2 = normed * mv_ref[8:9, :] + mv_ref[9:10, :]
    h2_ref[...] = h2.astype(BF16)
    width = h2.shape[1]
    h2t_ref[:width, :] = h2.T.astype(BF16)
    h2t_ref[width:, :] = jnp.ones((h2t_ref.shape[0] - width, h2.shape[0]), BF16)


def ffn_kernel(
    tuned,
    geo_ref, h2_ref, h2t_ref, gy_ref, gyt_ref, mask_ref, own_ref, oth_ref, hv_ref, wu_in_ref, wd_in_ref,
    gown_ref, gsend_ref, act_ref, df_ref, hg_ref, wu_ref, wd_ref,
    f_ref, gm_ref, gp_ref, dc_ref, ul_ref, ur_ref, g0_ref, u0_ref, da_ref,
    upg_ref, dng_ref,
):
    me = my_index(tuned)
    capacity, width = h2_ref.shape
    hidden = hv_ref.shape[1]
    cw, rn = width // PARTS_W, width // PARTS_N
    tiles = capacity // TILE
    tails = 128 * PARTS_W

    place_pieces(oth_ref, 1 - (me & 1), me, wu_ref, wd_ref)
    for pair in range(PARTS_W // 2):
        got = [
            rows_of(*[piece_of(own_ref, oth_ref, w * PARTS_N + n, me, 4, 5, mixed_slot) for w in (2 * pair, 2 * pair + 1)])
            for n in range(PARTS_N)
        ]
        ends = lanes(*[g[:, : 2 * REST] for g in got]).astype(BF16)
        wd_ref[pl.ds(pair * 2 * cw, 2 * cw), pl.ds(tails, 2 * REST * PARTS_N)] = ends

    area, w0, w1 = geo_ref[0] * geo_ref[2], geo_ref[2], geo_ref[3]
    split = pl.multiple_of(jnp.minimum(area // TILE, tiles - 1) * TILE, TILE)

    for ref in (f_ref, gm_ref, gp_ref, dc_ref, ul_ref, ur_ref):
        ref[:, :PAD, :] = jnp.zeros((ref.shape[0], PAD, 128), F32)
        ref[:, PAD + capacity :, :] = jnp.zeros((ref.shape[0], PAD, 128), F32)


    def fold(values):
        return jnp.sum(values.reshape(TILE // 8, 8, 128), axis=0)

    halves = CHUNK // 128
    chunks = hidden // CHUNK
    zero = jnp.zeros((8, 128), F32)

    def columns(c):
        return pl.ds(pl.multiple_of(c * CHUNK, CHUNK), CHUNK)

    def vector(c, k, j):
        return hv_ref[k : k + 1, pl.ds(pl.multiple_of(c * CHUNK + j * 128, 128), 128)]

    def put_vector(c, k, j, value):
        hg_ref[k : k + 1, pl.ds(pl.multiple_of(c * CHUNK + j * 128, 128), 128)] = value

    def act_grad(c, at):
        da_ref[at, :] = dot_nn(gy_ref[at, :], wd_ref[:, columns(c)])

    def down_grad(c, at):
        dng_ref[at, columns(c)] = dot_nn(gyt_ref[at, :], act_ref[:, columns(c)])

    def tasks(product, c, rows, size):
        return [functools.partial(product, c, pl.ds(r, min(size, rows - r))) for r in range(0, rows, size)]

    def interleave(steps, products):
        done = 0
        for i, step in enumerate(steps):
            step()
            while done < len(products) and done * len(steps) < (i + 1) * len(products):
                products[done]()
                done += 1

    def chunk_step(c, carry):
        v = [[vector(c, k, j) for k in range(11)] for j in range(halves)]

        def taps_of(j, r, mask_left, mask_right):
            here = f_ref[c * halves + j, pl.ds(PAD + r, TILE), :]
            left = f_ref[c * halves + j, pl.ds(PAD + r - 1, TILE), :] * mask_left
            right = f_ref[c * halves + j, pl.ds(PAD + r + 1, TILE), :] * mask_right
            return left, here, right

        def row_length(r):
            return jnp.where(area > r, w0, w1)

        def column_taps(r):
            at = pl.ds(r, TILE)
            masks = mask_ref[0, at, :], mask_ref[1, at, :]
            for j in range(halves):
                left, here, right = taps_of(j, r, *masks)
                u = v[j]
                gm_ref[j, pl.ds(PAD + r, TILE), :] = u[2] * left + u[3] * here + u[4] * right
                g0_ref[j, at, :] = u[1] + u[5] * left + u[6] * here + u[7] * right
                gp_ref[j, pl.ds(PAD + r, TILE), :] = u[8] * left + u[9] * here + u[10] * right

        def column_taps_split():
            at = pl.ds(split, TILE)
            for j in range(halves):
                g0_ref[j, at, :] += (
                    mask_ref[4, at, :] * gm_ref[j, pl.ds(PAD + split - w1, TILE), :]
                    + mask_ref[5, at, :] * gp_ref[j, pl.ds(PAD + split + w1, TILE), :]
                )

        conv_sums = [zero] * halves

        def activate(r):
            at = pl.ds(r, TILE)
            length = row_length(r)
            above, below = mask_ref[2, at, :], mask_ref[3, at, :]
            for j in range(halves):
                conv = (
                    g0_ref[j, at, :]
                    + above * gm_ref[j, pl.ds(PAD + r - length, TILE), :]
                    + below * gp_ref[j, pl.ds(PAD + r + length, TILE), :]
                )
                half = 0.5 * (1.0 + lax.erf(conv * 2.0 ** (-0.5)))
                act_ref[at, pl.ds(pl.multiple_of(c * CHUNK + j * 128, 128), 128)] = (conv * half).astype(BF16)
                slope = half + conv * ((2.0 * math.pi) ** (-0.5) * jnp.exp2(conv * conv * (-0.5 / math.log(2.0))))
                value = da_ref[at, pl.ds(j * 128, 128)] * slope
                dc_ref[j, pl.ds(PAD + r, TILE), :] = value
                conv_sums[j] = conv_sums[j] + fold(value)

        tap_sums = [[zero] * 9 for _ in range(halves)]

        def tap_back(r):
            at = pl.ds(r, TILE)
            length = row_length(r)
            masks = [mask_ref[k, at, :] for k in range(4)]
            for j in range(halves):
                left, here, right = taps_of(j, r, *masks[:2])
                u = v[j]
                below = masks[3] * dc_ref[j, pl.ds(PAD + r + length, TILE), :]
                level = dc_ref[j, pl.ds(PAD + r, TILE), :]
                above = masks[2] * dc_ref[j, pl.ds(PAD + r - length, TILE), :]
                ul_ref[j, pl.ds(PAD + r, TILE), :] = u[2] * below + u[5] * level + u[8] * above
                u0_ref[j, at, :] = u[3] * below + u[6] * level + u[9] * above
                ur_ref[j, pl.ds(PAD + r, TILE), :] = u[4] * below + u[7] * level + u[10] * above
                grads = [fold(d * f) for d in (below, level, above) for f in (left, here, right)]
                tap_sums[j] = [a + b for a, b in zip(tap_sums[j], grads)]

        def tap_back_split():
            at, padded = pl.ds(split, TILE), pl.ds(PAD + split, TILE)
            masks = [mask_ref[k, at, :] for k in (0, 1, 4, 5)]
            for j in range(halves):
                left, here, right = taps_of(j, split, *masks[:2])
                u = v[j]
                below = masks[3] * dc_ref[j, pl.ds(PAD + split + w1, TILE), :]
                above = masks[2] * dc_ref[j, pl.ds(PAD + split - w1, TILE), :]
                ul_ref[j, padded, :] += u[2] * below + u[8] * above
                u0_ref[j, at, :] += u[3] * below + u[9] * above
                ur_ref[j, padded, :] += u[4] * below + u[10] * above
                grads = [fold(d * f) for d in (below, above) for f in (left, here, right)]
                tap_sums[j] = [a + b for a, b in zip(tap_sums[j], grads[:3] + [zero] * 3 + grads[3:])]

        def spread_back(r):
            at = pl.ds(r, TILE)
            mask_left, mask_right = mask_ref[0, at, :], mask_ref[1, at, :]
            for j in range(halves):
                value = (
                    u0_ref[j, at, :]
                    + mask_left * ur_ref[j, pl.ds(PAD + r - 1, TILE), :]
                    + mask_right * ul_ref[j, pl.ds(PAD + r + 1, TILE), :]
                ).astype(BF16)
                df_ref[at, pl.ds(pl.multiple_of(c * CHUNK + j * 128, 128), 128)] = value

        def steps(step):
            return [functools.partial(step, r) for r in range(0, capacity, TILE)]

        interleave(steps(column_taps) + [column_taps_split], tasks(act_grad, c, capacity, MROWS))
        interleave(
            steps(activate),
            [],
        )
        interleave(steps(tap_back) + [tap_back_split], tasks(down_grad, c, width, MROWS))
        interleave(steps(spread_back), [])
        for j in range(halves):
            put_vector(c, 1, j, column_sum(conv_sums[j]))
            for k in range(9):
                put_vector(c, 2 + k, j, column_sum(tap_sums[j][k]))
        return carry

    for c in range(chunks):
        value = dot_nn(h2_ref[...], wu_ref[:, c * CHUNK : (c + 1) * CHUNK])
        for j in range(halves):
            bias = hv_ref[0:1, pl.ds(c * CHUNK + j * 128, 128)]
            f_ref[c * halves + j, pl.ds(PAD, capacity), :] = value[:, j * 128 : (j + 1) * 128] + bias
    lax.fori_loop(0, chunks, chunk_step, 0)
    upg_ref[...] = dot_nn(h2t_ref[...], df_ref[...])
    hg_ref[0:1, :] = upg_ref[width : width + 1, :]
    hg_ref[11:, :] = jnp.zeros((hg_ref.shape[0] - 11, hidden), F32)

    def value_of(w, n):
        down = pl.ds(w * cw, cw)
        up = [pl.ds(n * rn + e * cw, cw) for e in range(2)]
        return lanes(
            dng_ref[down, pl.ds(256 * n, 256)],
            *[upg_ref[e, pl.ds(128 * w, 128)] for e in up],
            dng_ref[down, pl.ds(tails + 2 * REST * n, 2 * REST)],
            *[upg_ref[e, pl.ds(tails + REST * w, REST)] for e in up],
        )

    store_pieces(gown_ref, gsend_ref, me, value_of, mixed_slot)


def store_pieces(own_ref, send_ref, me, value_of, order):
    even = (me & 1) == 0
    for w in range(PARTS_W):
        for x in range(PARTS_N // 2):
            first, second = value_of(w, 2 * x), value_of(w, 2 * x + 1)
            slot0, slot1 = (order(w * PARTS_N + 2 * x + c, me) for c in range(2))
            own_ref[jnp.where(even, slot0, slot1)] = jnp.where(even, first, second).astype(BF16)
            send_ref[jnp.where(even, slot1, slot0)] = jnp.where(even, second, first).astype(BF16)


def score_back_kernel(
    df_ref, wu_ref, n2_ref, r2_ref, gy_ref, mv_ref, vb_ref, p_ref, o_ref, wp_ref,
    gp_ref, dob_ref, ds_ref, bp_ref, dx2_ref, mg_ref,
    dp_ref, dh2_ref,
):
    capacity, width = n2_ref.shape
    keys = capacity // 4

    dh2_ref[...] = dot_nt(df_ref[...], wu_ref[...])

    def norm_back(i, carry):
        at = pl.ds(pl.multiple_of(i * 64, 64), 64)
        gy = gy_ref[at, :].astype(F32)
        grad, normed = dh2_ref[at, :], n2_ref[at, :]
        dx2_ref[at, :] = gy + normalise_back(grad, normed, r2_ref[at, :], mv_ref[8:9, :])
        return tuple(a + column_sum(b) for a, b in zip(carry, (grad * normed, grad, gy)))

    zero = jnp.zeros((1, width), F32)
    sums = lax.fori_loop(0, capacity // 64, norm_back, (zero, zero, zero), unroll=True)
    mg_ref[...] = jnp.zeros_like(mg_ref)
    for k in range(3):
        mg_ref[8 + k : 9 + k, :] = sums[k]

    datt = dx2_ref[...].astype(BF16)
    bp_ref[...] = column_sum(datt.astype(F32))
    gp_ref[...] = dot_tn(datt, o_ref[...])
    dob = dot_nn(datt, wp_ref[...]).astype(BF16)
    dob_ref[...] = dob
    dp_ref[...] = dot_nt(dob, vb_ref[...])

    def soften_back(i, carry):
        at = pl.ds(pl.multiple_of(i * 64, 64), 64)
        for h in range(HEADS):
            lane_at = pl.ds(h * keys, keys)
            p = p_ref[at, lane_at]
            dp = dp_ref[at, lane_at]
            row = jnp.sum(p * dp, axis=-1, keepdims=True)
            ds_ref[at, lane_at] = (p * (dp - row)).astype(BF16)
        return carry

    lax.fori_loop(0, capacity // 64, soften_back, 0, unroll=True)


def attend_back_kernel(
    tuned,
    dob_ref, ds_ref, gp_ref, h1_ref, patch_ref, nk_ref, rk_ref, kn_ref, q_ref, kb_ref, p_ref,
    wr_ref, wkv_ref, mv_ref,
    gown_ref, gsend_ref, dq_ref, dpatch_ref, vk_ref,
    gr_ref, gq_ref, gkv_ref,
):
    me = my_index(tuned)
    capacity, width = h1_ref.shape
    cw, rn = width // PARTS_W, width // PARTS_N
    keys = capacity // 4
    dim = width // HEADS
    scale = dim ** (-0.5)

    ds = ds_ref[...]
    dq = (dot_nn(ds, kb_ref[...]) * scale).astype(BF16)
    dq_ref[...] = dq
    dk_all = dot_tn(ds, q_ref[...])
    dv_all = dot_tn(p_ref[...].astype(BF16), dob_ref[...])
    lane = lax.broadcasted_iota(jnp.int32, (keys, width), 1)
    dk = jnp.zeros((keys, width), F32)
    dv = jnp.zeros((keys, width), F32)
    for h in range(HEADS):
        inside = (lane >= h * dim) & (lane < (h + 1) * dim)
        dk = jnp.where(inside, dk_all[h * keys : (h + 1) * keys], dk)
        dv = jnp.where(inside, dv_all[h * keys : (h + 1) * keys], dv)
    dk = (dk * scale).astype(BF16)
    dv = dv.astype(BF16)
    gq_ref[...] = dot_tn(dq, h1_ref[...])
    kn = kn_ref[...]
    gkv_ref[pl.ds(0, width), :] = dot_tn(dk, kn)
    gkv_ref[pl.ds(width, width), :] = dot_tn(dv, kn)
    dkn = dot_nn(dk, wkv_ref[pl.ds(0, width), :]) + dot_nn(dv, wkv_ref[pl.ds(width, width), :])
    nk = nk_ref[...]
    dsr = normalise_back(dkn, nk, rk_ref[...], mv_ref[5:6, :]).astype(BF16)
    vk_ref[...] = rows_of(
        column_sum(dq.astype(F32)),
        column_sum(dv.astype(F32)),
        column_sum(dsr.astype(F32)),
        column_sum(dkn * nk),
        column_sum(dkn),
        jnp.zeros((3, width), F32),
    )
    for n in range(4):
        at = pl.ds(n * keys, keys)
        gr_ref[n] = dot_tn(dsr, patch_ref[at, :])
        dpatch_ref[at, :] = dot_nn(dsr, wr_ref[n])

    def value_of(w, n):
        at, lane_at = pl.ds(w * cw, cw), pl.ds(n * rn, rn)
        return lanes(
            gr_ref[n, at, :],
            gq_ref[at, lane_at],
            gkv_ref[pl.ds(2 * w * cw, cw), lane_at],
            gkv_ref[pl.ds(2 * w * cw + cw, cw), lane_at],
            gp_ref[at, lane_at],
        )

    store_pieces(gown_ref, gsend_ref, me, value_of, round_slot)


def mixed_kernel(x2_ref, act_ref, wd_ref, mv_ref, mask_ref, mixed_ref):
    width = x2_ref.shape[1]
    occupied = mask_ref[6]
    occupied = lanes(*([occupied] * (width // 128)), occupied[:, : width % 128])
    mixed = x2_ref[...] + dot_nt(act_ref[...], wd_ref[...]) + mv_ref[10:11, :]
    mixed_ref[...] = (mixed * occupied).T.astype(BF16)


def fold_rows(value, unit):
    rest = value[8:]
    beside = lanes(rest[:, : 3 * unit], jnp.zeros((8, 256 - 3 * unit), F32))
    below = lanes(rest[:, 3 * unit :], jnp.zeros((8, 256 - 2 * unit), F32))
    return lanes(value[:8], (beside + pltpu.roll(below, 3, 0))[:, : 3 * unit])


def unfold_rows(value, unit):
    beside = lanes(value[:, 5 * unit :], jnp.zeros((8, 256 - 3 * unit), F32))
    below = pltpu.roll(beside, 5, 0)
    return rows_of(value[:, : 5 * unit], lanes(beside[:, : 3 * unit], below[:, : 2 * unit]))


def token_back_kernel(
    tuned,
    dx2_ref, dq_ref, dpatch_ref, n1_ref, r1_ref, chosen_ref, wq_ref, mv_ref, mg_ref, hg_ref, vk_ref, bp_ref,
    tg_ref, vown_ref, vsend_ref,
):
    me = my_index(tuned)
    capacity, width = dx2_ref.shape
    rn = width // PARTS_N
    chosen = chosen_ref[...]
    high = dpatch_ref[...].astype(BF16)
    low = (dpatch_ref[...] - high.astype(F32)).astype(BF16)
    dh1 = dot_nn(dq_ref[...], wq_ref[...]) + dot_tn(chosen, high) + dot_tn(chosen, low)
    n1 = n1_ref[...]
    vk = vk_ref[...]
    token_grad = dx2_ref[...] + normalise_back(dh1, n1, r1_ref[...], mv_ref[0:1, :])
    tg_ref[...] = token_grad.T.astype(BF16)
    sums = rows_of(column_sum(dh1 * n1), column_sum(dh1), vk[0:5], bp_ref[...], mg_ref[8:16, :])
    hg = hg_ref[...]
    value = []
    for n in range(PARTS_N):
        parts = []
        for w in (2 * n, 2 * n + 1):
            parts += [hg[:, 128 * w : 128 * (w + 1)], hg[:, 1024 + REST * w : 1024 + REST * (w + 1)]]
        value.append(fold_rows(lanes(sums[:, n * rn : (n + 1) * rn], *parts), rn))
    even = (me & 1) == 0
    for x in range(2):
        slot = x ^ ((me >> 1) & 1)
        vown_ref[slot] = jnp.where(even, value[2 * x], value[2 * x + 1]).astype(BF16)
        vsend_ref[slot] = jnp.where(even, value[2 * x + 1], value[2 * x]).astype(BF16)


def total_of(refs):
    value = refs[0][...].astype(F32)
    for ref in refs[1:]:
        value = value + ref[...].astype(F32)
    return value


def halve_kernel(keep_ref, got_ref, low_ref, high_ref):
    half = low_ref.shape[0]
    low_ref[...] = (keep_ref[:half].astype(F32) + got_ref[:half].astype(F32)).astype(BF16)
    high_ref[...] = (keep_ref[half:].astype(F32) + got_ref[half:].astype(F32)).astype(BF16)


def halve_core_kernel(keep_ref, got_ref, vkeep_ref, vgot_ref, low_ref, vlow_ref, send_ref):
    half = low_ref.shape[0]
    low_ref[...] = (keep_ref[:half].astype(F32) + got_ref[:half].astype(F32)).astype(BF16)
    parts = [keep_ref[half + k].astype(F32) + got_ref[half + k].astype(F32) for k in range(half)]
    vector = total_of((vkeep_ref, vgot_ref))
    vlow_ref[...] = vector.astype(BF16)
    send_ref[...] = rows_of(*parts, vector[0], vector[1]).astype(BF16)


def halve_round_kernel(tuned, keep_ref, vkeep_ref, got_ref, low_ref, vlow_ref, send_ref):
    half, cw = low_ref.shape[:2]
    rows = vkeep_ref.shape[1]
    got = got_ref[...].astype(F32)
    parts = [keep_ref[k].astype(F32) + got[k * cw : (k + 1) * cw] for k in range(2 * half)]
    for k in range(half):
        low_ref[k] = parts[k].astype(BF16)
    got0, got1 = (got[2 * half * cw + k * rows : 2 * half * cw + (k + 1) * rows] for k in range(2))
    keep0, keep1 = vkeep_ref[0].astype(F32), vkeep_ref[1].astype(F32)
    even = (my_index(tuned) & 1) == 0
    low = keep0 + jnp.where(even, got0, got1)
    vlow_ref[0] = low.astype(BF16)
    send_ref[...] = rows_of(*parts[half:], jnp.where(even, keep1 + got1, low)).astype(BF16)


def quarter_vector_kernel(keep_ref, vkeep_ref, got_ref, *out_refs):
    cw = keep_ref.shape[1]
    got = got_ref[...].astype(F32)
    vector = vkeep_ref[0].astype(F32) + got[4 * cw :]
    for k, ref in enumerate(out_refs):
        ref[...] = rows_of(keep_ref[k].astype(F32) + got[k * cw : (k + 1) * cw], vector).astype(BF16)


def finish_kernel(
    a_ref, b_ref, c_ref, d_ref, ffn_ref, ffn_got_ref,
    q_ref, kv_ref, red_ref, proj_ref, up_ref, down_ref, vm_ref, vh_ref,
):
    total = total_of((a_ref, b_ref, c_ref, d_ref))
    cw, width = red_ref.shape
    rn = q_ref.shape[1]
    red_ref[...] = total[:cw, :width]
    unit = [total[:cw, width + k * rn : width + (k + 1) * rn] for k in range(4)]
    q_ref[...] = unit[0]
    kv_ref[...] = rows_of(unit[1], unit[2]).T
    proj_ref[...] = unit[3]
    vector = unfold_rows(total[cw:], rn)
    vm_ref[...] = vector[: vm_ref.shape[0], :rn]
    vh_ref[...] = vector[: vh_ref.shape[0], rn:]
    total = total_of((ffn_ref, ffn_got_ref))[0]
    columns = [
        lanes(total[:, 128 * k : 128 * (k + 1)], total[:, 512 + REST * k : 512 + REST * (k + 1)]) for k in range(4)
    ]
    down_ref[...] = lanes(*columns[:2])
    up_ref[...] = rows_of(*columns[2:])


def call(kernel, inputs, outputs, scratch=(), scalars=0, limit=24, flops=0, moved=0, aliases={}):
    vmem = pl.BlockSpec(memory_space=pltpu.VMEM)
    smem = pl.BlockSpec(memory_space=pltpu.SMEM)
    return pl.pallas_call(
        kernel,
        out_shape=[jax.ShapeDtypeStruct(shape, kind) for shape, kind in outputs],
        in_specs=[smem] * scalars + [vmem] * (len(inputs) - scalars),
        out_specs=[vmem] * len(outputs),
        scratch_shapes=[pltpu.VMEM(shape, kind) for shape, kind in scratch],
        input_output_aliases=aliases,
        compiler_params=pltpu.CompilerParams(vmem_limit_bytes=limit * 2**20),
        cost_estimate=pl.CostEstimate(flops=flops, bytes_accessed=moved, transcendentals=0),
    )(*inputs)


def after(value, *others):
    return lax.optimization_barrier((value, *others))[0]


def on_device(
    mesh_shape,
    tokens, cotangent, img_rows, img_cols,
    q_weight, kv_weight, reduce_weight, proj_weight, up_weight, down_weight, vec_model, vec_hidden,
):
    wide, narrow = mesh_shape
    tuned = (wide, narrow) == (PARTS_W, PARTS_N)
    capacity, width = tokens.shape
    hidden = vec_hidden.shape[1] * narrow
    cw, rn = width // PARTS_W, width // PARTS_N
    keys = capacity // 4
    piece = (cw, 2 * width)
    vpiece, gpiece = (16, 2 * width), (8, 2 * width)

    def join(*parts):
        return jnp.concatenate(parts, axis=0)

    def swap(value, mask, other=None):
        masks = (mask, mask if other is None else other)
        pairs = [(i, i ^ masks[i & 1]) for i in range(wide * narrow)]
        return lax.ppermute(value, ("wide", "narrow"), pairs)

    tokens_f32 = ((capacity, width), F32)
    tokens_low = ((capacity, width), BF16)
    x, n1, r1, chosen, live, geo = prepare(img_rows, img_cols, tokens.T)
    if tuned:
        pack_a, pack_b, pack_v = pack(
            (
                q_weight.T, kv_weight, reduce_weight.T, proj_weight.T, up_weight, down_weight.T,
                vec_model, vec_hidden,
            ),
            piece, vpiece,
        )
        line_a = [swap(pack_a, m) for m in (8, 16, 24)]
        got_b, got_v = swap(pack_b, 2, 4), swap(pack_v, 1)
        *line_a, got_b, got_v = lax.optimization_barrier((*line_a, got_b, got_v, x, n1, chosen))[:5]
        buf_a, buf_b, vecs = join(pack_a, *line_a), join(pack_b, got_b), join(pack_v, got_v)
        buf_a, buf_b = join(buf_a, swap(buf_a, 2, 4)), join(buf_b, swap(buf_b, 16))
        got = lax.optimization_barrier((swap(buf_a, 4, 2), swap(buf_b, 8), swap(vecs, 2)))
        own_a, half_b, vecs = (join(v, g) for v, g in zip((buf_a, buf_b, vecs), got))
        oth_a = swap(own_a, 1)
        rest_b = swap(half_b, 4, 2)
        oth_half_b = swap(after(half_b, oth_a), 1)
    else:
        own_a, oth_a, own_b, oth_b, vecs = gather_plain(
            q_weight, kv_weight, reduce_weight, proj_weight, up_weight, down_weight, vec_model, vec_hidden
        )

    square = (width, width)
    (
        x2, h1, patches, nk, rk, kn, q, kb, vb, p, o, wr, wq, wkv, wp, mv, hv, gy, gyt, masks,
    ) = call(
        functools.partial(attend_kernel, tuned),
        (geo, cotangent.T, x, n1, chosen, live, own_a, oth_a, vecs),
        (
            tokens_f32, tokens_low,
            ((capacity, width), BF16), ((keys, width), F32), ((keys, 1), F32), ((keys, width), BF16),
            ((capacity, width), BF16), ((HEADS * keys, width), BF16), ((HEADS * keys, width), BF16),
            ((capacity, HEADS * keys), F32), ((capacity, width), BF16),
            ((4,) + square, BF16), (square, BF16), ((2 * width, width), BF16), (square, BF16),
            ((16, width), F32), ((16, hidden), F32),
            tokens_low, ((width, capacity), BF16), ((7, capacity, 128), F32),
        ),
        scratch=(((capacity, HEADS * keys), F32),),
        scalars=1,
        flops=8 * 10**9,
    )

    if tuned:
        rest_b = after(rest_b, x2)
        own_b = join(half_b, rest_b)
        oth_b = join(oth_half_b, swap(rest_b, 1))
    padded = ((CHUNK // 128, capacity + 2 * PAD, 128), F32)
    halved = ((CHUNK // 128, capacity, 128), F32)
    chunked = ((capacity, CHUNK), F32)
    n2, r2, h2, h2t, wu, wd = call(
        functools.partial(prepare_two_kernel, tuned),
        (x2, mv, own_b),
        (
            tokens_f32, ((capacity, 1), F32), tokens_low, ((width + 16, capacity), BF16),
            ((width, hidden), BF16), ((width, hidden), BF16),
        ),
        flops=10**9,
    )
    gown_b, gsend_b, act, df, hg, wu, wd = call(
        functools.partial(ffn_kernel, tuned),
        (geo, h2, h2t, gy, gyt, masks, own_b, oth_b, hv, wu, wd),
        (
            ((SLOTS,) + piece, BF16), ((SLOTS,) + piece, BF16),
            ((capacity, hidden), BF16), ((capacity, hidden), BF16), ((16, hidden), F32),
            ((width, hidden), BF16), ((width, hidden), BF16),
        ),
        aliases={9: 5, 10: 6},
        scratch=(
            ((hidden // 128, capacity + 2 * PAD, 128), F32), padded, padded, padded, padded, padded,
            halved, halved, chunked,
            ((width + 16, hidden), F32), ((width, hidden), F32),
        ),
        scalars=1,
        flops=33 * 10**9,
    )

    if tuned:
        got_b = swap(gsend_b, 1)
    gp, dob, ds, bp, dx2, mg = call(
        score_back_kernel,
        (df, wu, n2, r2, gy, mv, vb, p, o, wp),
        (
            (square, F32), ((capacity, width), BF16), ((capacity, HEADS * keys), BF16), ((1, width), F32),
            tokens_f32, ((16, width), F32),
        ),
        scratch=(((capacity, HEADS * keys), F32), tokens_f32),
        flops=25 * 10**8,
    )
    def halve(keep, got, flops=0):
        shape = ((keep.shape[0] // 2,) + piece, BF16)
        return call(halve_kernel, (keep, got), (shape, shape), flops=flops)

    if tuned:
        got_b = after(got_b, ds)
        low_b, high_b = halve(gown_b, got_b)
        ds = after(ds, high_b)
        got_b = swap(high_b, 4, 2)
    gown_a, gsend_a, dq, dpatch, vk = call(
        functools.partial(attend_back_kernel, tuned),
        (dob, ds, gp, h1, patches, nk, rk, kn, q, kb, p, wr, wkv, mv),
        (
            ((SLOTS,) + piece, BF16), ((SLOTS,) + piece, BF16), ((capacity, width), BF16), ((capacity, width), F32),
            ((8, width), F32),
        ),
        scratch=(((4,) + square, F32), (square, F32), ((2 * width, width), F32)),
        flops=0,
    )
    if tuned:
        got_a = swap(gsend_a, 1)
        low_b, high_b = halve(low_b, got_b, flops=7 * 10**9)
        gown_a = after(gown_a, high_b)
    (mixed,) = call(mixed_kernel, (x2, act, wd, mv, masks), (((width, capacity), BF16),), flops=10**9)
    token_grad, vown, vsend = call(
        functools.partial(token_back_kernel, tuned),
        (dx2, dq, dpatch, n1, r1, chosen, wq, mv, mg, hg, vk, bp),
        (((width, capacity), BF16), ((2,) + gpiece, BF16), ((2,) + gpiece, BF16)),
    )

    if not tuned:
        grads = scatter_plain(mesh_shape, width, gown_a, gsend_a, gown_b, gsend_b, vown, vsend)
        return (mixed.T, token_grad.T) + grads

    vrows = gpiece[0]
    low_a, vlow, high_a = call(
        halve_core_kernel,
        (gown_a, got_a, vown, swap(vsend, 1)),
        (((8,) + piece, BF16), ((2,) + gpiece, BF16), ((8 * cw + 2 * vrows, 2 * width), BF16)),
    )
    got_a, got_b, mixed = lax.optimization_barrier((swap(high_a, 4, 2), swap(high_b, 8), mixed))
    low_a, vlow, high_a = call(
        functools.partial(halve_round_kernel, tuned),
        (low_a, vlow, got_a),
        (((4,) + piece, BF16), ((1,) + gpiece, BF16), ((4 * cw + vrows, 2 * width), BF16)),
    )
    low_b, high_b = halve(low_b, got_b)
    got_a, got_b = swap(high_a, 2, 4), swap(high_b, 16)
    near_a = list(call(quarter_vector_kernel, (low_a, vlow, got_a), (((cw + vrows, 2 * width), BF16),) * 4))
    line_a = [swap(near_a[k], 8 * k) for k in (1, 2, 3)]
    low_b, high_b = halve(low_b, got_b)
    q_grad, kv_grad, reduce_grad, proj_grad, up_grad, down_grad, vm_grad, vh_grad = call(
        finish_kernel,
        (near_a[0], *line_a, low_b, swap(high_b, 2, 4)),
        (
            ((cw, rn), F32), ((rn, 2 * cw), F32), ((cw, width), F32), ((cw, rn), F32),
            ((rn, 4 * cw), F32), ((cw, width), F32), ((11, rn), F32), ((11, width), F32),
        ),
    )
    return (
        mixed.T, token_grad.T, q_grad.T, kv_grad, reduce_grad.T, proj_grad.T, up_grad, down_grad.T, vm_grad, vh_grad,
    )


def gather_plain(q, kv, reduce, proj, up, down, vec_model, vec_hidden):
    def whole(value):
        rows = lax.all_gather(value, "narrow", axis=0, tiled=True)
        return lax.all_gather(rows, "wide", axis=1, tiled=True).T

    q, kv, reduce, proj, up, down = (whole(v) for v in (q, kv, reduce, proj, up, down))
    width = q.shape[0]
    cw, rn = width // PARTS_W, width // PARTS_N

    def pieces(turned, blocks):
        split = turned.reshape(PARTS_W, blocks, cw, PARTS_N, -1)
        return split.transpose(0, 3, 2, 1, 4).reshape(PARTS_W, PARTS_N, cw, -1)

    def slots(value, mixed=False):
        value = value.reshape(2, 2, 2, 2, 2, cw, -1)
        orders = ((2, 1, 0, 3), (3, 1, 0, 2)) if mixed else ((2, 3, 0, 1), (3, 2, 0, 1))
        return tuple(
            value[:, :, :, :, core].transpose(*order, 4, 5).reshape(SLOTS, cw, -1) for core, order in enumerate(orders)
        )

    a = jnp.concatenate([pieces(reduce, 1), pieces(q, 1), pieces(kv, 2), pieces(proj, 1)], axis=-1)
    columns = pieces(down, 1).reshape(PARTS_W, PARTS_N, cw, 2, RUN)
    columns = [columns[..., e, :] for e in range(2)]
    halves = up.T.reshape(PARTS_N, 2, cw, PARTS_W, RUN).transpose(1, 3, 0, 2, 4)
    columns += [halves[0], halves[1]]
    b = jnp.concatenate([c[..., :128] for c in columns] + [c[..., 128:] for c in columns], axis=-1)
    vm = lax.all_gather(vec_model, "narrow", axis=1, tiled=True)
    vh = lax.all_gather(vec_hidden, "narrow", axis=1, tiled=True)
    both = jnp.concatenate([vm.reshape(11, PARTS_N, rn), vh.reshape(11, PARTS_N, width)], axis=-1)
    vecs = jnp.pad(both.transpose(1, 0, 2), ((0, 0), (0, 5), (0, 3 * rn)))
    return (*slots(a), *slots(b, True), vecs)


def scatter_plain(mesh_shape, width, gown_a, gsend_a, gown_b, gsend_b, vown, vsend):
    cw, rn = width // PARTS_W, width // PARTS_N

    def devices(own, send, mixed=False):
        orders = ((2, 1, 0, 3), (3, 1, 0, 2)) if mixed else ((2, 3, 0, 1), (3, 2, 0, 1))
        parts = []
        for value, order in zip((own, send), orders):
            back = sorted(range(4), key=lambda k: order[k])
            parts.append(value.reshape(2, 2, 2, 2, cw, -1).transpose(*back, 4, 5))
        return jnp.stack(parts, axis=4).reshape(PARTS_W, PARTS_N, cw, -1)

    def natural(value, blocks):
        split = value.reshape(PARTS_W, PARTS_N, cw, blocks, -1).transpose(0, 3, 2, 1, 4)
        return split.reshape(PARTS_W * blocks * cw, -1).T

    def share(value):
        columns = lax.psum_scatter(value.astype(BF16), "wide", scatter_dimension=1, tiled=True)
        return lax.psum_scatter(columns, "narrow", scatter_dimension=0, tiled=True).astype(F32)

    a = devices(gown_a, gsend_a)
    b = devices(gown_b, gsend_b, True)
    reduce = natural(a[..., :width], 1)
    q = natural(a[..., width : width + rn], 1)
    kv = natural(a[..., width + rn : width + 3 * rn], 2)
    proj = natural(a[..., width + 3 * rn :], 1)
    columns = [
        jnp.concatenate([b[..., 128 * k : 128 * (k + 1)], b[..., 512 + REST * k : 512 + REST * (k + 1)]], axis=-1)
        for k in range(4)
    ]
    down = natural(jnp.concatenate(columns[:2], axis=-1), 1)
    up = jnp.stack(columns[2:]).transpose(2, 0, 3, 1, 4).reshape(width, -1)
    vectors = jnp.stack([vown, vsend], axis=1).reshape(PARTS_N, 8, -1)
    beside = vectors[..., 5 * rn :]
    beside = jnp.concatenate([beside[:, :3], beside[:, 3:6, : 2 * rn]], axis=-1)
    vectors = jnp.concatenate([vectors[..., : 5 * rn], beside], axis=1).transpose(1, 0, 2)
    vm = vectors[..., :rn].reshape(11, width)
    vh = vectors[..., rn : rn + width].reshape(11, PARTS_N * width)

    def share_vector(value):
        total = lax.psum(value.astype(BF16), "wide")
        return lax.psum_scatter(total, "narrow", scatter_dimension=1, tiled=True).astype(F32)

    return tuple(share(v) for v in (q, kv, reduce, proj, up, down)) + (share_vector(vm), share_vector(vh))


def solution(mesh):
    both, rows, weight, vector = P(("wide", "narrow"), None), P(("wide", "narrow")), P("narrow", "wide"), P(None, "narrow")
    return jax.shard_map(
        functools.partial(on_device, (mesh.shape["wide"], mesh.shape["narrow"])),
        mesh=mesh,
        in_specs=(both, both, rows, rows) + (weight,) * 6 + (vector,) * 2,
        out_specs=(both, both) + (weight,) * 6 + (vector,) * 2,
        check_vma=False,
    )
```

```python
import functools
import math

import jax
import jax.numpy as jnp
from jax import lax
from jax.experimental import pallas as pl
from jax.experimental.pallas import tpu as pltpu
from jax.sharding import PartitionSpec as P

HEADS = 5
EPSILON = 1e-06
MASKED = -1000000000.0
F32 = jnp.float32
BF16 = jnp.bfloat16

PARTS_W = 8
PARTS_N = 4
SLOTS = 16
TILE = 32
CHUNK = 256
PAD = 40
MROWS = 512
RUN = 160
REST = RUN - 128


def dot_nn(left, right):
    return jnp.dot(left, right, preferred_element_type=F32)


def dot_nt(left, right):
    return lax.dot_general(left, right, (((1,), (1,)), ((), ())), preferred_element_type=F32)


def dot_tn(left, right):
    return lax.dot_general(left, right, (((0,), (0,)), ((), ())), preferred_element_type=F32)


def lanes(*parts):
    return jnp.concatenate(parts, axis=1)


def rows_of(*parts):
    return jnp.concatenate(parts, axis=0)


def my_index(tuned):
    if not tuned:
        return jnp.int32(0)
    return lax.axis_index("wide") * PARTS_N + lax.axis_index("narrow")


def round_slot(device, me):
    delta = device ^ me
    first, second = (delta >> 1) & 1, (delta >> 2) & 1
    if device & 1:
        first, second = second, first
    return second * 8 + first * 4 + (delta >> 3)


def mixed_slot(device, me):
    delta = device ^ me
    x, y = (delta >> 1) & 1, (delta >> 2) & 1
    odd = (device & 1) == 1
    first, second = jnp.where(odd, y, x), jnp.where(odd, x, y)
    return second * 8 + ((delta >> 3) & 1) * 4 + ((delta >> 4) & 1) * 2 + first


def normalise(values):
    centre = values - jnp.mean(values, axis=-1, keepdims=True)
    inverse = lax.rsqrt(jnp.mean(centre * centre, axis=-1, keepdims=True) + EPSILON)
    return centre * inverse, inverse


def normalise_back(grad, normed, inverse, gain):
    scaled = grad * gain
    first = jnp.mean(scaled, axis=-1, keepdims=True)
    second = jnp.mean(scaled * normed, axis=-1, keepdims=True)
    return (scaled - first - normed * second) * inverse


def column_sum(values):
    return jnp.sum(values, axis=0, keepdims=True)


def piece_of(own_ref, other_ref, device, me, first=0, last=5, order=round_slot):
    slot = order(device, me)
    mine = ((device ^ me) & 1) == 0
    at = pl.ds(128 * first, 128 * (last - first))
    return jnp.where(mine, own_ref[slot, :, at].astype(F32), other_ref[slot, :, at].astype(F32))


def token_geometry(geo_ref, capacity, width):
    row0, row1, col0, col1 = (geo_ref[k] for k in range(4))
    area0, area1 = row0 * col0, row1 * col1
    position = lax.broadcasted_iota(jnp.int32, (capacity, width), 0)
    first = position < area0
    second = jnp.logical_and(position >= area0, position < area0 + area1)
    widths = jnp.maximum(jnp.where(second, col1, col0), 2)
    heights = jnp.where(second, row1, row0)
    local = position - jnp.where(second, area0, 0)
    row = ((local.astype(F32) + 0.5) / widths.astype(F32)).astype(jnp.int32)
    col = local - row * widths
    return first, second, row, col, heights, widths


def pack_kernel(*refs):
    sources, (a_ref, b_ref, v_ref), held, semaphores = refs[:8], refs[8:11], refs[11:19], refs[19]
    copies = [pltpu.make_async_copy(source, ref, semaphores.at[i]) for i, (source, ref) in enumerate(zip(sources, held))]
    for copy in copies:
        copy.start()
    for copy in copies:
        copy.wait()
    q_ref, kv_ref, red_ref, proj_ref, up_ref, down_ref, vm_ref, vh_ref = held
    cw = q_ref.shape[0]

    def wider(ref):
        return ref[...].astype(F32)

    kv = wider(kv_ref).T
    a_ref[0] = lanes(wider(red_ref), wider(q_ref), kv[:cw], kv[cw:], wider(proj_ref)).astype(BF16)
    up, down = wider(up_ref), wider(down_ref)
    columns = (down[:, :RUN], down[:, RUN:], up[:cw], up[cw:])
    b_ref[0] = lanes(*[c[:, :128] for c in columns], *[c[:, 128:] for c in columns]).astype(BF16)
    v_ref[0] = jnp.zeros_like(v_ref[0])
    both = lanes(wider(vm_ref), wider(vh_ref))
    v_ref[0, : both.shape[0], : both.shape[1]] = both.astype(BF16)


def pack(arguments, piece, vpiece):
    vmem = pl.BlockSpec(memory_space=pltpu.VMEM)
    return pl.pallas_call(
        pack_kernel,
        out_shape=[jax.ShapeDtypeStruct((1,) + shape, BF16) for shape in (piece, piece, vpiece)],
        in_specs=[pl.BlockSpec(memory_space=pl.ANY)] * len(arguments),
        out_specs=[vmem] * 3,
        scratch_shapes=[pltpu.VMEM(v.shape, v.dtype) for v in arguments] + [pltpu.SemaphoreType.DMA((len(arguments),))],
        compiler_params=pltpu.CompilerParams(vmem_limit_bytes=60 * 2**20),
    )(*arguments)


def prepare_kernel(
    rows_hbm, cols_hbm, tok_hbm, x_ref, n1_ref, r1_ref, chosen_ref, live_ref, geo_ref,
    rows_ref, cols_ref, tok_ref, semaphores,
):
    copies = [
        pltpu.make_async_copy(source, target, semaphores.at[i])
        for i, (source, target) in enumerate(((rows_hbm, rows_ref), (cols_hbm, cols_ref), (tok_hbm, tok_ref)))
    ]
    for copy in copies:
        copy.start()
    for copy in copies:
        copy.wait()
    capacity = tok_ref.shape[1]
    for j in range(2):
        geo_ref[j] = rows_ref[j]
        geo_ref[2 + j] = cols_ref[j]
    tokens = tok_ref[...].astype(F32).T
    x_ref[...] = tokens
    normed, inverse = normalise(tokens)
    n1_ref[...] = normed
    r1_ref[...] = inverse
    chosen_ref[...] = one_hot(rows_ref, cols_ref, capacity)
    area0, area1 = rows_ref[0] * cols_ref[0], rows_ref[1] * cols_ref[1]
    quarter0, quarter1 = area0 // 4, area1 // 4
    token = lax.broadcasted_iota(jnp.int32, live_ref.shape, 0)
    key = lax.broadcasted_iota(jnp.int32, live_ref.shape, 1)
    live = ((token < area0) & (key < quarter0)) | (
        (token >= area0) & (token < area0 + area1) & (key >= quarter0) & (key < quarter0 + quarter1)
    )
    live_ref[...] = jnp.where(live, 1.0, 0.0)


def prepare(img_rows, img_cols, tokens):
    width, capacity = tokens.shape
    keys = capacity // 4
    vmem, smem = (pl.BlockSpec(memory_space=space) for space in (pltpu.VMEM, pltpu.SMEM))
    outputs = (
        ((capacity, width), F32), ((capacity, width), F32), ((capacity, 1), F32), ((capacity, capacity), BF16),
        ((capacity, keys), F32), ((4,), jnp.int32),
    )
    return pl.pallas_call(
        prepare_kernel,
        out_shape=[jax.ShapeDtypeStruct(shape, kind) for shape, kind in outputs],
        in_specs=[pl.BlockSpec(memory_space=pl.ANY)] * 3,
        out_specs=[vmem] * 5 + [smem],
        scratch_shapes=[
            pltpu.SMEM((2,), jnp.int32), pltpu.SMEM((2,), jnp.int32), pltpu.VMEM((width, capacity), BF16),
            pltpu.SemaphoreType.DMA((3,)),
        ],
        compiler_params=pltpu.CompilerParams(vmem_limit_bytes=60 * 2**20),
        cost_estimate=pl.CostEstimate(flops=2 * 10**9, bytes_accessed=0, transcendentals=0),
    )(img_rows, img_cols, tokens)


def attend_kernel(
    tuned,
    geo_ref, cot_ref, x_ref, n1_ref, chosen_ref, live_ref, own_ref, oth_ref, vec_ref,
    x2_ref, h1_ref, patch_ref, nk_ref, rk_ref, kn_ref, q_ref, kb_ref, vb_ref,
    p_ref, o_ref, wr_ref, wq_ref, wkv_ref, wp_ref, mv_ref, hv_ref, gy_ref, gyt_ref, mask_ref,
    score_ref,
):
    me = my_index(tuned)
    capacity, width = x_ref.shape
    cw, rn = width // PARTS_W, width // PARTS_N
    keys = capacity // 4
    dim = width // HEADS

    pieces = [vec_ref[n ^ (me & 3)].astype(F32) for n in range(PARTS_N)]
    mv = lanes(*[p[:, :rn] for p in pieces])
    mv_ref[...] = mv
    runs = [p[:, rn + e * RUN : rn + (e + 1) * RUN] for p in pieces for e in range(2)]
    hv_ref[...] = lanes(*[r[:, :128] for r in runs], *[r[:, 128:] for r in runs])

    for pair in range(PARTS_W // 2):
        got = [
            [piece_of(own_ref, oth_ref, w * PARTS_N + n, me) for n in range(PARTS_N)]
            for w in (2 * pair, 2 * pair + 1)
        ]
        at = pl.ds(pair * 2 * cw, 2 * cw)
        for n in range(PARTS_N):
            wr_ref[n, at, :] = rows_of(got[0][n][:, :width], got[1][n][:, :width]).astype(BF16)

        def unit(w, k):
            return lanes(*[got[w][n][:, width + k * rn : width + (k + 1) * rn] for n in range(PARTS_N)])

        wq_ref[at, :] = rows_of(unit(0, 0), unit(1, 0)).astype(BF16)
        wkv_ref[pl.ds(pair * 4 * cw, 4 * cw), :] = rows_of(
            unit(0, 1), unit(0, 2), unit(1, 1), unit(1, 2)
        ).astype(BF16)
        wp_ref[at, :] = rows_of(unit(0, 3), unit(1, 3)).astype(BF16)

    h1 = (n1_ref[...] * mv[0:1] + mv[1:2]).astype(BF16)
    h1_ref[...] = h1
    q = (dot_nt(h1, wq_ref[...]) + mv[2:3]).astype(BF16)
    q_ref[...] = q

    patches = dot_nn(chosen_ref[...], h1).astype(BF16)
    patch_ref[...] = patches
    reduced = mv[4:5]
    for n in range(4):
        reduced = reduced + dot_nt(patches[n * keys : (n + 1) * keys], wr_ref[n])
    nk, rk = normalise(reduced)
    nk_ref[...] = nk
    rk_ref[...] = rk
    kn = (nk * mv[5:6] + mv[6:7]).astype(BF16)
    kn_ref[...] = kn
    kv = dot_nt(kn, wkv_ref[...])
    k = kv[:, :width].astype(BF16).astype(F32)
    v = (kv[:, width:] + mv[3:4]).astype(BF16).astype(F32)
    lane = lax.broadcasted_iota(jnp.int32, (keys, width), 1)
    for h in range(HEADS):
        inside = (lane >= h * dim) & (lane < (h + 1) * dim)
        at = pl.ds(h * keys, keys)
        kb_ref[at, :] = jnp.where(inside, k, 0.0).astype(BF16)
        vb_ref[at, :] = jnp.where(inside, v, 0.0).astype(BF16)

    score_ref[...] = dot_nt(q, kb_ref[...]) * dim ** (-0.5)
    def soften(i, carry):
        at = pl.ds(pl.multiple_of(i * 64, 64), 64)
        live = live_ref[at, :] > 0.5
        for h in range(HEADS):
            lane_at = pl.ds(h * keys, keys)
            s = jnp.where(live, score_ref[at, lane_at], MASKED)
            e = jnp.exp(s - jnp.max(s, axis=-1, keepdims=True))
            p_ref[at, lane_at] = e / jnp.sum(e, axis=-1, keepdims=True)
        return carry

    lax.fori_loop(0, capacity // 64, soften, 0, unroll=True)
    o = dot_nn(p_ref[...].astype(BF16), vb_ref[...]).astype(BF16)
    o_ref[...] = o
    x2_ref[...] = x_ref[...] + dot_nt(o, wp_ref[...]) + mv[7:8]
    mask_gradient(geo_ref, cot_ref, gy_ref, gyt_ref, mask_ref)


def one_hot(rows_ref, cols_ref, capacity):
    row0, row1, col0, col1 = rows_ref[0], rows_ref[1], cols_ref[0], cols_ref[1]
    area0, area1 = row0 * col0, row1 * col1
    quarter0, quarter1 = area0 // 4, area1 // 4
    keys = capacity // 4
    index = lax.broadcasted_iota(jnp.int32, (capacity, 128), 0)
    tap = index // keys
    key = index - tap * keys
    first = key < quarter0
    second = jnp.logical_and(key >= quarter0, key < quarter0 + quarter1)
    width = jnp.maximum(jnp.where(second, col1, col0), 2)
    half = width // 2
    local = key - jnp.where(second, quarter0, 0)
    row = ((local.astype(F32) + 0.5) / half.astype(F32)).astype(jnp.int32)
    col = local - row * half
    token = jnp.where(second, area0, 0) + (2 * row + tap // 2) * width + 2 * col + tap % 2
    token = jnp.where(first | second, token, -1)
    lane = lax.broadcasted_iota(jnp.int32, (capacity, 128), 1)
    return lanes(
        *[jnp.where(token == lane + t * 128, 1.0, 0.0).astype(BF16) for t in range(capacity // 128)]
    )


def mask_gradient(geo_ref, cot_ref, gy_ref, gyt_ref, mask_ref):
    width, capacity = cot_ref.shape
    area = geo_ref[0] * geo_ref[2] + geo_ref[1] * geo_ref[3]
    position = lax.broadcasted_iota(jnp.int32, (width, capacity), 1)
    gyt = jnp.where(position < area, cot_ref[...].astype(F32), 0.0)
    gyt_ref[...] = gyt.astype(BF16)
    gy_ref[...] = gyt.T.astype(BF16)
    first, second, row, col, heights, widths = token_geometry(geo_ref, capacity, 128)
    live = first | second
    start = lax.broadcasted_iota(jnp.int32, (capacity, 128), 0) // TILE * TILE
    late = start >= geo_ref[0] * geo_ref[2]
    early = jnp.logical_not(late)
    usual = (late & second) | (early & first)
    apart = second & early
    conditions = (
        live & (col > 0),
        live & (col < widths - 1),
        usual & (row > 0),
        usual & (row < heights - 1),
        apart & (row > 0),
        apart & (row < heights - 1),
        live,
    )
    for k, condition in enumerate(conditions):
        mask_ref[k] = jnp.where(condition, 1.0, 0.0)


def place_pieces(ref, core, me, wu_ref, wd_ref):
    cw = ref.shape[1]
    rn = 2 * cw
    tails = 128 * PARTS_W
    for x in range(PARTS_N // 2):
        n = 2 * x + core
        pieces = [ref[mixed_slot(w * PARTS_N + n, me)].astype(F32) for w in range(PARTS_W)]
        lane_at = pl.ds(pl.multiple_of(256 * n, 256), 256)
        for pair in range(PARTS_W // 2):
            value = rows_of(pieces[2 * pair][:, :256], pieces[2 * pair + 1][:, :256])
            wd_ref[pl.ds(pair * 2 * cw, 2 * cw), lane_at] = value.astype(BF16)
        at = pl.ds(pl.multiple_of(rn * n, 16), rn)
        for w, p in enumerate(pieces):
            wu_ref[at, pl.ds(128 * w, 128)] = rows_of(p[:, 256:384], p[:, 384:512]).astype(BF16)
        ends = [rows_of(p[:, 512 + 2 * REST : 512 + 3 * REST], p[:, 512 + 3 * REST :]) for p in pieces]
        wu_ref[at, pl.ds(tails, REST * PARTS_W)] = lanes(*ends).astype(BF16)


def prepare_two_kernel(tuned, x2_ref, mv_ref, own_ref, n2_ref, r2_ref, h2_ref, h2t_ref, wu_ref, wd_ref):
    me = my_index(tuned)
    place_pieces(own_ref, me & 1, me, wu_ref, wd_ref)
    normed, inverse = normalise(x2_ref[...])
    n2_ref[...] = normed
    r2_ref[...] = inverse
    h2 = normed * mv_ref[8:9, :] + mv_ref[9:10, :]
    h2_ref[...] = h2.astype(BF16)
    width = h2.shape[1]
    h2t_ref[:width, :] = h2.T.astype(BF16)
    h2t_ref[width:, :] = jnp.ones((h2t_ref.shape[0] - width, h2.shape[0]), BF16)


def ffn_kernel(
    tuned,
    geo_ref, h2_ref, h2t_ref, gy_ref, gyt_ref, mask_ref, own_ref, oth_ref, hv_ref, wu_in_ref, wd_in_ref,
    gown_ref, gsend_ref, act_ref, df_ref, hg_ref, wu_ref, wd_ref,
    f_ref, gm_ref, gp_ref, dc_ref, ul_ref, ur_ref, g0_ref, u0_ref, da_ref,
    upg_ref, dng_ref,
):
    me = my_index(tuned)
    capacity, width = h2_ref.shape
    hidden = hv_ref.shape[1]
    cw, rn = width // PARTS_W, width // PARTS_N
    tiles = capacity // TILE
    tails = 128 * PARTS_W

    place_pieces(oth_ref, 1 - (me & 1), me, wu_ref, wd_ref)
    for pair in range(PARTS_W // 2):
        got = [
            rows_of(*[piece_of(own_ref, oth_ref, w * PARTS_N + n, me, 4, 5, mixed_slot) for w in (2 * pair, 2 * pair + 1)])
            for n in range(PARTS_N)
        ]
        ends = lanes(*[g[:, : 2 * REST] for g in got]).astype(BF16)
        wd_ref[pl.ds(pair * 2 * cw, 2 * cw), pl.ds(tails, 2 * REST * PARTS_N)] = ends

    area, w0, w1 = geo_ref[0] * geo_ref[2], geo_ref[2], geo_ref[3]
    split = pl.multiple_of(jnp.minimum(area // TILE, tiles - 1) * TILE, TILE)

    for ref in (f_ref, gm_ref, gp_ref, dc_ref, ul_ref, ur_ref):
        ref[:, :PAD, :] = jnp.zeros((ref.shape[0], PAD, 128), F32)
        ref[:, PAD + capacity :, :] = jnp.zeros((ref.shape[0], PAD, 128), F32)


    def fold(values):
        return jnp.sum(values.reshape(TILE // 8, 8, 128), axis=0)

    halves = CHUNK // 128
    chunks = hidden // CHUNK
    zero = jnp.zeros((8, 128), F32)

    def columns(c):
        return pl.ds(pl.multiple_of(c * CHUNK, CHUNK), CHUNK)

    def vector(c, k, j):
        return hv_ref[k : k + 1, pl.ds(pl.multiple_of(c * CHUNK + j * 128, 128), 128)]

    def put_vector(c, k, j, value):
        hg_ref[k : k + 1, pl.ds(pl.multiple_of(c * CHUNK + j * 128, 128), 128)] = value

    def act_grad(c, at):
        da_ref[at, :] = dot_nn(gy_ref[at, :], wd_ref[:, columns(c)])

    def down_grad(c, at):
        dng_ref[at, columns(c)] = dot_nn(gyt_ref[at, :], act_ref[:, columns(c)])

    def tasks(product, c, rows, size):
        return [functools.partial(product, c, pl.ds(r, min(size, rows - r))) for r in range(0, rows, size)]

    def interleave(steps, products):
        done = 0
        for i, step in enumerate(steps):
            step()
            while done < len(products) and done * len(steps) < (i + 1) * len(products):
                products[done]()
                done += 1

    def chunk_step(c, carry):
        v = [[vector(c, k, j) for k in range(11)] for j in range(halves)]

        def taps_of(j, r, mask_left, mask_right):
            here = f_ref[c * halves + j, pl.ds(PAD + r, TILE), :]
            left = f_ref[c * halves + j, pl.ds(PAD + r - 1, TILE), :] * mask_left
            right = f_ref[c * halves + j, pl.ds(PAD + r + 1, TILE), :] * mask_right
            return left, here, right

        def row_length(r):
            return jnp.where(area > r, w0, w1)

        def column_taps(r):
            at = pl.ds(r, TILE)
            masks = mask_ref[0, at, :], mask_ref[1, at, :]
            for j in range(halves):
                left, here, right = taps_of(j, r, *masks)
                u = v[j]
                gm_ref[j, pl.ds(PAD + r, TILE), :] = u[2] * left + u[3] * here + u[4] * right
                g0_ref[j, at, :] = u[1] + u[5] * left + u[6] * here + u[7] * right
                gp_ref[j, pl.ds(PAD + r, TILE), :] = u[8] * left + u[9] * here + u[10] * right

        def column_taps_split():
            at = pl.ds(split, TILE)
            for j in range(halves):
                g0_ref[j, at, :] += (
                    mask_ref[4, at, :] * gm_ref[j, pl.ds(PAD + split - w1, TILE), :]
                    + mask_ref[5, at, :] * gp_ref[j, pl.ds(PAD + split + w1, TILE), :]
                )

        conv_sums = [zero] * halves

        def activate(r):
            at = pl.ds(r, TILE)
            length = row_length(r)
            above, below = mask_ref[2, at, :], mask_ref[3, at, :]
            for j in range(halves):
                conv = (
                    g0_ref[j, at, :]
                    + above * gm_ref[j, pl.ds(PAD + r - length, TILE), :]
                    + below * gp_ref[j, pl.ds(PAD + r + length, TILE), :]
                )
                half = 0.5 * (1.0 + lax.erf(conv * 2.0 ** (-0.5)))
                act_ref[at, pl.ds(pl.multiple_of(c * CHUNK + j * 128, 128), 128)] = (conv * half).astype(BF16)
                slope = half + conv * ((2.0 * math.pi) ** (-0.5) * jnp.exp2(conv * conv * (-0.5 / math.log(2.0))))
                value = da_ref[at, pl.ds(j * 128, 128)] * slope
                dc_ref[j, pl.ds(PAD + r, TILE), :] = value
                conv_sums[j] = conv_sums[j] + fold(value)

        tap_sums = [[zero] * 9 for _ in range(halves)]

        def tap_back(r):
            at = pl.ds(r, TILE)
            length = row_length(r)
            masks = [mask_ref[k, at, :] for k in range(4)]
            for j in range(halves):
                left, here, right = taps_of(j, r, *masks[:2])
                u = v[j]
                below = masks[3] * dc_ref[j, pl.ds(PAD + r + length, TILE), :]
                level = dc_ref[j, pl.ds(PAD + r, TILE), :]
                above = masks[2] * dc_ref[j, pl.ds(PAD + r - length, TILE), :]
                ul_ref[j, pl.ds(PAD + r, TILE), :] = u[2] * below + u[5] * level + u[8] * above
                u0_ref[j, at, :] = u[3] * below + u[6] * level + u[9] * above
                ur_ref[j, pl.ds(PAD + r, TILE), :] = u[4] * below + u[7] * level + u[10] * above
                grads = [fold(d * f) for d in (below, level, above) for f in (left, here, right)]
                tap_sums[j] = [a + b for a, b in zip(tap_sums[j], grads)]

        def tap_back_split():
            at, padded = pl.ds(split, TILE), pl.ds(PAD + split, TILE)
            masks = [mask_ref[k, at, :] for k in (0, 1, 4, 5)]
            for j in range(halves):
                left, here, right = taps_of(j, split, *masks[:2])
                u = v[j]
                below = masks[3] * dc_ref[j, pl.ds(PAD + split + w1, TILE), :]
                above = masks[2] * dc_ref[j, pl.ds(PAD + split - w1, TILE), :]
                ul_ref[j, padded, :] += u[2] * below + u[8] * above
                u0_ref[j, at, :] += u[3] * below + u[9] * above
                ur_ref[j, padded, :] += u[4] * below + u[10] * above
                grads = [fold(d * f) for d in (below, above) for f in (left, here, right)]
                tap_sums[j] = [a + b for a, b in zip(tap_sums[j], grads[:3] + [zero] * 3 + grads[3:])]

        def spread_back(r):
            at = pl.ds(r, TILE)
            mask_left, mask_right = mask_ref[0, at, :], mask_ref[1, at, :]
            for j in range(halves):
                value = (
                    u0_ref[j, at, :]
                    + mask_left * ur_ref[j, pl.ds(PAD + r - 1, TILE), :]
                    + mask_right * ul_ref[j, pl.ds(PAD + r + 1, TILE), :]
                ).astype(BF16)
                df_ref[at, pl.ds(pl.multiple_of(c * CHUNK + j * 128, 128), 128)] = value

        def steps(step):
            return [functools.partial(step, r) for r in range(0, capacity, TILE)]

        interleave(steps(column_taps) + [column_taps_split], tasks(act_grad, c, capacity, MROWS))
        interleave(
            steps(activate),
            [],
        )
        interleave(steps(tap_back) + [tap_back_split], tasks(down_grad, c, width, MROWS))
        interleave(steps(spread_back), [])
        for j in range(halves):
            put_vector(c, 1, j, column_sum(conv_sums[j]))
            for k in range(9):
                put_vector(c, 2 + k, j, column_sum(tap_sums[j][k]))
        return carry

    for c in range(chunks):
        value = dot_nn(h2_ref[...], wu_ref[:, c * CHUNK : (c + 1) * CHUNK])
        for j in range(halves):
            bias = hv_ref[0:1, pl.ds(c * CHUNK + j * 128, 128)]
            f_ref[c * halves + j, pl.ds(PAD, capacity), :] = value[:, j * 128 : (j + 1) * 128] + bias
    lax.fori_loop(0, chunks, chunk_step, 0)
    upg_ref[...] = dot_nn(h2t_ref[...], df_ref[...])
    hg_ref[0:1, :] = upg_ref[width : width + 1, :]
    hg_ref[11:, :] = jnp.zeros((hg_ref.shape[0] - 11, hidden), F32)

    def value_of(w, n):
        down = pl.ds(w * cw, cw)
        up = [pl.ds(n * rn + e * cw, cw) for e in range(2)]
        return lanes(
            dng_ref[down, pl.ds(256 * n, 256)],
            *[upg_ref[e, pl.ds(128 * w, 128)] for e in up],
            dng_ref[down, pl.ds(tails + 2 * REST * n, 2 * REST)],
            *[upg_ref[e, pl.ds(tails + REST * w, REST)] for e in up],
        )

    store_pieces(gown_ref, gsend_ref, me, value_of, mixed_slot)


def store_pieces(own_ref, send_ref, me, value_of, order):
    even = (me & 1) == 0
    for w in range(PARTS_W):
        for x in range(PARTS_N // 2):
            first, second = value_of(w, 2 * x), value_of(w, 2 * x + 1)
            slot0, slot1 = (order(w * PARTS_N + 2 * x + c, me) for c in range(2))
            own_ref[jnp.where(even, slot0, slot1)] = jnp.where(even, first, second).astype(BF16)
            send_ref[jnp.where(even, slot1, slot0)] = jnp.where(even, second, first).astype(BF16)


def norm_two_back_kernel(df_ref, wu_ref, n2_ref, r2_ref, gy_ref, mv_ref, dx2_ref, mg_ref, dh2_ref):
    capacity, width = n2_ref.shape
    dh2_ref[...] = dot_nt(df_ref[...], wu_ref[...])

    def norm_back(i, carry):
        at = pl.ds(pl.multiple_of(i * 64, 64), 64)
        gy = gy_ref[at, :].astype(F32)
        grad, normed = dh2_ref[at, :], n2_ref[at, :]
        dx2_ref[at, :] = gy + normalise_back(grad, normed, r2_ref[at, :], mv_ref[8:9, :])
        return tuple(a + column_sum(b) for a, b in zip(carry, (grad * normed, grad, gy)))

    zero = jnp.zeros((1, width), F32)
    sums = lax.fori_loop(0, capacity // 64, norm_back, (zero, zero, zero), unroll=True)
    mg_ref[...] = jnp.zeros_like(mg_ref)
    for k in range(3):
        mg_ref[8 + k : 9 + k, :] = sums[k]


def score_back_kernel(dx2_ref, vb_ref, p_ref, o_ref, wp_ref, gp_ref, dob_ref, ds_ref, bp_ref, dp_ref):
    capacity = dx2_ref.shape[0]
    keys = capacity // 4
    datt = dx2_ref[...].astype(BF16)
    bp_ref[...] = column_sum(datt.astype(F32))
    gp_ref[...] = dot_tn(datt, o_ref[...])
    dob = dot_nn(datt, wp_ref[...]).astype(BF16)
    dob_ref[...] = dob
    dp_ref[...] = dot_nt(dob, vb_ref[...])

    def soften_back(i, carry):
        at = pl.ds(pl.multiple_of(i * 64, 64), 64)
        for h in range(HEADS):
            lane_at = pl.ds(h * keys, keys)
            p = p_ref[at, lane_at]
            dp = dp_ref[at, lane_at]
            row = jnp.sum(p * dp, axis=-1, keepdims=True)
            ds_ref[at, lane_at] = (p * (dp - row)).astype(BF16)
        return carry

    lax.fori_loop(0, capacity // 64, soften_back, 0, unroll=True)


def attend_back_kernel(
    tuned,
    dob_ref, ds_ref, gp_ref, h1_ref, patch_ref, nk_ref, rk_ref, kn_ref, q_ref, kb_ref, p_ref,
    wr_ref, wkv_ref, mv_ref,
    gown_ref, gsend_ref, dq_ref, dpatch_ref, vk_ref,
    gr_ref, gq_ref, gkv_ref,
):
    me = my_index(tuned)
    capacity, width = h1_ref.shape
    cw, rn = width // PARTS_W, width // PARTS_N
    keys = capacity // 4
    dim = width // HEADS
    scale = dim ** (-0.5)

    ds = ds_ref[...]
    dq = (dot_nn(ds, kb_ref[...]) * scale).astype(BF16)
    dq_ref[...] = dq
    dk_all = dot_tn(ds, q_ref[...])
    dv_all = dot_tn(p_ref[...].astype(BF16), dob_ref[...])
    lane = lax.broadcasted_iota(jnp.int32, (keys, width), 1)
    dk = jnp.zeros((keys, width), F32)
    dv = jnp.zeros((keys, width), F32)
    for h in range(HEADS):
        inside = (lane >= h * dim) & (lane < (h + 1) * dim)
        dk = jnp.where(inside, dk_all[h * keys : (h + 1) * keys], dk)
        dv = jnp.where(inside, dv_all[h * keys : (h + 1) * keys], dv)
    dk = (dk * scale).astype(BF16)
    dv = dv.astype(BF16)
    gq_ref[...] = dot_tn(dq, h1_ref[...])
    kn = kn_ref[...]
    gkv_ref[pl.ds(0, width), :] = dot_tn(dk, kn)
    gkv_ref[pl.ds(width, width), :] = dot_tn(dv, kn)
    dkn = dot_nn(dk, wkv_ref[pl.ds(0, width), :]) + dot_nn(dv, wkv_ref[pl.ds(width, width), :])
    nk = nk_ref[...]
    dsr = normalise_back(dkn, nk, rk_ref[...], mv_ref[5:6, :]).astype(BF16)
    vk_ref[...] = rows_of(
        column_sum(dq.astype(F32)),
        column_sum(dv.astype(F32)),
        column_sum(dsr.astype(F32)),
        column_sum(dkn * nk),
        column_sum(dkn),
        jnp.zeros((3, width), F32),
    )
    for n in range(4):
        at = pl.ds(n * keys, keys)
        gr_ref[n] = dot_tn(dsr, patch_ref[at, :])
        dpatch_ref[at, :] = dot_nn(dsr, wr_ref[n])

    def value_of(w, n):
        at, lane_at = pl.ds(w * cw, cw), pl.ds(n * rn, rn)
        return lanes(
            gr_ref[n, at, :],
            gq_ref[at, lane_at],
            gkv_ref[pl.ds(2 * w * cw, cw), lane_at],
            gkv_ref[pl.ds(2 * w * cw + cw, cw), lane_at],
            gp_ref[at, lane_at],
        )

    store_pieces(gown_ref, gsend_ref, me, value_of, round_slot)


def token_grad_kernel(dx2_ref, dh1_ref, n1_ref, r1_ref, mv_ref, tg_ref):
    value = dx2_ref[...] + normalise_back(dh1_ref[...], n1_ref[...], r1_ref[...], mv_ref[0:1, :])
    tg_ref[...] = value.T.astype(BF16)


def mixed_kernel(x2_ref, act_ref, wd_ref, mv_ref, mask_ref, mixed_ref):
    width = x2_ref.shape[1]
    occupied = mask_ref[6]
    occupied = lanes(*([occupied] * (width // 128)), occupied[:, : width % 128])
    mixed = x2_ref[...] + dot_nt(act_ref[...], wd_ref[...]) + mv_ref[10:11, :]
    mixed_ref[...] = (mixed * occupied).T.astype(BF16)


def fold_rows(value, unit):
    rest = value[8:]
    beside = lanes(rest[:, : 3 * unit], jnp.zeros((8, 256 - 3 * unit), F32))
    below = lanes(rest[:, 3 * unit :], jnp.zeros((8, 256 - 2 * unit), F32))
    return lanes(value[:8], (beside + pltpu.roll(below, 3, 0))[:, : 3 * unit])


def unfold_rows(value, unit):
    beside = lanes(value[:, 5 * unit :], jnp.zeros((8, 256 - 3 * unit), F32))
    below = pltpu.roll(beside, 5, 0)
    return rows_of(value[:, : 5 * unit], lanes(beside[:, : 3 * unit], below[:, : 2 * unit]))


def token_back_kernel(
    tuned,
    dq_ref, dpatch_ref, n1_ref, chosen_ref, wq_ref, mg_ref, hg_ref, vk_ref, bp_ref,
    dh1_ref, vown_ref, vsend_ref,
):
    me = my_index(tuned)
    width = n1_ref.shape[1]
    rn = width // PARTS_N
    chosen = chosen_ref[...]
    high = dpatch_ref[...].astype(BF16)
    low = (dpatch_ref[...] - high.astype(F32)).astype(BF16)
    dh1 = dot_nn(dq_ref[...], wq_ref[...]) + dot_tn(chosen, high) + dot_tn(chosen, low)
    n1 = n1_ref[...]
    vk = vk_ref[...]
    dh1_ref[...] = dh1
    sums = rows_of(column_sum(dh1 * n1), column_sum(dh1), vk[0:5], bp_ref[...], mg_ref[8:16, :])
    hg = hg_ref[...]
    value = []
    for n in range(PARTS_N):
        parts = []
        for w in (2 * n, 2 * n + 1):
            parts += [hg[:, 128 * w : 128 * (w + 1)], hg[:, 1024 + REST * w : 1024 + REST * (w + 1)]]
        value.append(fold_rows(lanes(sums[:, n * rn : (n + 1) * rn], *parts), rn))
    even = (me & 1) == 0
    for x in range(2):
        slot = x ^ ((me >> 1) & 1)
        vown_ref[slot] = jnp.where(even, value[2 * x], value[2 * x + 1]).astype(BF16)
        vsend_ref[slot] = jnp.where(even, value[2 * x + 1], value[2 * x]).astype(BF16)


def total_of(refs):
    value = refs[0][...].astype(F32)
    for ref in refs[1:]:
        value = value + ref[...].astype(F32)
    return value


def halve_kernel(keep_ref, got_ref, low_ref, high_ref):
    half = low_ref.shape[0]
    low_ref[...] = (keep_ref[:half].astype(F32) + got_ref[:half].astype(F32)).astype(BF16)
    high_ref[...] = (keep_ref[half:].astype(F32) + got_ref[half:].astype(F32)).astype(BF16)


def core_high_kernel(own_ref, got_ref, high_ref):
    half = high_ref.shape[0]
    high_ref[...] = (own_ref[half:].astype(F32) + got_ref[...].astype(F32)).astype(BF16)


def core_low_kernel(own_ref, core_ref, got_ref, low_ref, high_ref):
    half = low_ref.shape[0]
    total = own_ref[: 2 * half].astype(F32) + core_ref[...].astype(F32) + got_ref[...].astype(F32)
    low_ref[...] = total[:half].astype(BF16)
    high_ref[...] = total[half:].astype(BF16)


def halve_core_kernel(keep_ref, got_ref, vkeep_ref, vgot_ref, low_ref, vlow_ref, send_ref):
    half = low_ref.shape[0]
    low_ref[...] = (keep_ref[:half].astype(F32) + got_ref[:half].astype(F32)).astype(BF16)
    parts = [keep_ref[half + k].astype(F32) + got_ref[half + k].astype(F32) for k in range(half)]
    vector = total_of((vkeep_ref, vgot_ref))
    vlow_ref[...] = vector.astype(BF16)
    send_ref[...] = rows_of(*parts, vector[0], vector[1]).astype(BF16)


def halve_round_kernel(tuned, keep_ref, vkeep_ref, got_ref, low_ref, vlow_ref, send_ref):
    half, cw = low_ref.shape[:2]
    rows = vkeep_ref.shape[1]
    got = got_ref[...].astype(F32)
    parts = [keep_ref[k].astype(F32) + got[k * cw : (k + 1) * cw] for k in range(2 * half)]
    for k in range(half):
        low_ref[k] = parts[k].astype(BF16)
    got0, got1 = (got[2 * half * cw + k * rows : 2 * half * cw + (k + 1) * rows] for k in range(2))
    keep0, keep1 = vkeep_ref[0].astype(F32), vkeep_ref[1].astype(F32)
    even = (my_index(tuned) & 1) == 0
    low = keep0 + jnp.where(even, got0, got1)
    vlow_ref[0] = low.astype(BF16)
    send_ref[...] = rows_of(*parts[half:], jnp.where(even, keep1 + got1, low)).astype(BF16)


def quarter_vector_kernel(keep_ref, vkeep_ref, got_ref, *out_refs):
    cw = keep_ref.shape[1]
    got = got_ref[...].astype(F32)
    vector = vkeep_ref[0].astype(F32) + got[4 * cw :]
    for k, ref in enumerate(out_refs):
        ref[...] = rows_of(keep_ref[k].astype(F32) + got[k * cw : (k + 1) * cw], vector).astype(BF16)


def finish_kernel(
    a_ref, b_ref, c_ref, d_ref, ffn_ref, ffn_got_ref,
    q_ref, kv_ref, red_ref, proj_ref, up_ref, down_ref, vm_ref, vh_ref,
):
    total = total_of((a_ref, b_ref, c_ref, d_ref))
    cw, width = red_ref.shape
    rn = q_ref.shape[1]
    red_ref[...] = total[:cw, :width]
    unit = [total[:cw, width + k * rn : width + (k + 1) * rn] for k in range(4)]
    q_ref[...] = unit[0]
    kv_ref[...] = rows_of(unit[1], unit[2]).T
    proj_ref[...] = unit[3]
    vector = unfold_rows(total[cw:], rn)
    vm_ref[...] = vector[: vm_ref.shape[0], :rn]
    vh_ref[...] = vector[: vh_ref.shape[0], rn:]
    total = total_of((ffn_ref, ffn_got_ref))[0]
    columns = [
        lanes(total[:, 128 * k : 128 * (k + 1)], total[:, 512 + REST * k : 512 + REST * (k + 1)]) for k in range(4)
    ]
    down_ref[...] = lanes(*columns[:2])
    up_ref[...] = rows_of(*columns[2:])


def call(kernel, inputs, outputs, scratch=(), scalars=0, limit=24, flops=0, moved=0, aliases={}):
    vmem = pl.BlockSpec(memory_space=pltpu.VMEM)
    smem = pl.BlockSpec(memory_space=pltpu.SMEM)
    return pl.pallas_call(
        kernel,
        out_shape=[jax.ShapeDtypeStruct(shape, kind) for shape, kind in outputs],
        in_specs=[smem] * scalars + [vmem] * (len(inputs) - scalars),
        out_specs=[vmem] * len(outputs),
        scratch_shapes=[pltpu.VMEM(shape, kind) for shape, kind in scratch],
        input_output_aliases=aliases,
        compiler_params=pltpu.CompilerParams(vmem_limit_bytes=limit * 2**20),
        cost_estimate=pl.CostEstimate(flops=flops, bytes_accessed=moved, transcendentals=0),
    )(*inputs)


def after(value, *others):
    return lax.optimization_barrier((value, *others))[0]


def on_device(
    mesh_shape,
    tokens, cotangent, img_rows, img_cols,
    q_weight, kv_weight, reduce_weight, proj_weight, up_weight, down_weight, vec_model, vec_hidden,
):
    wide, narrow = mesh_shape
    tuned = (wide, narrow) == (PARTS_W, PARTS_N)
    capacity, width = tokens.shape
    hidden = vec_hidden.shape[1] * narrow
    cw, rn = width // PARTS_W, width // PARTS_N
    keys = capacity // 4
    piece = (cw, 2 * width)
    vpiece, gpiece = (16, 2 * width), (8, 2 * width)

    def join(*parts):
        return jnp.concatenate(parts, axis=0)

    def swap(value, mask, other=None):
        masks = (mask, mask if other is None else other)
        pairs = [(i, i ^ masks[i & 1]) for i in range(wide * narrow)]
        return lax.ppermute(value, ("wide", "narrow"), pairs)

    tokens_f32 = ((capacity, width), F32)
    tokens_low = ((capacity, width), BF16)
    x, n1, r1, chosen, live, geo = prepare(img_rows, img_cols, tokens.T)
    if tuned:
        pack_a, pack_b, pack_v = pack(
            (
                q_weight.T, kv_weight, reduce_weight.T, proj_weight.T, up_weight, down_weight.T,
                vec_model, vec_hidden,
            ),
            piece, vpiece,
        )
        line_a = [swap(pack_a, m) for m in (8, 16, 24)]
        got_b, got_v = swap(pack_b, 2, 4), swap(pack_v, 1)
        *line_a, got_b, got_v = lax.optimization_barrier((*line_a, got_b, got_v, x, n1, chosen))[:5]
        buf_a, buf_b, vecs = join(pack_a, *line_a), join(pack_b, got_b), join(pack_v, got_v)
        buf_a, buf_b = join(buf_a, swap(buf_a, 2, 4)), join(buf_b, swap(buf_b, 16))
        got = lax.optimization_barrier((swap(buf_a, 4, 2), swap(buf_b, 8), swap(vecs, 2)))
        own_a, half_b, vecs = (join(v, g) for v, g in zip((buf_a, buf_b, vecs), got))
        oth_a = swap(own_a, 1)
        rest_b = swap(half_b, 4, 2)
        oth_half_b = swap(after(half_b, oth_a), 1)
    else:
        own_a, oth_a, own_b, oth_b, vecs = gather_plain(
            q_weight, kv_weight, reduce_weight, proj_weight, up_weight, down_weight, vec_model, vec_hidden
        )

    square = (width, width)
    (
        x2, h1, patches, nk, rk, kn, q, kb, vb, p, o, wr, wq, wkv, wp, mv, hv, gy, gyt, masks,
    ) = call(
        functools.partial(attend_kernel, tuned),
        (geo, cotangent.T, x, n1, chosen, live, own_a, oth_a, vecs),
        (
            tokens_f32, tokens_low,
            ((capacity, width), BF16), ((keys, width), F32), ((keys, 1), F32), ((keys, width), BF16),
            ((capacity, width), BF16), ((HEADS * keys, width), BF16), ((HEADS * keys, width), BF16),
            ((capacity, HEADS * keys), F32), ((capacity, width), BF16),
            ((4,) + square, BF16), (square, BF16), ((2 * width, width), BF16), (square, BF16),
            ((16, width), F32), ((16, hidden), F32),
            tokens_low, ((width, capacity), BF16), ((7, capacity, 128), F32),
        ),
        scratch=(((capacity, HEADS * keys), F32),),
        scalars=1,
        flops=8 * 10**9,
    )

    if tuned:
        rest_b = after(rest_b, x2)
        own_b = join(half_b, rest_b)
        oth_b = join(oth_half_b, swap(rest_b, 1))
    padded = ((CHUNK // 128, capacity + 2 * PAD, 128), F32)
    halved = ((CHUNK // 128, capacity, 128), F32)
    chunked = ((capacity, CHUNK), F32)
    n2, r2, h2, h2t, wu, wd = call(
        functools.partial(prepare_two_kernel, tuned),
        (x2, mv, own_b),
        (
            tokens_f32, ((capacity, 1), F32), tokens_low, ((width + 16, capacity), BF16),
            ((width, hidden), BF16), ((width, hidden), BF16),
        ),
        flops=10**9,
    )
    gown_b, gsend_b, act, df, hg, wu, wd = call(
        functools.partial(ffn_kernel, tuned),
        (geo, h2, h2t, gy, gyt, masks, own_b, oth_b, hv, wu, wd),
        (
            ((SLOTS,) + piece, BF16), ((SLOTS,) + piece, BF16),
            ((capacity, hidden), BF16), ((capacity, hidden), BF16), ((16, hidden), F32),
            ((width, hidden), BF16), ((width, hidden), BF16),
        ),
        aliases={9: 5, 10: 6},
        scratch=(
            ((hidden // 128, capacity + 2 * PAD, 128), F32), padded, padded, padded, padded, padded,
            halved, halved, chunked,
            ((width + 16, hidden), F32), ((width, hidden), F32),
        ),
        scalars=1,
        flops=33 * 10**9,
    )

    dx2, mg = call(
        norm_two_back_kernel,
        (df, wu, n2, r2, gy, mv),
        (tokens_f32, ((16, width), F32)),
        scratch=(tokens_f32,),
        flops=10**9,
    )
    if tuned:
        core_high, core_low = swap(gsend_b[8:], 1), swap(gsend_b[:8], 1)
        core_high, dx2 = lax.optimization_barrier((core_high, dx2))
        (high_b,) = call(core_high_kernel, (gown_b, core_high), (((8,) + piece, BF16),))
        got_b = swap(high_b, 4, 2)
        dx2 = after(dx2, high_b)
    gp, dob, ds, bp = call(
        score_back_kernel,
        (dx2, vb, p, o, wp),
        (
            (square, F32), ((capacity, width), BF16), ((capacity, HEADS * keys), BF16), ((1, width), F32),
        ),
        scratch=(((capacity, HEADS * keys), F32),),
        flops=0,
    )

    def halve(keep, got, flops=0):
        shape = ((keep.shape[0] // 2,) + piece, BF16)
        return call(halve_kernel, (keep, got), (shape, shape), flops=flops)

    gown_a, gsend_a, dq, dpatch, vk = call(
        functools.partial(attend_back_kernel, tuned),
        (dob, ds, gp, h1, patches, nk, rk, kn, q, kb, p, wr, wkv, mv),
        (
            ((SLOTS,) + piece, BF16), ((SLOTS,) + piece, BF16), ((capacity, width), BF16), ((capacity, width), F32),
            ((8, width), F32),
        ),
        scratch=(((4,) + square, F32), (square, F32), ((2 * width, width), F32)),
        flops=0,
    )
    if tuned:
        got_a = swap(gsend_a, 1)
        low_b, high_b = call(
            core_low_kernel, (gown_b, core_low, got_b), (((4,) + piece, BF16),) * 2, flops=7*10**9
        )
        gown_a = after(gown_a, high_b)
    (mixed,) = call(mixed_kernel, (x2, act, wd, mv, masks), (((width, capacity), BF16),), flops=10**9)
    dh1, vown, vsend = call(
        functools.partial(token_back_kernel, tuned),
        (dq, dpatch, n1, chosen, wq, mg, hg, vk, bp),
        (tokens_f32, ((2,) + gpiece, BF16), ((2,) + gpiece, BF16)),
    )

    (token_grad,) = call(token_grad_kernel, (dx2, dh1, n1, r1, mv), (((width, capacity), BF16),), flops=10**9)

    if not tuned:
        grads = scatter_plain(mesh_shape, width, gown_a, gsend_a, gown_b, gsend_b, vown, vsend)
        return (mixed.T, token_grad.T) + grads

    vrows = gpiece[0]
    low_a, vlow, high_a = call(
        halve_core_kernel,
        (gown_a, got_a, vown, swap(vsend, 1)),
        (((8,) + piece, BF16), ((2,) + gpiece, BF16), ((8 * cw + 2 * vrows, 2 * width), BF16)),
    )
    got_a, got_b, mixed, token_grad = lax.optimization_barrier((swap(high_a, 4, 2), swap(high_b, 8), mixed, token_grad))
    low_a, vlow, high_a = call(
        functools.partial(halve_round_kernel, tuned),
        (low_a, vlow, got_a),
        (((4,) + piece, BF16), ((1,) + gpiece, BF16), ((4 * cw + vrows, 2 * width), BF16)),
    )
    low_b, high_b = halve(low_b, got_b)
    got_a, got_b = swap(high_a, 2, 4), swap(high_b, 16)
    near_a = list(call(quarter_vector_kernel, (low_a, vlow, got_a), (((cw + vrows, 2 * width), BF16),) * 4))
    line_a = [swap(near_a[k], 8 * k) for k in (1, 2, 3)]
    low_b, high_b = halve(low_b, got_b)
    q_grad, kv_grad, reduce_grad, proj_grad, up_grad, down_grad, vm_grad, vh_grad = call(
        finish_kernel,
        (near_a[0], *line_a, low_b, swap(high_b, 2, 4)),
        (
            ((cw, rn), F32), ((rn, 2 * cw), F32), ((cw, width), F32), ((cw, rn), F32),
            ((rn, 4 * cw), F32), ((cw, width), F32), ((11, rn), F32), ((11, width), F32),
        ),
    )
    return (
        mixed.T, token_grad.T, q_grad.T, kv_grad, reduce_grad.T, proj_grad.T, up_grad, down_grad.T, vm_grad, vh_grad,
    )


def gather_plain(q, kv, reduce, proj, up, down, vec_model, vec_hidden):
    def whole(value):
        rows = lax.all_gather(value, "narrow", axis=0, tiled=True)
        return lax.all_gather(rows, "wide", axis=1, tiled=True).T

    q, kv, reduce, proj, up, down = (whole(v) for v in (q, kv, reduce, proj, up, down))
    width = q.shape[0]
    cw, rn = width // PARTS_W, width // PARTS_N

    def pieces(turned, blocks):
        split = turned.reshape(PARTS_W, blocks, cw, PARTS_N, -1)
        return split.transpose(0, 3, 2, 1, 4).reshape(PARTS_W, PARTS_N, cw, -1)

    def slots(value, mixed=False):
        value = value.reshape(2, 2, 2, 2, 2, cw, -1)
        orders = ((2, 1, 0, 3), (3, 1, 0, 2)) if mixed else ((2, 3, 0, 1), (3, 2, 0, 1))
        return tuple(
            value[:, :, :, :, core].transpose(*order, 4, 5).reshape(SLOTS, cw, -1) for core, order in enumerate(orders)
        )

    a = jnp.concatenate([pieces(reduce, 1), pieces(q, 1), pieces(kv, 2), pieces(proj, 1)], axis=-1)
    columns = pieces(down, 1).reshape(PARTS_W, PARTS_N, cw, 2, RUN)
    columns = [columns[..., e, :] for e in range(2)]
    halves = up.T.reshape(PARTS_N, 2, cw, PARTS_W, RUN).transpose(1, 3, 0, 2, 4)
    columns += [halves[0], halves[1]]
    b = jnp.concatenate([c[..., :128] for c in columns] + [c[..., 128:] for c in columns], axis=-1)
    vm = lax.all_gather(vec_model, "narrow", axis=1, tiled=True)
    vh = lax.all_gather(vec_hidden, "narrow", axis=1, tiled=True)
    both = jnp.concatenate([vm.reshape(11, PARTS_N, rn), vh.reshape(11, PARTS_N, width)], axis=-1)
    vecs = jnp.pad(both.transpose(1, 0, 2), ((0, 0), (0, 5), (0, 3 * rn)))
    return (*slots(a), *slots(b, True), vecs)


def scatter_plain(mesh_shape, width, gown_a, gsend_a, gown_b, gsend_b, vown, vsend):
    cw, rn = width // PARTS_W, width // PARTS_N

    def devices(own, send, mixed=False):
        orders = ((2, 1, 0, 3), (3, 1, 0, 2)) if mixed else ((2, 3, 0, 1), (3, 2, 0, 1))
        parts = []
        for value, order in zip((own, send), orders):
            back = sorted(range(4), key=lambda k: order[k])
            parts.append(value.reshape(2, 2, 2, 2, cw, -1).transpose(*back, 4, 5))
        return jnp.stack(parts, axis=4).reshape(PARTS_W, PARTS_N, cw, -1)

    def natural(value, blocks):
        split = value.reshape(PARTS_W, PARTS_N, cw, blocks, -1).transpose(0, 3, 2, 1, 4)
        return split.reshape(PARTS_W * blocks * cw, -1).T

    def share(value):
        columns = lax.psum_scatter(value.astype(BF16), "wide", scatter_dimension=1, tiled=True)
        return lax.psum_scatter(columns, "narrow", scatter_dimension=0, tiled=True).astype(F32)

    a = devices(gown_a, gsend_a)
    b = devices(gown_b, gsend_b, True)
    reduce = natural(a[..., :width], 1)
    q = natural(a[..., width : width + rn], 1)
    kv = natural(a[..., width + rn : width + 3 * rn], 2)
    proj = natural(a[..., width + 3 * rn :], 1)
    columns = [
        jnp.concatenate([b[..., 128 * k : 128 * (k + 1)], b[..., 512 + REST * k : 512 + REST * (k + 1)]], axis=-1)
        for k in range(4)
    ]
    down = natural(jnp.concatenate(columns[:2], axis=-1), 1)
    up = jnp.stack(columns[2:]).transpose(2, 0, 3, 1, 4).reshape(width, -1)
    vectors = jnp.stack([vown, vsend], axis=1).reshape(PARTS_N, 8, -1)
    beside = vectors[..., 5 * rn :]
    beside = jnp.concatenate([beside[:, :3], beside[:, 3:6, : 2 * rn]], axis=-1)
    vectors = jnp.concatenate([vectors[..., : 5 * rn], beside], axis=1).transpose(1, 0, 2)
    vm = vectors[..., :rn].reshape(11, width)
    vh = vectors[..., rn : rn + width].reshape(11, PARTS_N * width)

    def share_vector(value):
        total = lax.psum(value.astype(BF16), "wide")
        return lax.psum_scatter(total, "narrow", scatter_dimension=1, tiled=True).astype(F32)

    return tuple(share(v) for v in (q, kv, reduce, proj, up, down)) + (share_vector(vm), share_vector(vh))


def solution(mesh):
    both, rows, weight, vector = P(("wide", "narrow"), None), P(("wide", "narrow")), P("narrow", "wide"), P(None, "narrow")
    return jax.shard_map(
        functools.partial(on_device, (mesh.shape["wide"], mesh.shape["narrow"])),
        mesh=mesh,
        in_specs=(both, both, rows, rows) + (weight,) * 6 + (vector,) * 2,
        out_specs=(both, both) + (weight,) * 6 + (vector,) * 2,
        check_vma=False,
    )
```

```python
import functools
import math

import jax
import jax.numpy as jnp
from jax import lax
from jax.experimental import pallas as pl
from jax.experimental.pallas import tpu as pltpu
from jax.sharding import PartitionSpec as P

HEADS = 5
EPSILON = 1e-06
MASKED = -1000000000.0
F32 = jnp.float32
BF16 = jnp.bfloat16

PARTS_W = 8
PARTS_N = 4
SLOTS = 16
TILE = 32
CHUNK = 256
PAD = 40
MROWS = 256
RUN = 160
REST = RUN - 128


def dot_nn(left, right):
    return jnp.dot(left, right, preferred_element_type=F32)


def dot_nt(left, right):
    return lax.dot_general(left, right, (((1,), (1,)), ((), ())), preferred_element_type=F32)


def dot_tn(left, right):
    return lax.dot_general(left, right, (((0,), (0,)), ((), ())), preferred_element_type=F32)


def lanes(*parts):
    return jnp.concatenate(parts, axis=1)


def rows_of(*parts):
    return jnp.concatenate(parts, axis=0)


def my_index(tuned):
    if not tuned:
        return jnp.int32(0)
    return lax.axis_index("wide") * PARTS_N + lax.axis_index("narrow")


def round_slot(device, me):
    delta = device ^ me
    first, second = (delta >> 1) & 1, (delta >> 2) & 1
    if device & 1:
        first, second = second, first
    return second * 8 + first * 4 + (delta >> 3)


def mixed_slot(device, me):
    delta = device ^ me
    x, y = (delta >> 1) & 1, (delta >> 2) & 1
    odd = (device & 1) == 1
    first, second = jnp.where(odd, y, x), jnp.where(odd, x, y)
    return second * 8 + ((delta >> 3) & 1) * 4 + ((delta >> 4) & 1) * 2 + first


def normalise(values):
    centre = values - jnp.mean(values, axis=-1, keepdims=True)
    inverse = lax.rsqrt(jnp.mean(centre * centre, axis=-1, keepdims=True) + EPSILON)
    return centre * inverse, inverse


def normalise_back(grad, normed, inverse, gain):
    scaled = grad * gain
    first = jnp.mean(scaled, axis=-1, keepdims=True)
    second = jnp.mean(scaled * normed, axis=-1, keepdims=True)
    return (scaled - first - normed * second) * inverse


def column_sum(values):
    return jnp.sum(values, axis=0, keepdims=True)


def piece_of(own_ref, other_ref, device, me, first=0, last=5, order=round_slot):
    slot = order(device, me)
    mine = ((device ^ me) & 1) == 0
    at = pl.ds(128 * first, 128 * (last - first))
    return jnp.where(mine, own_ref[slot, :, at].astype(F32), other_ref[slot, :, at].astype(F32))


def token_geometry(geo_ref, capacity, width):
    row0, row1, col0, col1 = (geo_ref[k] for k in range(4))
    area0, area1 = row0 * col0, row1 * col1
    position = lax.broadcasted_iota(jnp.int32, (capacity, width), 0)
    first = position < area0
    second = jnp.logical_and(position >= area0, position < area0 + area1)
    widths = jnp.maximum(jnp.where(second, col1, col0), 2)
    heights = jnp.where(second, row1, row0)
    local = position - jnp.where(second, area0, 0)
    row = ((local.astype(F32) + 0.5) / widths.astype(F32)).astype(jnp.int32)
    col = local - row * widths
    return first, second, row, col, heights, widths


def pack_kernel(*refs):
    sources, (a_ref, b_ref, v_ref), held, semaphores = refs[:8], refs[8:11], refs[11:19], refs[19]
    copies = [pltpu.make_async_copy(source, ref, semaphores.at[i]) for i, (source, ref) in enumerate(zip(sources, held))]
    for copy in copies:
        copy.start()
    for copy in copies:
        copy.wait()
    q_ref, kv_ref, red_ref, proj_ref, up_ref, down_ref, vm_ref, vh_ref = held
    cw = q_ref.shape[0]

    def wider(ref):
        return ref[...].astype(F32)

    kv = wider(kv_ref).T
    a_ref[0] = lanes(wider(red_ref), wider(q_ref), kv[:cw], kv[cw:], wider(proj_ref)).astype(BF16)
    up, down = wider(up_ref), wider(down_ref)
    columns = (down[:, :RUN], down[:, RUN:], up[:cw], up[cw:])
    b_ref[0] = lanes(*[c[:, :128] for c in columns], *[c[:, 128:] for c in columns]).astype(BF16)
    v_ref[0] = jnp.zeros_like(v_ref[0])
    both = lanes(wider(vm_ref), wider(vh_ref))
    v_ref[0, : both.shape[0], : both.shape[1]] = both.astype(BF16)


def pack(arguments, piece, vpiece):
    vmem = pl.BlockSpec(memory_space=pltpu.VMEM)
    return pl.pallas_call(
        pack_kernel,
        out_shape=[jax.ShapeDtypeStruct((1,) + shape, BF16) for shape in (piece, piece, vpiece)],
        in_specs=[pl.BlockSpec(memory_space=pl.ANY)] * len(arguments),
        out_specs=[vmem] * 3,
        scratch_shapes=[pltpu.VMEM(v.shape, v.dtype) for v in arguments] + [pltpu.SemaphoreType.DMA((len(arguments),))],
        compiler_params=pltpu.CompilerParams(vmem_limit_bytes=60 * 2**20),
    )(*arguments)


def prepare_kernel(
    rows_hbm, cols_hbm, tok_hbm, x_ref, n1_ref, r1_ref, chosen_ref, live_ref, geo_ref,
    rows_ref, cols_ref, tok_ref, semaphores,
):
    copies = [
        pltpu.make_async_copy(source, target, semaphores.at[i])
        for i, (source, target) in enumerate(((rows_hbm, rows_ref), (cols_hbm, cols_ref), (tok_hbm, tok_ref)))
    ]
    for copy in copies:
        copy.start()
    for copy in copies:
        copy.wait()
    capacity = tok_ref.shape[1]
    for j in range(2):
        geo_ref[j] = rows_ref[j]
        geo_ref[2 + j] = cols_ref[j]
    tokens = tok_ref[...].astype(F32).T
    x_ref[...] = tokens
    normed, inverse = normalise(tokens)
    n1_ref[...] = normed
    r1_ref[...] = inverse
    chosen_ref[...] = one_hot(rows_ref, cols_ref, capacity)
    area0, area1 = rows_ref[0] * cols_ref[0], rows_ref[1] * cols_ref[1]
    quarter0, quarter1 = area0 // 4, area1 // 4
    token = lax.broadcasted_iota(jnp.int32, live_ref.shape, 0)
    key = lax.broadcasted_iota(jnp.int32, live_ref.shape, 1)
    live = ((token < area0) & (key < quarter0)) | (
        (token >= area0) & (token < area0 + area1) & (key >= quarter0) & (key < quarter0 + quarter1)
    )
    live_ref[...] = jnp.where(live, 1.0, 0.0)


def prepare(img_rows, img_cols, tokens):
    width, capacity = tokens.shape
    keys = capacity // 4
    vmem, smem = (pl.BlockSpec(memory_space=space) for space in (pltpu.VMEM, pltpu.SMEM))
    outputs = (
        ((capacity, width), F32), ((capacity, width), F32), ((capacity, 1), F32), ((capacity, capacity), BF16),
        ((capacity, keys), F32), ((4,), jnp.int32),
    )
    return pl.pallas_call(
        prepare_kernel,
        out_shape=[jax.ShapeDtypeStruct(shape, kind) for shape, kind in outputs],
        in_specs=[pl.BlockSpec(memory_space=pl.ANY)] * 3,
        out_specs=[vmem] * 5 + [smem],
        scratch_shapes=[
            pltpu.SMEM((2,), jnp.int32), pltpu.SMEM((2,), jnp.int32), pltpu.VMEM((width, capacity), BF16),
            pltpu.SemaphoreType.DMA((3,)),
        ],
        compiler_params=pltpu.CompilerParams(vmem_limit_bytes=60 * 2**20),
        cost_estimate=pl.CostEstimate(flops=2 * 10**9, bytes_accessed=0, transcendentals=0),
    )(img_rows, img_cols, tokens)


def attend_kernel(
    tuned,
    geo_ref, cot_ref, x_ref, n1_ref, chosen_ref, live_ref, own_ref, oth_ref, vec_ref,
    x2_ref, h1_ref, patch_ref, nk_ref, rk_ref, kn_ref, q_ref, kb_ref, vb_ref,
    p_ref, o_ref, wr_ref, wq_ref, wkv_ref, wp_ref, mv_ref, hv_ref, gy_ref, gyt_ref, mask_ref,
    score_ref,
):
    me = my_index(tuned)
    capacity, width = x_ref.shape
    cw, rn = width // PARTS_W, width // PARTS_N
    keys = capacity // 4
    dim = width // HEADS

    pieces = [vec_ref[n ^ (me & 3)].astype(F32) for n in range(PARTS_N)]
    mv = lanes(*[p[:, :rn] for p in pieces])
    mv_ref[...] = mv
    runs = [p[:, rn + e * RUN : rn + (e + 1) * RUN] for p in pieces for e in range(2)]
    hv_ref[...] = lanes(*[r[:, :128] for r in runs], *[r[:, 128:] for r in runs])

    for pair in range(PARTS_W // 2):
        got = [
            [piece_of(own_ref, oth_ref, w * PARTS_N + n, me) for n in range(PARTS_N)]
            for w in (2 * pair, 2 * pair + 1)
        ]
        at = pl.ds(pair * 2 * cw, 2 * cw)
        for n in range(PARTS_N):
            wr_ref[n, at, :] = rows_of(got[0][n][:, :width], got[1][n][:, :width]).astype(BF16)

        def unit(w, k):
            return lanes(*[got[w][n][:, width + k * rn : width + (k + 1) * rn] for n in range(PARTS_N)])

        wq_ref[at, :] = rows_of(unit(0, 0), unit(1, 0)).astype(BF16)
        wkv_ref[pl.ds(pair * 4 * cw, 4 * cw), :] = rows_of(
            unit(0, 1), unit(0, 2), unit(1, 1), unit(1, 2)
        ).astype(BF16)
        wp_ref[at, :] = rows_of(unit(0, 3), unit(1, 3)).astype(BF16)

    h1 = (n1_ref[...] * mv[0:1] + mv[1:2]).astype(BF16)
    h1_ref[...] = h1
    q = (dot_nt(h1, wq_ref[...]) + mv[2:3]).astype(BF16)
    q_ref[...] = q

    patches = dot_nn(chosen_ref[...], h1).astype(BF16)
    patch_ref[...] = patches
    reduced = mv[4:5]
    for n in range(4):
        reduced = reduced + dot_nt(patches[n * keys : (n + 1) * keys], wr_ref[n])
    nk, rk = normalise(reduced)
    nk_ref[...] = nk
    rk_ref[...] = rk
    kn = (nk * mv[5:6] + mv[6:7]).astype(BF16)
    kn_ref[...] = kn
    kv = dot_nt(kn, wkv_ref[...])
    k = kv[:, :width].astype(BF16).astype(F32)
    v = (kv[:, width:] + mv[3:4]).astype(BF16).astype(F32)
    lane = lax.broadcasted_iota(jnp.int32, (keys, width), 1)
    for h in range(HEADS):
        inside = (lane >= h * dim) & (lane < (h + 1) * dim)
        at = pl.ds(h * keys, keys)
        kb_ref[at, :] = jnp.where(inside, k, 0.0).astype(BF16)
        vb_ref[at, :] = jnp.where(inside, v, 0.0).astype(BF16)

    score_ref[...] = dot_nt(q, kb_ref[...]) * dim ** (-0.5)
    def soften(i, carry):
        at = pl.ds(pl.multiple_of(i * 64, 64), 64)
        live = live_ref[at, :] > 0.5
        for h in range(HEADS):
            lane_at = pl.ds(h * keys, keys)
            s = jnp.where(live, score_ref[at, lane_at], MASKED)
            e = jnp.exp(s - jnp.max(s, axis=-1, keepdims=True))
            p_ref[at, lane_at] = e / jnp.sum(e, axis=-1, keepdims=True)
        return carry

    lax.fori_loop(0, capacity // 64, soften, 0, unroll=True)
    o = dot_nn(p_ref[...].astype(BF16), vb_ref[...]).astype(BF16)
    o_ref[...] = o
    x2_ref[...] = x_ref[...] + dot_nt(o, wp_ref[...]) + mv[7:8]
    mask_gradient(geo_ref, cot_ref, gy_ref, gyt_ref, mask_ref)


def one_hot(rows_ref, cols_ref, capacity):
    row0, row1, col0, col1 = rows_ref[0], rows_ref[1], cols_ref[0], cols_ref[1]
    area0, area1 = row0 * col0, row1 * col1
    quarter0, quarter1 = area0 // 4, area1 // 4
    keys = capacity // 4
    index = lax.broadcasted_iota(jnp.int32, (capacity, 128), 0)
    tap = index // keys
    key = index - tap * keys
    first = key < quarter0
    second = jnp.logical_and(key >= quarter0, key < quarter0 + quarter1)
    width = jnp.maximum(jnp.where(second, col1, col0), 2)
    half = width // 2
    local = key - jnp.where(second, quarter0, 0)
    row = ((local.astype(F32) + 0.5) / half.astype(F32)).astype(jnp.int32)
    col = local - row * half
    token = jnp.where(second, area0, 0) + (2 * row + tap // 2) * width + 2 * col + tap % 2
    token = jnp.where(first | second, token, -1)
    lane = lax.broadcasted_iota(jnp.int32, (capacity, 128), 1)
    return lanes(
        *[jnp.where(token == lane + t * 128, 1.0, 0.0).astype(BF16) for t in range(capacity // 128)]
    )


def mask_gradient(geo_ref, cot_ref, gy_ref, gyt_ref, mask_ref):
    width, capacity = cot_ref.shape
    area = geo_ref[0] * geo_ref[2] + geo_ref[1] * geo_ref[3]
    position = lax.broadcasted_iota(jnp.int32, (width, capacity), 1)
    gyt = jnp.where(position < area, cot_ref[...].astype(F32), 0.0)
    gyt_ref[...] = gyt.astype(BF16)
    gy_ref[...] = gyt.T.astype(BF16)
    first, second, row, col, heights, widths = token_geometry(geo_ref, capacity, 128)
    live = first | second
    start = lax.broadcasted_iota(jnp.int32, (capacity, 128), 0) // TILE * TILE
    late = start >= geo_ref[0] * geo_ref[2]
    early = jnp.logical_not(late)
    usual = (late & second) | (early & first)
    apart = second & early
    conditions = (
        live & (col > 0),
        live & (col < widths - 1),
        usual & (row > 0),
        usual & (row < heights - 1),
        apart & (row > 0),
        apart & (row < heights - 1),
        live,
    )
    for k, condition in enumerate(conditions):
        mask_ref[k] = jnp.where(condition, 1.0, 0.0)


def place_pieces(ref, core, me, wu_ref, wd_ref):
    cw = ref.shape[1]
    rn = 2 * cw
    tails = 128 * PARTS_W
    for x in range(PARTS_N // 2):
        n = 2 * x + core
        pieces = [ref[mixed_slot(w * PARTS_N + n, me)].astype(F32) for w in range(PARTS_W)]
        lane_at = pl.ds(pl.multiple_of(256 * n, 256), 256)
        for pair in range(PARTS_W // 2):
            value = rows_of(pieces[2 * pair][:, :256], pieces[2 * pair + 1][:, :256])
            wd_ref[pl.ds(pair * 2 * cw, 2 * cw), lane_at] = value.astype(BF16)
        at = pl.ds(pl.multiple_of(rn * n, 16), rn)
        for w, p in enumerate(pieces):
            wu_ref[at, pl.ds(128 * w, 128)] = rows_of(p[:, 256:384], p[:, 384:512]).astype(BF16)
        ends = [rows_of(p[:, 512 + 2 * REST : 512 + 3 * REST], p[:, 512 + 3 * REST :]) for p in pieces]
        wu_ref[at, pl.ds(tails, REST * PARTS_W)] = lanes(*ends).astype(BF16)


def prepare_two_kernel(tuned, x2_ref, mv_ref, own_ref, n2_ref, r2_ref, h2_ref, h2t_ref, wu_ref, wd_ref):
    me = my_index(tuned)
    place_pieces(own_ref, me & 1, me, wu_ref, wd_ref)
    normed, inverse = normalise(x2_ref[...])
    n2_ref[...] = normed
    r2_ref[...] = inverse
    h2 = normed * mv_ref[8:9, :] + mv_ref[9:10, :]
    h2_ref[...] = h2.astype(BF16)
    width = h2.shape[1]
    h2t_ref[:width, :] = h2.T.astype(BF16)
    h2t_ref[width:, :] = jnp.ones((h2t_ref.shape[0] - width, h2.shape[0]), BF16)


def ffn_kernel(
    tuned,
    geo_ref, h2_ref, h2t_ref, gy_ref, gyt_ref, mask_ref, own_ref, oth_ref, hv_ref, wu_in_ref, wd_in_ref,
    gown_ref, gsend_ref, act_ref, df_ref, hg_ref, wu_ref, wd_ref,
    f_ref, gm_ref, gp_ref, dc_ref, ul_ref, ur_ref, g0_ref, u0_ref, da_ref,
    upg_ref, dng_ref,
):
    me = my_index(tuned)
    capacity, width = h2_ref.shape
    hidden = hv_ref.shape[1]
    cw, rn = width // PARTS_W, width // PARTS_N
    tiles = capacity // TILE
    tails = 128 * PARTS_W

    place_pieces(oth_ref, 1 - (me & 1), me, wu_ref, wd_ref)
    for pair in range(PARTS_W // 2):
        got = [
            rows_of(*[piece_of(own_ref, oth_ref, w * PARTS_N + n, me, 4, 5, mixed_slot) for w in (2 * pair, 2 * pair + 1)])
            for n in range(PARTS_N)
        ]
        ends = lanes(*[g[:, : 2 * REST] for g in got]).astype(BF16)
        wd_ref[pl.ds(pair * 2 * cw, 2 * cw), pl.ds(tails, 2 * REST * PARTS_N)] = ends

    area, w0, w1 = geo_ref[0] * geo_ref[2], geo_ref[2], geo_ref[3]
    split = pl.multiple_of(jnp.minimum(area // TILE, tiles - 1) * TILE, TILE)

    for ref in (f_ref, gm_ref, gp_ref, dc_ref, ul_ref, ur_ref):
        ref[:, :PAD, :] = jnp.zeros((ref.shape[0], PAD, 128), F32)
        ref[:, PAD + capacity :, :] = jnp.zeros((ref.shape[0], PAD, 128), F32)


    def fold(values):
        return jnp.sum(values.reshape(TILE // 8, 8, 128), axis=0)

    halves = CHUNK // 128
    chunks = hidden // CHUNK
    zero = jnp.zeros((8, 128), F32)

    def columns(c):
        return pl.ds(pl.multiple_of(c * CHUNK, CHUNK), CHUNK)

    def vector(c, k, j):
        return hv_ref[k : k + 1, pl.ds(pl.multiple_of(c * CHUNK + j * 128, 128), 128)]

    def put_vector(c, k, j, value):
        hg_ref[k : k + 1, pl.ds(pl.multiple_of(c * CHUNK + j * 128, 128), 128)] = value

    def act_grad(c, at):
        da_ref[at, :] = dot_nn(gy_ref[at, :], wd_ref[:, columns(c)])

    def down_grad(c, at):
        dng_ref[at, columns(c)] = dot_nn(gyt_ref[at, :], act_ref[:, columns(c)])

    def tasks(product, c, rows, size):
        return [functools.partial(product, c, pl.ds(r, min(size, rows - r))) for r in range(0, rows, size)]

    def interleave(steps, products):
        done = 0
        for i, step in enumerate(steps):
            step()
            while done < len(products) and done * len(steps) < (i + 1) * len(products):
                products[done]()
                done += 1

    def chunk_step(c, carry):
        v = [[vector(c, k, j) for k in range(11)] for j in range(halves)]

        def taps_of(j, r, mask_left, mask_right):
            here = f_ref[c * halves + j, pl.ds(PAD + r, TILE), :]
            left = f_ref[c * halves + j, pl.ds(PAD + r - 1, TILE), :] * mask_left
            right = f_ref[c * halves + j, pl.ds(PAD + r + 1, TILE), :] * mask_right
            return left, here, right

        def row_length(r):
            return jnp.where(area > r, w0, w1)

        def column_taps(r):
            at = pl.ds(r, TILE)
            masks = mask_ref[0, at, :], mask_ref[1, at, :]
            for j in range(halves):
                left, here, right = taps_of(j, r, *masks)
                u = v[j]
                gm_ref[j, pl.ds(PAD + r, TILE), :] = u[2] * left + u[3] * here + u[4] * right
                g0_ref[j, at, :] = u[1] + u[5] * left + u[6] * here + u[7] * right
                gp_ref[j, pl.ds(PAD + r, TILE), :] = u[8] * left + u[9] * here + u[10] * right

        def column_taps_split():
            at = pl.ds(split, TILE)
            for j in range(halves):
                g0_ref[j, at, :] += (
                    mask_ref[4, at, :] * gm_ref[j, pl.ds(PAD + split - w1, TILE), :]
                    + mask_ref[5, at, :] * gp_ref[j, pl.ds(PAD + split + w1, TILE), :]
                )

        conv_sums = [zero] * halves

        def activate(r):
            at = pl.ds(r, TILE)
            length = row_length(r)
            above, below = mask_ref[2, at, :], mask_ref[3, at, :]
            for j in range(halves):
                conv = (
                    g0_ref[j, at, :]
                    + above * gm_ref[j, pl.ds(PAD + r - length, TILE), :]
                    + below * gp_ref[j, pl.ds(PAD + r + length, TILE), :]
                )
                half = 0.5 * (1.0 + lax.erf(conv * 2.0 ** (-0.5)))
                act_ref[at, pl.ds(pl.multiple_of(c * CHUNK + j * 128, 128), 128)] = (conv * half).astype(BF16)
                slope = half + conv * ((2.0 * math.pi) ** (-0.5) * jnp.exp2(conv * conv * (-0.5 / math.log(2.0))))
                value = da_ref[at, pl.ds(j * 128, 128)] * slope
                dc_ref[j, pl.ds(PAD + r, TILE), :] = value
                conv_sums[j] = conv_sums[j] + fold(value)

        tap_sums = [[zero] * 9 for _ in range(halves)]

        def tap_back(r):
            at = pl.ds(r, TILE)
            length = row_length(r)
            masks = [mask_ref[k, at, :] for k in range(4)]
            for j in range(halves):
                left, here, right = taps_of(j, r, *masks[:2])
                u = v[j]
                below = masks[3] * dc_ref[j, pl.ds(PAD + r + length, TILE), :]
                level = dc_ref[j, pl.ds(PAD + r, TILE), :]
                above = masks[2] * dc_ref[j, pl.ds(PAD + r - length, TILE), :]
                ul_ref[j, pl.ds(PAD + r, TILE), :] = u[2] * below + u[5] * level + u[8] * above
                u0_ref[j, at, :] = u[3] * below + u[6] * level + u[9] * above
                ur_ref[j, pl.ds(PAD + r, TILE), :] = u[4] * below + u[7] * level + u[10] * above
                grads = [fold(d * f) for d in (below, level, above) for f in (left, here, right)]
                tap_sums[j] = [a + b for a, b in zip(tap_sums[j], grads)]

        def tap_back_split():
            at, padded = pl.ds(split, TILE), pl.ds(PAD + split, TILE)
            masks = [mask_ref[k, at, :] for k in (0, 1, 4, 5)]
            for j in range(halves):
                left, here, right = taps_of(j, split, *masks[:2])
                u = v[j]
                below = masks[3] * dc_ref[j, pl.ds(PAD + split + w1, TILE), :]
                above = masks[2] * dc_ref[j, pl.ds(PAD + split - w1, TILE), :]
                ul_ref[j, padded, :] += u[2] * below + u[8] * above
                u0_ref[j, at, :] += u[3] * below + u[9] * above
                ur_ref[j, padded, :] += u[4] * below + u[10] * above
                grads = [fold(d * f) for d in (below, above) for f in (left, here, right)]
                tap_sums[j] = [a + b for a, b in zip(tap_sums[j], grads[:3] + [zero] * 3 + grads[3:])]

        def spread_back(r):
            at = pl.ds(r, TILE)
            mask_left, mask_right = mask_ref[0, at, :], mask_ref[1, at, :]
            for j in range(halves):
                value = (
                    u0_ref[j, at, :]
                    + mask_left * ur_ref[j, pl.ds(PAD + r - 1, TILE), :]
                    + mask_right * ul_ref[j, pl.ds(PAD + r + 1, TILE), :]
                ).astype(BF16)
                df_ref[at, pl.ds(pl.multiple_of(c * CHUNK + j * 128, 128), 128)] = value

        def steps(step):
            return [functools.partial(step, r) for r in range(0, capacity, TILE)]

        interleave(steps(column_taps) + [column_taps_split], tasks(act_grad, c, capacity, MROWS))
        interleave(
            steps(activate),
            [],
        )
        interleave(steps(tap_back) + [tap_back_split], tasks(down_grad, c, width, MROWS))
        interleave(steps(spread_back), [])
        for j in range(halves):
            put_vector(c, 1, j, column_sum(conv_sums[j]))
            for k in range(9):
                put_vector(c, 2 + k, j, column_sum(tap_sums[j][k]))
        return carry

    for c in range(chunks):
        value = dot_nn(h2_ref[...], wu_ref[:, c * CHUNK : (c + 1) * CHUNK])
        for j in range(halves):
            bias = hv_ref[0:1, pl.ds(c * CHUNK + j * 128, 128)]
            f_ref[c * halves + j, pl.ds(PAD, capacity), :] = value[:, j * 128 : (j + 1) * 128] + bias
    lax.fori_loop(0, chunks, chunk_step, 0)
    upg_ref[...] = dot_nn(h2t_ref[...], df_ref[...])
    hg_ref[0:1, :] = upg_ref[width : width + 1, :]
    hg_ref[11:, :] = jnp.zeros((hg_ref.shape[0] - 11, hidden), F32)

    def value_of(w, n):
        down = pl.ds(w * cw, cw)
        up = [pl.ds(n * rn + e * cw, cw) for e in range(2)]
        return lanes(
            dng_ref[down, pl.ds(256 * n, 256)],
            *[upg_ref[e, pl.ds(128 * w, 128)] for e in up],
            dng_ref[down, pl.ds(tails + 2 * REST * n, 2 * REST)],
            *[upg_ref[e, pl.ds(tails + REST * w, REST)] for e in up],
        )

    store_pieces(gown_ref, gsend_ref, me, value_of, mixed_slot)


def store_pieces(own_ref, send_ref, me, value_of, order):
    even = (me & 1) == 0
    for w in range(PARTS_W):
        for x in range(PARTS_N // 2):
            first, second = value_of(w, 2 * x), value_of(w, 2 * x + 1)
            slot0, slot1 = (order(w * PARTS_N + 2 * x + c, me) for c in range(2))
            own_ref[jnp.where(even, slot0, slot1)] = jnp.where(even, first, second).astype(BF16)
            send_ref[jnp.where(even, slot1, slot0)] = jnp.where(even, second, first).astype(BF16)


def norm_two_back_kernel(df_ref, wu_ref, n2_ref, r2_ref, gy_ref, mv_ref, dx2_ref, mg_ref, dh2_ref):
    capacity, width = n2_ref.shape
    dh2_ref[...] = dot_nt(df_ref[...], wu_ref[...])

    def norm_back(i, carry):
        at = pl.ds(pl.multiple_of(i * 64, 64), 64)
        gy = gy_ref[at, :].astype(F32)
        grad, normed = dh2_ref[at, :], n2_ref[at, :]
        dx2_ref[at, :] = gy + normalise_back(grad, normed, r2_ref[at, :], mv_ref[8:9, :])
        return tuple(a + column_sum(b) for a, b in zip(carry, (grad * normed, grad, gy)))

    zero = jnp.zeros((1, width), F32)
    sums = lax.fori_loop(0, capacity // 64, norm_back, (zero, zero, zero), unroll=True)
    mg_ref[...] = jnp.zeros_like(mg_ref)
    for k in range(3):
        mg_ref[8 + k : 9 + k, :] = sums[k]


def score_back_kernel(dx2_ref, vb_ref, p_ref, o_ref, wp_ref, gp_ref, dob_ref, ds_ref, bp_ref, dp_ref):
    capacity = dx2_ref.shape[0]
    keys = capacity // 4
    datt = dx2_ref[...].astype(BF16)
    bp_ref[...] = column_sum(datt.astype(F32))
    gp_ref[...] = dot_tn(datt, o_ref[...])
    dob = dot_nn(datt, wp_ref[...]).astype(BF16)
    dob_ref[...] = dob
    dp_ref[...] = dot_nt(dob, vb_ref[...])

    def soften_back(i, carry):
        at = pl.ds(pl.multiple_of(i * 64, 64), 64)
        for h in range(HEADS):
            lane_at = pl.ds(h * keys, keys)
            p = p_ref[at, lane_at]
            dp = dp_ref[at, lane_at]
            row = jnp.sum(p * dp, axis=-1, keepdims=True)
            ds_ref[at, lane_at] = (p * (dp - row)).astype(BF16)
        return carry

    lax.fori_loop(0, capacity // 64, soften_back, 0, unroll=True)


def attend_back_kernel(
    tuned,
    dob_ref, ds_ref, gp_ref, h1_ref, patch_ref, nk_ref, rk_ref, kn_ref, q_ref, kb_ref, p_ref,
    wr_ref, wkv_ref, mv_ref,
    gown_ref, gsend_ref, dq_ref, dpatch_ref, vk_ref,
    gr_ref, gq_ref, gkv_ref,
):
    me = my_index(tuned)
    capacity, width = h1_ref.shape
    cw, rn = width // PARTS_W, width // PARTS_N
    keys = capacity // 4
    dim = width // HEADS
    scale = dim ** (-0.5)

    ds = ds_ref[...]
    dq = (dot_nn(ds, kb_ref[...]) * scale).astype(BF16)
    dq_ref[...] = dq
    dk_all = dot_tn(ds, q_ref[...])
    dv_all = dot_tn(p_ref[...].astype(BF16), dob_ref[...])
    lane = lax.broadcasted_iota(jnp.int32, (keys, width), 1)
    dk = jnp.zeros((keys, width), F32)
    dv = jnp.zeros((keys, width), F32)
    for h in range(HEADS):
        inside = (lane >= h * dim) & (lane < (h + 1) * dim)
        dk = jnp.where(inside, dk_all[h * keys : (h + 1) * keys], dk)
        dv = jnp.where(inside, dv_all[h * keys : (h + 1) * keys], dv)
    dk = (dk * scale).astype(BF16)
    dv = dv.astype(BF16)
    gq_ref[...] = dot_tn(dq, h1_ref[...])
    kn = kn_ref[...]
    gkv_ref[pl.ds(0, width), :] = dot_tn(dk, kn)
    gkv_ref[pl.ds(width, width), :] = dot_tn(dv, kn)
    dkn = dot_nn(dk, wkv_ref[pl.ds(0, width), :]) + dot_nn(dv, wkv_ref[pl.ds(width, width), :])
    nk = nk_ref[...]
    dsr = normalise_back(dkn, nk, rk_ref[...], mv_ref[5:6, :]).astype(BF16)
    vk_ref[...] = rows_of(
        column_sum(dq.astype(F32)),
        column_sum(dv.astype(F32)),
        column_sum(dsr.astype(F32)),
        column_sum(dkn * nk),
        column_sum(dkn),
        jnp.zeros((3, width), F32),
    )
    for n in range(4):
        at = pl.ds(n * keys, keys)
        gr_ref[n] = dot_tn(dsr, patch_ref[at, :])
        dpatch_ref[at, :] = dot_nn(dsr, wr_ref[n])

    def value_of(w, n):
        at, lane_at = pl.ds(w * cw, cw), pl.ds(n * rn, rn)
        return lanes(
            gr_ref[n, at, :],
            gq_ref[at, lane_at],
            gkv_ref[pl.ds(2 * w * cw, cw), lane_at],
            gkv_ref[pl.ds(2 * w * cw + cw, cw), lane_at],
            gp_ref[at, lane_at],
        )

    store_pieces(gown_ref, gsend_ref, me, value_of, round_slot)


def token_grad_kernel(dx2_ref, dh1_ref, n1_ref, r1_ref, mv_ref, tg_ref):
    value = dx2_ref[...] + normalise_back(dh1_ref[...], n1_ref[...], r1_ref[...], mv_ref[0:1, :])
    tg_ref[...] = value.T.astype(BF16)


def mixed_kernel(x2_ref, act_ref, wd_ref, mv_ref, mask_ref, mixed_ref):
    width = x2_ref.shape[1]
    occupied = mask_ref[6]
    occupied = lanes(*([occupied] * (width // 128)), occupied[:, : width % 128])
    mixed = x2_ref[...] + dot_nt(act_ref[...], wd_ref[...]) + mv_ref[10:11, :]
    mixed_ref[...] = (mixed * occupied).T.astype(BF16)


def fold_rows(value, unit):
    rest = value[8:]
    beside = lanes(rest[:, : 3 * unit], jnp.zeros((8, 256 - 3 * unit), F32))
    below = lanes(rest[:, 3 * unit :], jnp.zeros((8, 256 - 2 * unit), F32))
    return lanes(value[:8], (beside + pltpu.roll(below, 3, 0))[:, : 3 * unit])


def unfold_rows(value, unit):
    beside = lanes(value[:, 5 * unit :], jnp.zeros((8, 256 - 3 * unit), F32))
    below = pltpu.roll(beside, 5, 0)
    return rows_of(value[:, : 5 * unit], lanes(beside[:, : 3 * unit], below[:, : 2 * unit]))


def token_back_kernel(
    tuned,
    dq_ref, dpatch_ref, n1_ref, chosen_ref, wq_ref, mg_ref, hg_ref, vk_ref, bp_ref,
    dh1_ref, vown_ref, vsend_ref,
):
    me = my_index(tuned)
    width = n1_ref.shape[1]
    rn = width // PARTS_N
    chosen = chosen_ref[...]
    high = dpatch_ref[...].astype(BF16)
    low = (dpatch_ref[...] - high.astype(F32)).astype(BF16)
    dh1 = dot_nn(dq_ref[...], wq_ref[...]) + dot_tn(chosen, high) + dot_tn(chosen, low)
    n1 = n1_ref[...]
    vk = vk_ref[...]
    dh1_ref[...] = dh1
    sums = rows_of(column_sum(dh1 * n1), column_sum(dh1), vk[0:5], bp_ref[...], mg_ref[8:16, :])
    hg = hg_ref[...]
    value = []
    for n in range(PARTS_N):
        parts = []
        for w in (2 * n, 2 * n + 1):
            parts += [hg[:, 128 * w : 128 * (w + 1)], hg[:, 1024 + REST * w : 1024 + REST * (w + 1)]]
        value.append(fold_rows(lanes(sums[:, n * rn : (n + 1) * rn], *parts), rn))
    even = (me & 1) == 0
    for x in range(2):
        slot = x ^ ((me >> 1) & 1)
        vown_ref[slot] = jnp.where(even, value[2 * x], value[2 * x + 1]).astype(BF16)
        vsend_ref[slot] = jnp.where(even, value[2 * x + 1], value[2 * x]).astype(BF16)


def total_of(refs):
    value = refs[0][...].astype(F32)
    for ref in refs[1:]:
        value = value + ref[...].astype(F32)
    return value


def halve_kernel(keep_ref, got_ref, low_ref, high_ref):
    half = low_ref.shape[0]
    low_ref[...] = (keep_ref[:half].astype(F32) + got_ref[:half].astype(F32)).astype(BF16)
    high_ref[...] = (keep_ref[half:].astype(F32) + got_ref[half:].astype(F32)).astype(BF16)


def core_high_kernel(own_ref, got_ref, high_ref):
    half = high_ref.shape[0]
    high_ref[...] = (own_ref[half:].astype(F32) + got_ref[...].astype(F32)).astype(BF16)


def core_low_kernel(own_ref, core_ref, got_ref, low_ref, high_ref):
    half = low_ref.shape[0]
    total = own_ref[: 2 * half].astype(F32) + core_ref[...].astype(F32) + got_ref[...].astype(F32)
    low_ref[...] = total[:half].astype(BF16)
    high_ref[...] = total[half:].astype(BF16)


def halve_core_kernel(keep_ref, got_ref, vkeep_ref, vgot_ref, low_ref, vlow_ref, send_ref):
    half = low_ref.shape[0]
    low_ref[...] = (keep_ref[:half].astype(F32) + got_ref[:half].astype(F32)).astype(BF16)
    parts = [keep_ref[half + k].astype(F32) + got_ref[half + k].astype(F32) for k in range(half)]
    vector = total_of((vkeep_ref, vgot_ref))
    vlow_ref[...] = vector.astype(BF16)
    send_ref[...] = rows_of(*parts, vector[0], vector[1]).astype(BF16)


def halve_round_kernel(tuned, keep_ref, vkeep_ref, got_ref, low_ref, vlow_ref, send_ref):
    half, cw = low_ref.shape[:2]
    rows = vkeep_ref.shape[1]
    got = got_ref[...].astype(F32)
    parts = [keep_ref[k].astype(F32) + got[k * cw : (k + 1) * cw] for k in range(2 * half)]
    for k in range(half):
        low_ref[k] = parts[k].astype(BF16)
    got0, got1 = (got[2 * half * cw + k * rows : 2 * half * cw + (k + 1) * rows] for k in range(2))
    keep0, keep1 = vkeep_ref[0].astype(F32), vkeep_ref[1].astype(F32)
    even = (my_index(tuned) & 1) == 0
    low = keep0 + jnp.where(even, got0, got1)
    vlow_ref[0] = low.astype(BF16)
    send_ref[...] = rows_of(*parts[half:], jnp.where(even, keep1 + got1, low)).astype(BF16)


def quarter_vector_kernel(keep_ref, vkeep_ref, got_ref, *out_refs):
    cw = keep_ref.shape[1]
    got = got_ref[...].astype(F32)
    vector = vkeep_ref[0].astype(F32) + got[4 * cw :]
    for k, ref in enumerate(out_refs):
        ref[...] = rows_of(keep_ref[k].astype(F32) + got[k * cw : (k + 1) * cw], vector).astype(BF16)


def finish_kernel(
    a_ref, b_ref, c_ref, d_ref, ffn_ref, ffn_got_ref,
    q_ref, kv_ref, red_ref, proj_ref, up_ref, down_ref, vm_ref, vh_ref,
):
    total = total_of((a_ref, b_ref, c_ref, d_ref))
    cw, width = red_ref.shape
    rn = q_ref.shape[1]
    red_ref[...] = total[:cw, :width]
    unit = [total[:cw, width + k * rn : width + (k + 1) * rn] for k in range(4)]
    q_ref[...] = unit[0]
    kv_ref[...] = rows_of(unit[1], unit[2]).T
    proj_ref[...] = unit[3]
    vector = unfold_rows(total[cw:], rn)
    vm_ref[...] = vector[: vm_ref.shape[0], :rn]
    vh_ref[...] = vector[: vh_ref.shape[0], rn:]
    total = total_of((ffn_ref, ffn_got_ref))[0]
    columns = [
        lanes(total[:, 128 * k : 128 * (k + 1)], total[:, 512 + REST * k : 512 + REST * (k + 1)]) for k in range(4)
    ]
    down_ref[...] = lanes(*columns[:2])
    up_ref[...] = rows_of(*columns[2:])


def call(kernel, inputs, outputs, scratch=(), scalars=0, limit=24, flops=0, moved=0, aliases={}):
    vmem = pl.BlockSpec(memory_space=pltpu.VMEM)
    smem = pl.BlockSpec(memory_space=pltpu.SMEM)
    return pl.pallas_call(
        kernel,
        out_shape=[jax.ShapeDtypeStruct(shape, kind) for shape, kind in outputs],
        in_specs=[smem] * scalars + [vmem] * (len(inputs) - scalars),
        out_specs=[vmem] * len(outputs),
        scratch_shapes=[pltpu.VMEM(shape, kind) for shape, kind in scratch],
        input_output_aliases=aliases,
        compiler_params=pltpu.CompilerParams(vmem_limit_bytes=limit * 2**20),
        cost_estimate=pl.CostEstimate(flops=flops, bytes_accessed=moved, transcendentals=0),
    )(*inputs)


def after(value, *others):
    return lax.optimization_barrier((value, *others))[0]


def on_device(
    mesh_shape,
    tokens, cotangent, img_rows, img_cols,
    q_weight, kv_weight, reduce_weight, proj_weight, up_weight, down_weight, vec_model, vec_hidden,
):
    wide, narrow = mesh_shape
    tuned = (wide, narrow) == (PARTS_W, PARTS_N)
    capacity, width = tokens.shape
    hidden = vec_hidden.shape[1] * narrow
    cw, rn = width // PARTS_W, width // PARTS_N
    keys = capacity // 4
    piece = (cw, 2 * width)
    vpiece, gpiece = (16, 2 * width), (8, 2 * width)

    def join(*parts):
        return jnp.concatenate(parts, axis=0)

    def swap(value, mask, other=None):
        masks = (mask, mask if other is None else other)
        pairs = [(i, i ^ masks[i & 1]) for i in range(wide * narrow)]
        return lax.ppermute(value, ("wide", "narrow"), pairs)

    tokens_f32 = ((capacity, width), F32)
    tokens_low = ((capacity, width), BF16)
    x, n1, r1, chosen, live, geo = prepare(img_rows, img_cols, tokens.T)
    if tuned:
        pack_a, pack_b, pack_v = pack(
            (
                q_weight.T, kv_weight, reduce_weight.T, proj_weight.T, up_weight, down_weight.T,
                vec_model, vec_hidden,
            ),
            piece, vpiece,
        )
        line_a = [swap(pack_a, m) for m in (8, 16, 24)]
        got_b, got_v = swap(pack_b, 2, 4), swap(pack_v, 1)
        *line_a, got_b, got_v = lax.optimization_barrier((*line_a, got_b, got_v, x, n1, chosen))[:5]
        buf_a, buf_b, vecs = join(pack_a, *line_a), join(pack_b, got_b), join(pack_v, got_v)
        buf_a, buf_b = join(buf_a, swap(buf_a, 2, 4)), join(buf_b, swap(buf_b, 16))
        got = lax.optimization_barrier((swap(buf_a, 4, 2), swap(buf_b, 8), swap(vecs, 2)))
        own_a, half_b, vecs = (join(v, g) for v, g in zip((buf_a, buf_b, vecs), got))
        oth_a = swap(own_a, 1)
        rest_b = swap(half_b, 4, 2)
        oth_half_b = swap(after(half_b, oth_a), 1)
    else:
        own_a, oth_a, own_b, oth_b, vecs = gather_plain(
            q_weight, kv_weight, reduce_weight, proj_weight, up_weight, down_weight, vec_model, vec_hidden
        )

    square = (width, width)
    (
        x2, h1, patches, nk, rk, kn, q, kb, vb, p, o, wr, wq, wkv, wp, mv, hv, gy, gyt, masks,
    ) = call(
        functools.partial(attend_kernel, tuned),
        (geo, cotangent.T, x, n1, chosen, live, own_a, oth_a, vecs),
        (
            tokens_f32, tokens_low,
            ((capacity, width), BF16), ((keys, width), F32), ((keys, 1), F32), ((keys, width), BF16),
            ((capacity, width), BF16), ((HEADS * keys, width), BF16), ((HEADS * keys, width), BF16),
            ((capacity, HEADS * keys), F32), ((capacity, width), BF16),
            ((4,) + square, BF16), (square, BF16), ((2 * width, width), BF16), (square, BF16),
            ((16, width), F32), ((16, hidden), F32),
            tokens_low, ((width, capacity), BF16), ((7, capacity, 128), F32),
        ),
        scratch=(((capacity, HEADS * keys), F32),),
        scalars=1,
        flops=8 * 10**9,
    )

    if tuned:
        rest_b = after(rest_b, x2)
        own_b = join(half_b, rest_b)
        oth_b = join(oth_half_b, swap(rest_b, 1))
    padded = ((CHUNK // 128, capacity + 2 * PAD, 128), F32)
    halved = ((CHUNK // 128, capacity, 128), F32)
    chunked = ((capacity, CHUNK), F32)
    n2, r2, h2, h2t, wu, wd = call(
        functools.partial(prepare_two_kernel, tuned),
        (x2, mv, own_b),
        (
            tokens_f32, ((capacity, 1), F32), tokens_low, ((width + 16, capacity), BF16),
            ((width, hidden), BF16), ((width, hidden), BF16),
        ),
        flops=10**9,
    )
    gown_b, gsend_b, act, df, hg, wu, wd = call(
        functools.partial(ffn_kernel, tuned),
        (geo, h2, h2t, gy, gyt, masks, own_b, oth_b, hv, wu, wd),
        (
            ((SLOTS,) + piece, BF16), ((SLOTS,) + piece, BF16),
            ((capacity, hidden), BF16), ((capacity, hidden), BF16), ((16, hidden), F32),
            ((width, hidden), BF16), ((width, hidden), BF16),
        ),
        aliases={9: 5, 10: 6},
        scratch=(
            ((hidden // 128, capacity + 2 * PAD, 128), F32), padded, padded, padded, padded, padded,
            halved, halved, chunked,
            ((width + 16, hidden), F32), ((width, hidden), F32),
        ),
        scalars=1,
        flops=33 * 10**9,
    )

    dx2, mg = call(
        norm_two_back_kernel,
        (df, wu, n2, r2, gy, mv),
        (tokens_f32, ((16, width), F32)),
        scratch=(tokens_f32,),
        flops=10**9,
    )
    if tuned:
        core_high, core_low = swap(gsend_b[8:], 1), swap(gsend_b[:8], 1)
        core_high, dx2 = lax.optimization_barrier((core_high, dx2))
        (high_b,) = call(core_high_kernel, (gown_b, core_high), (((8,) + piece, BF16),))
        got_b = swap(high_b, 4, 2)
        dx2 = after(dx2, high_b)
    gp, dob, ds, bp = call(
        score_back_kernel,
        (dx2, vb, p, o, wp),
        (
            (square, F32), ((capacity, width), BF16), ((capacity, HEADS * keys), BF16), ((1, width), F32),
        ),
        scratch=(((capacity, HEADS * keys), F32),),
        flops=0,
    )

    def halve(keep, got, flops=0):
        shape = ((keep.shape[0] // 2,) + piece, BF16)
        return call(halve_kernel, (keep, got), (shape, shape), flops=flops)

    gown_a, gsend_a, dq, dpatch, vk = call(
        functools.partial(attend_back_kernel, tuned),
        (dob, ds, gp, h1, patches, nk, rk, kn, q, kb, p, wr, wkv, mv),
        (
            ((SLOTS,) + piece, BF16), ((SLOTS,) + piece, BF16), ((capacity, width), BF16), ((capacity, width), F32),
            ((8, width), F32),
        ),
        scratch=(((4,) + square, F32), (square, F32), ((2 * width, width), F32)),
        flops=0,
    )
    if tuned:
        got_a = swap(gsend_a, 1)
        low_b, high_b = call(
            core_low_kernel, (gown_b, core_low, got_b), (((4,) + piece, BF16),) * 2, flops=7*10**9
        )
        gown_a = after(gown_a, high_b)
    (mixed,) = call(mixed_kernel, (x2, act, wd, mv, masks), (((width, capacity), BF16),), flops=10**9)
    dh1, vown, vsend = call(
        functools.partial(token_back_kernel, tuned),
        (dq, dpatch, n1, chosen, wq, mg, hg, vk, bp),
        (tokens_f32, ((2,) + gpiece, BF16), ((2,) + gpiece, BF16)),
    )

    (token_grad,) = call(token_grad_kernel, (dx2, dh1, n1, r1, mv), (((width, capacity), BF16),), flops=10**9)

    if not tuned:
        grads = scatter_plain(mesh_shape, width, gown_a, gsend_a, gown_b, gsend_b, vown, vsend)
        return (mixed.T, token_grad.T) + grads

    vrows = gpiece[0]
    low_a, vlow, high_a = call(
        halve_core_kernel,
        (gown_a, got_a, vown, swap(vsend, 1)),
        (((8,) + piece, BF16), ((2,) + gpiece, BF16), ((8 * cw + 2 * vrows, 2 * width), BF16)),
    )
    got_a, got_b, mixed, token_grad = lax.optimization_barrier((swap(high_a, 4, 2), swap(high_b, 8), mixed, token_grad))
    low_a, vlow, high_a = call(
        functools.partial(halve_round_kernel, tuned),
        (low_a, vlow, got_a),
        (((4,) + piece, BF16), ((1,) + gpiece, BF16), ((4 * cw + vrows, 2 * width), BF16)),
    )
    low_b, high_b = halve(low_b, got_b)
    got_a, got_b = swap(high_a, 2, 4), swap(high_b, 16)
    near_a = list(call(quarter_vector_kernel, (low_a, vlow, got_a), (((cw + vrows, 2 * width), BF16),) * 4))
    line_a = [swap(near_a[k], 8 * k) for k in (1, 2, 3)]
    low_b, high_b = halve(low_b, got_b)
    q_grad, kv_grad, reduce_grad, proj_grad, up_grad, down_grad, vm_grad, vh_grad = call(
        finish_kernel,
        (near_a[0], *line_a, low_b, swap(high_b, 2, 4)),
        (
            ((cw, rn), F32), ((rn, 2 * cw), F32), ((cw, width), F32), ((cw, rn), F32),
            ((rn, 4 * cw), F32), ((cw, width), F32), ((11, rn), F32), ((11, width), F32),
        ),
    )
    return (
        mixed.T, token_grad.T, q_grad.T, kv_grad, reduce_grad.T, proj_grad.T, up_grad, down_grad.T, vm_grad, vh_grad,
    )


def gather_plain(q, kv, reduce, proj, up, down, vec_model, vec_hidden):
    def whole(value):
        rows = lax.all_gather(value, "narrow", axis=0, tiled=True)
        return lax.all_gather(rows, "wide", axis=1, tiled=True).T

    q, kv, reduce, proj, up, down = (whole(v) for v in (q, kv, reduce, proj, up, down))
    width = q.shape[0]
    cw, rn = width // PARTS_W, width // PARTS_N

    def pieces(turned, blocks):
        split = turned.reshape(PARTS_W, blocks, cw, PARTS_N, -1)
        return split.transpose(0, 3, 2, 1, 4).reshape(PARTS_W, PARTS_N, cw, -1)

    def slots(value, mixed=False):
        value = value.reshape(2, 2, 2, 2, 2, cw, -1)
        orders = ((2, 1, 0, 3), (3, 1, 0, 2)) if mixed else ((2, 3, 0, 1), (3, 2, 0, 1))
        return tuple(
            value[:, :, :, :, core].transpose(*order, 4, 5).reshape(SLOTS, cw, -1) for core, order in enumerate(orders)
        )

    a = jnp.concatenate([pieces(reduce, 1), pieces(q, 1), pieces(kv, 2), pieces(proj, 1)], axis=-1)
    columns = pieces(down, 1).reshape(PARTS_W, PARTS_N, cw, 2, RUN)
    columns = [columns[..., e, :] for e in range(2)]
    halves = up.T.reshape(PARTS_N, 2, cw, PARTS_W, RUN).transpose(1, 3, 0, 2, 4)
    columns += [halves[0], halves[1]]
    b = jnp.concatenate([c[..., :128] for c in columns] + [c[..., 128:] for c in columns], axis=-1)
    vm = lax.all_gather(vec_model, "narrow", axis=1, tiled=True)
    vh = lax.all_gather(vec_hidden, "narrow", axis=1, tiled=True)
    both = jnp.concatenate([vm.reshape(11, PARTS_N, rn), vh.reshape(11, PARTS_N, width)], axis=-1)
    vecs = jnp.pad(both.transpose(1, 0, 2), ((0, 0), (0, 5), (0, 3 * rn)))
    return (*slots(a), *slots(b, True), vecs)


def scatter_plain(mesh_shape, width, gown_a, gsend_a, gown_b, gsend_b, vown, vsend):
    cw, rn = width // PARTS_W, width // PARTS_N

    def devices(own, send, mixed=False):
        orders = ((2, 1, 0, 3), (3, 1, 0, 2)) if mixed else ((2, 3, 0, 1), (3, 2, 0, 1))
        parts = []
        for value, order in zip((own, send), orders):
            back = sorted(range(4), key=lambda k: order[k])
            parts.append(value.reshape(2, 2, 2, 2, cw, -1).transpose(*back, 4, 5))
        return jnp.stack(parts, axis=4).reshape(PARTS_W, PARTS_N, cw, -1)

    def natural(value, blocks):
        split = value.reshape(PARTS_W, PARTS_N, cw, blocks, -1).transpose(0, 3, 2, 1, 4)
        return split.reshape(PARTS_W * blocks * cw, -1).T

    def share(value):
        columns = lax.psum_scatter(value.astype(BF16), "wide", scatter_dimension=1, tiled=True)
        return lax.psum_scatter(columns, "narrow", scatter_dimension=0, tiled=True).astype(F32)

    a = devices(gown_a, gsend_a)
    b = devices(gown_b, gsend_b, True)
    reduce = natural(a[..., :width], 1)
    q = natural(a[..., width : width + rn], 1)
    kv = natural(a[..., width + rn : width + 3 * rn], 2)
    proj = natural(a[..., width + 3 * rn :], 1)
    columns = [
        jnp.concatenate([b[..., 128 * k : 128 * (k + 1)], b[..., 512 + REST * k : 512 + REST * (k + 1)]], axis=-1)
        for k in range(4)
    ]
    down = natural(jnp.concatenate(columns[:2], axis=-1), 1)
    up = jnp.stack(columns[2:]).transpose(2, 0, 3, 1, 4).reshape(width, -1)
    vectors = jnp.stack([vown, vsend], axis=1).reshape(PARTS_N, 8, -1)
    beside = vectors[..., 5 * rn :]
    beside = jnp.concatenate([beside[:, :3], beside[:, 3:6, : 2 * rn]], axis=-1)
    vectors = jnp.concatenate([vectors[..., : 5 * rn], beside], axis=1).transpose(1, 0, 2)
    vm = vectors[..., :rn].reshape(11, width)
    vh = vectors[..., rn : rn + width].reshape(11, PARTS_N * width)

    def share_vector(value):
        total = lax.psum(value.astype(BF16), "wide")
        return lax.psum_scatter(total, "narrow", scatter_dimension=1, tiled=True).astype(F32)

    return tuple(share(v) for v in (q, kv, reduce, proj, up, down)) + (share_vector(vm), share_vector(vh))


def solution(mesh):
    both, rows, weight, vector = P(("wide", "narrow"), None), P(("wide", "narrow")), P("narrow", "wide"), P(None, "narrow")
    return jax.shard_map(
        functools.partial(on_device, (mesh.shape["wide"], mesh.shape["narrow"])),
        mesh=mesh,
        in_specs=(both, both, rows, rows) + (weight,) * 6 + (vector,) * 2,
        out_specs=(both, both) + (weight,) * 6 + (vector,) * 2,
        check_vma=False,
    )
```

```python
import functools
import math

import jax
import jax.numpy as jnp
from jax import lax
from jax.experimental import pallas as pl
from jax.experimental.pallas import tpu as pltpu
from jax.sharding import PartitionSpec as P

HEADS = 5
EPSILON = 1e-06
MASKED = -1000000000.0
F32 = jnp.float32
BF16 = jnp.bfloat16

PARTS_W = 8
PARTS_N = 4
SLOTS = 16
TILE = 32
CHUNK = 256
PAD = 40
MROWS = 256
RUN = 160
REST = RUN - 128


def dot_nn(left, right):
    return jnp.dot(left, right, preferred_element_type=F32)


def dot_nt(left, right):
    return lax.dot_general(left, right, (((1,), (1,)), ((), ())), preferred_element_type=F32)


def dot_tn(left, right):
    return lax.dot_general(left, right, (((0,), (0,)), ((), ())), preferred_element_type=F32)


def lanes(*parts):
    return jnp.concatenate(parts, axis=1)


def rows_of(*parts):
    return jnp.concatenate(parts, axis=0)


def my_index(tuned):
    if not tuned:
        return jnp.int32(0)
    return lax.axis_index("wide") * PARTS_N + lax.axis_index("narrow")


def round_slot(device, me):
    delta = device ^ me
    first, second = (delta >> 1) & 1, (delta >> 2) & 1
    if device & 1:
        first, second = second, first
    return second * 8 + first * 4 + (delta >> 3)


def mixed_slot(device, me):
    delta = device ^ me
    x, y = (delta >> 1) & 1, (delta >> 2) & 1
    odd = (device & 1) == 1
    first, second = jnp.where(odd, y, x), jnp.where(odd, x, y)
    return second * 8 + ((delta >> 3) & 1) * 4 + ((delta >> 4) & 1) * 2 + first


def normalise(values):
    centre = values - jnp.mean(values, axis=-1, keepdims=True)
    inverse = lax.rsqrt(jnp.mean(centre * centre, axis=-1, keepdims=True) + EPSILON)
    return centre * inverse, inverse


def normalise_back(grad, normed, inverse, gain):
    scaled = grad * gain
    first = jnp.mean(scaled, axis=-1, keepdims=True)
    second = jnp.mean(scaled * normed, axis=-1, keepdims=True)
    return (scaled - first - normed * second) * inverse


def column_sum(values):
    return jnp.sum(values, axis=0, keepdims=True)


def piece_of(own_ref, other_ref, device, me, first=0, last=5, order=round_slot):
    slot = order(device, me)
    mine = ((device ^ me) & 1) == 0
    at = pl.ds(128 * first, 128 * (last - first))
    return jnp.where(mine, own_ref[slot, :, at].astype(F32), other_ref[slot, :, at].astype(F32))


def token_geometry(geo_ref, capacity, width):
    row0, row1, col0, col1 = (geo_ref[k] for k in range(4))
    area0, area1 = row0 * col0, row1 * col1
    position = lax.broadcasted_iota(jnp.int32, (capacity, width), 0)
    first = position < area0
    second = jnp.logical_and(position >= area0, position < area0 + area1)
    widths = jnp.maximum(jnp.where(second, col1, col0), 2)
    heights = jnp.where(second, row1, row0)
    local = position - jnp.where(second, area0, 0)
    row = ((local.astype(F32) + 0.5) / widths.astype(F32)).astype(jnp.int32)
    col = local - row * widths
    return first, second, row, col, heights, widths


def pack_kernel(*refs):
    sources, (a_ref, b_ref, v_ref), held, semaphores = refs[:8], refs[8:11], refs[11:19], refs[19]
    copies = [pltpu.make_async_copy(source, ref, semaphores.at[i]) for i, (source, ref) in enumerate(zip(sources, held))]
    for copy in copies:
        copy.start()
    for copy in copies:
        copy.wait()
    q_ref, kv_ref, red_ref, proj_ref, up_ref, down_ref, vm_ref, vh_ref = held
    cw = q_ref.shape[0]

    def wider(ref):
        return ref[...].astype(F32)

    kv = wider(kv_ref).T
    a_ref[0] = lanes(wider(red_ref), wider(q_ref), kv[:cw], kv[cw:], wider(proj_ref)).astype(BF16)
    up, down = wider(up_ref), wider(down_ref)
    columns = (down[:, :RUN], down[:, RUN:], up[:cw], up[cw:])
    b_ref[0] = lanes(*[c[:, :128] for c in columns], *[c[:, 128:] for c in columns]).astype(BF16)
    v_ref[0] = jnp.zeros_like(v_ref[0])
    both = lanes(wider(vm_ref), wider(vh_ref))
    v_ref[0, : both.shape[0], : both.shape[1]] = both.astype(BF16)


def pack(arguments, piece, vpiece):
    vmem = pl.BlockSpec(memory_space=pltpu.VMEM)
    return pl.pallas_call(
        pack_kernel,
        out_shape=[jax.ShapeDtypeStruct((1,) + shape, BF16) for shape in (piece, piece, vpiece)],
        in_specs=[pl.BlockSpec(memory_space=pl.ANY)] * len(arguments),
        out_specs=[vmem] * 3,
        scratch_shapes=[pltpu.VMEM(v.shape, v.dtype) for v in arguments] + [pltpu.SemaphoreType.DMA((len(arguments),))],
        compiler_params=pltpu.CompilerParams(vmem_limit_bytes=60 * 2**20),
    )(*arguments)


def prepare_kernel(
    rows_hbm, cols_hbm, tok_hbm, x_ref, n1_ref, r1_ref, chosen_ref, live_ref, geo_ref,
    rows_ref, cols_ref, tok_ref, semaphores,
):
    copies = [
        pltpu.make_async_copy(source, target, semaphores.at[i])
        for i, (source, target) in enumerate(((rows_hbm, rows_ref), (cols_hbm, cols_ref), (tok_hbm, tok_ref)))
    ]
    for copy in copies:
        copy.start()
    for copy in copies[:2]:
        copy.wait()
    capacity = tok_ref.shape[1]
    for j in range(2):
        geo_ref[j] = rows_ref[j]
        geo_ref[2 + j] = cols_ref[j]
    chosen_ref[...] = one_hot(rows_ref, cols_ref, capacity)
    area0, area1 = rows_ref[0] * cols_ref[0], rows_ref[1] * cols_ref[1]
    quarter0, quarter1 = area0 // 4, area1 // 4
    token = lax.broadcasted_iota(jnp.int32, live_ref.shape, 0)
    key = lax.broadcasted_iota(jnp.int32, live_ref.shape, 1)
    live = ((token < area0) & (key < quarter0)) | (
        (token >= area0) & (token < area0 + area1) & (key >= quarter0) & (key < quarter0 + quarter1)
    )
    live_ref[...] = jnp.where(live, 1.0, 0.0)
    copies[2].wait()
    tokens = tok_ref[...].astype(F32).T
    x_ref[...] = tokens
    normed, inverse = normalise(tokens)
    n1_ref[...] = normed
    r1_ref[...] = inverse


def prepare(img_rows, img_cols, tokens):
    width, capacity = tokens.shape
    keys = capacity // 4
    vmem, smem = (pl.BlockSpec(memory_space=space) for space in (pltpu.VMEM, pltpu.SMEM))
    outputs = (
        ((capacity, width), F32), ((capacity, width), F32), ((capacity, 1), F32), ((capacity, capacity), BF16),
        ((capacity, keys), F32), ((4,), jnp.int32),
    )
    return pl.pallas_call(
        prepare_kernel,
        out_shape=[jax.ShapeDtypeStruct(shape, kind) for shape, kind in outputs],
        in_specs=[pl.BlockSpec(memory_space=pl.ANY)] * 3,
        out_specs=[vmem] * 5 + [smem],
        scratch_shapes=[
            pltpu.SMEM((2,), jnp.int32), pltpu.SMEM((2,), jnp.int32), pltpu.VMEM((width, capacity), BF16),
            pltpu.SemaphoreType.DMA((3,)),
        ],
        compiler_params=pltpu.CompilerParams(vmem_limit_bytes=60 * 2**20),
        cost_estimate=pl.CostEstimate(flops=2 * 10**9, bytes_accessed=0, transcendentals=0),
    )(img_rows, img_cols, tokens)


def attend_kernel(
    tuned,
    geo_ref, cot_ref, x_ref, n1_ref, chosen_ref, live_ref, own_ref, oth_ref, vec_ref,
    x2_ref, h1_ref, patch_ref, nk_ref, rk_ref, kn_ref, q_ref, kb_ref, vb_ref,
    p_ref, o_ref, wr_ref, wq_ref, wkv_ref, wp_ref, mv_ref, hv_ref, gy_ref, gyt_ref, mask_ref,
    score_ref,
):
    me = my_index(tuned)
    capacity, width = x_ref.shape
    cw, rn = width // PARTS_W, width // PARTS_N
    keys = capacity // 4
    dim = width // HEADS

    pieces = [vec_ref[n ^ (me & 3)].astype(F32) for n in range(PARTS_N)]
    mv = lanes(*[p[:, :rn] for p in pieces])
    mv_ref[...] = mv
    runs = [p[:, rn + e * RUN : rn + (e + 1) * RUN] for p in pieces for e in range(2)]
    hv_ref[...] = lanes(*[r[:, :128] for r in runs], *[r[:, 128:] for r in runs])

    for pair in range(PARTS_W // 2):
        got = [
            [piece_of(own_ref, oth_ref, w * PARTS_N + n, me) for n in range(PARTS_N)]
            for w in (2 * pair, 2 * pair + 1)
        ]
        at = pl.ds(pair * 2 * cw, 2 * cw)
        for n in range(PARTS_N):
            wr_ref[n, at, :] = rows_of(got[0][n][:, :width], got[1][n][:, :width]).astype(BF16)

        def unit(w, k):
            return lanes(*[got[w][n][:, width + k * rn : width + (k + 1) * rn] for n in range(PARTS_N)])

        wq_ref[at, :] = rows_of(unit(0, 0), unit(1, 0)).astype(BF16)
        wkv_ref[pl.ds(pair * 4 * cw, 4 * cw), :] = rows_of(
            unit(0, 1), unit(0, 2), unit(1, 1), unit(1, 2)
        ).astype(BF16)
        wp_ref[at, :] = rows_of(unit(0, 3), unit(1, 3)).astype(BF16)

    h1 = (n1_ref[...] * mv[0:1] + mv[1:2]).astype(BF16)
    h1_ref[...] = h1
    q = (dot_nt(h1, wq_ref[...]) + mv[2:3]).astype(BF16)
    q_ref[...] = q

    patches = dot_nn(chosen_ref[...], h1).astype(BF16)
    patch_ref[...] = patches
    reduced = mv[4:5]
    for n in range(4):
        reduced = reduced + dot_nt(patches[n * keys : (n + 1) * keys], wr_ref[n])
    nk, rk = normalise(reduced)
    nk_ref[...] = nk
    rk_ref[...] = rk
    kn = (nk * mv[5:6] + mv[6:7]).astype(BF16)
    kn_ref[...] = kn
    kv = dot_nt(kn, wkv_ref[...])
    k = kv[:, :width].astype(BF16).astype(F32)
    v = (kv[:, width:] + mv[3:4]).astype(BF16).astype(F32)
    lane = lax.broadcasted_iota(jnp.int32, (keys, width), 1)
    for h in range(HEADS):
        inside = (lane >= h * dim) & (lane < (h + 1) * dim)
        at = pl.ds(h * keys, keys)
        kb_ref[at, :] = jnp.where(inside, k, 0.0).astype(BF16)
        vb_ref[at, :] = jnp.where(inside, v, 0.0).astype(BF16)

    score_ref[...] = dot_nt(q, kb_ref[...]) * dim ** (-0.5)
    def soften(i, carry):
        at = pl.ds(pl.multiple_of(i * 64, 64), 64)
        live = live_ref[at, :] > 0.5
        for h in range(HEADS):
            lane_at = pl.ds(h * keys, keys)
            s = jnp.where(live, score_ref[at, lane_at], MASKED)
            e = jnp.exp(s - jnp.max(s, axis=-1, keepdims=True))
            p_ref[at, lane_at] = e / jnp.sum(e, axis=-1, keepdims=True)
        return carry

    lax.fori_loop(0, capacity // 64, soften, 0, unroll=True)
    o = dot_nn(p_ref[...].astype(BF16), vb_ref[...]).astype(BF16)
    o_ref[...] = o
    x2_ref[...] = x_ref[...] + dot_nt(o, wp_ref[...]) + mv[7:8]
    mask_gradient(geo_ref, cot_ref, gy_ref, gyt_ref, mask_ref)


def one_hot(rows_ref, cols_ref, capacity):
    row0, row1, col0, col1 = rows_ref[0], rows_ref[1], cols_ref[0], cols_ref[1]
    area0, area1 = row0 * col0, row1 * col1
    quarter0, quarter1 = area0 // 4, area1 // 4
    keys = capacity // 4
    index = lax.broadcasted_iota(jnp.int32, (capacity, 128), 0)
    tap = index // keys
    key = index - tap * keys
    first = key < quarter0
    second = jnp.logical_and(key >= quarter0, key < quarter0 + quarter1)
    width = jnp.maximum(jnp.where(second, col1, col0), 2)
    half = width // 2
    local = key - jnp.where(second, quarter0, 0)
    row = ((local.astype(F32) + 0.5) / half.astype(F32)).astype(jnp.int32)
    col = local - row * half
    token = jnp.where(second, area0, 0) + (2 * row + tap // 2) * width + 2 * col + tap % 2
    token = jnp.where(first | second, token, -1)
    lane = lax.broadcasted_iota(jnp.int32, (capacity, 128), 1)
    return lanes(
        *[jnp.where(token == lane + t * 128, 1.0, 0.0).astype(BF16) for t in range(capacity // 128)]
    )


def mask_gradient(geo_ref, cot_ref, gy_ref, gyt_ref, mask_ref):
    width, capacity = cot_ref.shape
    area = geo_ref[0] * geo_ref[2] + geo_ref[1] * geo_ref[3]
    position = lax.broadcasted_iota(jnp.int32, (width, capacity), 1)
    gyt = jnp.where(position < area, cot_ref[...].astype(F32), 0.0)
    gyt_ref[...] = gyt.astype(BF16)
    gy_ref[...] = gyt.T.astype(BF16)
    first, second, row, col, heights, widths = token_geometry(geo_ref, capacity, 128)
    live = first | second
    start = lax.broadcasted_iota(jnp.int32, (capacity, 128), 0) // TILE * TILE
    late = start >= geo_ref[0] * geo_ref[2]
    early = jnp.logical_not(late)
    usual = (late & second) | (early & first)
    apart = second & early
    conditions = (
        live & (col > 0),
        live & (col < widths - 1),
        usual & (row > 0),
        usual & (row < heights - 1),
        apart & (row > 0),
        apart & (row < heights - 1),
        live,
    )
    for k, condition in enumerate(conditions):
        mask_ref[k] = jnp.where(condition, 1.0, 0.0)


def place_pieces(ref, core, me, wu_ref, wd_ref):
    cw = ref.shape[1]
    rn = 2 * cw
    tails = 128 * PARTS_W
    for x in range(PARTS_N // 2):
        n = 2 * x + core
        pieces = [ref[mixed_slot(w * PARTS_N + n, me)].astype(F32) for w in range(PARTS_W)]
        lane_at = pl.ds(pl.multiple_of(256 * n, 256), 256)
        for pair in range(PARTS_W // 2):
            value = rows_of(pieces[2 * pair][:, :256], pieces[2 * pair + 1][:, :256])
            wd_ref[pl.ds(pair * 2 * cw, 2 * cw), lane_at] = value.astype(BF16)
        at = pl.ds(pl.multiple_of(rn * n, 16), rn)
        for w, p in enumerate(pieces):
            wu_ref[at, pl.ds(128 * w, 128)] = rows_of(p[:, 256:384], p[:, 384:512]).astype(BF16)
        ends = [rows_of(p[:, 512 + 2 * REST : 512 + 3 * REST], p[:, 512 + 3 * REST :]) for p in pieces]
        wu_ref[at, pl.ds(tails, REST * PARTS_W)] = lanes(*ends).astype(BF16)


def prepare_two_kernel(tuned, x2_ref, mv_ref, own_ref, n2_ref, r2_ref, h2_ref, h2t_ref, wu_ref, wd_ref):
    me = my_index(tuned)
    place_pieces(own_ref, me & 1, me, wu_ref, wd_ref)
    normed, inverse = normalise(x2_ref[...])
    n2_ref[...] = normed
    r2_ref[...] = inverse
    h2 = normed * mv_ref[8:9, :] + mv_ref[9:10, :]
    h2_ref[...] = h2.astype(BF16)
    width = h2.shape[1]
    h2t_ref[:width, :] = h2.T.astype(BF16)
    h2t_ref[width:, :] = jnp.ones((h2t_ref.shape[0] - width, h2.shape[0]), BF16)


def ffn_kernel(
    tuned,
    geo_ref, h2_ref, h2t_ref, gy_ref, gyt_ref, mask_ref, own_ref, oth_ref, hv_ref, wu_in_ref, wd_in_ref,
    gown_ref, gsend_ref, act_ref, df_ref, hg_ref, wu_ref, wd_ref,
    f_ref, gm_ref, gp_ref, dc_ref, ul_ref, ur_ref, g0_ref, u0_ref, da_ref,
    upg_ref, dng_ref,
):
    me = my_index(tuned)
    capacity, width = h2_ref.shape
    hidden = hv_ref.shape[1]
    cw, rn = width // PARTS_W, width // PARTS_N
    tiles = capacity // TILE
    tails = 128 * PARTS_W

    place_pieces(oth_ref, 1 - (me & 1), me, wu_ref, wd_ref)
    for pair in range(PARTS_W // 2):
        got = [
            rows_of(*[piece_of(own_ref, oth_ref, w * PARTS_N + n, me, 4, 5, mixed_slot) for w in (2 * pair, 2 * pair + 1)])
            for n in range(PARTS_N)
        ]
        ends = lanes(*[g[:, : 2 * REST] for g in got]).astype(BF16)
        wd_ref[pl.ds(pair * 2 * cw, 2 * cw), pl.ds(tails, 2 * REST * PARTS_N)] = ends

    area, w0, w1 = geo_ref[0] * geo_ref[2], geo_ref[2], geo_ref[3]
    split = pl.multiple_of(jnp.minimum(area // TILE, tiles - 1) * TILE, TILE)

    for ref in (f_ref, gm_ref, gp_ref, dc_ref, ul_ref, ur_ref):
        ref[:, :PAD, :] = jnp.zeros((ref.shape[0], PAD, 128), F32)
        ref[:, PAD + capacity :, :] = jnp.zeros((ref.shape[0], PAD, 128), F32)


    def fold(values):
        return jnp.sum(values.reshape(TILE // 8, 8, 128), axis=0)

    halves = CHUNK // 128
    chunks = hidden // CHUNK
    zero = jnp.zeros((8, 128), F32)

    def columns(c):
        return pl.ds(pl.multiple_of(c * CHUNK, CHUNK), CHUNK)

    def vector(c, k, j):
        return hv_ref[k : k + 1, pl.ds(pl.multiple_of(c * CHUNK + j * 128, 128), 128)]

    def put_vector(c, k, j, value):
        hg_ref[k : k + 1, pl.ds(pl.multiple_of(c * CHUNK + j * 128, 128), 128)] = value

    def act_grad(c, at):
        da_ref[at, :] = dot_nn(gy_ref[at, :], wd_ref[:, columns(c)])

    def down_grad(c, at):
        dng_ref[at, columns(c)] = dot_nn(gyt_ref[at, :], act_ref[:, columns(c)])

    def tasks(product, c, rows, size):
        return [functools.partial(product, c, pl.ds(r, min(size, rows - r))) for r in range(0, rows, size)]

    def interleave(steps, products):
        done = 0
        for i, step in enumerate(steps):
            step()
            while done < len(products) and done * len(steps) < (i + 1) * len(products):
                products[done]()
                done += 1

    def chunk_step(c, carry):
        v = [[vector(c, k, j) for k in range(11)] for j in range(halves)]

        def taps_of(j, r, mask_left, mask_right):
            here = f_ref[c * halves + j, pl.ds(PAD + r, TILE), :]
            left = f_ref[c * halves + j, pl.ds(PAD + r - 1, TILE), :] * mask_left
            right = f_ref[c * halves + j, pl.ds(PAD + r + 1, TILE), :] * mask_right
            return left, here, right

        def row_length(r):
            return jnp.where(area > r, w0, w1)

        def column_taps(r):
            at = pl.ds(r, TILE)
            masks = mask_ref[0, at, :], mask_ref[1, at, :]
            for j in range(halves):
                left, here, right = taps_of(j, r, *masks)
                u = v[j]
                gm_ref[j, pl.ds(PAD + r, TILE), :] = u[2] * left + u[3] * here + u[4] * right
                g0_ref[j, at, :] = u[1] + u[5] * left + u[6] * here + u[7] * right
                gp_ref[j, pl.ds(PAD + r, TILE), :] = u[8] * left + u[9] * here + u[10] * right

        def column_taps_split():
            at = pl.ds(split, TILE)
            for j in range(halves):
                g0_ref[j, at, :] += (
                    mask_ref[4, at, :] * gm_ref[j, pl.ds(PAD + split - w1, TILE), :]
                    + mask_ref[5, at, :] * gp_ref[j, pl.ds(PAD + split + w1, TILE), :]
                )

        conv_sums = [zero] * halves

        def activate(r):
            at = pl.ds(r, TILE)
            length = row_length(r)
            above, below = mask_ref[2, at, :], mask_ref[3, at, :]
            for j in range(halves):
                conv = (
                    g0_ref[j, at, :]
                    + above * gm_ref[j, pl.ds(PAD + r - length, TILE), :]
                    + below * gp_ref[j, pl.ds(PAD + r + length, TILE), :]
                )
                half = 0.5 * (1.0 + lax.erf(conv * 2.0 ** (-0.5)))
                act_ref[at, pl.ds(pl.multiple_of(c * CHUNK + j * 128, 128), 128)] = (conv * half).astype(BF16)
                slope = half + conv * ((2.0 * math.pi) ** (-0.5) * jnp.exp2(conv * conv * (-0.5 / math.log(2.0))))
                value = da_ref[at, pl.ds(j * 128, 128)] * slope
                dc_ref[j, pl.ds(PAD + r, TILE), :] = value
                conv_sums[j] = conv_sums[j] + fold(value)

        tap_sums = [[zero] * 9 for _ in range(halves)]

        def tap_back(r):
            at = pl.ds(r, TILE)
            length = row_length(r)
            masks = [mask_ref[k, at, :] for k in range(4)]
            for j in range(halves):
                left, here, right = taps_of(j, r, *masks[:2])
                u = v[j]
                below = masks[3] * dc_ref[j, pl.ds(PAD + r + length, TILE), :]
                level = dc_ref[j, pl.ds(PAD + r, TILE), :]
                above = masks[2] * dc_ref[j, pl.ds(PAD + r - length, TILE), :]
                ul_ref[j, pl.ds(PAD + r, TILE), :] = u[2] * below + u[5] * level + u[8] * above
                u0_ref[j, at, :] = u[3] * below + u[6] * level + u[9] * above
                ur_ref[j, pl.ds(PAD + r, TILE), :] = u[4] * below + u[7] * level + u[10] * above
                grads = [fold(d * f) for d in (below, level, above) for f in (left, here, right)]
                tap_sums[j] = [a + b for a, b in zip(tap_sums[j], grads)]

        def tap_back_split():
            at, padded = pl.ds(split, TILE), pl.ds(PAD + split, TILE)
            masks = [mask_ref[k, at, :] for k in (0, 1, 4, 5)]
            for j in range(halves):
                left, here, right = taps_of(j, split, *masks[:2])
                u = v[j]
                below = masks[3] * dc_ref[j, pl.ds(PAD + split + w1, TILE), :]
                above = masks[2] * dc_ref[j, pl.ds(PAD + split - w1, TILE), :]
                ul_ref[j, padded, :] += u[2] * below + u[8] * above
                u0_ref[j, at, :] += u[3] * below + u[9] * above
                ur_ref[j, padded, :] += u[4] * below + u[10] * above
                grads = [fold(d * f) for d in (below, above) for f in (left, here, right)]
                tap_sums[j] = [a + b for a, b in zip(tap_sums[j], grads[:3] + [zero] * 3 + grads[3:])]

        def spread_back(r):
            at = pl.ds(r, TILE)
            mask_left, mask_right = mask_ref[0, at, :], mask_ref[1, at, :]
            for j in range(halves):
                value = (
                    u0_ref[j, at, :]
                    + mask_left * ur_ref[j, pl.ds(PAD + r - 1, TILE), :]
                    + mask_right * ul_ref[j, pl.ds(PAD + r + 1, TILE), :]
                ).astype(BF16)
                df_ref[at, pl.ds(pl.multiple_of(c * CHUNK + j * 128, 128), 128)] = value

        def steps(step):
            return [functools.partial(step, r) for r in range(0, capacity, TILE)]

        interleave(steps(column_taps) + [column_taps_split], tasks(act_grad, c, capacity, MROWS))
        interleave(
            steps(activate),
            [],
        )
        interleave(steps(tap_back) + [tap_back_split], tasks(down_grad, c, width, MROWS))
        interleave(steps(spread_back), [])
        for j in range(halves):
            put_vector(c, 1, j, column_sum(conv_sums[j]))
            for k in range(9):
                put_vector(c, 2 + k, j, column_sum(tap_sums[j][k]))
        return carry

    for c in range(chunks):
        value = dot_nn(h2_ref[...], wu_ref[:, c * CHUNK : (c + 1) * CHUNK])
        for j in range(halves):
            bias = hv_ref[0:1, pl.ds(c * CHUNK + j * 128, 128)]
            f_ref[c * halves + j, pl.ds(PAD, capacity), :] = value[:, j * 128 : (j + 1) * 128] + bias
    lax.fori_loop(0, chunks, chunk_step, 0)
    upg_ref[...] = dot_nn(h2t_ref[...], df_ref[...])
    hg_ref[0:1, :] = upg_ref[width : width + 1, :]
    hg_ref[11:, :] = jnp.zeros((hg_ref.shape[0] - 11, hidden), F32)

    def value_of(w, n):
        down = pl.ds(w * cw, cw)
        up = [pl.ds(n * rn + e * cw, cw) for e in range(2)]
        return lanes(
            dng_ref[down, pl.ds(256 * n, 256)],
            *[upg_ref[e, pl.ds(128 * w, 128)] for e in up],
            dng_ref[down, pl.ds(tails + 2 * REST * n, 2 * REST)],
            *[upg_ref[e, pl.ds(tails + REST * w, REST)] for e in up],
        )

    store_pieces(gown_ref, gsend_ref, me, value_of, mixed_slot)


def store_pieces(own_ref, send_ref, me, value_of, order):
    even = (me & 1) == 0
    for w in range(PARTS_W):
        for x in range(PARTS_N // 2):
            first, second = value_of(w, 2 * x), value_of(w, 2 * x + 1)
            slot0, slot1 = (order(w * PARTS_N + 2 * x + c, me) for c in range(2))
            own_ref[jnp.where(even, slot0, slot1)] = jnp.where(even, first, second).astype(BF16)
            send_ref[jnp.where(even, slot1, slot0)] = jnp.where(even, second, first).astype(BF16)


def norm_two_back_kernel(df_ref, wu_ref, n2_ref, r2_ref, gy_ref, mv_ref, dx2_ref, mg_ref, dh2_ref):
    capacity, width = n2_ref.shape
    dh2_ref[...] = dot_nt(df_ref[...], wu_ref[...])

    def norm_back(i, carry):
        at = pl.ds(pl.multiple_of(i * 64, 64), 64)
        gy = gy_ref[at, :].astype(F32)
        grad, normed = dh2_ref[at, :], n2_ref[at, :]
        dx2_ref[at, :] = gy + normalise_back(grad, normed, r2_ref[at, :], mv_ref[8:9, :])
        return tuple(a + column_sum(b) for a, b in zip(carry, (grad * normed, grad, gy)))

    zero = jnp.zeros((1, width), F32)
    sums = lax.fori_loop(0, capacity // 64, norm_back, (zero, zero, zero), unroll=True)
    mg_ref[...] = jnp.zeros_like(mg_ref)
    for k in range(3):
        mg_ref[8 + k : 9 + k, :] = sums[k]


def score_back_kernel(dx2_ref, vb_ref, p_ref, o_ref, wp_ref, gp_ref, dob_ref, ds_ref, bp_ref, dp_ref):
    capacity = dx2_ref.shape[0]
    keys = capacity // 4
    datt = dx2_ref[...].astype(BF16)
    bp_ref[...] = column_sum(datt.astype(F32))
    gp_ref[...] = dot_tn(datt, o_ref[...])
    dob = dot_nn(datt, wp_ref[...]).astype(BF16)
    dob_ref[...] = dob
    dp_ref[...] = dot_nt(dob, vb_ref[...])

    def soften_back(i, carry):
        at = pl.ds(pl.multiple_of(i * 64, 64), 64)
        for h in range(HEADS):
            lane_at = pl.ds(h * keys, keys)
            p = p_ref[at, lane_at]
            dp = dp_ref[at, lane_at]
            row = jnp.sum(p * dp, axis=-1, keepdims=True)
            ds_ref[at, lane_at] = (p * (dp - row)).astype(BF16)
        return carry

    lax.fori_loop(0, capacity // 64, soften_back, 0, unroll=True)


def attend_back_kernel(
    tuned,
    dob_ref, ds_ref, gp_ref, h1_ref, patch_ref, nk_ref, rk_ref, kn_ref, q_ref, kb_ref, p_ref,
    wr_ref, wkv_ref, mv_ref,
    gown_ref, gsend_ref, dq_ref, dpatch_ref, vk_ref,
    gr_ref, gq_ref, gkv_ref,
):
    me = my_index(tuned)
    capacity, width = h1_ref.shape
    cw, rn = width // PARTS_W, width // PARTS_N
    keys = capacity // 4
    dim = width // HEADS
    scale = dim ** (-0.5)

    ds = ds_ref[...]
    dq = (dot_nn(ds, kb_ref[...]) * scale).astype(BF16)
    dq_ref[...] = dq
    dk_all = dot_tn(ds, q_ref[...])
    dv_all = dot_tn(p_ref[...].astype(BF16), dob_ref[...])
    lane = lax.broadcasted_iota(jnp.int32, (keys, width), 1)
    dk = jnp.zeros((keys, width), F32)
    dv = jnp.zeros((keys, width), F32)
    for h in range(HEADS):
        inside = (lane >= h * dim) & (lane < (h + 1) * dim)
        dk = jnp.where(inside, dk_all[h * keys : (h + 1) * keys], dk)
        dv = jnp.where(inside, dv_all[h * keys : (h + 1) * keys], dv)
    dk = (dk * scale).astype(BF16)
    dv = dv.astype(BF16)
    gq_ref[...] = dot_tn(dq, h1_ref[...])
    kn = kn_ref[...]
    gkv_ref[pl.ds(0, width), :] = dot_tn(dk, kn)
    gkv_ref[pl.ds(width, width), :] = dot_tn(dv, kn)
    dkn = dot_nn(dk, wkv_ref[pl.ds(0, width), :]) + dot_nn(dv, wkv_ref[pl.ds(width, width), :])
    nk = nk_ref[...]
    dsr = normalise_back(dkn, nk, rk_ref[...], mv_ref[5:6, :]).astype(BF16)
    vk_ref[...] = rows_of(
        column_sum(dq.astype(F32)),
        column_sum(dv.astype(F32)),
        column_sum(dsr.astype(F32)),
        column_sum(dkn * nk),
        column_sum(dkn),
        jnp.zeros((3, width), F32),
    )
    for n in range(4):
        at = pl.ds(n * keys, keys)
        gr_ref[n] = dot_tn(dsr, patch_ref[at, :])
        dpatch_ref[at, :] = dot_nn(dsr, wr_ref[n])

    def value_of(w, n):
        at, lane_at = pl.ds(w * cw, cw), pl.ds(n * rn, rn)
        return lanes(
            gr_ref[n, at, :],
            gq_ref[at, lane_at],
            gkv_ref[pl.ds(2 * w * cw, cw), lane_at],
            gkv_ref[pl.ds(2 * w * cw + cw, cw), lane_at],
            gp_ref[at, lane_at],
        )

    store_pieces(gown_ref, gsend_ref, me, value_of, round_slot)


def token_grad_kernel(dx2_ref, dh1_ref, n1_ref, r1_ref, mv_ref, tg_ref):
    value = dx2_ref[...] + normalise_back(dh1_ref[...], n1_ref[...], r1_ref[...], mv_ref[0:1, :])
    tg_ref[...] = value.T.astype(BF16)


def mixed_kernel(x2_ref, act_ref, wd_ref, mv_ref, mask_ref, mixed_ref):
    width = x2_ref.shape[1]
    occupied = mask_ref[6]
    occupied = lanes(*([occupied] * (width // 128)), occupied[:, : width % 128])
    mixed = x2_ref[...] + dot_nt(act_ref[...], wd_ref[...]) + mv_ref[10:11, :]
    mixed_ref[...] = (mixed * occupied).T.astype(BF16)


def fold_rows(value, unit):
    rest = value[8:]
    beside = lanes(rest[:, : 3 * unit], jnp.zeros((8, 256 - 3 * unit), F32))
    below = lanes(rest[:, 3 * unit :], jnp.zeros((8, 256 - 2 * unit), F32))
    return lanes(value[:8], (beside + pltpu.roll(below, 3, 0))[:, : 3 * unit])


def unfold_rows(value, unit):
    beside = lanes(value[:, 5 * unit :], jnp.zeros((8, 256 - 3 * unit), F32))
    below = pltpu.roll(beside, 5, 0)
    return rows_of(value[:, : 5 * unit], lanes(beside[:, : 3 * unit], below[:, : 2 * unit]))


def token_back_kernel(
    tuned,
    dq_ref, dpatch_ref, n1_ref, chosen_ref, wq_ref, mg_ref, hg_ref, vk_ref, bp_ref,
    dh1_ref, vown_ref, vsend_ref,
):
    me = my_index(tuned)
    width = n1_ref.shape[1]
    rn = width // PARTS_N
    chosen = chosen_ref[...]
    high = dpatch_ref[...].astype(BF16)
    low = (dpatch_ref[...] - high.astype(F32)).astype(BF16)
    dh1 = dot_nn(dq_ref[...], wq_ref[...]) + dot_tn(chosen, high) + dot_tn(chosen, low)
    n1 = n1_ref[...]
    vk = vk_ref[...]
    dh1_ref[...] = dh1
    sums = rows_of(column_sum(dh1 * n1), column_sum(dh1), vk[0:5], bp_ref[...], mg_ref[8:16, :])
    hg = hg_ref[...]
    value = []
    for n in range(PARTS_N):
        parts = []
        for w in (2 * n, 2 * n + 1):
            parts += [hg[:, 128 * w : 128 * (w + 1)], hg[:, 1024 + REST * w : 1024 + REST * (w + 1)]]
        value.append(fold_rows(lanes(sums[:, n * rn : (n + 1) * rn], *parts), rn))
    even = (me & 1) == 0
    for x in range(2):
        slot = x ^ ((me >> 1) & 1)
        vown_ref[slot] = jnp.where(even, value[2 * x], value[2 * x + 1]).astype(BF16)
        vsend_ref[slot] = jnp.where(even, value[2 * x + 1], value[2 * x]).astype(BF16)


def total_of(refs):
    value = refs[0][...].astype(F32)
    for ref in refs[1:]:
        value = value + ref[...].astype(F32)
    return value


def halve_kernel(keep_ref, got_ref, low_ref, high_ref):
    half = low_ref.shape[0]
    low_ref[...] = (keep_ref[:half].astype(F32) + got_ref[:half].astype(F32)).astype(BF16)
    high_ref[...] = (keep_ref[half:].astype(F32) + got_ref[half:].astype(F32)).astype(BF16)


def core_high_kernel(own_ref, got_ref, high_ref):
    half = high_ref.shape[0]
    high_ref[...] = (own_ref[half:].astype(F32) + got_ref[...].astype(F32)).astype(BF16)


def core_low_kernel(own_ref, core_ref, got_ref, low_ref, high_ref):
    half = low_ref.shape[0]
    total = own_ref[: 2 * half].astype(F32) + core_ref[...].astype(F32) + got_ref[...].astype(F32)
    low_ref[...] = total[:half].astype(BF16)
    high_ref[...] = total[half:].astype(BF16)


def halve_core_kernel(keep_ref, got_ref, vkeep_ref, vgot_ref, low_ref, vlow_ref, send_ref):
    half = low_ref.shape[0]
    low_ref[...] = (keep_ref[:half].astype(F32) + got_ref[:half].astype(F32)).astype(BF16)
    parts = [keep_ref[half + k].astype(F32) + got_ref[half + k].astype(F32) for k in range(half)]
    vector = total_of((vkeep_ref, vgot_ref))
    vlow_ref[...] = vector.astype(BF16)
    send_ref[...] = rows_of(*parts, vector[0], vector[1]).astype(BF16)


def halve_round_kernel(tuned, keep_ref, vkeep_ref, got_ref, low_ref, vlow_ref, send_ref):
    half, cw = low_ref.shape[:2]
    rows = vkeep_ref.shape[1]
    got = got_ref[...].astype(F32)
    parts = [keep_ref[k].astype(F32) + got[k * cw : (k + 1) * cw] for k in range(2 * half)]
    for k in range(half):
        low_ref[k] = parts[k].astype(BF16)
    got0, got1 = (got[2 * half * cw + k * rows : 2 * half * cw + (k + 1) * rows] for k in range(2))
    keep0, keep1 = vkeep_ref[0].astype(F32), vkeep_ref[1].astype(F32)
    even = (my_index(tuned) & 1) == 0
    low = keep0 + jnp.where(even, got0, got1)
    vlow_ref[0] = low.astype(BF16)
    send_ref[...] = rows_of(*parts[half:], jnp.where(even, keep1 + got1, low)).astype(BF16)


def quarter_vector_kernel(keep_ref, vkeep_ref, got_ref, *out_refs):
    cw = keep_ref.shape[1]
    got = got_ref[...].astype(F32)
    vector = vkeep_ref[0].astype(F32) + got[4 * cw :]
    for k, ref in enumerate(out_refs):
        ref[...] = rows_of(keep_ref[k].astype(F32) + got[k * cw : (k + 1) * cw], vector).astype(BF16)


def finish_kernel(
    a_ref, b_ref, c_ref, d_ref, ffn_ref, ffn_got_ref,
    q_ref, kv_ref, red_ref, proj_ref, up_ref, down_ref, vm_ref, vh_ref,
):
    total = total_of((a_ref, b_ref, c_ref, d_ref))
    cw, width = red_ref.shape
    rn = q_ref.shape[1]
    red_ref[...] = total[:cw, :width]
    unit = [total[:cw, width + k * rn : width + (k + 1) * rn] for k in range(4)]
    q_ref[...] = unit[0]
    kv_ref[...] = rows_of(unit[1], unit[2]).T
    proj_ref[...] = unit[3]
    vector = unfold_rows(total[cw:], rn)
    vm_ref[...] = vector[: vm_ref.shape[0], :rn]
    vh_ref[...] = vector[: vh_ref.shape[0], rn:]
    total = total_of((ffn_ref, ffn_got_ref))[0]
    columns = [
        lanes(total[:, 128 * k : 128 * (k + 1)], total[:, 512 + REST * k : 512 + REST * (k + 1)]) for k in range(4)
    ]
    down_ref[...] = lanes(*columns[:2])
    up_ref[...] = rows_of(*columns[2:])


def call(kernel, inputs, outputs, scratch=(), scalars=0, limit=24, flops=0, moved=0, aliases={}):
    vmem = pl.BlockSpec(memory_space=pltpu.VMEM)
    smem = pl.BlockSpec(memory_space=pltpu.SMEM)
    return pl.pallas_call(
        kernel,
        out_shape=[jax.ShapeDtypeStruct(shape, kind) for shape, kind in outputs],
        in_specs=[smem] * scalars + [vmem] * (len(inputs) - scalars),
        out_specs=[vmem] * len(outputs),
        scratch_shapes=[pltpu.VMEM(shape, kind) for shape, kind in scratch],
        input_output_aliases=aliases,
        compiler_params=pltpu.CompilerParams(vmem_limit_bytes=limit * 2**20),
        cost_estimate=pl.CostEstimate(flops=flops, bytes_accessed=moved, transcendentals=0),
    )(*inputs)


def after(value, *others):
    return lax.optimization_barrier((value, *others))[0]


def on_device(
    mesh_shape,
    tokens, cotangent, img_rows, img_cols,
    q_weight, kv_weight, reduce_weight, proj_weight, up_weight, down_weight, vec_model, vec_hidden,
):
    wide, narrow = mesh_shape
    tuned = (wide, narrow) == (PARTS_W, PARTS_N)
    capacity, width = tokens.shape
    hidden = vec_hidden.shape[1] * narrow
    cw, rn = width // PARTS_W, width // PARTS_N
    keys = capacity // 4
    piece = (cw, 2 * width)
    vpiece, gpiece = (16, 2 * width), (8, 2 * width)

    def join(*parts):
        return jnp.concatenate(parts, axis=0)

    def swap(value, mask, other=None):
        masks = (mask, mask if other is None else other)
        pairs = [(i, i ^ masks[i & 1]) for i in range(wide * narrow)]
        return lax.ppermute(value, ("wide", "narrow"), pairs)

    tokens_f32 = ((capacity, width), F32)
    tokens_low = ((capacity, width), BF16)
    x, n1, r1, chosen, live, geo = prepare(img_rows, img_cols, tokens.T)
    if tuned:
        pack_a, pack_b, pack_v = pack(
            (
                q_weight.T, kv_weight, reduce_weight.T, proj_weight.T, up_weight, down_weight.T,
                vec_model, vec_hidden,
            ),
            piece, vpiece,
        )
        line_a = [swap(pack_a, m) for m in (8, 16, 24)]
        got_b, got_v = swap(pack_b, 2, 4), swap(pack_v, 1)
        *line_a, got_b, got_v = lax.optimization_barrier((*line_a, got_b, got_v, x, n1, chosen))[:5]
        buf_a, buf_b, vecs = join(pack_a, *line_a), join(pack_b, got_b), join(pack_v, got_v)
        buf_a, buf_b = join(buf_a, swap(buf_a, 2, 4)), join(buf_b, swap(buf_b, 16))
        got = lax.optimization_barrier((swap(buf_a, 4, 2), swap(buf_b, 8), swap(vecs, 2)))
        own_a, half_b, vecs = (join(v, g) for v, g in zip((buf_a, buf_b, vecs), got))
        oth_a = swap(own_a, 1)
        rest_b = swap(half_b, 4, 2)
        oth_half_b = swap(after(half_b, oth_a), 1)
    else:
        own_a, oth_a, own_b, oth_b, vecs = gather_plain(
            q_weight, kv_weight, reduce_weight, proj_weight, up_weight, down_weight, vec_model, vec_hidden
        )

    square = (width, width)
    (
        x2, h1, patches, nk, rk, kn, q, kb, vb, p, o, wr, wq, wkv, wp, mv, hv, gy, gyt, masks,
    ) = call(
        functools.partial(attend_kernel, tuned),
        (geo, cotangent.T, x, n1, chosen, live, own_a, oth_a, vecs),
        (
            tokens_f32, tokens_low,
            ((capacity, width), BF16), ((keys, width), F32), ((keys, 1), F32), ((keys, width), BF16),
            ((capacity, width), BF16), ((HEADS * keys, width), BF16), ((HEADS * keys, width), BF16),
            ((capacity, HEADS * keys), F32), ((capacity, width), BF16),
            ((4,) + square, BF16), (square, BF16), ((2 * width, width), BF16), (square, BF16),
            ((16, width), F32), ((16, hidden), F32),
            tokens_low, ((width, capacity), BF16), ((7, capacity, 128), F32),
        ),
        scratch=(((capacity, HEADS * keys), F32),),
        scalars=1,
        flops=8 * 10**9,
    )

    if tuned:
        rest_b = after(rest_b, x2)
        own_b = join(half_b, rest_b)
        oth_b = join(oth_half_b, swap(rest_b, 1))
    padded = ((CHUNK // 128, capacity + 2 * PAD, 128), F32)
    halved = ((CHUNK // 128, capacity, 128), F32)
    chunked = ((capacity, CHUNK), F32)
    n2, r2, h2, h2t, wu, wd = call(
        functools.partial(prepare_two_kernel, tuned),
        (x2, mv, own_b),
        (
            tokens_f32, ((capacity, 1), F32), tokens_low, ((width + 16, capacity), BF16),
            ((width, hidden), BF16), ((width, hidden), BF16),
        ),
        flops=10**9,
    )
    gown_b, gsend_b, act, df, hg, wu, wd = call(
        functools.partial(ffn_kernel, tuned),
        (geo, h2, h2t, gy, gyt, masks, own_b, oth_b, hv, wu, wd),
        (
            ((SLOTS,) + piece, BF16), ((SLOTS,) + piece, BF16),
            ((capacity, hidden), BF16), ((capacity, hidden), BF16), ((16, hidden), F32),
            ((width, hidden), BF16), ((width, hidden), BF16),
        ),
        aliases={9: 5, 10: 6},
        scratch=(
            ((hidden // 128, capacity + 2 * PAD, 128), F32), padded, padded, padded, padded, padded,
            halved, halved, chunked,
            ((width + 16, hidden), F32), ((width, hidden), F32),
        ),
        scalars=1,
        flops=33 * 10**9,
    )

    dx2, mg = call(
        norm_two_back_kernel,
        (df, wu, n2, r2, gy, mv),
        (tokens_f32, ((16, width), F32)),
        scratch=(tokens_f32,),
        flops=10**9,
    )
    if tuned:
        core_high, core_low = swap(gsend_b[8:], 1), swap(gsend_b[:8], 1)
        core_high, dx2 = lax.optimization_barrier((core_high, dx2))
        (high_b,) = call(core_high_kernel, (gown_b, core_high), (((8,) + piece, BF16),))
        got_b = swap(high_b, 4, 2)
        dx2 = after(dx2, high_b)
    gp, dob, ds, bp = call(
        score_back_kernel,
        (dx2, vb, p, o, wp),
        (
            (square, F32), ((capacity, width), BF16), ((capacity, HEADS * keys), BF16), ((1, width), F32),
        ),
        scratch=(((capacity, HEADS * keys), F32),),
        flops=0,
    )

    def halve(keep, got, flops=0):
        shape = ((keep.shape[0] // 2,) + piece, BF16)
        return call(halve_kernel, (keep, got), (shape, shape), flops=flops)

    gown_a, gsend_a, dq, dpatch, vk = call(
        functools.partial(attend_back_kernel, tuned),
        (dob, ds, gp, h1, patches, nk, rk, kn, q, kb, p, wr, wkv, mv),
        (
            ((SLOTS,) + piece, BF16), ((SLOTS,) + piece, BF16), ((capacity, width), BF16), ((capacity, width), F32),
            ((8, width), F32),
        ),
        scratch=(((4,) + square, F32), (square, F32), ((2 * width, width), F32)),
        flops=0,
    )
    if tuned:
        got_a = swap(gsend_a, 1)
        low_b, high_b = call(
            core_low_kernel, (gown_b, core_low, got_b), (((4,) + piece, BF16),) * 2, flops=7*10**9
        )
        gown_a = after(gown_a, high_b)
    (mixed,) = call(mixed_kernel, (x2, act, wd, mv, masks), (((width, capacity), BF16),), flops=10**9)
    dh1, vown, vsend = call(
        functools.partial(token_back_kernel, tuned),
        (dq, dpatch, n1, chosen, wq, mg, hg, vk, bp),
        (tokens_f32, ((2,) + gpiece, BF16), ((2,) + gpiece, BF16)),
    )

    (token_grad,) = call(token_grad_kernel, (dx2, dh1, n1, r1, mv), (((width, capacity), BF16),), flops=10**9)

    if not tuned:
        grads = scatter_plain(mesh_shape, width, gown_a, gsend_a, gown_b, gsend_b, vown, vsend)
        return (mixed.T, token_grad.T) + grads

    vrows = gpiece[0]
    low_a, vlow, high_a = call(
        halve_core_kernel,
        (gown_a, got_a, vown, swap(vsend, 1)),
        (((8,) + piece, BF16), ((2,) + gpiece, BF16), ((8 * cw + 2 * vrows, 2 * width), BF16)),
    )
    got_a, got_b, mixed, token_grad = lax.optimization_barrier((swap(high_a, 4, 2), swap(high_b, 8), mixed, token_grad))
    low_a, vlow, high_a = call(
        functools.partial(halve_round_kernel, tuned),
        (low_a, vlow, got_a),
        (((4,) + piece, BF16), ((1,) + gpiece, BF16), ((4 * cw + vrows, 2 * width), BF16)),
    )
    low_b, high_b = halve(low_b, got_b)
    got_a, got_b = swap(high_a, 2, 4), swap(high_b, 16)
    near_a = list(call(quarter_vector_kernel, (low_a, vlow, got_a), (((cw + vrows, 2 * width), BF16),) * 4))
    line_a = [swap(near_a[k], 8 * k) for k in (1, 2, 3)]
    low_b, high_b = halve(low_b, got_b)
    q_grad, kv_grad, reduce_grad, proj_grad, up_grad, down_grad, vm_grad, vh_grad = call(
        finish_kernel,
        (near_a[0], *line_a, low_b, swap(high_b, 2, 4)),
        (
            ((cw, rn), F32), ((rn, 2 * cw), F32), ((cw, width), F32), ((cw, rn), F32),
            ((rn, 4 * cw), F32), ((cw, width), F32), ((11, rn), F32), ((11, width), F32),
        ),
    )
    return (
        mixed.T, token_grad.T, q_grad.T, kv_grad, reduce_grad.T, proj_grad.T, up_grad, down_grad.T, vm_grad, vh_grad,
    )


def gather_plain(q, kv, reduce, proj, up, down, vec_model, vec_hidden):
    def whole(value):
        rows = lax.all_gather(value, "narrow", axis=0, tiled=True)
        return lax.all_gather(rows, "wide", axis=1, tiled=True).T

    q, kv, reduce, proj, up, down = (whole(v) for v in (q, kv, reduce, proj, up, down))
    width = q.shape[0]
    cw, rn = width // PARTS_W, width // PARTS_N

    def pieces(turned, blocks):
        split = turned.reshape(PARTS_W, blocks, cw, PARTS_N, -1)
        return split.transpose(0, 3, 2, 1, 4).reshape(PARTS_W, PARTS_N, cw, -1)

    def slots(value, mixed=False):
        value = value.reshape(2, 2, 2, 2, 2, cw, -1)
        orders = ((2, 1, 0, 3), (3, 1, 0, 2)) if mixed else ((2, 3, 0, 1), (3, 2, 0, 1))
        return tuple(
            value[:, :, :, :, core].transpose(*order, 4, 5).reshape(SLOTS, cw, -1) for core, order in enumerate(orders)
        )

    a = jnp.concatenate([pieces(reduce, 1), pieces(q, 1), pieces(kv, 2), pieces(proj, 1)], axis=-1)
    columns = pieces(down, 1).reshape(PARTS_W, PARTS_N, cw, 2, RUN)
    columns = [columns[..., e, :] for e in range(2)]
    halves = up.T.reshape(PARTS_N, 2, cw, PARTS_W, RUN).transpose(1, 3, 0, 2, 4)
    columns += [halves[0], halves[1]]
    b = jnp.concatenate([c[..., :128] for c in columns] + [c[..., 128:] for c in columns], axis=-1)
    vm = lax.all_gather(vec_model, "narrow", axis=1, tiled=True)
    vh = lax.all_gather(vec_hidden, "narrow", axis=1, tiled=True)
    both = jnp.concatenate([vm.reshape(11, PARTS_N, rn), vh.reshape(11, PARTS_N, width)], axis=-1)
    vecs = jnp.pad(both.transpose(1, 0, 2), ((0, 0), (0, 5), (0, 3 * rn)))
    return (*slots(a), *slots(b, True), vecs)


def scatter_plain(mesh_shape, width, gown_a, gsend_a, gown_b, gsend_b, vown, vsend):
    cw, rn = width // PARTS_W, width // PARTS_N

    def devices(own, send, mixed=False):
        orders = ((2, 1, 0, 3), (3, 1, 0, 2)) if mixed else ((2, 3, 0, 1), (3, 2, 0, 1))
        parts = []
        for value, order in zip((own, send), orders):
            back = sorted(range(4), key=lambda k: order[k])
            parts.append(value.reshape(2, 2, 2, 2, cw, -1).transpose(*back, 4, 5))
        return jnp.stack(parts, axis=4).reshape(PARTS_W, PARTS_N, cw, -1)

    def natural(value, blocks):
        split = value.reshape(PARTS_W, PARTS_N, cw, blocks, -1).transpose(0, 3, 2, 1, 4)
        return split.reshape(PARTS_W * blocks * cw, -1).T

    def share(value):
        columns = lax.psum_scatter(value.astype(BF16), "wide", scatter_dimension=1, tiled=True)
        return lax.psum_scatter(columns, "narrow", scatter_dimension=0, tiled=True).astype(F32)

    a = devices(gown_a, gsend_a)
    b = devices(gown_b, gsend_b, True)
    reduce = natural(a[..., :width], 1)
    q = natural(a[..., width : width + rn], 1)
    kv = natural(a[..., width + rn : width + 3 * rn], 2)
    proj = natural(a[..., width + 3 * rn :], 1)
    columns = [
        jnp.concatenate([b[..., 128 * k : 128 * (k + 1)], b[..., 512 + REST * k : 512 + REST * (k + 1)]], axis=-1)
        for k in range(4)
    ]
    down = natural(jnp.concatenate(columns[:2], axis=-1), 1)
    up = jnp.stack(columns[2:]).transpose(2, 0, 3, 1, 4).reshape(width, -1)
    vectors = jnp.stack([vown, vsend], axis=1).reshape(PARTS_N, 8, -1)
    beside = vectors[..., 5 * rn :]
    beside = jnp.concatenate([beside[:, :3], beside[:, 3:6, : 2 * rn]], axis=-1)
    vectors = jnp.concatenate([vectors[..., : 5 * rn], beside], axis=1).transpose(1, 0, 2)
    vm = vectors[..., :rn].reshape(11, width)
    vh = vectors[..., rn : rn + width].reshape(11, PARTS_N * width)

    def share_vector(value):
        total = lax.psum(value.astype(BF16), "wide")
        return lax.psum_scatter(total, "narrow", scatter_dimension=1, tiled=True).astype(F32)

    return tuple(share(v) for v in (q, kv, reduce, proj, up, down)) + (share_vector(vm), share_vector(vh))


def solution(mesh):
    both, rows, weight, vector = P(("wide", "narrow"), None), P(("wide", "narrow")), P("narrow", "wide"), P(None, "narrow")
    return jax.shard_map(
        functools.partial(on_device, (mesh.shape["wide"], mesh.shape["narrow"])),
        mesh=mesh,
        in_specs=(both, both, rows, rows) + (weight,) * 6 + (vector,) * 2,
        out_specs=(both, both) + (weight,) * 6 + (vector,) * 2,
        check_vma=False,
    )
```
